32 devices in a mesh: fsdp: 4 (over y, x), seq: 8 (over z, core).
Axes of the slice: x: 2, y: 2, z: 4, core: 2. Of those that a mesh axis runs over, the one named last changes fastest.
Arguments:
- tokens: bfloat16 [16384, 1024], P(('fsdp', 'seq')), may hold values from -6 to 6
- cotangent: bfloat16 [16384, 1024], P(('fsdp', 'seq')), may hold values from -6 to 6
- segment_ids: int32 [16384], P(('fsdp', 'seq')), may hold values from 0 to 1, as said below
- valid: int32 [16384], P(('fsdp', 'seq')), may hold values from 0 to 1, as said below
- project_in: float32 [1024, 3072], P(('fsdp', 'seq')), may hold values from -0.1875 to 0.1875
- project_out: float32 [1024, 1024], P(('fsdp', 'seq')), may hold values from -4 to 4
- hidden_up: float32 [1024, 4096], P(('fsdp', 'seq')), may hold values from -0.1875 to 0.1875
- hidden_down: float32 [4096, 1024], P(('fsdp', 'seq')), may hold values from -0.09375 to 0.09375
- gains_biases: float32 [14, 1024], P(None, ('fsdp', 'seq')), may hold values from -0.9 to 1.45
- moment_in: float32 [1024, 3072], P(('fsdp', 'seq')), may hold values from -56 to 56
- moment_out: float32 [1024, 1024], P(('fsdp', 'seq')), may hold values from -6 to 6
- moment_up: float32 [1024, 4096], P(('fsdp', 'seq')), may hold values from -20 to 20
- moment_down: float32 [4096, 1024], P(('fsdp', 'seq')), may hold values from -40 to 40
- moment_gains: float32 [14, 1024], P(None, ('fsdp', 'seq')), may hold values from -64 to 64
- square_in: float32 [1024, 3072], P(('fsdp', 'seq')), may hold values from 7.0144 to 28.0576
- square_out: float32 [1024, 1024], P(('fsdp', 'seq')), may hold values from 0.04704 to 0.18816
- square_up: float32 [1024, 4096], P(('fsdp', 'seq')), may hold values from 0.9864 to 3.9456
- square_down: float32 [4096, 1024], P(('fsdp', 'seq')), may hold values from 3.9456 to 15.7824
- square_gains: float32 [14, 1024], P(None, ('fsdp', 'seq')), may hold values from 10.96 to 43.84
Outputs:
- block_output: bfloat16 [16384, 1024], P(('fsdp', 'seq'))
- input_grad: float32 [16384, 1024], P(('fsdp', 'seq'))
- new_project_in: float32 [1024, 3072], P(('fsdp', 'seq'))
- new_project_out: float32 [1024, 1024], P(('fsdp', 'seq'))
- new_hidden_up: float32 [1024, 4096], P(('fsdp', 'seq'))
- new_hidden_down: float32 [4096, 1024], P(('fsdp', 'seq'))
- new_gains: float32 [14, 1024], P(None, ('fsdp', 'seq'))
- new_moment_in: float32 [1024, 3072], P(('fsdp', 'seq'))
- new_moment_out: float32 [1024, 1024], P(('fsdp', 'seq'))
- new_moment_up: float32 [1024, 4096], P(('fsdp', 'seq'))
- new_moment_down: float32 [4096, 1024], P(('fsdp', 'seq'))
- new_moment_gains: float32 [14, 1024], P(None, ('fsdp', 'seq'))
- new_square_in: float32 [1024, 3072], P(('fsdp', 'seq'))
- new_square_out: float32 [1024, 1024], P(('fsdp', 'seq'))
- new_square_up: float32 [1024, 4096], P(('fsdp', 'seq'))
- new_square_down: float32 [4096, 1024], P(('fsdp', 'seq'))
- new_square_gains: float32 [14, 1024], P(None, ('fsdp', 'seq'))
- down_bias_gradient: float32 [1024], P(('fsdp', 'seq'))
The draws below stay inside these ranges and needn't reach their ends.
Inputs may be any that keep to these rules, and one draw needn't show every extreme that they name: `segment_ids`: each stream of 4096 consecutive tokens holds 2 images in order, each 1370 consecutive tokens, with padding between and around them; ids never fall within a stream and start again at 0 in the next; padding carries the id of the image before it, 0 before the first. `valid`: 1 exactly on the tokens of the images.
All inputs are finite; a program needn't handle non-finite values.
Results may differ from the reference program's by a relative error of at most 0.012.
The reference program's roundings to bfloat16 on the way count: a program that leaves them out, or rounds other values in their place, can miss the bound.
Values may be sent and summed in bfloat16 or wider, within the bound.
No kernel may reach another device: no remote copies, remote signals or barrier semaphores. Data moves between devices by JAX's collectives and lax.ppermute only.
A program may use at most 192 MiB of HBM per device.

```python
import math
from functools import partial
import jax
import jax.numpy as jnp
from jax import lax

D = 1024
FF = 4096
HEADS = 16
HEAD_DIM = 64
IMG_LEN = 1370
STEP = 10
STREAM = 4096
STREAMS = 4
IMGS = 2
TOKENS = 16384
VALID_ALL = 10960
VEC = 14


def stream_layout(key):

    def one_stream(stream_key):
        cuts = jnp.sort(jax.random.randint(stream_key, (IMGS,), 0, STREAM - IMGS * IMG_LEN + 1))
        starts = cuts + jnp.arange(IMGS, dtype=jnp.int32) * IMG_LEN
        position = jnp.arange(STREAM, dtype=jnp.int32)
        begun = (position[:, None] >= starts[None, :]).astype(jnp.int32)
        inside = begun * (position[:, None] < starts[None, :] + IMG_LEN).astype(jnp.int32)
        image_ids = jnp.maximum(jnp.sum(begun, axis=1) - 1, 0)
        return (image_ids.astype(jnp.int32), jnp.sum(inside, axis=1).astype(jnp.int32))
    stream_keys = jax.random.split(key, STREAMS)
    image_ids, inside = jax.vmap(one_stream)(stream_keys)
    return (image_ids.reshape(TOKENS), inside.reshape(TOKENS))


def draw_segment_ids(key, part):
    return stream_layout(key)[0]


def draw_valid(key, part):
    return stream_layout(key)[1]


def draw_gains_biases(key, part):
    key = jax.random.fold_in(key, 7)
    noise = jnp.clip(jax.random.normal(key, (VEC, D), jnp.float32), -3.0, 3.0)
    rows = jnp.arange(VEC)
    is_gain = (rows == 0) | (rows == 5) | (rows == 6) | (rows == 9)
    return jnp.where(is_gain[:, None], 1.0 + 0.15 * noise, 0.3 * noise).astype(jnp.float32)


def steps_of(rng, shape, cuts, smallest, largest):
    level, own = 1.0, jax.random.fold_in(rng, 6)
    for axis_at, parts in cuts:
        heights = jnp.exp(jax.random.uniform(jax.random.fold_in(own, axis_at), (parts,), jnp.float32, smallest / len(cuts), largest / len(cuts)))
        level = level * jnp.repeat(heights, shape[axis_at] // parts).reshape([-1 if axis == axis_at else 1 for axis in range(len(shape))])
    return level


def scatter_about(own_key, shape, scale, reach, shards=(), kind=jnp.bfloat16):
    drawn = scale * jax.random.normal(own_key, shape, jnp.float32)
    if shards:
        drawn = drawn * steps_of(own_key, shape, shards, -0.22, 0.18)
    return jnp.clip(drawn, -reach, reach).astype(kind)


def setup_inputs(seed: int = 0) -> dict:
    arg_keys = jax.random.split(jax.random.key(seed), 20)
    tokens = scatter_about(arg_keys[0], (TOKENS, D), 1.0, 6.0, ((0, 32),))
    cotangent = scatter_about(arg_keys[1], (TOKENS, D), 1.0, 6.0, ((0, 32),))
    segment_ids = draw_segment_ids(jax.random.fold_in(arg_keys[19], 71), 0)
    valid = draw_valid(jax.random.fold_in(arg_keys[19], 71), 0)
    project_in = scatter_about(arg_keys[4], (D, 3 * D), D ** -0.5, 0.1875, ((0, 32),), jnp.float32)
    project_out = scatter_about(arg_keys[5], (D, D), (max(1, 4 * D // IMG_LEN)) ** -0.5, 4.0, ((0, 32),), jnp.float32)
    hidden_up = scatter_about(arg_keys[6], (D, FF), D ** -0.5, 0.1875, ((0, 32),), jnp.float32)
    hidden_down = scatter_about(arg_keys[7], (FF, D), FF ** -0.5, 0.09375, ((0, 32),), jnp.float32)
    gains_biases = draw_gains_biases(jax.random.fold_in(arg_keys[19], 71), 0)
    moment_in = scatter_about(arg_keys[9], (D, 3 * D), (0.111 * 0.8 * VALID_ALL ** 0.5), 56.0, ((0, 32),), jnp.float32)
    moment_out = scatter_about(arg_keys[10], (D, D), (0.111 * 1.4 * (3.0 / IMG_LEN) ** 0.5 * VALID_ALL ** 0.5), 6.0, ((0, 32),), jnp.float32)
    moment_up = scatter_about(arg_keys[11], (D, FF), (0.111 * 0.3 * VALID_ALL ** 0.5), 20.0, ((0, 32),), jnp.float32)
    moment_down = scatter_about(arg_keys[12], (FF, D), (0.111 * 0.6 * VALID_ALL ** 0.5), 40.0, ((0, 32),), jnp.float32)
    moment_gains = scatter_about(arg_keys[13], (VEC, D), (0.111 * VALID_ALL ** 0.5), 64.0, ((1, 32),), jnp.float32)
    square_in = jnp.clip(jnp.exp(math.log(28.0576) - 1.3862944 * jax.random.uniform(arg_keys[14], (D, 3 * D), jnp.float32) ** steps_of(arg_keys[14], (D, 3 * D), ((0, 32),), -0.2, 0.2)), 7.0144, 28.0576)
    square_out = jnp.clip(jnp.exp(math.log(0.18816) - 1.3862944 * jax.random.uniform(arg_keys[15], (D, D), jnp.float32) ** steps_of(arg_keys[15], (D, D), ((0, 32),), -0.2, 0.2)), 0.04704, 0.18816)
    square_up = jnp.clip(jnp.exp(math.log(3.9456) - 1.3862944 * jax.random.uniform(arg_keys[16], (D, FF), jnp.float32) ** steps_of(arg_keys[16], (D, FF), ((0, 32),), -0.2, 0.2)), 0.9864, 3.9456)
    square_down = jnp.clip(jnp.exp(math.log(15.7824) - 1.3862944 * jax.random.uniform(arg_keys[17], (FF, D), jnp.float32) ** steps_of(arg_keys[17], (FF, D), ((0, 32),), -0.2, 0.2)), 3.9456, 15.7824)
    square_gains = jnp.clip(jnp.exp(math.log(43.84) - 1.3862944 * jax.random.uniform(arg_keys[18], (VEC, D), jnp.float32) ** steps_of(arg_keys[18], (VEC, D), ((1, 32),), -0.2, 0.2)), 10.96, 43.84)
    return {"tokens": tokens, "cotangent": cotangent, "segment_ids": segment_ids, "valid": valid, "project_in": project_in, "project_out": project_out, "hidden_up": hidden_up, "hidden_down": hidden_down, "gains_biases": gains_biases, "moment_in": moment_in, "moment_out": moment_out, "moment_up": moment_up, "moment_down": moment_down, "moment_gains": moment_gains, "square_in": square_in, "square_out": square_out, "square_up": square_up, "square_down": square_down, "square_gains": square_gains}


@jax.custom_vjp
def low(v):
    return lax.optimization_barrier(v.astype(jnp.bfloat16)).astype(jnp.float32)

@jax.custom_vjp
def low_back(v):
    return v

def low_keep(v):
    return (low(v), None)

def low_pass(kept, grad):
    return (grad,)

def back_keep(v):
    return (v, None)

def back_low(kept, grad):
    return (low(grad),)
low.defvjp(low_keep, low_pass)
low_back.defvjp(back_keep, back_low)

def layer_norm(values, gain, shift):
    average = lax.optimization_barrier(jnp.mean(values, axis=-1, keepdims=True))
    centered = values - average
    variance = lax.optimization_barrier(jnp.mean(centered * centered, axis=-1, keepdims=True))
    return centered * lax.rsqrt(variance + 1e-06) * gain + shift

def matmul(left, right):
    return jnp.dot(left, right, precision=lax.Precision.HIGHEST, preferred_element_type=jnp.float32)

def adamw(param, moment, square, grad, rate, decay):
    new_moment = 0.9 * moment + 0.1 * grad
    new_square = 0.999 * square + 0.001 * grad * grad
    corrected = new_moment / (1.0 - 0.9 ** STEP)
    scaled = jnp.sqrt(new_square / (1.0 - 0.999 ** STEP)) + 1e-08
    return (param - rate * (corrected / scaled + decay * param), new_moment, new_square)

def layer_forward(inputs, project_in, project_out, hidden_up, hidden_down, gains_biases, starts, slot, keep):
    weight_in = low(project_in)
    weight_out = low(project_out)
    weight_up = low(hidden_up)
    weight_down = low(hidden_down)
    vectors = low(gains_biases)
    bias_in = jnp.concatenate([vectors[2], jnp.zeros_like(vectors[2]), vectors[3]])
    normed_one = low(layer_norm(inputs, vectors[0], vectors[1]))
    mixed = low(low_back(matmul(normed_one, weight_in) + bias_in))
    heads = mixed.reshape(TOKENS, 3, HEADS, HEAD_DIM)

    def one_image(start):
        part = lax.dynamic_slice_in_dim(heads, start, IMG_LEN, 0)
        scores = jnp.einsum('qhd,khd->hqk', part[:, 0], part[:, 1], precision=lax.Precision.HIGHEST)
        scores = low_back(scores * HEAD_DIM ** (-0.5))
        top = lax.optimization_barrier(jnp.max(scores, axis=-1, keepdims=True))
        weights = jnp.exp(scores - top)
        probs = low(weights / lax.optimization_barrier(jnp.sum(weights, axis=-1, keepdims=True)))
        return jnp.einsum('hqk,khd->qhd', probs, part[:, 2], precision=lax.Precision.HIGHEST)
    per_image = lax.map(jax.checkpoint(one_image), starts)
    attended = per_image.reshape(-1, HEADS, HEAD_DIM)[slot] * keep
    attended = low(low_back(attended.reshape(TOKENS, D)))
    projected = low_back(matmul(attended, weight_out) + vectors[4])
    second = inputs + vectors[5] * projected
    normed_two = low(layer_norm(second, vectors[6], vectors[7]))
    upward = low_back(matmul(normed_two, weight_up) + vectors[10:].reshape(-1))
    active = low(jax.nn.gelu(upward, approximate=False))
    branch = low_back(matmul(active, weight_down) + vectors[8])
    return second + vectors[9] * branch

def reference(tokens, cotangent, segment_ids, valid, project_in, project_out, hidden_up, hidden_down, gains_biases, moment_in, moment_out, moment_up, moment_down, moment_gains, square_in, square_out, square_up, square_down, square_gains):
    position = jnp.arange(STREAM, dtype=jnp.int32)
    images = jnp.arange(IMGS, dtype=jnp.int32)
    seg_grid = segment_ids.reshape(STREAMS, STREAM)
    valid_grid = valid.reshape(STREAMS, STREAM)
    found = (seg_grid[:, :, None] == images[None, None, :]) & (valid_grid[:, :, None] == 1)
    first = lax.optimization_barrier(jnp.min(jnp.where(found, position[None, :, None], STREAM), axis=1)).astype(jnp.int32)
    offsets = (jnp.arange(STREAMS, dtype=jnp.int32) * STREAM)[:, None]
    starts = (first + offsets).reshape(-1).astype(jnp.int32)
    token = jnp.arange(TOKENS, dtype=jnp.int32)
    image_of = (segment_ids + token // STREAM * IMGS).astype(jnp.int32)
    slot = jnp.clip(image_of * IMG_LEN + token - starts[image_of], 0, STREAMS * IMGS * IMG_LEN - 1).astype(jnp.int32)
    keep = valid.astype(jnp.float32)[:, None, None]
    forward = partial(layer_forward, starts=starts, slot=slot, keep=keep)
    output, backward = jax.vjp(forward, tokens.astype(jnp.float32), project_in, project_out, hidden_up, hidden_down, gains_biases)
    seed_grad = cotangent.astype(jnp.float32) * valid.astype(jnp.float32)[:, None]
    input_grad, grad_in, grad_out, grad_up, grad_down, grad_gains = backward(seed_grad)
    rate_out = max(1, 4 * D // IMG_LEN) ** (-0.5)
    new_in, new_moment_in, new_square_in = adamw(project_in, moment_in, square_in, grad_in, D ** (-0.5), 0.04)
    new_out, new_moment_out, new_square_out = adamw(project_out, moment_out, square_out, grad_out, rate_out, 0.04)
    new_up, new_moment_up, new_square_up = adamw(hidden_up, moment_up, square_up, grad_up, D ** (-0.5), 0.04)
    new_down, new_moment_down, new_square_down = adamw(hidden_down, moment_down, square_down, grad_down, FF ** (-0.5), 0.04)
    new_gains, new_moment_gains, new_square_gains = adamw(gains_biases, moment_gains, square_gains, grad_gains, 0.2, 0.0)
    return (output.astype(jnp.bfloat16), input_grad, new_in, new_out, new_up, new_down, new_gains, new_moment_in, new_moment_out, new_moment_up, new_moment_down, new_moment_gains, new_square_in, new_square_out, new_square_up, new_square_down, new_square_gains, grad_gains[8])
```

```python
import jax
import jax.numpy as jnp
from jax import lax
from jax.experimental import pallas as pl
from jax.experimental.pallas import tpu as pltpu
from jax.sharding import PartitionSpec as P

D = 1024
FF = 4096
HEADS = 16
HEAD_DIM = 64
IMG_LEN = 1370
WINDOW = 1408
TILE = 352
VMEM_BYTES = 56 * 1024 * 1024
STEP = 10


masked_score = -1e30


def layer_norm(values, gain, shift):
    average = jnp.mean(values, axis=-1, keepdims=True)
    centered = values - average
    variance = jnp.mean(centered * centered, axis=-1, keepdims=True)
    return centered * lax.rsqrt(variance + 1e-06) * gain + shift


def exact_gelu(values):
    return jax.nn.gelu(values, approximate=False)


def plain_product(left, right):
    return jnp.dot(left, right, preferred_element_type=jnp.float32)


def inner_rows(left, right):
    return lax.dot_general(
        left, right, (((0,), (0,)), ((), ())), preferred_element_type=jnp.float32
    )


def inner_cols(left, right):
    return lax.dot_general(
        left, right, (((1,), (1,)), ((), ())), preferred_element_type=jnp.float32
    )


def adamw(param, moment, square, grad, rate, decay):
    new_moment = 0.9 * moment + 0.1 * grad
    new_square = 0.999 * square + 0.001 * grad * grad
    corrected = new_moment / (1.0 - 0.9**STEP)
    scaled = jnp.sqrt(new_square / (1.0 - 0.999**STEP)) + 1e-08
    return (param - rate * (corrected / scaled + decay * param), new_moment, new_square)


def head_lanes(shape):
    return lax.broadcasted_iota(jnp.int32, shape, 1) // HEAD_DIM


def window_of(starts_ref, image, length):
    start = starts_ref[image]
    base = jnp.clip(start // 16 * 16, 0, length - WINDOW)
    return (pl.multiple_of(base, 16), start - base)


def image_mask(position, offset):
    return (position >= offset) & (position < offset + IMG_LEN)


def attend_kernel(starts_ref, q_ref, k_ref, v_ref, wide_ref, out_ref, log_ref):
    image, tile = pl.program_id(0), pl.program_id(1)
    length, lanes = q_ref.shape
    base, offset = window_of(starts_ref, image, length)
    rows = pl.ds(pl.multiple_of(base + tile * TILE, 16), TILE)

    @pl.when((image == 0) & (tile == 0))
    def clear():
        wide_ref[...] = jnp.zeros_like(wide_ref)
        out_ref[...] = jnp.zeros_like(out_ref)
        log_ref[...] = jnp.zeros_like(log_ref)

    query = q_ref[rows, :].astype(jnp.float32) * HEAD_DIM ** (-0.5)
    keys = k_ref[pl.ds(base, WINDOW), :]
    values = v_ref[pl.ds(base, WINDOW), :]
    key_ok = image_mask(lax.broadcasted_iota(jnp.int32, (1, WINDOW), 1), offset)
    bias = jnp.where(key_ok, 0.0, masked_score)
    row_ok = image_mask(lax.broadcasted_iota(jnp.int32, (TILE, 1), 0) + tile * TILE, offset)
    head_of = head_lanes((TILE, lanes))
    total_out = jnp.zeros((TILE, lanes), jnp.float32)
    total_log = jnp.zeros((TILE, lanes), jnp.float32)
    for head in range(lanes // HEAD_DIM):
        mine = head_of == head
        part = jnp.where(mine, query, 0.0).astype(jnp.bfloat16)
        scores = inner_cols(part, keys) + bias
        top = jnp.max(scores, axis=1, keepdims=True)
        weights = jnp.exp(scores - top)
        total = jnp.sum(weights, axis=1, keepdims=True)
        probs = (weights * (1.0 / total)).astype(jnp.bfloat16)
        total_out = jnp.where(mine, plain_product(probs, values), total_out)
        total_log = jnp.where(mine, top + jnp.log(total), total_log)
    merged = jnp.where(row_ok, total_out, wide_ref[rows, :])
    wide_ref[rows, :] = merged
    out_ref[rows, :] = merged.astype(jnp.bfloat16)
    log_ref[rows, :] = jnp.where(row_ok, total_log, log_ref[rows, :])


def attend(starts, query, keys, values):
    length, lanes = query.shape
    whole = pl.BlockSpec((length, lanes), lambda image, tile, starts: (0, 0))
    wide = jax.ShapeDtypeStruct((length, lanes), jnp.float32)
    images = length // IMG_LEN
    return pl.pallas_call(
        attend_kernel,
        grid_spec=pltpu.PrefetchScalarGridSpec(
            num_scalar_prefetch=1,
            grid=(images, WINDOW // TILE),
            in_specs=[whole] * 3,
            out_specs=[whole] * 3,
        ),
        out_shape=(wide, jax.ShapeDtypeStruct((length, lanes), jnp.bfloat16), wide),
        compiler_params=pltpu.CompilerParams(
            vmem_limit_bytes=VMEM_BYTES, dimension_semantics=("arbitrary", "arbitrary")
        ),
        cost_estimate=pl.CostEstimate(
            flops=images * WINDOW * WINDOW * lanes * 8,
            bytes_accessed=length * lanes * 16,
            transcendentals=images * WINDOW * WINDOW * lanes // HEAD_DIM,
        ),
        name="attend_forward",
    )(starts, query, keys, values)


def attend_back_kernel(
    starts_ref, q_ref, k_ref, v_ref, wide_ref, log_ref, go_ref, grad_ref, key_acc, value_acc
):
    image, tile = pl.program_id(0), pl.program_id(1)
    length, lanes = q_ref.shape
    base, offset = window_of(starts_ref, image, length)
    rows = pl.ds(pl.multiple_of(base + tile * TILE, 16), TILE)
    window = pl.ds(base, WINDOW)

    @pl.when((image == 0) & (tile == 0))
    def clear():
        grad_ref[...] = jnp.zeros_like(grad_ref)

    @pl.when(tile == 0)
    def clear_sums():
        key_acc[...] = jnp.zeros_like(key_acc)
        value_acc[...] = jnp.zeros_like(value_acc)

    query = q_ref[rows, :].astype(jnp.float32) * HEAD_DIM ** (-0.5)
    keys = k_ref[window, :]
    values = v_ref[window, :]
    key_ok = image_mask(lax.broadcasted_iota(jnp.int32, (1, WINDOW), 1), offset)
    bias = jnp.where(key_ok, 0.0, masked_score)
    row_ok = image_mask(lax.broadcasted_iota(jnp.int32, (TILE, 1), 0) + tile * TILE, offset)
    head_of = head_lanes((TILE, lanes))
    grad_out = jnp.where(row_ok, go_ref[rows, :].astype(jnp.float32), 0.0)
    centre_parts = grad_out * wide_ref[rows, :]
    logs = jnp.where(row_ok, log_ref[rows, :], -masked_score)
    query_grad = jnp.zeros((TILE, lanes), jnp.float32)
    for head in range(lanes // HEAD_DIM):
        mine = head_of == head
        part = jnp.where(mine, query, 0.0).astype(jnp.bfloat16)
        grad_part = jnp.where(mine, grad_out, 0.0).astype(jnp.bfloat16)
        centre = jnp.sum(jnp.where(mine, centre_parts, 0.0), axis=1, keepdims=True)
        log_total = jnp.max(jnp.where(mine, logs, masked_score), axis=1, keepdims=True)
        probs = jnp.exp(inner_cols(part, keys) + bias - log_total)
        grad_probs = inner_cols(grad_part, values)
        grad_scores = (probs * (grad_probs - centre)).astype(jnp.bfloat16)
        query_grad = jnp.where(mine, plain_product(grad_scores, keys), query_grad)
        key_acc[...] += inner_rows(part, grad_scores)
        value_acc[...] += inner_rows(grad_part, probs.astype(jnp.bfloat16))
    old = grad_ref[rows, 0:lanes].astype(jnp.float32)
    merged = jnp.where(row_ok, query_grad * HEAD_DIM ** (-0.5), old)
    grad_ref[rows, 0:lanes] = merged.astype(jnp.bfloat16)

    @pl.when(tile == pl.num_programs(1) - 1)
    def flush():
        inside = image_mask(lax.broadcasted_iota(jnp.int32, (WINDOW, 1), 0), offset)
        for slot, sums in ((1, key_acc), (2, value_acc)):
            columns = slice(slot * lanes, (slot + 1) * lanes)
            old = grad_ref[window, columns].astype(jnp.float32)
            merged = jnp.where(inside, sums[...].T, old)
            grad_ref[window, columns] = merged.astype(jnp.bfloat16)


def attend_back(starts, query, keys, values, wide, logs, grad_out):
    length, lanes = query.shape
    whole = pl.BlockSpec((length, lanes), lambda image, tile, starts: (0, 0))
    images = length // IMG_LEN
    return pl.pallas_call(
        attend_back_kernel,
        grid_spec=pltpu.PrefetchScalarGridSpec(
            num_scalar_prefetch=1,
            grid=(images, WINDOW // TILE),
            in_specs=[whole] * 6,
            out_specs=pl.BlockSpec((length, 3 * lanes), lambda image, tile, starts: (0, 0)),
            scratch_shapes=[pltpu.VMEM((lanes, WINDOW), jnp.float32)] * 2,
        ),
        out_shape=jax.ShapeDtypeStruct((length, 3 * lanes), jnp.bfloat16),
        compiler_params=pltpu.CompilerParams(
            vmem_limit_bytes=VMEM_BYTES, dimension_semantics=("arbitrary", "arbitrary")
        ),
        cost_estimate=pl.CostEstimate(
            flops=images * WINDOW * WINDOW * lanes * 20,
            bytes_accessed=length * lanes * 22,
            transcendentals=images * WINDOW * WINDOW * lanes // HEAD_DIM,
        ),
        name="attend_backward",
    )(starts, query, keys, values, wide, logs, grad_out)


def norm_mix_kernel(x_ref, gain_ref, shift_ref, weight_ref, bias_ref, a_ref, q_ref, k_ref, v_ref):
    lanes = q_ref.shape[1]
    normed = layer_norm(x_ref[...].astype(jnp.float32), gain_ref[...], shift_ref[...])
    normed = normed.astype(jnp.bfloat16)
    a_ref[...] = normed
    mixed = (plain_product(normed, weight_ref[...]) + bias_ref[...]).astype(jnp.bfloat16)
    q_ref[...] = mixed[:, :lanes]
    k_ref[...] = mixed[:, lanes : 2 * lanes]
    v_ref[...] = mixed[:, 2 * lanes :]


def norm_mix(stream, gain, shift, weight, bias):
    length, width = stream.shape
    lanes = weight.shape[1] // 3
    block = 512
    row = lambda size: pl.BlockSpec((block, size), lambda i: (i, 0))
    fixed = lambda *shape: pl.BlockSpec(shape, lambda i: (0, 0))
    part = jax.ShapeDtypeStruct((length, lanes), jnp.bfloat16)
    return pl.pallas_call(
        norm_mix_kernel,
        grid=(length // block,),
        in_specs=[
            row(width), fixed(1, width), fixed(1, width), fixed(width, 3 * lanes), fixed(1, 3 * lanes)
        ],
        out_specs=[row(width), row(lanes), row(lanes), row(lanes)],
        out_shape=(jax.ShapeDtypeStruct((length, width), jnp.bfloat16), part, part, part),
        compiler_params=pltpu.CompilerParams(vmem_limit_bytes=VMEM_BYTES),
        cost_estimate=pl.CostEstimate(
            flops=length * width * lanes * 6, bytes_accessed=length * width * 4, transcendentals=0
        ),
        name="norm_mix",
    )(stream, gain[None], shift[None], weight, bias[None])


def on_device(
    tokens,
    cotangent,
    segment_ids,
    valid,
    project_in,
    project_out,
    hidden_up,
    hidden_down,
    gains_biases,
    moment_in,
    moment_out,
    moment_up,
    moment_down,
    moment_gains,
    square_in,
    square_out,
    square_up,
    square_down,
    square_gains,
):
    rows = tokens.shape[0]
    width = tokens.shape[1]
    both = ("fsdp", "seq")
    streams, group = lax.axis_size("fsdp"), lax.axis_size("seq")
    count = streams * group
    share = width // count
    lanes = width // group
    length = rows * group
    images = length // IMG_LEN

    owned = project_in.astype(jnp.bfloat16).reshape(share, 3, group, lanes)
    owned = owned.transpose(2, 0, 1, 3).reshape(group, share, 3 * lanes)
    position = lax.broadcasted_iota(jnp.int32, (images, rows), 1)
    found = (segment_ids[None, :] == lax.broadcasted_iota(jnp.int32, (images, rows), 0)) & (
        valid[None, :] == 1
    )
    first = jnp.min(jnp.where(found, position, rows), axis=1)
    small = jnp.concatenate(
        [
            gains_biases.astype(jnp.bfloat16).reshape(-1),
            (first // 32).astype(jnp.bfloat16),
            (first % 32).astype(jnp.bfloat16),
        ]
    )
    vector_size = gains_biases.size
    extra = -(-small.shape[0] // (3 * lanes))
    small = jnp.pad(small, (0, extra * 3 * lanes - small.shape[0])).reshape(1, extra, 3 * lanes)
    blocks = jnp.concatenate([owned, jnp.broadcast_to(small, (group, extra, 3 * lanes))], axis=1)
    blocks = jnp.broadcast_to(blocks[None], (streams, *blocks.shape))
    blocks = blocks.reshape(count, share + extra, 3 * lanes)
    blocks = lax.all_to_all(blocks, both, split_axis=0, concat_axis=0, tiled=True)
    mine_in = blocks[:, :share].reshape(width, 3 * lanes)
    small = blocks[:, share:].reshape(count, -1)
    vectors = small[:, :vector_size].reshape(count, -1, share).transpose(1, 0, 2)
    vectors = vectors.reshape(-1, width).astype(jnp.float32)
    first = small[:, vector_size : vector_size + 2 * images].astype(jnp.int32)
    first = first[:, :images] * 32 + first[:, images:]
    first = lax.dynamic_slice_in_dim(first, lax.axis_index("fsdp") * group, group, 0)
    offsets = lax.broadcasted_iota(jnp.int32, (group, images), 0) * rows
    starts = jnp.min(jnp.where(first < rows, first + offsets, length), axis=0)

    stream = lax.all_gather(tokens, "seq", axis=0, tiled=True)

    packed = jnp.concatenate(
        [
            project_in.astype(jnp.bfloat16).reshape(share, 3, width).transpose(1, 0, 2),
            project_out.astype(jnp.bfloat16)[None],
            hidden_up.astype(jnp.bfloat16).reshape(share, -1, width).transpose(1, 0, 2),
            hidden_down.astype(jnp.bfloat16).reshape(-1, share, width),
        ],
        axis=0,
    )
    gathered = lax.all_gather(packed, both, axis=0, tiled=False)
    fold = FF // width
    whole_in = gathered[:, 0:3].transpose(0, 2, 1, 3).reshape(width, 3 * width)
    whole_out = gathered[:, 3].reshape(width, width)
    whole_up = gathered[:, 4 : 4 + fold].transpose(0, 2, 1, 3).reshape(width, FF)
    whole_down = gathered[:, 4 + fold :].reshape(FF, width)

    gain_one, shift_one, bias_query, bias_value, bias_out = (
        vectors[0],
        vectors[1],
        vectors[2],
        vectors[3],
        vectors[4],
    )
    scale_one, gain_two, shift_two, bias_down, scale_two = (
        vectors[5],
        vectors[6],
        vectors[7],
        vectors[8],
        vectors[9],
    )
    bias_up = vectors[10:].reshape(-1)
    column = lax.axis_index("seq") * lanes
    bias_in = jnp.concatenate(
        [
            lax.dynamic_slice_in_dim(bias_query, column, lanes, 0),
            jnp.zeros((lanes,), jnp.float32),
            lax.dynamic_slice_in_dim(bias_value, column, lanes, 0),
        ]
    )
    normed_one, query, keys, values = norm_mix(stream, gain_one, shift_one, mine_in, bias_in)
    wide, attended, logs = attend(starts, query, keys, values)
    returned = lax.all_to_all(
        attended.reshape(group, rows, lanes), "seq", split_axis=0, concat_axis=0, tiled=True
    )
    attended_rows = returned.transpose(1, 0, 2).reshape(rows, width)
    inputs = tokens.astype(jnp.float32)
    projected = plain_product(attended_rows, whole_out) + bias_out
    second = inputs + scale_one * projected
    norm_two, norm_two_back = jax.vjp(layer_norm, second, gain_two, shift_two)
    normed_two = norm_two.astype(jnp.bfloat16)
    upward = plain_product(normed_two, whole_up) + bias_up
    activated, gelu_back = jax.vjp(exact_gelu, upward)
    active = activated.astype(jnp.bfloat16)
    branch = plain_product(active, whole_down) + bias_down
    block_output = (second + scale_two * branch).astype(jnp.bfloat16)
    grad_rows = cotangent.astype(jnp.float32) * valid.astype(jnp.float32)[:, None]
    grad_scale_two = jnp.sum(grad_rows * branch, axis=0)
    grad_branch = (scale_two * grad_rows).astype(jnp.bfloat16)
    grad_bias_down = jnp.sum(grad_branch.astype(jnp.float32), axis=0)
    grad_down = inner_rows(active, grad_branch)
    grad_active = inner_cols(grad_branch, whole_down)
    grad_upward = gelu_back(grad_active)[0].astype(jnp.bfloat16)
    grad_bias_up = jnp.sum(grad_upward.astype(jnp.float32), axis=0)
    grad_up = inner_rows(normed_two, grad_upward)
    grad_norm_two = inner_cols(grad_upward, whole_up)
    second_part, grad_gain_two, grad_shift_two = norm_two_back(grad_norm_two)
    grad_second = grad_rows + second_part
    grad_scale_one = jnp.sum(grad_second * projected, axis=0)
    grad_projected = (scale_one * grad_second).astype(jnp.bfloat16)
    grad_bias_out = jnp.sum(grad_projected.astype(jnp.float32), axis=0)
    grad_out = inner_rows(attended_rows, grad_projected)
    grad_attended = inner_cols(grad_projected, whole_out).astype(jnp.bfloat16)
    grad_stream = lax.all_to_all(
        grad_attended.reshape(rows, group, lanes).transpose(1, 0, 2),
        "seq",
        split_axis=0,
        concat_axis=0,
        tiled=True,
    ).reshape(length, lanes)

    grad_packed = jnp.concatenate(
        [
            grad_out.astype(jnp.bfloat16).reshape(count, 1, share, width),
            grad_up.astype(jnp.bfloat16).reshape(count, share, fold, width).transpose(0, 2, 1, 3),
            grad_down.astype(jnp.bfloat16).reshape(count, fold, share, width),
        ],
        axis=1,
    )
    summed = lax.psum_scatter(grad_packed, both, scatter_dimension=0, tiled=True)[0]
    summed = summed.astype(jnp.float32)
    summed_out = summed[0]
    summed_up = summed[1 : 1 + fold].transpose(1, 0, 2).reshape(share, FF)
    summed_down = summed[1 + fold :].reshape(fold * share, width)

    grad_mixed_stream = attend_back(starts, query, keys, values, wide, logs, grad_stream)
    grad_mixed = lax.all_to_all(
        grad_mixed_stream.reshape(group, rows, 3 * lanes),
        "seq",
        split_axis=0,
        concat_axis=0,
        tiled=True,
    )
    grad_mixed = grad_mixed.reshape(group, rows, 3, lanes).transpose(1, 2, 0, 3)
    grad_mixed = grad_mixed.reshape(rows, 3 * width)
    grad_in = inner_rows(normed_one, grad_mixed_stream).astype(jnp.bfloat16)
    parts = lax.all_to_all(
        grad_in.reshape(count, share, 3 * lanes), both, split_axis=0, concat_axis=0, tiled=True
    )
    parts = parts.reshape(streams, group, share, 3, lanes).astype(jnp.float32)
    summed_in = jnp.sum(parts, axis=0).transpose(1, 2, 0, 3).reshape(share, 3 * width)

    grad_mixed_wide = grad_mixed.astype(jnp.float32)
    grad_bias_query = jnp.sum(grad_mixed_wide[:, :width], axis=0)
    grad_bias_value = jnp.sum(grad_mixed_wide[:, 2 * width :], axis=0)
    grad_norm_one = inner_cols(grad_mixed, whole_in)
    norm_one_back = jax.vjp(layer_norm, inputs, gain_one, shift_one)[1]
    first_part, grad_gain_one, grad_shift_one = norm_one_back(grad_norm_one)
    input_grad = grad_second + first_part
    grad_small = jnp.concatenate(
        [
            jnp.stack(
                [
                    grad_gain_one,
                    grad_shift_one,
                    grad_bias_query,
                    grad_bias_value,
                    grad_bias_out,
                    grad_scale_one,
                    grad_gain_two,
                    grad_shift_two,
                    grad_bias_down,
                    grad_scale_two,
                ]
            ),
            grad_bias_up.reshape(-1, width),
        ],
        axis=0,
    )
    small_rows = grad_small.shape[0]
    parts = grad_small.reshape(small_rows, count, share).transpose(1, 0, 2)
    parts = lax.all_to_all(
        parts.reshape(count, small_rows * share), both, split_axis=0, concat_axis=0, tiled=True
    )
    summed_gains = jnp.sum(parts, axis=0).reshape(small_rows, share)
    rate_out = max(1, 4 * D // IMG_LEN) ** (-0.5)
    new_in, new_moment_in, new_square_in = adamw(
        project_in, moment_in, square_in, summed_in, D ** (-0.5), 0.04
    )
    new_out, new_moment_out, new_square_out = adamw(
        project_out, moment_out, square_out, summed_out, rate_out, 0.04
    )
    new_up, new_moment_up, new_square_up = adamw(
        hidden_up, moment_up, square_up, summed_up, D ** (-0.5), 0.04
    )
    new_down, new_moment_down, new_square_down = adamw(
        hidden_down, moment_down, square_down, summed_down, FF ** (-0.5), 0.04
    )
    new_gains, new_moment_gains, new_square_gains = adamw(
        gains_biases, moment_gains, square_gains, summed_gains, 0.2, 0.0
    )
    return (
        block_output,
        input_grad,
        new_in,
        new_out,
        new_up,
        new_down,
        new_gains,
        new_moment_in,
        new_moment_out,
        new_moment_up,
        new_moment_down,
        new_moment_gains,
        new_square_in,
        new_square_out,
        new_square_up,
        new_square_down,
        new_square_gains,
        summed_gains[8],
    )


def solution(mesh):
    return jax.shard_map(
        on_device,
        mesh=mesh,
        in_specs=(
            P(("fsdp", "seq"), None),
            P(("fsdp", "seq"), None),
            P(("fsdp", "seq")),
            P(("fsdp", "seq")),
            P(("fsdp", "seq"), None),
            P(("fsdp", "seq"), None),
            P(("fsdp", "seq"), None),
            P(("fsdp", "seq"), None),
            P(None, ("fsdp", "seq")),
            P(("fsdp", "seq"), None),
            P(("fsdp", "seq"), None),
            P(("fsdp", "seq"), None),
            P(("fsdp", "seq"), None),
            P(None, ("fsdp", "seq")),
            P(("fsdp", "seq"), None),
            P(("fsdp", "seq"), None),
            P(("fsdp", "seq"), None),
            P(("fsdp", "seq"), None),
            P(None, ("fsdp", "seq")),
        ),
        out_specs=(
            P(("fsdp", "seq"), None),
            P(("fsdp", "seq"), None),
            P(("fsdp", "seq"), None),
            P(("fsdp", "seq"), None),
            P(("fsdp", "seq"), None),
            P(("fsdp", "seq"), None),
            P(None, ("fsdp", "seq")),
            P(("fsdp", "seq"), None),
            P(("fsdp", "seq"), None),
            P(("fsdp", "seq"), None),
            P(("fsdp", "seq"), None),
            P(None, ("fsdp", "seq")),
            P(("fsdp", "seq"), None),
            P(("fsdp", "seq"), None),
            P(("fsdp", "seq"), None),
            P(("fsdp", "seq"), None),
            P(None, ("fsdp", "seq")),
            P(("fsdp", "seq")),
        ),
        check_vma=False,
    )
```

```python
import jax
import jax.numpy as jnp
from jax import lax
from jax.experimental import pallas as pl
from jax.experimental.pallas import tpu as pltpu
from jax.sharding import PartitionSpec as P

D = 1024
FF = 4096
HEADS = 16
HEAD_DIM = 64
IMG_LEN = 1370
WINDOW = 1408
TILE = 352
VMEM_BYTES = 56 * 1024 * 1024
STEP = 10


masked_score = -1e30


def layer_norm(values, gain, shift):
    average = jnp.mean(values, axis=-1, keepdims=True)
    centered = values - average
    variance = jnp.mean(centered * centered, axis=-1, keepdims=True)
    return centered * lax.rsqrt(variance + 1e-06) * gain + shift


def exact_gelu(values):
    return jax.nn.gelu(values, approximate=False)


def plain_product(left, right):
    return jnp.dot(left, right, preferred_element_type=jnp.float32)


def inner_rows(left, right):
    return lax.dot_general(
        left, right, (((0,), (0,)), ((), ())), preferred_element_type=jnp.float32
    )


def inner_cols(left, right):
    return lax.dot_general(
        left, right, (((1,), (1,)), ((), ())), preferred_element_type=jnp.float32
    )


def adamw(param, moment, square, grad, rate, decay):
    new_moment = 0.9 * moment + 0.1 * grad
    new_square = 0.999 * square + 0.001 * grad * grad
    corrected = new_moment / (1.0 - 0.9**STEP)
    scaled = jnp.sqrt(new_square / (1.0 - 0.999**STEP)) + 1e-08
    return (param - rate * (corrected / scaled + decay * param), new_moment, new_square)


def head_lanes(shape):
    return lax.broadcasted_iota(jnp.int32, shape, 1) // HEAD_DIM


def window_of(starts_ref, image, length):
    start = starts_ref[image]
    base = jnp.clip(start // 16 * 16, 0, length - WINDOW)
    return (pl.multiple_of(base, 16), start - base)


def image_mask(position, offset):
    return (position >= offset) & (position < offset + IMG_LEN)


def attend_kernel(starts_ref, q_ref, k_ref, v_ref, wide_ref, out_ref, log_ref):
    image, tile = pl.program_id(0), pl.program_id(1)
    length, lanes = q_ref.shape
    base, offset = window_of(starts_ref, image, length)
    rows = pl.ds(pl.multiple_of(base + tile * TILE, 16), TILE)

    @pl.when((image == 0) & (tile == 0))
    def clear():
        wide_ref[...] = jnp.zeros_like(wide_ref)
        out_ref[...] = jnp.zeros_like(out_ref)
        log_ref[...] = jnp.zeros_like(log_ref)

    query = q_ref[rows, :].astype(jnp.float32) * HEAD_DIM ** (-0.5)
    keys = k_ref[pl.ds(base, WINDOW), :]
    values = v_ref[pl.ds(base, WINDOW), :]
    key_ok = image_mask(lax.broadcasted_iota(jnp.int32, (1, WINDOW), 1), offset)
    bias = jnp.where(key_ok, 0.0, masked_score)
    row_ok = image_mask(lax.broadcasted_iota(jnp.int32, (TILE, 1), 0) + tile * TILE, offset)
    head_of = head_lanes((TILE, lanes))
    total_out = jnp.zeros((TILE, lanes), jnp.float32)
    total_log = jnp.zeros((TILE, lanes), jnp.float32)
    for head in range(lanes // HEAD_DIM):
        mine = head_of == head
        part = jnp.where(mine, query, 0.0).astype(jnp.bfloat16)
        scores = inner_cols(part, keys) + bias
        top = jnp.max(scores, axis=1, keepdims=True)
        weights = jnp.exp(scores - top)
        total = jnp.sum(weights, axis=1, keepdims=True)
        probs = (weights * (1.0 / total)).astype(jnp.bfloat16)
        total_out = jnp.where(mine, plain_product(probs, values), total_out)
        total_log = jnp.where(mine, top + jnp.log(total), total_log)
    merged = jnp.where(row_ok, total_out, wide_ref[rows, :])
    wide_ref[rows, :] = merged
    out_ref[rows, :] = merged.astype(jnp.bfloat16)
    log_ref[rows, :] = jnp.where(row_ok, total_log, log_ref[rows, :])


def attend(starts, query, keys, values):
    length, lanes = query.shape
    whole = pl.BlockSpec((length, lanes), lambda image, tile, starts: (0, 0))
    wide = jax.ShapeDtypeStruct((length, lanes), jnp.float32)
    images = length // IMG_LEN
    return pl.pallas_call(
        attend_kernel,
        grid_spec=pltpu.PrefetchScalarGridSpec(
            num_scalar_prefetch=1,
            grid=(images, WINDOW // TILE),
            in_specs=[whole] * 3,
            out_specs=[whole] * 3,
        ),
        out_shape=(wide, jax.ShapeDtypeStruct((length, lanes), jnp.bfloat16), wide),
        compiler_params=pltpu.CompilerParams(
            vmem_limit_bytes=VMEM_BYTES, dimension_semantics=("arbitrary", "arbitrary")
        ),
        cost_estimate=pl.CostEstimate(
            flops=images * WINDOW * WINDOW * lanes * 8,
            bytes_accessed=length * lanes * 16,
            transcendentals=images * WINDOW * WINDOW * lanes // HEAD_DIM,
        ),
        name="attend_forward",
    )(starts, query, keys, values)


def attend_back_kernel(
    starts_ref, q_ref, k_ref, v_ref, wide_ref, log_ref, go_ref, grad_ref, key_acc, value_acc
):
    image, tile = pl.program_id(0), pl.program_id(1)
    length, lanes = q_ref.shape
    base, offset = window_of(starts_ref, image, length)
    rows = pl.ds(pl.multiple_of(base + tile * TILE, 16), TILE)
    window = pl.ds(base, WINDOW)

    @pl.when((image == 0) & (tile == 0))
    def clear():
        grad_ref[...] = jnp.zeros_like(grad_ref)

    @pl.when(tile == 0)
    def clear_sums():
        key_acc[...] = jnp.zeros_like(key_acc)
        value_acc[...] = jnp.zeros_like(value_acc)

    query = q_ref[rows, :].astype(jnp.float32) * HEAD_DIM ** (-0.5)
    keys = k_ref[window, :]
    values = v_ref[window, :]
    key_ok = image_mask(lax.broadcasted_iota(jnp.int32, (1, WINDOW), 1), offset)
    bias = jnp.where(key_ok, 0.0, masked_score)
    row_ok = image_mask(lax.broadcasted_iota(jnp.int32, (TILE, 1), 0) + tile * TILE, offset)
    head_of = head_lanes((TILE, lanes))
    grad_out = jnp.where(row_ok, go_ref[rows, :].astype(jnp.float32), 0.0)
    centre_parts = grad_out * wide_ref[rows, :]
    logs = jnp.where(row_ok, log_ref[rows, :], -masked_score)
    query_grad = jnp.zeros((TILE, lanes), jnp.float32)
    for head in range(lanes // HEAD_DIM):
        mine = head_of == head
        part = jnp.where(mine, query, 0.0).astype(jnp.bfloat16)
        grad_part = jnp.where(mine, grad_out, 0.0).astype(jnp.bfloat16)
        centre = jnp.sum(jnp.where(mine, centre_parts, 0.0), axis=1, keepdims=True)
        log_total = jnp.max(jnp.where(mine, logs, masked_score), axis=1, keepdims=True)
        probs = jnp.exp(inner_cols(part, keys) + bias - log_total)
        grad_probs = inner_cols(grad_part, values)
        grad_scores = (probs * (grad_probs - centre)).astype(jnp.bfloat16)
        query_grad = jnp.where(mine, plain_product(grad_scores, keys), query_grad)
        key_acc[...] += inner_rows(part, grad_scores)
        value_acc[...] += inner_rows(grad_part, probs.astype(jnp.bfloat16))
    old = grad_ref[rows, 0:lanes].astype(jnp.float32)
    merged = jnp.where(row_ok, query_grad * HEAD_DIM ** (-0.5), old)
    grad_ref[rows, 0:lanes] = merged.astype(jnp.bfloat16)

    @pl.when(tile == pl.num_programs(1) - 1)
    def flush():
        inside = image_mask(lax.broadcasted_iota(jnp.int32, (WINDOW, 1), 0), offset)
        for slot, sums in ((1, key_acc), (2, value_acc)):
            columns = slice(slot * lanes, (slot + 1) * lanes)
            old = grad_ref[window, columns].astype(jnp.float32)
            merged = jnp.where(inside, sums[...].T, old)
            grad_ref[window, columns] = merged.astype(jnp.bfloat16)


def attend_back(starts, query, keys, values, wide, logs, grad_out):
    length, lanes = query.shape
    whole = pl.BlockSpec((length, lanes), lambda image, tile, starts: (0, 0))
    images = length // IMG_LEN
    return pl.pallas_call(
        attend_back_kernel,
        grid_spec=pltpu.PrefetchScalarGridSpec(
            num_scalar_prefetch=1,
            grid=(images, WINDOW // TILE),
            in_specs=[whole] * 6,
            out_specs=pl.BlockSpec((length, 3 * lanes), lambda image, tile, starts: (0, 0)),
            scratch_shapes=[pltpu.VMEM((lanes, WINDOW), jnp.float32)] * 2,
        ),
        out_shape=jax.ShapeDtypeStruct((length, 3 * lanes), jnp.bfloat16),
        compiler_params=pltpu.CompilerParams(
            vmem_limit_bytes=VMEM_BYTES, dimension_semantics=("arbitrary", "arbitrary")
        ),
        cost_estimate=pl.CostEstimate(
            flops=images * WINDOW * WINDOW * lanes * 20,
            bytes_accessed=length * lanes * 22,
            transcendentals=images * WINDOW * WINDOW * lanes // HEAD_DIM,
        ),
        name="attend_backward",
    )(starts, query, keys, values, wide, logs, grad_out)


def norm_mix_kernel(
    core_ref, own_ref, other_ref, gain_ref, shift_ref, weight_ref, bias_ref, a_ref, q_ref, k_ref, v_ref
):
    lanes = q_ref.shape[1]
    mine = lax.rem(pl.program_id(0), 2) == core_ref[0]
    own, other = own_ref[...].astype(jnp.float32), other_ref[...].astype(jnp.float32)
    normed = layer_norm(jnp.where(mine, own, other), gain_ref[...], shift_ref[...])
    normed = normed.astype(jnp.bfloat16)
    a_ref[...] = normed
    mixed = (plain_product(normed, weight_ref[...]) + bias_ref[...]).astype(jnp.bfloat16)
    q_ref[...] = mixed[:, :lanes]
    k_ref[...] = mixed[:, lanes : 2 * lanes]
    v_ref[...] = mixed[:, 2 * lanes :]


def norm_mix(core, own, other, block, gain, shift, weight, bias):
    length, width = own.shape[0] * 2, own.shape[1]
    lanes = weight.shape[1] // 3
    row = lambda size: pl.BlockSpec((block, size), lambda i, core: (i, 0))
    half = pl.BlockSpec((block, width), lambda i, core: (i // 2, 0))
    fixed = lambda *shape: pl.BlockSpec(shape, lambda i, core: (0, 0))
    part = jax.ShapeDtypeStruct((length, lanes), jnp.bfloat16)
    return pl.pallas_call(
        norm_mix_kernel,
        grid_spec=pltpu.PrefetchScalarGridSpec(
            num_scalar_prefetch=1,
            grid=(length // block,),
            in_specs=[
                half,
                half,
                fixed(1, width),
                fixed(1, width),
                fixed(width, 3 * lanes),
                fixed(1, 3 * lanes),
            ],
            out_specs=[row(width), row(lanes), row(lanes), row(lanes)],
        ),
        out_shape=(jax.ShapeDtypeStruct((length, width), jnp.bfloat16), part, part, part),
        compiler_params=pltpu.CompilerParams(vmem_limit_bytes=VMEM_BYTES),
        cost_estimate=pl.CostEstimate(
            flops=length * width * lanes * 6, bytes_accessed=length * width * 4, transcendentals=0
        ),
        name="norm_mix",
    )(core, own, other, gain[None], shift[None], weight, bias[None])


def mlp_kernel(
    h_ref, gm_ref, up_ref, down_ref, bias_ref, grad_ref, m_ref, gh_ref, bias_grad_ref, turned_ref
):
    tile = pl.program_id(0)
    width = h_ref.shape[1]
    chips, up_rows, units = up_ref.shape
    part, down_rows = down_ref.shape[0], down_ref.shape[1]
    folds = width // units

    @pl.when(tile == 0)
    def clear():
        m_ref[...] = jnp.zeros_like(m_ref)
        gh_ref[...] = jnp.zeros_like(gh_ref)
        turned_ref[...] = h_ref[...].T

    weight_up = up_ref[...].reshape(width, units)
    weight_down = down_ref[...].reshape(units, width)
    gm = gm_ref[...]
    upward = plain_product(h_ref[...], weight_up) + bias_ref[...]
    normal = 0.5 * (1.0 + lax.erf(upward * 0.5**0.5))
    slope = normal + upward * jnp.exp(upward * upward * -0.5) * (0.5 / jnp.pi) ** 0.5
    active = (upward * normal).astype(jnp.bfloat16)
    grad_up = (inner_cols(gm, weight_down) * slope).astype(jnp.bfloat16)
    bias_grad_ref[...] = jnp.sum(grad_up.astype(jnp.float32), axis=0, keepdims=True)
    m_ref[...] += plain_product(active, weight_down)
    gh_ref[...] += inner_cols(grad_up, weight_up)
    up_grad = plain_product(turned_ref[...], grad_up).astype(jnp.bfloat16)
    row = pl.multiple_of(tile // folds * up_rows, up_rows)
    column = pl.multiple_of(lax.rem(tile, folds) * units, units)
    grad_ref[:, pl.ds(row, up_rows), pl.ds(column, units)] = up_grad.reshape(chips, up_rows, units)
    down_grad = inner_rows(active, gm).astype(jnp.bfloat16).reshape(part, down_rows, width)
    base = 2 * up_rows
    if chips > 1:
        grad_ref[pl.ds(tile * part, part), base : base + down_rows, :] = down_grad
    else:
        start = pl.multiple_of(base + tile * down_rows, down_rows)
        grad_ref[:, pl.ds(start, down_rows), :] = down_grad


def mlp(normed, gm, packed, up_rows, bias):
    rows, width = normed.shape
    chips = packed.shape[0]
    hidden = bias.shape[0]
    units = 256
    folds = width // units
    once = dict(pipeline_mode=pl.Buffered(1))
    fixed = pl.BlockSpec((rows, width), lambda j: (0, 0), **once)
    if chips > 1:
        part = units * chips // hidden
        down = pl.BlockSpec((part, units // part, width), lambda j: (j, 2 * up_rows * part // units, 0))
    else:
        down = pl.BlockSpec((1, units, width), lambda j: (0, 2 * up_rows // units + j, 0))
    total = jax.ShapeDtypeStruct((rows, width), jnp.float32)
    return pl.pallas_call(
        mlp_kernel,
        grid=(hidden // units,),
        in_specs=[
            fixed,
            fixed,
            pl.BlockSpec((chips, up_rows, units), lambda j: (0, j // folds, lax.rem(j, folds))),
            down,
            pl.BlockSpec((1, units), lambda j: (0, j)),
        ],
        out_specs=[
            pl.BlockSpec(packed.shape, lambda j: (0, 0, 0), **once),
            fixed,
            fixed,
            pl.BlockSpec((1, units), lambda j: (0, j)),
        ],
        out_shape=(
            jax.ShapeDtypeStruct(packed.shape, jnp.bfloat16),
            total,
            total,
            jax.ShapeDtypeStruct((1, hidden), jnp.float32),
        ),
        scratch_shapes=[pltpu.VMEM((width, rows), jnp.bfloat16)],
        compiler_params=pltpu.CompilerParams(vmem_limit_bytes=VMEM_BYTES),
        cost_estimate=pl.CostEstimate(
            flops=rows * width * hidden * 12,
            bytes_accessed=packed.size * 4 + rows * width * 12,
            transcendentals=rows * hidden * 2,
        ),
        name="mlp_both_ways",
    )(normed, gm, packed, packed, bias[None])


def finish_kernel(
    grad_ref, weight_ref, x_ref, gx_ref, gain_ref, out_ref, gain_grad_ref, shift_grad_ref, sums_ref, acc_ref
):
    step = pl.program_id(0)
    parts = [grad_ref[slot] for slot in range(grad_ref.shape[0])]
    grad = jnp.concatenate(parts, axis=1)
    width = x_ref.shape[1]
    product = inner_cols(grad, weight_ref[...].reshape(width, width))
    sums_ref[...] = jnp.sum(grad.astype(jnp.float32), axis=0, keepdims=True)[None]

    @pl.when(step == 0)
    def begin():
        acc_ref[...] = product

    @pl.when(step > 0)
    def further():
        acc_ref[...] += product

    @pl.when(step == pl.num_programs(0) - 1)
    def end():
        values = x_ref[...].astype(jnp.float32)
        centered = values - jnp.mean(values, axis=1, keepdims=True)
        scale = lax.rsqrt(jnp.mean(centered * centered, axis=1, keepdims=True) + 1e-06)
        unit = centered * scale
        grad_norm = acc_ref[...]
        gain_grad_ref[...] = jnp.sum(grad_norm * unit, axis=0, keepdims=True)
        shift_grad_ref[...] = jnp.sum(grad_norm, axis=0, keepdims=True)
        grad_unit = grad_norm * gain_ref[...]
        mean = jnp.mean(grad_unit, axis=1, keepdims=True)
        slant = jnp.mean(grad_unit * unit, axis=1, keepdims=True)
        out_ref[...] = gx_ref[...] + scale * (grad_unit - mean - unit * slant)


def finish(grads, weights, inputs, gx, gain):
    rows, width = inputs.shape
    group, lanes = grads.shape[0], grads.shape[2] // 3
    if lanes % 128:
        grads = grads.reshape(group, rows, 3, lanes).transpose(2, 0, 1, 3)
        grads = grads.reshape(3 * group, rows, lanes)
        grad_spec = pl.BlockSpec((group, rows, lanes), lambda k: (k, 0, 0))
    else:
        grad_spec = pl.BlockSpec((group, rows, lanes), lambda k: (0, 0, k))
    share = weights.shape[1] // 3
    if share % 16:
        weights = weights.reshape(-1, 3, share, width).transpose(1, 0, 2, 3).reshape(1, -1, width)
        share = width
    fixed = lambda *shape: pl.BlockSpec(shape, lambda k: (0, 0))
    vector = jax.ShapeDtypeStruct((1, width), jnp.float32)
    return pl.pallas_call(
        finish_kernel,
        grid=(3,),
        in_specs=[
            grad_spec,
            pl.BlockSpec((weights.shape[0], share, width), lambda k: (0, k, 0)),
            fixed(rows, width),
            fixed(rows, width),
            fixed(1, width),
        ],
        out_specs=[
            fixed(rows, width),
            fixed(1, width),
            fixed(1, width),
            pl.BlockSpec((1, 1, width), lambda k: (k, 0, 0)),
        ],
        out_shape=(
            jax.ShapeDtypeStruct((rows, width), jnp.float32),
            vector,
            vector,
            jax.ShapeDtypeStruct((3, 1, width), jnp.float32),
        ),
        scratch_shapes=[pltpu.VMEM((rows, width), jnp.float32)],
        compiler_params=pltpu.CompilerParams(vmem_limit_bytes=VMEM_BYTES),
        cost_estimate=pl.CostEstimate(
            flops=rows * width * width * 6, bytes_accessed=width * width * 16, transcendentals=0
        ),
        name="finish_input",
    )(grads, weights, inputs, gx, gain[None])


def swap_cores(value):
    return lax.ppermute(value, "core", [(0, 1), (1, 0)])


def on_device(
    tokens,
    cotangent,
    segment_ids,
    valid,
    project_in,
    project_out,
    hidden_up,
    hidden_down,
    gains_biases,
    moment_in,
    moment_out,
    moment_up,
    moment_down,
    moment_gains,
    square_in,
    square_out,
    square_up,
    square_down,
    square_gains,
):
    rows = tokens.shape[0]
    width = tokens.shape[1]
    everyone = ("fsdp", "line", "core")
    chip_axes = ("fsdp", "line")
    seq = ("line", "core")
    streams, line = lax.axis_size("fsdp"), lax.axis_size("line")
    group = 2 * line
    count = streams * group
    chips = streams * line
    share = width // count
    lanes = width // group
    length = rows * group
    images = length // IMG_LEN
    core = lax.axis_index("core")
    first_core = core == 0

    def in_order(own, other, axis):
        return jnp.concatenate(
            [jnp.where(first_core, own, other), jnp.where(first_core, other, own)], axis=axis
        )

    line_tokens = lax.all_gather(tokens, "line", axis=0, tiled=True)

    owned = project_in.astype(jnp.bfloat16).reshape(share, 3, group, lanes)
    owned = owned.transpose(2, 0, 1, 3).reshape(group, share, 3 * lanes)
    position = lax.broadcasted_iota(jnp.int32, (images, rows), 1)
    found = (segment_ids[None, :] == lax.broadcasted_iota(jnp.int32, (images, rows), 0)) & (
        valid[None, :] == 1
    )
    first = jnp.min(jnp.where(found, position, rows), axis=1)
    small = jnp.concatenate(
        [
            gains_biases.astype(jnp.bfloat16).reshape(-1),
            (first // 32).astype(jnp.bfloat16),
            (first % 32).astype(jnp.bfloat16),
        ]
    )
    vector_size = gains_biases.size
    extra = -(-small.shape[0] // (3 * lanes))
    small = jnp.pad(small, (0, extra * 3 * lanes - small.shape[0])).reshape(1, extra, 3 * lanes)
    blocks = jnp.concatenate([owned, jnp.broadcast_to(small, (group, extra, 3 * lanes))], axis=1)
    blocks = lax.all_to_all(blocks, seq, split_axis=0, concat_axis=0, tiled=True)
    blocks = jnp.broadcast_to(blocks[None], (streams, *blocks.shape))
    blocks = lax.all_to_all(blocks, "fsdp", split_axis=0, concat_axis=0, tiled=True)
    blocks = blocks.reshape(count, share + extra, 3 * lanes)
    mine_in = blocks[:, :share].reshape(width, 3 * lanes)
    small = blocks[:, share:].reshape(count, -1)
    vectors = small[:, :vector_size].reshape(count, -1, share).transpose(1, 0, 2)
    vectors = vectors.reshape(-1, width).astype(jnp.float32)
    first = small[:, vector_size : vector_size + 2 * images].astype(jnp.int32)
    first = first[:, :images] * 32 + first[:, images:]
    first = lax.dynamic_slice_in_dim(first, lax.axis_index("fsdp") * group, group, 0)
    offsets = lax.broadcasted_iota(jnp.int32, (group, images), 0) * rows
    starts = jnp.min(jnp.where(first < rows, first + offsets, length), axis=0)

    half = FF // 2
    unit_block = FF // count
    up_blocks = hidden_up.astype(jnp.bfloat16).reshape(share, chips, 2, unit_block)
    up_first = up_blocks[:, :, 0].reshape(share, half)
    up_second = up_blocks[:, :, 1].reshape(share, half)
    out_rows = project_out.astype(jnp.bfloat16)
    received = swap_cores(
        jnp.concatenate(
            [jnp.where(first_core, up_second, up_first).reshape(-1, width), out_rows], axis=0
        )
    )
    folds = half // width
    up_rows = in_order(
        jnp.where(first_core, up_first, up_second),
        received[: share * folds].reshape(share, half),
        0,
    )
    packed = jnp.concatenate(
        [
            up_rows.reshape(2 * share, folds, width).transpose(1, 0, 2).reshape(-1, width),
            hidden_down.astype(jnp.bfloat16),
            in_order(out_rows, received[share * folds :], 0),
        ],
        axis=0,
    )
    packed, line_tokens = lax.optimization_barrier((packed, line_tokens))
    gathered = lax.all_gather(packed, chip_axes, axis=0, tiled=False)
    in_rows = project_in.astype(jnp.bfloat16).reshape(share, 3, width).transpose(1, 0, 2)
    in_rows, gathered = lax.optimization_barrier((in_rows.reshape(-1, width), gathered))
    gathered_in = lax.all_gather(in_rows, everyone, axis=0, tiled=False)
    up_end = 2 * share * folds
    down_end = up_end + half // chips
    whole_out = gathered[:, down_end:].reshape(width, width)
    direct = (2 * share) % 16 == 0
    if direct:
        mlp_weights, mlp_up_rows = gathered, 2 * share
    else:
        mlp_weights = jnp.concatenate(
            [gathered[:, n * 2 * share : (n + 1) * 2 * share].reshape(width, width) for n in range(folds)]
            + [gathered[:, up_end:down_end].reshape(half, width)],
            axis=0,
        )[None]
        mlp_up_rows = width

    gain_one, shift_one, bias_query, bias_value, bias_out = (
        vectors[0],
        vectors[1],
        vectors[2],
        vectors[3],
        vectors[4],
    )
    scale_one, gain_two, shift_two, bias_down, scale_two = (
        vectors[5],
        vectors[6],
        vectors[7],
        vectors[8],
        vectors[9],
    )
    bias_up = lax.dynamic_index_in_dim(
        vectors[10:].reshape(chips, 2, unit_block), core, axis=1, keepdims=False
    ).reshape(half)
    column = lax.axis_index(seq) * lanes
    bias_in = jnp.concatenate(
        [
            lax.dynamic_slice_in_dim(bias_query, column, lanes, 0),
            jnp.zeros((lanes,), jnp.float32),
            lax.dynamic_slice_in_dim(bias_value, column, lanes, 0),
        ]
    )
    grad_rows = cotangent.astype(jnp.float32) * valid.astype(jnp.float32)[:, None]
    grad_branch = (scale_two * grad_rows).astype(jnp.bfloat16)
    grad_branch_chip = jnp.concatenate([grad_branch, swap_cores(grad_branch)], axis=0)

    normed_one, query, keys, values = norm_mix(
        core.reshape(1),
        line_tokens,
        swap_cores(line_tokens),
        rows,
        gain_one,
        shift_one,
        mine_in,
        bias_in,
    )
    wide, attended, logs = attend(starts, query, keys, values)
    returned = lax.all_to_all(
        attended.reshape(group, rows, lanes), seq, split_axis=0, concat_axis=0, tiled=True
    )
    attended_rows = returned.transpose(1, 0, 2).reshape(rows, width)
    inputs = tokens.astype(jnp.float32)
    projected = plain_product(attended_rows, whole_out) + bias_out
    second = inputs + scale_one * projected
    norm_two, norm_two_back = jax.vjp(layer_norm, second, gain_two, shift_two)
    normed_two = norm_two.astype(jnp.bfloat16)
    normed_chip = jnp.concatenate([normed_two, swap_cores(normed_two)], axis=0)
    grad_packed, branch_part, grad_norm_part, grad_bias_up = mlp(
        normed_chip, grad_branch_chip, mlp_weights, mlp_up_rows, bias_up
    )
    grad_norm_two = grad_norm_part[:rows] + swap_cores(grad_norm_part[rows:])
    branch = branch_part[:rows] + swap_cores(branch_part[rows:]) + bias_down
    block_output = (second + scale_two * branch).astype(jnp.bfloat16)
    grad_scale_two = jnp.sum(grad_rows * branch, axis=0)
    grad_bias_down = jnp.sum(grad_branch.astype(jnp.float32), axis=0)
    second_part, grad_gain_two, grad_shift_two = norm_two_back(grad_norm_two)
    grad_second = grad_rows + second_part
    grad_scale_one = jnp.sum(grad_second * projected, axis=0)
    grad_projected = (scale_one * grad_second).astype(jnp.bfloat16)
    grad_bias_out = jnp.sum(grad_projected.astype(jnp.float32), axis=0)
    grad_attended = inner_cols(grad_projected, whole_out).astype(jnp.bfloat16)
    grad_stream = lax.all_to_all(
        grad_attended.reshape(rows, group, lanes).transpose(1, 0, 2),
        seq,
        split_axis=0,
        concat_axis=0,
        tiled=True,
    ).reshape(length, lanes)
    grad_out = inner_rows(attended_rows, grad_projected).astype(jnp.bfloat16)
    grad_out = grad_out.reshape(chips, 2 * share, width)
    if direct:
        grad_packed = lax.dynamic_update_slice_in_dim(grad_packed, grad_out, down_end, 1)
    else:
        grad_packed = jnp.concatenate(
            [
                grad_packed[0, n * width : (n + 1) * width].reshape(chips, 2 * share, width)
                for n in range(folds)
            ]
            + [grad_packed[0, folds * width :].reshape(chips, -1, width), grad_out],
            axis=1,
        )
    summed = lax.psum_scatter(grad_packed, chip_axes, scatter_dimension=0, tiled=True)[0]

    grad_mixed_stream = attend_back(starts, query, keys, values, wide, logs, grad_stream)
    grad_mixed = lax.all_to_all(
        grad_mixed_stream.reshape(group, rows, 3 * lanes), seq, split_axis=0, concat_axis=0, tiled=True
    )
    grad_in = inner_rows(normed_one, grad_mixed_stream).astype(jnp.bfloat16)
    parts = lax.all_to_all(
        grad_in.reshape(streams, group * share, 3 * lanes),
        "fsdp",
        split_axis=0,
        concat_axis=0,
        tiled=True,
    )
    parts = jnp.sum(parts.astype(jnp.float32), axis=0).reshape(group, share, 3 * lanes)
    parts = lax.all_to_all(parts, seq, split_axis=0, concat_axis=0, tiled=True)
    summed_in = parts.reshape(group, share, 3, lanes).transpose(1, 2, 0, 3).reshape(share, 3 * width)

    input_grad, grad_gain_one, grad_shift_one, mixed_sums = finish(
        grad_mixed, gathered_in, tokens, grad_second, gain_one
    )
    up_sums = grad_bias_up.reshape(chips, unit_block)
    up_sums = jnp.where(
        (lax.broadcasted_iota(jnp.int32, (1, 2, 1), 1) == core), up_sums[:, None, :], 0.0
    )
    grad_small = jnp.concatenate(
        [
            jnp.stack(
                [
                    grad_gain_one[0],
                    grad_shift_one[0],
                    mixed_sums[0, 0],
                    mixed_sums[2, 0],
                    grad_bias_out,
                    grad_scale_one,
                    grad_gain_two,
                    grad_shift_two,
                    grad_bias_down,
                    grad_scale_two,
                ]
            ),
            up_sums.reshape(-1, width),
        ],
        axis=0,
    )
    small_rows = grad_small.shape[0]
    parts = grad_small.reshape(small_rows, count, share).transpose(1, 0, 2)
    parts = lax.all_to_all(
        parts.reshape(count, small_rows * share), everyone, split_axis=0, concat_axis=0, tiled=True
    )
    summed_gains = jnp.sum(parts, axis=0).reshape(small_rows, share)

    up_sum = summed[:up_end].reshape(folds, 2, share, width)
    out_sum = summed[down_end:].reshape(1, 2, share, width)
    both_sums = jnp.concatenate([up_sum, out_sum], axis=0)
    own_sums = jnp.where(first_core, both_sums[:, 0], both_sums[:, 1])
    other_sums = swap_cores(jnp.where(first_core, both_sums[:, 1], both_sums[:, 0]))
    summed_down = summed[up_end:down_end].astype(jnp.float32)
    summed_out = own_sums[folds].astype(jnp.float32) + other_sums[folds].astype(jnp.float32)
    own_up = own_sums[:folds].transpose(1, 0, 2).reshape(share, chips, 1, unit_block)
    other_up = other_sums[:folds].transpose(1, 0, 2).reshape(share, chips, 1, unit_block)
    summed_up = in_order(own_up, other_up, 2).reshape(share, FF).astype(jnp.float32)
    rate_out = max(1, 4 * D // IMG_LEN) ** (-0.5)
    new_in, new_moment_in, new_square_in = adamw(
        project_in, moment_in, square_in, summed_in, D ** (-0.5), 0.04
    )
    new_out, new_moment_out, new_square_out = adamw(
        project_out, moment_out, square_out, summed_out, rate_out, 0.04
    )
    new_up, new_moment_up, new_square_up = adamw(
        hidden_up, moment_up, square_up, summed_up, D ** (-0.5), 0.04
    )
    new_down, new_moment_down, new_square_down = adamw(
        hidden_down, moment_down, square_down, summed_down, FF ** (-0.5), 0.04
    )
    new_gains, new_moment_gains, new_square_gains = adamw(
        gains_biases, moment_gains, square_gains, summed_gains, 0.2, 0.0
    )
    return (
        block_output,
        input_grad,
        new_in,
        new_out,
        new_up,
        new_down,
        new_gains,
        new_moment_in,
        new_moment_out,
        new_moment_up,
        new_moment_down,
        new_moment_gains,
        new_square_in,
        new_square_out,
        new_square_up,
        new_square_down,
        new_square_gains,
        summed_gains[8],
    )


def solution(mesh):
    streams, group = mesh.shape["fsdp"], mesh.shape["seq"]
    fine = jax.sharding.Mesh(
        mesh.devices.reshape(streams, group // 2, 2), ("fsdp", "line", "core")
    )
    return jax.shard_map(
        on_device,
        mesh=fine,
        in_specs=(
            P(("fsdp", "line", "core"), None),
            P(("fsdp", "line", "core"), None),
            P(("fsdp", "line", "core")),
            P(("fsdp", "line", "core")),
            P(("fsdp", "line", "core"), None),
            P(("fsdp", "line", "core"), None),
            P(("fsdp", "line", "core"), None),
            P(("fsdp", "line", "core"), None),
            P(None, ("fsdp", "line", "core")),
            P(("fsdp", "line", "core"), None),
            P(("fsdp", "line", "core"), None),
            P(("fsdp", "line", "core"), None),
            P(("fsdp", "line", "core"), None),
            P(None, ("fsdp", "line", "core")),
            P(("fsdp", "line", "core"), None),
            P(("fsdp", "line", "core"), None),
            P(("fsdp", "line", "core"), None),
            P(("fsdp", "line", "core"), None),
            P(None, ("fsdp", "line", "core")),
        ),
        out_specs=(
            P(("fsdp", "line", "core"), None),
            P(("fsdp", "line", "core"), None),
            P(("fsdp", "line", "core"), None),
            P(("fsdp", "line", "core"), None),
            P(("fsdp", "line", "core"), None),
            P(("fsdp", "line", "core"), None),
            P(None, ("fsdp", "line", "core")),
            P(("fsdp", "line", "core"), None),
            P(("fsdp", "line", "core"), None),
            P(("fsdp", "line", "core"), None),
            P(("fsdp", "line", "core"), None),
            P(None, ("fsdp", "line", "core")),
            P(("fsdp", "line", "core"), None),
            P(("fsdp", "line", "core"), None),
            P(("fsdp", "line", "core"), None),
            P(("fsdp", "line", "core"), None),
            P(None, ("fsdp", "line", "core")),
            P(("fsdp", "line", "core")),
        ),
        check_vma=False,
    )
```

```python
import math

import jax
import jax.numpy as jnp
from jax import lax
from jax.experimental import pallas as pl
from jax.experimental.pallas import tpu as pltpu
from jax.sharding import PartitionSpec as P

D = 1024
FF = 4096
HEADS = 16
HEAD_DIM = 64
IMG_LEN = 1370
WINDOW = 1408
TILE = 352
VMEM_BYTES = 56 * 1024 * 1024
STEP = 10


masked_score = -1e30


def layer_norm(values, gain, shift):
    average = jnp.mean(values, axis=-1, keepdims=True)
    centered = values - average
    variance = jnp.mean(centered * centered, axis=-1, keepdims=True)
    return centered * lax.rsqrt(variance + 1e-06) * gain + shift


def exact_gelu(values):
    return jax.nn.gelu(values, approximate=False)


def plain_product(left, right):
    return jnp.dot(left, right, preferred_element_type=jnp.float32)


def inner_rows(left, right):
    return lax.dot_general(
        left, right, (((0,), (0,)), ((), ())), preferred_element_type=jnp.float32
    )


def inner_cols(left, right):
    return lax.dot_general(
        left, right, (((1,), (1,)), ((), ())), preferred_element_type=jnp.float32
    )


def adamw(param, moment, square, grad, rate, decay):
    new_moment = 0.9 * moment + 0.1 * grad
    new_square = 0.999 * square + 0.001 * grad * grad
    corrected = new_moment / (1.0 - 0.9**STEP)
    scaled = jnp.sqrt(new_square / (1.0 - 0.999**STEP)) + 1e-08
    return (param - rate * (corrected / scaled + decay * param), new_moment, new_square)


def head_lanes(shape):
    return lax.broadcasted_iota(jnp.int32, shape, 1) // HEAD_DIM


def window_of(starts_ref, image, length):
    start = starts_ref[image]
    base = jnp.clip(start // 16 * 16, 0, length - WINDOW)
    return (pl.multiple_of(base, 16), start - base)


def image_mask(position, offset):
    return (position >= offset) & (position < offset + IMG_LEN)


def attend_kernel(starts_ref, q_ref, k_ref, v_ref, wide_ref, out_ref, log_ref):
    image, tile = pl.program_id(0), pl.program_id(1)
    length, lanes = q_ref.shape
    base, offset = window_of(starts_ref, image, length)
    rows = pl.ds(pl.multiple_of(base + tile * TILE, 16), TILE)

    @pl.when((image == 0) & (tile == 0))
    def clear():
        wide_ref[...] = jnp.zeros_like(wide_ref)
        out_ref[...] = jnp.zeros_like(out_ref)
        log_ref[...] = jnp.zeros_like(log_ref)

    query = q_ref[rows, :].astype(jnp.float32) * HEAD_DIM ** (-0.5)
    keys = k_ref[pl.ds(base, WINDOW), :]
    values = v_ref[pl.ds(base, WINDOW), :]
    key_ok = image_mask(lax.broadcasted_iota(jnp.int32, (1, WINDOW), 1), offset)
    bias = jnp.where(key_ok, 0.0, masked_score)
    row_ok = image_mask(lax.broadcasted_iota(jnp.int32, (TILE, 1), 0) + tile * TILE, offset)
    head_of = head_lanes((TILE, lanes))
    total_out = jnp.zeros((TILE, lanes), jnp.float32)
    total_log = jnp.zeros((TILE, lanes), jnp.float32)
    for head in range(lanes // HEAD_DIM):
        mine = head_of == head
        part = jnp.where(mine, query, 0.0).astype(jnp.bfloat16)
        scores = inner_cols(part, keys) + bias
        top = jnp.max(scores, axis=1, keepdims=True)
        weights = jnp.exp(scores - top)
        total = jnp.sum(weights, axis=1, keepdims=True)
        probs = (weights * (1.0 / total)).astype(jnp.bfloat16)
        total_out = jnp.where(mine, plain_product(probs, values), total_out)
        total_log = jnp.where(mine, top + jnp.log(total), total_log)
    merged = jnp.where(row_ok, total_out, wide_ref[rows, :])
    wide_ref[rows, :] = merged
    out_ref[rows, :] = merged.astype(jnp.bfloat16)
    log_ref[rows, :] = jnp.where(row_ok, total_log, log_ref[rows, :])


def attend(starts, query, keys, values):
    length, lanes = query.shape
    whole = pl.BlockSpec((length, lanes), lambda image, tile, starts: (0, 0))
    wide = jax.ShapeDtypeStruct((length, lanes), jnp.float32)
    images = length // IMG_LEN
    return pl.pallas_call(
        attend_kernel,
        grid_spec=pltpu.PrefetchScalarGridSpec(
            num_scalar_prefetch=1,
            grid=(images, WINDOW // TILE),
            in_specs=[whole] * 3,
            out_specs=[whole] * 3,
        ),
        out_shape=(wide, jax.ShapeDtypeStruct((length, lanes), jnp.bfloat16), wide),
        compiler_params=pltpu.CompilerParams(
            vmem_limit_bytes=VMEM_BYTES, dimension_semantics=("arbitrary", "arbitrary")
        ),
        cost_estimate=pl.CostEstimate(
            flops=images * WINDOW * WINDOW * lanes * 8,
            bytes_accessed=length * lanes * 16,
            transcendentals=images * WINDOW * WINDOW * lanes // HEAD_DIM,
        ),
        name="attend_forward",
    )(starts, query, keys, values)


def attend_back_kernel(
    starts_ref, q_ref, k_ref, v_ref, wide_ref, log_ref, go_ref, grad_ref, key_acc, value_acc
):
    image, tile = pl.program_id(0), pl.program_id(1)
    length, lanes = q_ref.shape
    base, offset = window_of(starts_ref, image, length)
    rows = pl.ds(pl.multiple_of(base + tile * TILE, 16), TILE)
    window = pl.ds(base, WINDOW)

    @pl.when((image == 0) & (tile == 0))
    def clear():
        grad_ref[...] = jnp.zeros_like(grad_ref)

    @pl.when(tile == 0)
    def clear_sums():
        key_acc[...] = jnp.zeros_like(key_acc)
        value_acc[...] = jnp.zeros_like(value_acc)

    query = q_ref[rows, :].astype(jnp.float32) * HEAD_DIM ** (-0.5)
    keys = k_ref[window, :]
    values = v_ref[window, :]
    key_ok = image_mask(lax.broadcasted_iota(jnp.int32, (1, WINDOW), 1), offset)
    bias = jnp.where(key_ok, 0.0, masked_score)
    row_ok = image_mask(lax.broadcasted_iota(jnp.int32, (TILE, 1), 0) + tile * TILE, offset)
    head_of = head_lanes((TILE, lanes))
    grad_out = jnp.where(row_ok, go_ref[rows, :].astype(jnp.float32), 0.0)
    centre_parts = grad_out * wide_ref[rows, :]
    logs = jnp.where(row_ok, log_ref[rows, :], -masked_score)
    query_grad = jnp.zeros((TILE, lanes), jnp.float32)
    for head in range(lanes // HEAD_DIM):
        mine = head_of == head
        part = jnp.where(mine, query, 0.0).astype(jnp.bfloat16)
        grad_part = jnp.where(mine, grad_out, 0.0).astype(jnp.bfloat16)
        centre = jnp.sum(jnp.where(mine, centre_parts, 0.0), axis=1, keepdims=True)
        log_total = jnp.max(jnp.where(mine, logs, masked_score), axis=1, keepdims=True)
        probs = jnp.exp(inner_cols(part, keys) + bias - log_total)
        grad_probs = inner_cols(grad_part, values)
        grad_scores = (probs * (grad_probs - centre)).astype(jnp.bfloat16)
        query_grad = jnp.where(mine, plain_product(grad_scores, keys), query_grad)
        key_acc[...] += inner_rows(part, grad_scores)
        value_acc[...] += inner_rows(grad_part, probs.astype(jnp.bfloat16))
    old = grad_ref[rows, 0:lanes].astype(jnp.float32)
    merged = jnp.where(row_ok, query_grad * HEAD_DIM ** (-0.5), old)
    grad_ref[rows, 0:lanes] = merged.astype(jnp.bfloat16)

    @pl.when(tile == pl.num_programs(1) - 1)
    def flush():
        inside = image_mask(lax.broadcasted_iota(jnp.int32, (WINDOW, 1), 0), offset)
        for slot, sums in ((1, key_acc), (2, value_acc)):
            columns = slice(slot * lanes, (slot + 1) * lanes)
            old = grad_ref[window, columns].astype(jnp.float32)
            merged = jnp.where(inside, sums[...].T, old)
            grad_ref[window, columns] = merged.astype(jnp.bfloat16)


def attend_back(starts, query, keys, values, wide, logs, grad_out):
    length, lanes = query.shape
    whole = pl.BlockSpec((length, lanes), lambda image, tile, starts: (0, 0))
    images = length // IMG_LEN
    return pl.pallas_call(
        attend_back_kernel,
        grid_spec=pltpu.PrefetchScalarGridSpec(
            num_scalar_prefetch=1,
            grid=(images, WINDOW // TILE),
            in_specs=[whole] * 6,
            out_specs=pl.BlockSpec((length, 3 * lanes), lambda image, tile, starts: (0, 0)),
            scratch_shapes=[pltpu.VMEM((lanes, WINDOW), jnp.float32)] * 2,
        ),
        out_shape=jax.ShapeDtypeStruct((length, 3 * lanes), jnp.bfloat16),
        compiler_params=pltpu.CompilerParams(
            vmem_limit_bytes=VMEM_BYTES, dimension_semantics=("arbitrary", "arbitrary")
        ),
        cost_estimate=pl.CostEstimate(
            flops=images * WINDOW * WINDOW * lanes * 20,
            bytes_accessed=length * lanes * 22,
            transcendentals=images * WINDOW * WINDOW * lanes // HEAD_DIM,
        ),
        name="attend_backward",
    )(starts, query, keys, values, wide, logs, grad_out)


def norm_mix_kernel(
    core_ref, own_ref, other_ref, gain_ref, shift_ref, weight_ref, bias_ref, a_ref, q_ref, k_ref, v_ref
):
    lanes = q_ref.shape[1]
    mine = lax.rem(pl.program_id(0), 2) == core_ref[0]
    own, other = own_ref[...].astype(jnp.float32), other_ref[...].astype(jnp.float32)
    normed = layer_norm(jnp.where(mine, own, other), gain_ref[...], shift_ref[...])
    normed = normed.astype(jnp.bfloat16)
    a_ref[...] = normed
    mixed = (plain_product(normed, weight_ref[...]) + bias_ref[...]).astype(jnp.bfloat16)
    q_ref[...] = mixed[:, :lanes]
    k_ref[...] = mixed[:, lanes : 2 * lanes]
    v_ref[...] = mixed[:, 2 * lanes :]


def norm_mix(core, own, other, block, gain, shift, weight, bias):
    length, width = own.shape[0] * 2, own.shape[1]
    lanes = weight.shape[1] // 3
    row = lambda size: pl.BlockSpec((block, size), lambda i, core: (i, 0))
    half = pl.BlockSpec((block, width), lambda i, core: (i // 2, 0))
    fixed = lambda *shape: pl.BlockSpec(shape, lambda i, core: (0, 0))
    part = jax.ShapeDtypeStruct((length, lanes), jnp.bfloat16)
    return pl.pallas_call(
        norm_mix_kernel,
        grid_spec=pltpu.PrefetchScalarGridSpec(
            num_scalar_prefetch=1,
            grid=(length // block,),
            in_specs=[
                half,
                half,
                fixed(1, width),
                fixed(1, width),
                fixed(width, 3 * lanes),
                fixed(1, 3 * lanes),
            ],
            out_specs=[row(width), row(lanes), row(lanes), row(lanes)],
        ),
        out_shape=(jax.ShapeDtypeStruct((length, width), jnp.bfloat16), part, part, part),
        compiler_params=pltpu.CompilerParams(vmem_limit_bytes=VMEM_BYTES),
        cost_estimate=pl.CostEstimate(
            flops=length * width * lanes * 6, bytes_accessed=length * width * 4, transcendentals=0
        ),
        name="norm_mix",
    )(core, own, other, gain[None], shift[None], weight, bias[None])


def mlp_kernel(
    h_ref,
    gm_ref,
    up_ref,
    down_ref,
    bias_ref,
    up_grad_ref,
    down_grad_ref,
    m_ref,
    gh_ref,
    bias_grad_ref,
    turned_ref,
):
    tile = pl.program_id(0)
    width = h_ref.shape[1]
    chips, up_rows, units = up_ref.shape
    folds = width // units

    @pl.when(tile == 0)
    def clear():
        m_ref[...] = jnp.zeros_like(m_ref)
        gh_ref[...] = jnp.zeros_like(gh_ref)
        turned_ref[...] = h_ref[...].T

    weight_up = up_ref[...].reshape(width, units)
    weight_down = down_ref[...].reshape(units, width)
    gm = gm_ref[...]
    upward = plain_product(h_ref[...], weight_up) + bias_ref[...]
    normal = 0.5 * (1.0 + lax.erf(upward * 0.5**0.5))
    slope = normal + upward * jnp.exp(upward * upward * -0.5) * (0.5 / jnp.pi) ** 0.5
    active = (upward * normal).astype(jnp.bfloat16)
    grad_up = (inner_cols(gm, weight_down) * slope).astype(jnp.bfloat16)
    bias_grad_ref[...] = jnp.sum(grad_up.astype(jnp.float32), axis=0, keepdims=True)
    m_ref[...] += plain_product(active, weight_down)
    gh_ref[...] += inner_cols(grad_up, weight_up)
    up_grad = plain_product(turned_ref[...], grad_up).astype(jnp.bfloat16)
    row = pl.multiple_of(tile // folds * up_rows, up_rows)
    column = pl.multiple_of(lax.rem(tile, folds) * units, units)
    up_grad = up_grad.reshape(chips, up_rows, units)
    up_grad_ref[:, pl.ds(row, up_rows), pl.ds(column, units)] = up_grad
    down_grad = inner_rows(active, gm).astype(jnp.bfloat16)
    down_grad_ref[...] = down_grad.reshape(down_grad_ref.shape)


def mlp(normed, gm, up, down, up_rows, bias):
    rows, width = normed.shape
    chips = up.shape[0]
    hidden = bias.shape[0]
    units = 256
    folds = width // units
    once = dict(pipeline_mode=pl.Buffered(1))
    fixed = pl.BlockSpec((rows, width), lambda j: (0, 0), **once)
    if chips > 1:
        part = units * chips // hidden
        down_spec = pl.BlockSpec((part, units // part, width), lambda j: (j, 0, 0))
    else:
        down_spec = pl.BlockSpec((1, units, width), lambda j: (0, j, 0))
    total = jax.ShapeDtypeStruct((rows, width), jnp.float32)
    return pl.pallas_call(
        mlp_kernel,
        grid=(hidden // units,),
        in_specs=[
            fixed,
            fixed,
            pl.BlockSpec((chips, up_rows, units), lambda j: (0, j // folds, lax.rem(j, folds))),
            down_spec,
            pl.BlockSpec((1, units), lambda j: (0, j)),
        ],
        out_specs=[
            pl.BlockSpec(up.shape, lambda j: (0, 0, 0), **once),
            down_spec,
            fixed,
            fixed,
            pl.BlockSpec((1, units), lambda j: (0, j)),
        ],
        out_shape=(
            jax.ShapeDtypeStruct(up.shape, jnp.bfloat16),
            jax.ShapeDtypeStruct(down.shape, jnp.bfloat16),
            total,
            total,
            jax.ShapeDtypeStruct((1, hidden), jnp.float32),
        ),
        scratch_shapes=[pltpu.VMEM((width, rows), jnp.bfloat16)],
        compiler_params=pltpu.CompilerParams(vmem_limit_bytes=VMEM_BYTES),
        cost_estimate=pl.CostEstimate(
            flops=rows * width * hidden * 12,
            bytes_accessed=(up.size + down.size) * 4 + rows * width * 12,
            transcendentals=rows * hidden * 2,
        ),
        name="mlp_both_ways",
    )(normed, gm, up, down, bias[None])


def finish_kernel(
    grad_ref, weight_ref, x_ref, gx_ref, gain_ref, out_ref, gain_grad_ref, shift_grad_ref, sums_ref, acc_ref
):
    step = pl.program_id(0)
    parts = [grad_ref[slot] for slot in range(grad_ref.shape[0])]
    grad = jnp.concatenate(parts, axis=1)
    width = x_ref.shape[1]
    product = inner_cols(grad, weight_ref[...].reshape(width, width))
    sums_ref[...] = jnp.sum(grad.astype(jnp.float32), axis=0, keepdims=True)[None]

    @pl.when(step == 0)
    def begin():
        acc_ref[...] = product

    @pl.when(step > 0)
    def further():
        acc_ref[...] += product

    @pl.when(step == pl.num_programs(0) - 1)
    def end():
        values = x_ref[...].astype(jnp.float32)
        centered = values - jnp.mean(values, axis=1, keepdims=True)
        scale = lax.rsqrt(jnp.mean(centered * centered, axis=1, keepdims=True) + 1e-06)
        unit = centered * scale
        grad_norm = acc_ref[...]
        gain_grad_ref[...] = jnp.sum(grad_norm * unit, axis=0, keepdims=True)
        shift_grad_ref[...] = jnp.sum(grad_norm, axis=0, keepdims=True)
        grad_unit = grad_norm * gain_ref[...]
        mean = jnp.mean(grad_unit, axis=1, keepdims=True)
        slant = jnp.mean(grad_unit * unit, axis=1, keepdims=True)
        out_ref[...] = gx_ref[...] + scale * (grad_unit - mean - unit * slant)


def finish(grads, weights, inputs, gx, gain):
    rows, width = inputs.shape
    group, lanes = grads.shape[0], grads.shape[2] // 3
    if lanes % 128:
        grads = grads.reshape(group, rows, 3, lanes).transpose(2, 0, 1, 3)
        grads = grads.reshape(3 * group, rows, lanes)
        grad_spec = pl.BlockSpec((group, rows, lanes), lambda k: (k, 0, 0))
    else:
        grad_spec = pl.BlockSpec((group, rows, lanes), lambda k: (0, 0, k))
    share = weights.shape[1] // 3
    if share % 16:
        weights = weights.reshape(-1, 3, share, width).transpose(1, 0, 2, 3).reshape(1, -1, width)
        share = width
    fixed = lambda *shape: pl.BlockSpec(shape, lambda k: (0, 0))
    vector = jax.ShapeDtypeStruct((1, width), jnp.float32)
    return pl.pallas_call(
        finish_kernel,
        grid=(3,),
        in_specs=[
            grad_spec,
            pl.BlockSpec((weights.shape[0], share, width), lambda k: (0, k, 0)),
            fixed(rows, width),
            fixed(rows, width),
            fixed(1, width),
        ],
        out_specs=[
            fixed(rows, width),
            fixed(1, width),
            fixed(1, width),
            pl.BlockSpec((1, 1, width), lambda k: (k, 0, 0)),
        ],
        out_shape=(
            jax.ShapeDtypeStruct((rows, width), jnp.float32),
            vector,
            vector,
            jax.ShapeDtypeStruct((3, 1, width), jnp.float32),
        ),
        scratch_shapes=[pltpu.VMEM((rows, width), jnp.float32)],
        compiler_params=pltpu.CompilerParams(vmem_limit_bytes=VMEM_BYTES),
        cost_estimate=pl.CostEstimate(
            flops=rows * width * width * 6, bytes_accessed=width * width * 16, transcendentals=0
        ),
        name="finish_input",
    )(grads, weights, inputs, gx, gain[None])


def swap_cores(value):
    return lax.ppermute(value, "core", [(0, 1), (1, 0)])


def line_pieces(value, axis):
    size = lax.axis_size(axis)
    if size == 2:
        other = lax.ppermute(value, axis, [(0, 1), (1, 0)])
        return [(None, other)]
    pieces = []
    for sign in (-1, 1):
        moving = value
        for step in range(1, size):
            pairs = [(i, i - sign) for i in range(size) if 0 <= i - sign < size]
            pairs = [(i, j) for i, j in pairs if 0 <= i + sign * (step - 1) < size]
            moving = lax.ppermute(moving, axis, pairs)
            pieces.append((sign * step, moving))
    return pieces


def line_order(value, pieces, axis):
    place = lax.axis_index(axis)
    size = lax.axis_size(axis)
    if size == 2:
        other = pieces[0][1]
        return jnp.where(place == 0, jnp.stack([value, other]), jnp.stack([other, value]))
    whole = jnp.zeros((size, *value.shape), value.dtype)
    for distance, piece in sorted(pieces, key=lambda item: -abs(item[0])) + [(0, value)]:
        slot = jnp.clip(place + distance, 0, size - 1)
        whole = lax.dynamic_update_index_in_dim(whole, piece, slot, 0)
    return whole


def gather_line(value, axis):
    return line_order(value, line_pieces(value, axis), axis)


def rounded_sum(*terms):
    return sum(term.astype(jnp.float32) for term in terms).astype(jnp.bfloat16)


def scatter_line(value, axis, dim):
    place = lax.axis_index(axis)
    size = lax.axis_size(axis)
    pick = lambda slot: lax.dynamic_index_in_dim(
        value, jnp.clip(slot, 0, size - 1), dim, keepdims=False
    )
    if size == 2:
        return rounded_sum(pick(place), lax.ppermute(pick(1 - place), axis, [(0, 1), (1, 0)]))
    sums = []
    for sign in (-1, 1):
        moving = None
        for step in range(1, size):
            start = 0 if sign < 0 else size - 1
            pairs = [(i, i - sign) for i in range(size) if 0 <= i - sign < size]
            pairs = [(i, j) for i, j in pairs if abs(i - start) <= step - 1]
            own = pick(place - sign * (size - step))
            payload = own if moving is None else rounded_sum(own, moving)
            moving = lax.ppermute(payload, axis, pairs)
        sums.append(moving)
    return rounded_sum(pick(place), *sums)


def on_device(
    tokens,
    cotangent,
    segment_ids,
    valid,
    project_in,
    project_out,
    hidden_up,
    hidden_down,
    gains_biases,
    moment_in,
    moment_out,
    moment_up,
    moment_down,
    moment_gains,
    square_in,
    square_out,
    square_up,
    square_down,
    square_gains,
):
    rows = tokens.shape[0]
    width = tokens.shape[1]
    everyone = ("outer", "inner", "line", "core")
    planes = ("outer", "inner")
    seq = ("line", "core")
    streams, line = lax.axis_size(planes), lax.axis_size("line")
    group = 2 * line
    count = streams * group
    chips = streams * line
    share = width // count
    lanes = width // group
    length = rows * group
    images = length // IMG_LEN
    core = lax.axis_index("core")
    first_core = core == 0

    def in_order(own, other, axis):
        return jnp.concatenate(
            [jnp.where(first_core, own, other), jnp.where(first_core, other, own)], axis=axis
        )

    pieces = line_pieces(tokens, "line")
    own_tokens = line_order(tokens, pieces, "line").reshape(-1, width)
    swapped = [(distance, swap_cores(piece)) for distance, piece in pieces]
    other_tokens = line_order(swap_cores(tokens), swapped, "line").reshape(-1, width)

    owned = project_in.astype(jnp.bfloat16).reshape(share, 3, group, lanes)
    owned = owned.transpose(2, 0, 1, 3).reshape(group, share, 3 * lanes)
    position = lax.broadcasted_iota(jnp.int32, (images, rows), 1)
    found = (segment_ids[None, :] == lax.broadcasted_iota(jnp.int32, (images, rows), 0)) & (
        valid[None, :] == 1
    )
    first = jnp.min(jnp.where(found, position, rows), axis=1)
    small = jnp.concatenate(
        [
            gains_biases.astype(jnp.bfloat16).reshape(-1),
            (first // 32).astype(jnp.bfloat16),
            (first % 32).astype(jnp.bfloat16),
        ]
    )
    vector_size = gains_biases.size
    extra = -(-small.shape[0] // (3 * lanes))
    small = jnp.pad(small, (0, extra * 3 * lanes - small.shape[0])).reshape(1, extra, 3 * lanes)
    blocks = jnp.concatenate([owned, jnp.broadcast_to(small, (group, extra, 3 * lanes))], axis=1)
    blocks = lax.all_to_all(blocks, seq, split_axis=0, concat_axis=0, tiled=True)
    blocks = gather_line(gather_line(blocks, "inner"), "outer")
    blocks = blocks.reshape(count, share + extra, 3 * lanes)
    mine_in = blocks[:, :share].reshape(width, 3 * lanes)
    small = blocks[:, share:].reshape(count, -1)
    vectors = small[:, :vector_size].reshape(count, -1, share).transpose(1, 0, 2)
    vectors = vectors.reshape(-1, width).astype(jnp.float32)
    first = small[:, vector_size : vector_size + 2 * images].astype(jnp.int32)
    first = first[:, :images] * 32 + first[:, images:]
    first = lax.dynamic_slice_in_dim(first, lax.axis_index(planes) * group, group, 0)
    offsets = lax.broadcasted_iota(jnp.int32, (group, images), 0) * rows
    starts = jnp.min(jnp.where(first < rows, first + offsets, length), axis=0)

    half = FF // 2
    unit_block = FF // count
    up_blocks = hidden_up.astype(jnp.bfloat16).reshape(share, chips, 2, unit_block)
    up_first = up_blocks[:, :, 0].reshape(share, half)
    up_second = up_blocks[:, :, 1].reshape(share, half)
    out_rows = project_out.astype(jnp.bfloat16)
    received = swap_cores(
        jnp.concatenate(
            [jnp.where(first_core, up_second, up_first).reshape(-1, width), out_rows], axis=0
        )
    )
    folds = half // width
    up_rows = in_order(
        jnp.where(first_core, up_first, up_second),
        received[: share * folds].reshape(share, half),
        0,
    )
    up_end = 2 * share * folds
    down_end = up_end + half // chips
    packed = jnp.concatenate(
        [
            up_rows.reshape(2 * share, folds, width).transpose(1, 0, 2).reshape(-1, width),
            hidden_down.astype(jnp.bfloat16),
            in_order(out_rows, received[share * folds :], 0),
        ],
        axis=0,
    )
    line_packed = gather_line(packed, "line")
    up_out = jnp.concatenate([line_packed[:, :up_end], line_packed[:, down_end:]], axis=1)
    up_out = gather_line(gather_line(up_out, "inner"), "outer").reshape(chips, -1, width)
    down = gather_line(line_packed[:, up_end:down_end], "outer")
    down = gather_line(down, "inner").swapaxes(0, 1).reshape(chips, -1, width)
    whole_out = up_out[:, up_end:].reshape(width, width)
    direct = (2 * share) % 16 == 0
    if direct:
        mlp_up, mlp_down, mlp_up_rows = up_out, down, 2 * share
    else:
        mlp_up = jnp.concatenate(
            [up_out[:, n * 2 * share : (n + 1) * 2 * share].reshape(width, width) for n in range(folds)],
            axis=0,
        )[None]
        mlp_down, mlp_up_rows = down.reshape(1, half, width), width

    gain_one, shift_one, bias_query, bias_value, bias_out = (
        vectors[0],
        vectors[1],
        vectors[2],
        vectors[3],
        vectors[4],
    )
    scale_one, gain_two, shift_two, bias_down, scale_two = (
        vectors[5],
        vectors[6],
        vectors[7],
        vectors[8],
        vectors[9],
    )
    bias_up = lax.dynamic_index_in_dim(
        vectors[10:].reshape(chips, 2, unit_block), core, axis=1, keepdims=False
    ).reshape(half)
    column = lax.axis_index(seq) * lanes
    bias_in = jnp.concatenate(
        [
            lax.dynamic_slice_in_dim(bias_query, column, lanes, 0),
            jnp.zeros((lanes,), jnp.float32),
            lax.dynamic_slice_in_dim(bias_value, column, lanes, 0),
        ]
    )
    grad_rows = cotangent.astype(jnp.float32) * valid.astype(jnp.float32)[:, None]
    grad_branch = (scale_two * grad_rows).astype(jnp.bfloat16)
    grad_branch_chip = jnp.concatenate([grad_branch, swap_cores(grad_branch)], axis=0)

    normed_one, query, keys, values = norm_mix(
        core.reshape(1),
        own_tokens,
        other_tokens,
        rows,
        gain_one,
        shift_one,
        mine_in,
        bias_in,
    )
    wide, attended, logs = attend(starts, query, keys, values)
    returned = lax.all_to_all(
        attended.reshape(group, rows, lanes), seq, split_axis=0, concat_axis=0, tiled=True
    )
    in_rows = project_in.astype(jnp.bfloat16).reshape(share, 3, width).transpose(1, 0, 2)
    in_rows, returned = lax.optimization_barrier((in_rows.reshape(-1, width), returned))
    gathered_in = lax.all_gather(in_rows, everyone, axis=0, tiled=False)
    attended_rows = returned.transpose(1, 0, 2).reshape(rows, width)
    inputs = tokens.astype(jnp.float32)
    projected = plain_product(attended_rows, whole_out) + bias_out
    second = inputs + scale_one * projected
    norm_two, norm_two_back = jax.vjp(layer_norm, second, gain_two, shift_two)
    normed_two = norm_two.astype(jnp.bfloat16)
    normed_chip = jnp.concatenate([normed_two, swap_cores(normed_two)], axis=0)
    grad_up, grad_down, branch_part, grad_norm_part, grad_bias_up = mlp(
        normed_chip, grad_branch_chip, mlp_up, mlp_down, mlp_up_rows, bias_up
    )
    grad_norm_two = grad_norm_part[:rows] + swap_cores(grad_norm_part[rows:])
    branch = branch_part[:rows] + swap_cores(branch_part[rows:]) + bias_down
    block_output = (second + scale_two * branch).astype(jnp.bfloat16)
    grad_scale_two = jnp.sum(grad_rows * branch, axis=0)
    grad_bias_down = jnp.sum(grad_branch.astype(jnp.float32), axis=0)
    second_part, grad_gain_two, grad_shift_two = norm_two_back(grad_norm_two)
    grad_second = grad_rows + second_part
    grad_scale_one = jnp.sum(grad_second * projected, axis=0)
    grad_projected = (scale_one * grad_second).astype(jnp.bfloat16)
    grad_bias_out = jnp.sum(grad_projected.astype(jnp.float32), axis=0)
    grad_attended = inner_cols(grad_projected, whole_out).astype(jnp.bfloat16)
    grad_stream = lax.all_to_all(
        grad_attended.reshape(rows, group, lanes).transpose(1, 0, 2),
        seq,
        split_axis=0,
        concat_axis=0,
        tiled=True,
    ).reshape(length, lanes)
    grad_out = inner_rows(attended_rows, grad_projected).astype(jnp.bfloat16)
    grad_out = grad_out.reshape(chips, 2 * share, width)
    if direct:
        grad_up = lax.dynamic_update_slice_in_dim(grad_up, grad_out, up_end, 1)
    else:
        grad_up = jnp.concatenate(
            [
                grad_up[0, n * width : (n + 1) * width].reshape(chips, 2 * share, width)
                for n in range(folds)
            ]
            + [grad_out],
            axis=1,
        )
    outer, inner = lax.axis_size("outer"), lax.axis_size("inner")
    grad_up = grad_up.reshape(outer, inner, line, -1, width)
    grad_down = grad_down.reshape(outer, inner, line, -1, width)
    grad_down = scatter_line(scatter_line(grad_down, "outer", 0), "inner", 0)
    grad_up = scatter_line(scatter_line(grad_up, "inner", 1), "outer", 0)
    summed = scatter_line(jnp.concatenate([grad_up, grad_down], axis=1), "line", 0)

    grad_mixed_stream = attend_back(starts, query, keys, values, wide, logs, grad_stream)
    grad_mixed = lax.all_to_all(
        grad_mixed_stream.reshape(group, rows, 3 * lanes), seq, split_axis=0, concat_axis=0, tiled=True
    )
    grad_in = inner_rows(normed_one, grad_mixed_stream).astype(jnp.bfloat16)
    parts = grad_in.reshape(outer, inner, group * share, 3 * lanes)
    parts = scatter_line(scatter_line(parts, "inner", 1), "outer", 0)
    parts = parts.reshape(group, share, 3 * lanes)
    parts = lax.all_to_all(parts, seq, split_axis=0, concat_axis=0, tiled=True)
    parts = parts.astype(jnp.float32)
    summed_in = parts.reshape(group, share, 3, lanes).transpose(1, 2, 0, 3).reshape(share, 3 * width)

    input_grad, grad_gain_one, grad_shift_one, mixed_sums = finish(
        grad_mixed, gathered_in, tokens, grad_second, gain_one
    )
    up_sums = grad_bias_up.reshape(chips, unit_block)
    up_sums = jnp.where(
        (lax.broadcasted_iota(jnp.int32, (1, 2, 1), 1) == core), up_sums[:, None, :], 0.0
    )
    grad_small = jnp.concatenate(
        [
            jnp.stack(
                [
                    grad_gain_one[0],
                    grad_shift_one[0],
                    mixed_sums[0, 0],
                    mixed_sums[2, 0],
                    grad_bias_out,
                    grad_scale_one,
                    grad_gain_two,
                    grad_shift_two,
                    grad_bias_down,
                    grad_scale_two,
                ]
            ),
            up_sums.reshape(-1, width),
        ],
        axis=0,
    )
    small_rows = grad_small.shape[0]
    parts = grad_small.reshape(small_rows, count, share).transpose(1, 0, 2)
    parts = lax.all_to_all(
        parts.reshape(count, small_rows * share), everyone, split_axis=0, concat_axis=0, tiled=True
    )
    summed_gains = jnp.sum(parts, axis=0).reshape(small_rows, share)

    up_sum = summed[:up_end].reshape(folds, 2, share, width)
    out_sum = summed[up_end : up_end + 2 * share].reshape(1, 2, share, width)
    both_sums = jnp.concatenate([up_sum, out_sum], axis=0)
    own_sums = jnp.where(first_core, both_sums[:, 0], both_sums[:, 1])
    other_sums = swap_cores(jnp.where(first_core, both_sums[:, 1], both_sums[:, 0]))
    summed_down = summed[up_end + 2 * share :].astype(jnp.float32)
    summed_out = own_sums[folds].astype(jnp.float32) + other_sums[folds].astype(jnp.float32)
    own_up = own_sums[:folds].transpose(1, 0, 2).reshape(share, chips, 1, unit_block)
    other_up = other_sums[:folds].transpose(1, 0, 2).reshape(share, chips, 1, unit_block)
    summed_up = in_order(own_up, other_up, 2).reshape(share, FF).astype(jnp.float32)
    rate_out = max(1, 4 * D // IMG_LEN) ** (-0.5)
    new_in, new_moment_in, new_square_in = adamw(
        project_in, moment_in, square_in, summed_in, D ** (-0.5), 0.04
    )
    new_out, new_moment_out, new_square_out = adamw(
        project_out, moment_out, square_out, summed_out, rate_out, 0.04
    )
    new_up, new_moment_up, new_square_up = adamw(
        hidden_up, moment_up, square_up, summed_up, D ** (-0.5), 0.04
    )
    new_down, new_moment_down, new_square_down = adamw(
        hidden_down, moment_down, square_down, summed_down, FF ** (-0.5), 0.04
    )
    new_gains, new_moment_gains, new_square_gains = adamw(
        gains_biases, moment_gains, square_gains, summed_gains, 0.2, 0.0
    )
    return (
        block_output,
        input_grad,
        new_in,
        new_out,
        new_up,
        new_down,
        new_gains,
        new_moment_in,
        new_moment_out,
        new_moment_up,
        new_moment_down,
        new_moment_gains,
        new_square_in,
        new_square_out,
        new_square_up,
        new_square_down,
        new_square_gains,
        summed_gains[8],
    )


def solution(mesh):
    streams, group = mesh.shape["fsdp"], mesh.shape["seq"]
    outer = math.isqrt(streams)
    fine = jax.sharding.Mesh(
        mesh.devices.reshape(outer, streams // outer, group // 2, 2),
        ("outer", "inner", "line", "core"),
    )
    return jax.shard_map(
        on_device,
        mesh=fine,
        in_specs=(
            P(("outer", "inner", "line", "core"), None),
            P(("outer", "inner", "line", "core"), None),
            P(("outer", "inner", "line", "core")),
            P(("outer", "inner", "line", "core")),
            P(("outer", "inner", "line", "core"), None),
            P(("outer", "inner", "line", "core"), None),
            P(("outer", "inner", "line", "core"), None),
            P(("outer", "inner", "line", "core"), None),
            P(None, ("outer", "inner", "line", "core")),
            P(("outer", "inner", "line", "core"), None),
            P(("outer", "inner", "line", "core"), None),
            P(("outer", "inner", "line", "core"), None),
            P(("outer", "inner", "line", "core"), None),
            P(None, ("outer", "inner", "line", "core")),
            P(("outer", "inner", "line", "core"), None),
            P(("outer", "inner", "line", "core"), None),
            P(("outer", "inner", "line", "core"), None),
            P(("outer", "inner", "line", "core"), None),
            P(None, ("outer", "inner", "line", "core")),
        ),
        out_specs=(
            P(("outer", "inner", "line", "core"), None),
            P(("outer", "inner", "line", "core"), None),
            P(("outer", "inner", "line", "core"), None),
            P(("outer", "inner", "line", "core"), None),
            P(("outer", "inner", "line", "core"), None),
            P(("outer", "inner", "line", "core"), None),
            P(None, ("outer", "inner", "line", "core")),
            P(("outer", "inner", "line", "core"), None),
            P(("outer", "inner", "line", "core"), None),
            P(("outer", "inner", "line", "core"), None),
            P(("outer", "inner", "line", "core"), None),
            P(None, ("outer", "inner", "line", "core")),
            P(("outer", "inner", "line", "core"), None),
            P(("outer", "inner", "line", "core"), None),
            P(("outer", "inner", "line", "core"), None),
            P(("outer", "inner", "line", "core"), None),
            P(None, ("outer", "inner", "line", "core")),
            P(("outer", "inner", "line", "core")),
        ),
        check_vma=False,
    )
```

```python
import functools
import math

import jax
import jax.numpy as jnp
from jax import lax
from jax.experimental import pallas as pl
from jax.experimental.pallas import tpu as pltpu
from jax.sharding import PartitionSpec as P

D = 1024
FF = 4096
HEADS = 16
HEAD_DIM = 64
IMG_LEN = 1370
WINDOW = 1408
TILE = 352
VMEM_BYTES = 56 * 1024 * 1024
STEP = 10


masked_score = -1e30


def layer_norm(values, gain, shift):
    average = jnp.mean(values, axis=-1, keepdims=True)
    centered = values - average
    variance = jnp.mean(centered * centered, axis=-1, keepdims=True)
    return centered * lax.rsqrt(variance + 1e-06) * gain + shift


def exact_gelu(values):
    return jax.nn.gelu(values, approximate=False)


def plain_product(left, right):
    return jnp.dot(left, right, preferred_element_type=jnp.float32)


def inner_rows(left, right):
    return lax.dot_general(
        left, right, (((0,), (0,)), ((), ())), preferred_element_type=jnp.float32
    )


def inner_cols(left, right):
    return lax.dot_general(
        left, right, (((1,), (1,)), ((), ())), preferred_element_type=jnp.float32
    )


def adamw(param, moment, square, grad, rate, decay):
    new_moment = 0.9 * moment + 0.1 * grad
    new_square = 0.999 * square + 0.001 * grad * grad
    corrected = new_moment / (1.0 - 0.9**STEP)
    scaled = jnp.sqrt(new_square / (1.0 - 0.999**STEP)) + 1e-08
    return (param - rate * (corrected / scaled + decay * param), new_moment, new_square)


def head_lanes(shape):
    return lax.broadcasted_iota(jnp.int32, shape, 1) // HEAD_DIM


def window_of(starts_ref, image, length):
    start = starts_ref[image]
    base = jnp.clip(start // 16 * 16, 0, length - WINDOW)
    return (pl.multiple_of(base, 16), start - base)


def image_mask(position, offset):
    return (position >= offset) & (position < offset + IMG_LEN)


def attend_kernel(starts_ref, q_ref, k_ref, v_ref, wide_ref, out_ref, log_ref):
    image, tile = pl.program_id(0), pl.program_id(1)
    length, lanes = q_ref.shape
    base, offset = window_of(starts_ref, image, length)
    rows = pl.ds(pl.multiple_of(base + tile * TILE, 16), TILE)

    @pl.when((image == 0) & (tile == 0))
    def clear():
        wide_ref[...] = jnp.zeros_like(wide_ref)
        out_ref[...] = jnp.zeros_like(out_ref)
        log_ref[...] = jnp.zeros_like(log_ref)

    query = q_ref[rows, :].astype(jnp.float32) * HEAD_DIM ** (-0.5)
    keys = k_ref[pl.ds(base, WINDOW), :]
    values = v_ref[pl.ds(base, WINDOW), :]
    key_ok = image_mask(lax.broadcasted_iota(jnp.int32, (1, WINDOW), 1), offset)
    bias = jnp.where(key_ok, 0.0, masked_score)
    row_ok = image_mask(lax.broadcasted_iota(jnp.int32, (TILE, 1), 0) + tile * TILE, offset)
    head_of = head_lanes((TILE, lanes))
    total_out = jnp.zeros((TILE, lanes), jnp.float32)
    total_log = jnp.zeros((TILE, lanes), jnp.float32)
    for head in range(lanes // HEAD_DIM):
        mine = head_of == head
        part = jnp.where(mine, query, 0.0).astype(jnp.bfloat16)
        scores = inner_cols(part, keys) + bias
        top = jnp.max(scores, axis=1, keepdims=True)
        weights = jnp.exp(scores - top)
        total = jnp.sum(weights, axis=1, keepdims=True)
        probs = (weights * (1.0 / total)).astype(jnp.bfloat16)
        total_out = jnp.where(mine, plain_product(probs, values), total_out)
        total_log = jnp.where(mine, top + jnp.log(total), total_log)
    merged = jnp.where(row_ok, total_out, wide_ref[rows, :])
    wide_ref[rows, :] = merged
    out_ref[rows, :] = merged.astype(jnp.bfloat16)
    log_ref[rows, :] = jnp.where(row_ok, total_log, log_ref[rows, :])


def attend(starts, query, keys, values):
    length, lanes = query.shape
    whole = pl.BlockSpec((length, lanes), lambda image, tile, starts: (0, 0))
    wide = jax.ShapeDtypeStruct((length, lanes), jnp.float32)
    images = length // IMG_LEN
    return pl.pallas_call(
        attend_kernel,
        grid_spec=pltpu.PrefetchScalarGridSpec(
            num_scalar_prefetch=1,
            grid=(images, WINDOW // TILE),
            in_specs=[whole] * 3,
            out_specs=[whole] * 3,
        ),
        out_shape=(wide, jax.ShapeDtypeStruct((length, lanes), jnp.bfloat16), wide),
        compiler_params=pltpu.CompilerParams(
            vmem_limit_bytes=VMEM_BYTES, dimension_semantics=("arbitrary", "arbitrary")
        ),
        cost_estimate=pl.CostEstimate(
            flops=images * WINDOW * WINDOW * lanes * 8,
            bytes_accessed=length * lanes * 16,
            transcendentals=images * WINDOW * WINDOW * lanes // HEAD_DIM,
        ),
        name="attend_forward",
    )(starts, query, keys, values)


def attend_back_kernel(
    starts_ref, q_ref, k_ref, v_ref, wide_ref, log_ref, go_ref, grad_ref, key_acc, value_acc
):
    image, tile = pl.program_id(0), pl.program_id(1)
    length, lanes = q_ref.shape
    base, offset = window_of(starts_ref, image, length)
    rows = pl.ds(pl.multiple_of(base + tile * TILE, 16), TILE)
    window = pl.ds(base, WINDOW)

    @pl.when((image == 0) & (tile == 0))
    def clear():
        grad_ref[...] = jnp.zeros_like(grad_ref)

    @pl.when(tile == 0)
    def clear_sums():
        key_acc[...] = jnp.zeros_like(key_acc)
        value_acc[...] = jnp.zeros_like(value_acc)

    query = q_ref[rows, :].astype(jnp.float32) * HEAD_DIM ** (-0.5)
    keys = k_ref[window, :]
    values = v_ref[window, :]
    key_ok = image_mask(lax.broadcasted_iota(jnp.int32, (1, WINDOW), 1), offset)
    bias = jnp.where(key_ok, 0.0, masked_score)
    row_ok = image_mask(lax.broadcasted_iota(jnp.int32, (TILE, 1), 0) + tile * TILE, offset)
    head_of = head_lanes((TILE, lanes))
    grad_out = jnp.where(row_ok, go_ref[rows, :].astype(jnp.float32), 0.0)
    centre_parts = grad_out * wide_ref[rows, :]
    logs = jnp.where(row_ok, log_ref[rows, :], -masked_score)
    query_grad = jnp.zeros((TILE, lanes), jnp.float32)
    for head in range(lanes // HEAD_DIM):
        mine = head_of == head
        part = jnp.where(mine, query, 0.0).astype(jnp.bfloat16)
        grad_part = jnp.where(mine, grad_out, 0.0).astype(jnp.bfloat16)
        centre = jnp.sum(jnp.where(mine, centre_parts, 0.0), axis=1, keepdims=True)
        log_total = jnp.max(jnp.where(mine, logs, masked_score), axis=1, keepdims=True)
        probs = jnp.exp(inner_cols(part, keys) + bias - log_total)
        grad_probs = inner_cols(grad_part, values)
        grad_scores = (probs * (grad_probs - centre)).astype(jnp.bfloat16)
        query_grad = jnp.where(mine, plain_product(grad_scores, keys), query_grad)
        key_acc[...] += inner_rows(part, grad_scores)
        value_acc[...] += inner_rows(grad_part, probs.astype(jnp.bfloat16))
    old = grad_ref[rows, 0:lanes].astype(jnp.float32)
    merged = jnp.where(row_ok, query_grad * HEAD_DIM ** (-0.5), old)
    grad_ref[rows, 0:lanes] = merged.astype(jnp.bfloat16)

    @pl.when(tile == pl.num_programs(1) - 1)
    def flush():
        inside = image_mask(lax.broadcasted_iota(jnp.int32, (WINDOW, 1), 0), offset)
        for slot, sums in ((1, key_acc), (2, value_acc)):
            columns = slice(slot * lanes, (slot + 1) * lanes)
            old = grad_ref[window, columns].astype(jnp.float32)
            merged = jnp.where(inside, sums[...].T, old)
            grad_ref[window, columns] = merged.astype(jnp.bfloat16)


def attend_back(starts, query, keys, values, wide, logs, grad_out):
    length, lanes = query.shape
    whole = pl.BlockSpec((length, lanes), lambda image, tile, starts: (0, 0))
    images = length // IMG_LEN
    return pl.pallas_call(
        attend_back_kernel,
        grid_spec=pltpu.PrefetchScalarGridSpec(
            num_scalar_prefetch=1,
            grid=(images, WINDOW // TILE),
            in_specs=[whole] * 6,
            out_specs=pl.BlockSpec((length, 3 * lanes), lambda image, tile, starts: (0, 0)),
            scratch_shapes=[pltpu.VMEM((lanes, WINDOW), jnp.float32)] * 2,
        ),
        out_shape=jax.ShapeDtypeStruct((length, 3 * lanes), jnp.bfloat16),
        compiler_params=pltpu.CompilerParams(
            vmem_limit_bytes=VMEM_BYTES, dimension_semantics=("arbitrary", "arbitrary")
        ),
        cost_estimate=pl.CostEstimate(
            flops=images * WINDOW * WINDOW * lanes * 20,
            bytes_accessed=length * lanes * 22,
            transcendentals=images * WINDOW * WINDOW * lanes // HEAD_DIM,
        ),
        name="attend_backward",
    )(starts, query, keys, values, wide, logs, grad_out)


def norm_mix_kernel(
    core_ref, own_ref, other_ref, gain_ref, shift_ref, weight_ref, bias_ref, a_ref, q_ref, k_ref, v_ref
):
    lanes = q_ref.shape[1]
    mine = lax.rem(pl.program_id(0), 2) == core_ref[0]
    own, other = own_ref[...].astype(jnp.float32), other_ref[...].astype(jnp.float32)
    normed = layer_norm(jnp.where(mine, own, other), gain_ref[...], shift_ref[...])
    normed = normed.astype(jnp.bfloat16)
    a_ref[...] = normed
    mixed = (plain_product(normed, weight_ref[...]) + bias_ref[...]).astype(jnp.bfloat16)
    q_ref[...] = mixed[:, :lanes]
    k_ref[...] = mixed[:, lanes : 2 * lanes]
    v_ref[...] = mixed[:, 2 * lanes :]


def norm_mix(core, own, other, block, gain, shift, weight, bias):
    length, width = own.shape[0] * 2, own.shape[1]
    lanes = weight.shape[1] // 3
    row = lambda size: pl.BlockSpec((block, size), lambda i, core: (i, 0))
    half = pl.BlockSpec((block, width), lambda i, core: (i // 2, 0))
    fixed = lambda *shape: pl.BlockSpec(shape, lambda i, core: (0, 0))
    part = jax.ShapeDtypeStruct((length, lanes), jnp.bfloat16)
    return pl.pallas_call(
        norm_mix_kernel,
        grid_spec=pltpu.PrefetchScalarGridSpec(
            num_scalar_prefetch=1,
            grid=(length // block,),
            in_specs=[
                half,
                half,
                fixed(1, width),
                fixed(1, width),
                fixed(width, 3 * lanes),
                fixed(1, 3 * lanes),
            ],
            out_specs=[row(width), row(lanes), row(lanes), row(lanes)],
        ),
        out_shape=(jax.ShapeDtypeStruct((length, width), jnp.bfloat16), part, part, part),
        compiler_params=pltpu.CompilerParams(vmem_limit_bytes=VMEM_BYTES),
        cost_estimate=pl.CostEstimate(
            flops=length * width * lanes * 6, bytes_accessed=length * width * 4, transcendentals=0
        ),
        name="norm_mix",
    )(core, own, other, gain[None], shift[None], weight, bias[None])


def mlp_kernel(
    pieces,
    core_ref,
    h_ref,
    gm_ref,
    bias_ref,
    *refs,
):
    up_refs, down_refs = refs[:pieces], refs[pieces : 2 * pieces]
    up_grad_ref, down_grad_ref, m_ref, gh_ref, bias_grad_ref, turned_ref = refs[2 * pieces :]
    tile = pl.program_id(0)
    width = h_ref.shape[1]
    chips = up_grad_ref.shape[0]
    up_rows = width // chips
    units = bias_ref.shape[1]
    folds = width // units

    @pl.when(tile == 0)
    def clear():
        m_ref[...] = jnp.zeros_like(m_ref)
        gh_ref[...] = jnp.zeros_like(gh_ref)
        turned_ref[...] = h_ref[...].T

    weight_up = jnp.concatenate([ref[...].reshape(width, -1) for ref in up_refs], axis=1)
    weight_down = jnp.concatenate([ref[...].reshape(-1, width) for ref in down_refs], axis=0)
    gm = gm_ref[...]
    upward = plain_product(h_ref[...], weight_up) + bias_ref[...]
    normal = 0.5 * (1.0 + lax.erf(upward * 0.5**0.5))
    slope = normal + upward * jnp.exp(upward * upward * -0.5) * (0.5 / jnp.pi) ** 0.5
    active = (upward * normal).astype(jnp.bfloat16)
    grad_up = (inner_cols(gm, weight_down) * slope).astype(jnp.bfloat16)
    bias_grad_ref[...] = jnp.sum(grad_up.astype(jnp.float32), axis=0, keepdims=True)
    m_ref[...] += plain_product(active, weight_down)
    gh_ref[...] += inner_cols(grad_up, weight_up)
    up_grad = plain_product(turned_ref[...], grad_up).astype(jnp.bfloat16)
    row = pl.multiple_of(tile // folds * up_rows, up_rows)
    column = pl.multiple_of(lax.rem(tile, folds) * units, units)
    up_grad = up_grad.reshape(chips, up_rows, units)
    up_grad_ref[:, pl.ds(row, up_rows), pl.ds(column, units)] = up_grad
    down_grad = inner_rows(active, gm).astype(jnp.bfloat16)
    down_grad_ref[...] = down_grad.reshape(down_grad_ref.shape)


def mlp(core, normed, gm, weights, bias, chips):
    rows, width = normed.shape
    count = 2 * chips
    share = width // count
    half = bias.shape[0]
    unit_block = half // chips
    units = 256
    folds = width // units
    once = dict(pipeline_mode=pl.Buffered(1))
    fixed = pl.BlockSpec((rows, width), lambda j, core: (0, 0), **once)
    if len(weights) == 1:
        pieces = units // unit_block
        lane_blocks = width // unit_block

        def up_spec(piece):
            def place(j, core):
                block = 2 * (j * pieces + piece) + core[0]
                return (0, block // lane_blocks, lax.rem(block, lane_blocks))

            return pl.BlockSpec((count, share, unit_block), place)

        def down_spec(piece):
            return pl.BlockSpec(
                (1, unit_block, width), lambda j, core: (2 * (j * pieces + piece) + core[0], 1, 0)
            )

        weights = list(weights) * (2 * pieces)
        weight_specs = [up_spec(n) for n in range(pieces)] + [down_spec(n) for n in range(pieces)]
        up_grad_shape = (chips, 2 * share * (half // width) + 2 * share, width)
        down_grad_shape = (chips, unit_block, width)
        down_grad_spec = pl.BlockSpec((pieces, unit_block, width), lambda j, core: (j, 0, 0))
    else:
        pieces = 1
        block = jnp.arange(half) // unit_block * 2 + core[0]
        index = block * unit_block + lax.rem(jnp.arange(half), unit_block)
        weights = [jnp.take(weights[0], index, axis=1), jnp.take(weights[1], index, axis=0)]
        weight_specs = [
            pl.BlockSpec((width, units), lambda j, core: (0, j)),
            pl.BlockSpec((units, width), lambda j, core: (j, 0)),
        ]
        up_grad_shape = (1, half // width * width, width)
        down_grad_shape = (1, half, width)
        down_grad_spec = pl.BlockSpec((1, units, width), lambda j, core: (0, j, 0))
    total = jax.ShapeDtypeStruct((rows, width), jnp.float32)
    outs = pl.pallas_call(
        functools.partial(mlp_kernel, pieces),
        grid_spec=pltpu.PrefetchScalarGridSpec(
            num_scalar_prefetch=1,
            grid=(half // units,),
            in_specs=[fixed, fixed, pl.BlockSpec((1, units), lambda j, core: (0, j)), *weight_specs],
            out_specs=[
                pl.BlockSpec(up_grad_shape, lambda j, core: (0, 0, 0), **once),
                down_grad_spec,
                fixed,
                fixed,
                pl.BlockSpec((1, units), lambda j, core: (0, j)),
            ],
            scratch_shapes=[pltpu.VMEM((width, rows), jnp.bfloat16)],
        ),
        out_shape=(
            jax.ShapeDtypeStruct(up_grad_shape, jnp.bfloat16),
            jax.ShapeDtypeStruct(down_grad_shape, jnp.bfloat16),
            total,
            total,
            jax.ShapeDtypeStruct((1, half), jnp.float32),
        ),
        compiler_params=pltpu.CompilerParams(vmem_limit_bytes=VMEM_BYTES),
        cost_estimate=pl.CostEstimate(
            flops=rows * width * half * 12,
            bytes_accessed=half * width * 8 + rows * width * 12,
            transcendentals=rows * half * 2,
        ),
        name="mlp_both_ways",
    )(core, normed, gm, bias[None], *weights)
    up_grad, down_grad = outs[0], outs[1]
    if pieces == 1:
        up_grad = up_grad.reshape(half // width, chips, 2 * share, width).swapaxes(0, 1)
        up_grad = up_grad.reshape(chips, -1, width)
        up_grad = jnp.pad(up_grad, ((0, 0), (0, 2 * share), (0, 0)))
        down_grad = down_grad.reshape(chips, unit_block, width)
    return (up_grad, down_grad, *outs[2:])


def finish_kernel(
    grad_ref, weight_ref, x_ref, gx_ref, gain_ref, out_ref, gain_grad_ref, shift_grad_ref, sums_ref, acc_ref
):
    step = pl.program_id(0)
    parts = [grad_ref[slot] for slot in range(grad_ref.shape[0])]
    grad = jnp.concatenate(parts, axis=1)
    width = x_ref.shape[1]
    product = inner_cols(grad, weight_ref[...].reshape(width, width))
    sums_ref[...] = jnp.sum(grad.astype(jnp.float32), axis=0, keepdims=True)[None]

    @pl.when(step == 0)
    def begin():
        acc_ref[...] = product

    @pl.when(step > 0)
    def further():
        acc_ref[...] += product

    @pl.when(step == pl.num_programs(0) - 1)
    def end():
        values = x_ref[...].astype(jnp.float32)
        centered = values - jnp.mean(values, axis=1, keepdims=True)
        scale = lax.rsqrt(jnp.mean(centered * centered, axis=1, keepdims=True) + 1e-06)
        unit = centered * scale
        grad_norm = acc_ref[...]
        gain_grad_ref[...] = jnp.sum(grad_norm * unit, axis=0, keepdims=True)
        shift_grad_ref[...] = jnp.sum(grad_norm, axis=0, keepdims=True)
        grad_unit = grad_norm * gain_ref[...]
        mean = jnp.mean(grad_unit, axis=1, keepdims=True)
        slant = jnp.mean(grad_unit * unit, axis=1, keepdims=True)
        out_ref[...] = gx_ref[...] + scale * (grad_unit - mean - unit * slant)


def finish(grads, weights, inputs, gx, gain):
    rows, width = inputs.shape
    group, lanes = grads.shape[0], grads.shape[2] // 3
    if lanes % 128:
        grads = grads.reshape(group, rows, 3, lanes).transpose(2, 0, 1, 3)
        grads = grads.reshape(3 * group, rows, lanes)
        grad_spec = pl.BlockSpec((group, rows, lanes), lambda k: (k, 0, 0))
    else:
        grad_spec = pl.BlockSpec((group, rows, lanes), lambda k: (0, 0, k))
    if weights.ndim == 3:
        share = width // weights.shape[0]
        first = weights.shape[1] // share - 3
        weight_spec = pl.BlockSpec((weights.shape[0], share, width), lambda k: (0, first + k, 0))
    else:
        weight_spec = pl.BlockSpec((width, width), lambda k: (0, k))
    fixed = lambda *shape: pl.BlockSpec(shape, lambda k: (0, 0))
    vector = jax.ShapeDtypeStruct((1, width), jnp.float32)
    return pl.pallas_call(
        finish_kernel,
        grid=(3,),
        in_specs=[
            grad_spec,
            weight_spec,
            fixed(rows, width),
            fixed(rows, width),
            fixed(1, width),
        ],
        out_specs=[
            fixed(rows, width),
            fixed(1, width),
            fixed(1, width),
            pl.BlockSpec((1, 1, width), lambda k: (k, 0, 0)),
        ],
        out_shape=(
            jax.ShapeDtypeStruct((rows, width), jnp.float32),
            vector,
            vector,
            jax.ShapeDtypeStruct((3, 1, width), jnp.float32),
        ),
        scratch_shapes=[pltpu.VMEM((rows, width), jnp.float32)],
        compiler_params=pltpu.CompilerParams(vmem_limit_bytes=VMEM_BYTES),
        cost_estimate=pl.CostEstimate(
            flops=rows * width * width * 6, bytes_accessed=width * width * 16, transcendentals=0
        ),
        name="finish_input",
    )(grads, weights, inputs, gx, gain[None])


def swap_cores(value):
    return lax.ppermute(value, "core", [(0, 1), (1, 0)])


def line_pieces(value, axis):
    size = lax.axis_size(axis)
    if size == 2:
        other = lax.ppermute(value, axis, [(0, 1), (1, 0)])
        return [(None, other)]
    pieces = []
    for sign in (-1, 1):
        moving = value
        for step in range(1, size):
            pairs = [(i, i - sign) for i in range(size) if 0 <= i - sign < size]
            pairs = [(i, j) for i, j in pairs if 0 <= i + sign * (step - 1) < size]
            moving = lax.ppermute(moving, axis, pairs)
            pieces.append((sign * step, moving))
    return pieces


def line_order(value, pieces, axis):
    place = lax.axis_index(axis)
    size = lax.axis_size(axis)
    if size == 2:
        other = pieces[0][1]
        return jnp.where(place == 0, jnp.stack([value, other]), jnp.stack([other, value]))
    whole = jnp.zeros((size, *value.shape), value.dtype)
    for distance, piece in sorted(pieces, key=lambda item: -abs(item[0])) + [(0, value)]:
        slot = jnp.clip(place + distance, 0, size - 1)
        whole = lax.dynamic_update_index_in_dim(whole, piece, slot, 0)
    return whole


def gather_line(value, axis):
    return line_order(value, line_pieces(value, axis), axis)


def rounded_sum(*terms):
    return sum(term.astype(jnp.float32) for term in terms).astype(jnp.bfloat16)


def scatter_line(value, axis, dim):
    place = lax.axis_index(axis)
    size = lax.axis_size(axis)
    pick = lambda slot: lax.dynamic_index_in_dim(
        value, jnp.clip(slot, 0, size - 1), dim, keepdims=False
    )
    if size == 2:
        return rounded_sum(pick(place), lax.ppermute(pick(1 - place), axis, [(0, 1), (1, 0)]))
    sums = []
    for sign in (-1, 1):
        moving = None
        for step in range(1, size):
            start = 0 if sign < 0 else size - 1
            pairs = [(i, i - sign) for i in range(size) if 0 <= i - sign < size]
            pairs = [(i, j) for i, j in pairs if abs(i - start) <= step - 1]
            own = pick(place - sign * (size - step))
            payload = own if moving is None else rounded_sum(own, moving)
            moving = lax.ppermute(payload, axis, pairs)
        sums.append(moving)
    return rounded_sum(pick(place), *sums)


def on_device(
    tokens,
    cotangent,
    segment_ids,
    valid,
    project_in,
    project_out,
    hidden_up,
    hidden_down,
    gains_biases,
    moment_in,
    moment_out,
    moment_up,
    moment_down,
    moment_gains,
    square_in,
    square_out,
    square_up,
    square_down,
    square_gains,
):
    rows = tokens.shape[0]
    width = tokens.shape[1]
    everyone = ("outer", "inner", "line", "core")
    planes = ("outer", "inner")
    seq = ("line", "core")
    streams, line = lax.axis_size(planes), lax.axis_size("line")
    group = 2 * line
    count = streams * group
    chips = streams * line
    share = width // count
    lanes = width // group
    length = rows * group
    images = length // IMG_LEN
    core = lax.axis_index("core")
    first_core = core == 0

    def in_order(own, other, axis):
        return jnp.concatenate(
            [jnp.where(first_core, own, other), jnp.where(first_core, other, own)], axis=axis
        )

    unit_block = FF // count
    low = lambda value: value.astype(jnp.bfloat16)
    if share % 16 == 0 and unit_block == 128:
        fold = lambda value: low(value).reshape(share, -1, width).swapaxes(0, 1).reshape(-1, width)
        packed = jnp.concatenate(
            [fold(hidden_up), low(hidden_down), low(project_out), fold(project_in)], axis=0
        )
        gathered = lax.all_gather(packed, everyone, axis=0, tiled=False)
        out_at = FF // width * share + unit_block
        whole_out = gathered[:, out_at : out_at + share].reshape(width, width)
        mlp_weights, whole_in = (gathered,), gathered
    else:
        whole_in, whole_out, whole_up, whole_down = (
            lax.all_gather(low(value), everyone, axis=0, tiled=True)
            for value in (project_in, project_out, hidden_up, hidden_down)
        )
        mlp_weights = (whole_up, whole_down)

    pieces = line_pieces(tokens, "line")
    own_tokens = line_order(tokens, pieces, "line").reshape(-1, width)
    swapped = [(distance, swap_cores(piece)) for distance, piece in pieces]
    other_tokens = line_order(swap_cores(tokens), swapped, "line").reshape(-1, width)

    owned = project_in.astype(jnp.bfloat16).reshape(share, 3, group, lanes)
    owned = owned.transpose(2, 0, 1, 3).reshape(group, share, 3 * lanes)
    position = lax.broadcasted_iota(jnp.int32, (images, rows), 1)
    found = (segment_ids[None, :] == lax.broadcasted_iota(jnp.int32, (images, rows), 0)) & (
        valid[None, :] == 1
    )
    first = jnp.min(jnp.where(found, position, rows), axis=1)
    small = jnp.concatenate(
        [
            gains_biases.astype(jnp.bfloat16).reshape(-1),
            (first // 32).astype(jnp.bfloat16),
            (first % 32).astype(jnp.bfloat16),
        ]
    )
    vector_size = gains_biases.size
    extra = -(-small.shape[0] // (3 * lanes))
    small = jnp.pad(small, (0, extra * 3 * lanes - small.shape[0])).reshape(1, extra, 3 * lanes)
    blocks = jnp.concatenate([owned, jnp.broadcast_to(small, (group, extra, 3 * lanes))], axis=1)
    blocks = lax.all_to_all(blocks, seq, split_axis=0, concat_axis=0, tiled=True)
    blocks = gather_line(gather_line(blocks, "inner"), "outer")
    blocks = blocks.reshape(count, share + extra, 3 * lanes)
    mine_in = blocks[:, :share].reshape(width, 3 * lanes)
    small = blocks[:, share:].reshape(count, -1)
    vectors = small[:, :vector_size].reshape(count, -1, share).transpose(1, 0, 2)
    vectors = vectors.reshape(-1, width).astype(jnp.float32)
    first = small[:, vector_size : vector_size + 2 * images].astype(jnp.int32)
    first = first[:, :images] * 32 + first[:, images:]
    first = lax.dynamic_slice_in_dim(first, lax.axis_index(planes) * group, group, 0)
    offsets = lax.broadcasted_iota(jnp.int32, (group, images), 0) * rows
    starts = jnp.min(jnp.where(first < rows, first + offsets, length), axis=0)

    half = FF // 2
    folds = half // width
    up_end = 2 * share * folds

    gain_one, shift_one, bias_query, bias_value, bias_out = (
        vectors[0],
        vectors[1],
        vectors[2],
        vectors[3],
        vectors[4],
    )
    scale_one, gain_two, shift_two, bias_down, scale_two = (
        vectors[5],
        vectors[6],
        vectors[7],
        vectors[8],
        vectors[9],
    )
    bias_up = lax.dynamic_index_in_dim(
        vectors[10:].reshape(chips, 2, unit_block), core, axis=1, keepdims=False
    ).reshape(half)
    column = lax.axis_index(seq) * lanes
    bias_in = jnp.concatenate(
        [
            lax.dynamic_slice_in_dim(bias_query, column, lanes, 0),
            jnp.zeros((lanes,), jnp.float32),
            lax.dynamic_slice_in_dim(bias_value, column, lanes, 0),
        ]
    )
    grad_rows = cotangent.astype(jnp.float32) * valid.astype(jnp.float32)[:, None]
    grad_branch = (scale_two * grad_rows).astype(jnp.bfloat16)
    grad_branch_chip = jnp.concatenate([grad_branch, swap_cores(grad_branch)], axis=0)

    normed_one, query, keys, values = norm_mix(
        core.reshape(1),
        own_tokens,
        other_tokens,
        rows,
        gain_one,
        shift_one,
        mine_in,
        bias_in,
    )
    wide, attended, logs = attend(starts, query, keys, values)
    returned = lax.all_to_all(
        attended.reshape(group, rows, lanes), seq, split_axis=0, concat_axis=0, tiled=True
    )
    attended_rows = returned.transpose(1, 0, 2).reshape(rows, width)
    inputs = tokens.astype(jnp.float32)
    projected = plain_product(attended_rows, whole_out) + bias_out
    second = inputs + scale_one * projected
    norm_two, norm_two_back = jax.vjp(layer_norm, second, gain_two, shift_two)
    normed_two = norm_two.astype(jnp.bfloat16)
    normed_chip = jnp.concatenate([normed_two, swap_cores(normed_two)], axis=0)
    grad_up, grad_down, branch_part, grad_norm_part, grad_bias_up = mlp(
        core.reshape(1), normed_chip, grad_branch_chip, mlp_weights, bias_up, chips
    )
    grad_norm_two = grad_norm_part[:rows] + swap_cores(grad_norm_part[rows:])
    branch = branch_part[:rows] + swap_cores(branch_part[rows:]) + bias_down
    block_output = (second + scale_two * branch).astype(jnp.bfloat16)
    grad_scale_two = jnp.sum(grad_rows * branch, axis=0)
    grad_bias_down = jnp.sum(grad_branch.astype(jnp.float32), axis=0)
    second_part, grad_gain_two, grad_shift_two = norm_two_back(grad_norm_two)
    grad_second = grad_rows + second_part
    grad_scale_one = jnp.sum(grad_second * projected, axis=0)
    grad_projected = (scale_one * grad_second).astype(jnp.bfloat16)
    grad_bias_out = jnp.sum(grad_projected.astype(jnp.float32), axis=0)
    grad_attended = inner_cols(grad_projected, whole_out).astype(jnp.bfloat16)
    grad_stream = lax.all_to_all(
        grad_attended.reshape(rows, group, lanes).transpose(1, 0, 2),
        seq,
        split_axis=0,
        concat_axis=0,
        tiled=True,
    ).reshape(length, lanes)
    grad_out = inner_rows(attended_rows, grad_projected).astype(jnp.bfloat16)
    grad_out = grad_out.reshape(chips, 2 * share, width)
    grad_up = lax.dynamic_update_slice_in_dim(grad_up, grad_out, up_end, 1)
    outer, inner = lax.axis_size("outer"), lax.axis_size("inner")
    grad_up = grad_up.reshape(outer, inner, line, -1, width)
    grad_down = grad_down.reshape(outer, inner, line, -1, width)
    grad_down = scatter_line(scatter_line(grad_down, "outer", 0), "inner", 0)
    grad_up = scatter_line(scatter_line(grad_up, "inner", 1), "outer", 0)
    grad_mixed_stream = attend_back(starts, query, keys, values, wide, logs, grad_stream)
    grad_mixed = lax.all_to_all(
        grad_mixed_stream.reshape(group, rows, 3 * lanes), seq, split_axis=0, concat_axis=0, tiled=True
    )
    plane_sums = jnp.concatenate([grad_up, grad_down], axis=1)
    grad_in = inner_rows(normed_one, grad_mixed_stream).astype(jnp.bfloat16)
    parts = grad_in.reshape(outer, inner, group * share, 3 * lanes)
    parts = scatter_line(scatter_line(parts, "inner", 1), "outer", 0)
    parts, plane_sums, grad_mixed = lax.optimization_barrier((parts, plane_sums, grad_mixed))
    summed = scatter_line(plane_sums, "line", 0)
    parts = parts.reshape(group, share, 3 * lanes)
    parts = lax.all_to_all(parts, seq, split_axis=0, concat_axis=0, tiled=True)
    parts = parts.astype(jnp.float32)
    summed_in = parts.reshape(group, share, 3, lanes).transpose(1, 2, 0, 3).reshape(share, 3 * width)

    input_grad, grad_gain_one, grad_shift_one, mixed_sums = finish(
        grad_mixed, whole_in, tokens, grad_second, gain_one
    )
    up_sums = grad_bias_up.reshape(chips, unit_block)
    up_sums = jnp.where(
        (lax.broadcasted_iota(jnp.int32, (1, 2, 1), 1) == core), up_sums[:, None, :], 0.0
    )
    grad_small = jnp.concatenate(
        [
            jnp.stack(
                [
                    grad_gain_one[0],
                    grad_shift_one[0],
                    mixed_sums[0, 0],
                    mixed_sums[2, 0],
                    grad_bias_out,
                    grad_scale_one,
                    grad_gain_two,
                    grad_shift_two,
                    grad_bias_down,
                    grad_scale_two,
                ]
            ),
            up_sums.reshape(-1, width),
        ],
        axis=0,
    )
    small_rows = grad_small.shape[0]
    parts = grad_small.reshape(small_rows, count, share).transpose(1, 0, 2)
    parts = lax.all_to_all(
        parts.reshape(count, small_rows * share), everyone, split_axis=0, concat_axis=0, tiled=True
    )
    summed_gains = jnp.sum(parts, axis=0).reshape(small_rows, share)

    up_sum = summed[:up_end].reshape(folds, 2, share, width)
    out_sum = summed[up_end : up_end + 2 * share].reshape(1, 2, share, width)
    both_sums = jnp.concatenate([up_sum, out_sum], axis=0)
    own_sums = jnp.where(first_core, both_sums[:, 0], both_sums[:, 1])
    other_sums = swap_cores(jnp.where(first_core, both_sums[:, 1], both_sums[:, 0]))
    summed_down = summed[up_end + 2 * share :].astype(jnp.float32)
    summed_out = own_sums[folds].astype(jnp.float32) + other_sums[folds].astype(jnp.float32)
    own_up = own_sums[:folds].transpose(1, 0, 2).reshape(share, chips, 1, unit_block)
    other_up = other_sums[:folds].transpose(1, 0, 2).reshape(share, chips, 1, unit_block)
    summed_up = in_order(own_up, other_up, 2).reshape(share, FF).astype(jnp.float32)
    rate_out = max(1, 4 * D // IMG_LEN) ** (-0.5)
    new_in, new_moment_in, new_square_in = adamw(
        project_in, moment_in, square_in, summed_in, D ** (-0.5), 0.04
    )
    new_out, new_moment_out, new_square_out = adamw(
        project_out, moment_out, square_out, summed_out, rate_out, 0.04
    )
    new_up, new_moment_up, new_square_up = adamw(
        hidden_up, moment_up, square_up, summed_up, D ** (-0.5), 0.04
    )
    new_down, new_moment_down, new_square_down = adamw(
        hidden_down, moment_down, square_down, summed_down, FF ** (-0.5), 0.04
    )
    new_gains, new_moment_gains, new_square_gains = adamw(
        gains_biases, moment_gains, square_gains, summed_gains, 0.2, 0.0
    )
    return (
        block_output,
        input_grad,
        new_in,
        new_out,
        new_up,
        new_down,
        new_gains,
        new_moment_in,
        new_moment_out,
        new_moment_up,
        new_moment_down,
        new_moment_gains,
        new_square_in,
        new_square_out,
        new_square_up,
        new_square_down,
        new_square_gains,
        summed_gains[8],
    )


def solution(mesh):
    streams, group = mesh.shape["fsdp"], mesh.shape["seq"]
    outer = math.isqrt(streams)
    fine = jax.sharding.Mesh(
        mesh.devices.reshape(outer, streams // outer, group // 2, 2),
        ("outer", "inner", "line", "core"),
    )
    return jax.shard_map(
        on_device,
        mesh=fine,
        in_specs=(
            P(("outer", "inner", "line", "core"), None),
            P(("outer", "inner", "line", "core"), None),
            P(("outer", "inner", "line", "core")),
            P(("outer", "inner", "line", "core")),
            P(("outer", "inner", "line", "core"), None),
            P(("outer", "inner", "line", "core"), None),
            P(("outer", "inner", "line", "core"), None),
            P(("outer", "inner", "line", "core"), None),
            P(None, ("outer", "inner", "line", "core")),
            P(("outer", "inner", "line", "core"), None),
            P(("outer", "inner", "line", "core"), None),
            P(("outer", "inner", "line", "core"), None),
            P(("outer", "inner", "line", "core"), None),
            P(None, ("outer", "inner", "line", "core")),
            P(("outer", "inner", "line", "core"), None),
            P(("outer", "inner", "line", "core"), None),
            P(("outer", "inner", "line", "core"), None),
            P(("outer", "inner", "line", "core"), None),
            P(None, ("outer", "inner", "line", "core")),
        ),
        out_specs=(
            P(("outer", "inner", "line", "core"), None),
            P(("outer", "inner", "line", "core"), None),
            P(("outer", "inner", "line", "core"), None),
            P(("outer", "inner", "line", "core"), None),
            P(("outer", "inner", "line", "core"), None),
            P(("outer", "inner", "line", "core"), None),
            P(None, ("outer", "inner", "line", "core")),
            P(("outer", "inner", "line", "core"), None),
            P(("outer", "inner", "line", "core"), None),
            P(("outer", "inner", "line", "core"), None),
            P(("outer", "inner", "line", "core"), None),
            P(None, ("outer", "inner", "line", "core")),
            P(("outer", "inner", "line", "core"), None),
            P(("outer", "inner", "line", "core"), None),
            P(("outer", "inner", "line", "core"), None),
            P(("outer", "inner", "line", "core"), None),
            P(None, ("outer", "inner", "line", "core")),
            P(("outer", "inner", "line", "core")),
        ),
        check_vma=False,
    )
```

```python
import functools
import math

import jax
import jax.numpy as jnp
from jax import lax
from jax.experimental import pallas as pl
from jax.experimental.pallas import tpu as pltpu
from jax.sharding import PartitionSpec as P

D = 1024
FF = 4096
HEADS = 16
HEAD_DIM = 64
IMG_LEN = 1370
WINDOW = 1408
TILE = 352
VMEM_BYTES = 56 * 1024 * 1024
STEP = 10


masked_score = -1e30


def layer_norm(values, gain, shift):
    average = jnp.mean(values, axis=-1, keepdims=True)
    centered = values - average
    variance = jnp.mean(centered * centered, axis=-1, keepdims=True)
    return centered * lax.rsqrt(variance + 1e-06) * gain + shift


def exact_gelu(values):
    return jax.nn.gelu(values, approximate=False)


def plain_product(left, right):
    return jnp.dot(left, right, preferred_element_type=jnp.float32)


def inner_rows(left, right):
    return lax.dot_general(
        left, right, (((0,), (0,)), ((), ())), preferred_element_type=jnp.float32
    )


def inner_cols(left, right):
    return lax.dot_general(
        left, right, (((1,), (1,)), ((), ())), preferred_element_type=jnp.float32
    )


def adamw(param, moment, square, grad, rate, decay):
    new_moment = 0.9 * moment + 0.1 * grad
    new_square = 0.999 * square + 0.001 * grad * grad
    corrected = new_moment / (1.0 - 0.9**STEP)
    scaled = jnp.sqrt(new_square / (1.0 - 0.999**STEP)) + 1e-08
    return (param - rate * (corrected / scaled + decay * param), new_moment, new_square)


def head_lanes(shape):
    return lax.broadcasted_iota(jnp.int32, shape, 1) // HEAD_DIM


def window_of(starts_ref, image, length):
    start = starts_ref[image]
    base = jnp.clip(start // 16 * 16, 0, length - WINDOW)
    return (pl.multiple_of(base, 16), start - base)


def image_mask(position, offset):
    return (position >= offset) & (position < offset + IMG_LEN)


def attend_kernel(starts_ref, q_ref, k_ref, v_ref, wide_ref, out_ref, log_ref):
    image, tile = pl.program_id(0), pl.program_id(1)
    length, lanes = q_ref.shape
    base, offset = window_of(starts_ref, image, length)
    rows = pl.ds(pl.multiple_of(base + tile * TILE, 16), TILE)

    @pl.when((image == 0) & (tile == 0))
    def clear():
        wide_ref[...] = jnp.zeros_like(wide_ref)
        out_ref[...] = jnp.zeros_like(out_ref)
        log_ref[...] = jnp.zeros_like(log_ref)

    query = q_ref[rows, :].astype(jnp.float32) * HEAD_DIM ** (-0.5)
    keys = k_ref[pl.ds(base, WINDOW), :]
    values = v_ref[pl.ds(base, WINDOW), :]
    key_ok = image_mask(lax.broadcasted_iota(jnp.int32, (1, WINDOW), 1), offset)
    bias = jnp.where(key_ok, 0.0, masked_score)
    row_ok = image_mask(lax.broadcasted_iota(jnp.int32, (TILE, 1), 0) + tile * TILE, offset)
    head_of = head_lanes((TILE, lanes))
    total_out = jnp.zeros((TILE, lanes), jnp.float32)
    total_log = jnp.zeros((TILE, lanes), jnp.float32)
    for head in range(lanes // HEAD_DIM):
        mine = head_of == head
        part = jnp.where(mine, query, 0.0).astype(jnp.bfloat16)
        scores = inner_cols(part, keys) + bias
        top = jnp.max(scores, axis=1, keepdims=True)
        weights = jnp.exp(scores - top)
        total = jnp.sum(weights, axis=1, keepdims=True)
        probs = (weights * (1.0 / total)).astype(jnp.bfloat16)
        total_out = jnp.where(mine, plain_product(probs, values), total_out)
        total_log = jnp.where(mine, top + jnp.log(total), total_log)
    merged = jnp.where(row_ok, total_out, wide_ref[rows, :])
    wide_ref[rows, :] = merged
    out_ref[rows, :] = merged.astype(jnp.bfloat16)
    log_ref[rows, :] = jnp.where(row_ok, total_log, log_ref[rows, :])


def attend(starts, query, keys, values):
    length, lanes = query.shape
    whole = pl.BlockSpec((length, lanes), lambda image, tile, starts: (0, 0))
    wide = jax.ShapeDtypeStruct((length, lanes), jnp.float32)
    images = length // IMG_LEN
    return pl.pallas_call(
        attend_kernel,
        grid_spec=pltpu.PrefetchScalarGridSpec(
            num_scalar_prefetch=1,
            grid=(images, WINDOW // TILE),
            in_specs=[whole] * 3,
            out_specs=[whole] * 3,
        ),
        out_shape=(wide, jax.ShapeDtypeStruct((length, lanes), jnp.bfloat16), wide),
        compiler_params=pltpu.CompilerParams(
            vmem_limit_bytes=VMEM_BYTES, dimension_semantics=("arbitrary", "arbitrary")
        ),
        cost_estimate=pl.CostEstimate(
            flops=images * WINDOW * WINDOW * lanes * 8,
            bytes_accessed=length * lanes * 16,
            transcendentals=images * WINDOW * WINDOW * lanes // HEAD_DIM,
        ),
        name="attend_forward",
    )(starts, query, keys, values)


def attend_back_kernel(
    starts_ref, q_ref, k_ref, v_ref, wide_ref, log_ref, go_ref, grad_ref, key_acc, value_acc
):
    image, tile = pl.program_id(0), pl.program_id(1)
    length, lanes = q_ref.shape
    base, offset = window_of(starts_ref, image, length)
    rows = pl.ds(pl.multiple_of(base + tile * TILE, 16), TILE)
    window = pl.ds(base, WINDOW)

    @pl.when((image == 0) & (tile == 0))
    def clear():
        grad_ref[...] = jnp.zeros_like(grad_ref)

    @pl.when(tile == 0)
    def clear_sums():
        key_acc[...] = jnp.zeros_like(key_acc)
        value_acc[...] = jnp.zeros_like(value_acc)

    query = q_ref[rows, :].astype(jnp.float32) * HEAD_DIM ** (-0.5)
    keys = k_ref[window, :]
    values = v_ref[window, :]
    key_ok = image_mask(lax.broadcasted_iota(jnp.int32, (1, WINDOW), 1), offset)
    bias = jnp.where(key_ok, 0.0, masked_score)
    row_ok = image_mask(lax.broadcasted_iota(jnp.int32, (TILE, 1), 0) + tile * TILE, offset)
    head_of = head_lanes((TILE, lanes))
    grad_out = jnp.where(row_ok, go_ref[rows, :].astype(jnp.float32), 0.0)
    centre_parts = grad_out * wide_ref[rows, :]
    logs = jnp.where(row_ok, log_ref[rows, :], -masked_score)
    query_grad = jnp.zeros((TILE, lanes), jnp.float32)
    for head in range(lanes // HEAD_DIM):
        mine = head_of == head
        part = jnp.where(mine, query, 0.0).astype(jnp.bfloat16)
        grad_part = jnp.where(mine, grad_out, 0.0).astype(jnp.bfloat16)
        centre = jnp.sum(jnp.where(mine, centre_parts, 0.0), axis=1, keepdims=True)
        log_total = jnp.max(jnp.where(mine, logs, masked_score), axis=1, keepdims=True)
        probs = jnp.exp(inner_cols(part, keys) + bias - log_total)
        grad_probs = inner_cols(grad_part, values)
        grad_scores = (probs * (grad_probs - centre)).astype(jnp.bfloat16)
        query_grad = jnp.where(mine, plain_product(grad_scores, keys), query_grad)
        key_acc[...] += inner_rows(part, grad_scores)
        value_acc[...] += inner_rows(grad_part, probs.astype(jnp.bfloat16))
    old = grad_ref[rows, 0:lanes].astype(jnp.float32)
    merged = jnp.where(row_ok, query_grad * HEAD_DIM ** (-0.5), old)
    grad_ref[rows, 0:lanes] = merged.astype(jnp.bfloat16)

    @pl.when(tile == pl.num_programs(1) - 1)
    def flush():
        inside = image_mask(lax.broadcasted_iota(jnp.int32, (WINDOW, 1), 0), offset)
        for slot, sums in ((1, key_acc), (2, value_acc)):
            columns = slice(slot * lanes, (slot + 1) * lanes)
            old = grad_ref[window, columns].astype(jnp.float32)
            merged = jnp.where(inside, sums[...].T, old)
            grad_ref[window, columns] = merged.astype(jnp.bfloat16)


def attend_back(starts, query, keys, values, wide, logs, grad_out):
    length, lanes = query.shape
    whole = pl.BlockSpec((length, lanes), lambda image, tile, starts: (0, 0))
    images = length // IMG_LEN
    return pl.pallas_call(
        attend_back_kernel,
        grid_spec=pltpu.PrefetchScalarGridSpec(
            num_scalar_prefetch=1,
            grid=(images, WINDOW // TILE),
            in_specs=[whole] * 6,
            out_specs=pl.BlockSpec((length, 3 * lanes), lambda image, tile, starts: (0, 0)),
            scratch_shapes=[pltpu.VMEM((lanes, WINDOW), jnp.float32)] * 2,
        ),
        out_shape=jax.ShapeDtypeStruct((length, 3 * lanes), jnp.bfloat16),
        compiler_params=pltpu.CompilerParams(
            vmem_limit_bytes=VMEM_BYTES, dimension_semantics=("arbitrary", "arbitrary")
        ),
        cost_estimate=pl.CostEstimate(
            flops=images * WINDOW * WINDOW * lanes * 20,
            bytes_accessed=length * lanes * 22,
            transcendentals=images * WINDOW * WINDOW * lanes // HEAD_DIM,
        ),
        name="attend_backward",
    )(starts, query, keys, values, wide, logs, grad_out)


def norm_mix_kernel(
    core_ref, own_ref, other_ref, gain_ref, shift_ref, weight_ref, bias_ref, a_ref, q_ref, k_ref, v_ref
):
    lanes = q_ref.shape[1]
    mine = lax.rem(pl.program_id(0), 2) == core_ref[0]
    own, other = own_ref[...].astype(jnp.float32), other_ref[...].astype(jnp.float32)
    normed = layer_norm(jnp.where(mine, own, other), gain_ref[...], shift_ref[...])
    normed = normed.astype(jnp.bfloat16)
    a_ref[...] = normed
    mixed = (plain_product(normed, weight_ref[...]) + bias_ref[...]).astype(jnp.bfloat16)
    q_ref[...] = mixed[:, :lanes]
    k_ref[...] = mixed[:, lanes : 2 * lanes]
    v_ref[...] = mixed[:, 2 * lanes :]


def norm_mix(core, own, other, block, gain, shift, weight, bias):
    length, width = own.shape[0] * 2, own.shape[1]
    lanes = weight.shape[1] // 3
    row = lambda size: pl.BlockSpec((block, size), lambda i, core: (i, 0))
    half = pl.BlockSpec((block, width), lambda i, core: (i // 2, 0))
    fixed = lambda *shape: pl.BlockSpec(shape, lambda i, core: (0, 0))
    part = jax.ShapeDtypeStruct((length, lanes), jnp.bfloat16)
    return pl.pallas_call(
        norm_mix_kernel,
        grid_spec=pltpu.PrefetchScalarGridSpec(
            num_scalar_prefetch=1,
            grid=(length // block,),
            in_specs=[
                half,
                half,
                fixed(1, width),
                fixed(1, width),
                fixed(width, 3 * lanes),
                fixed(1, 3 * lanes),
            ],
            out_specs=[row(width), row(lanes), row(lanes), row(lanes)],
        ),
        out_shape=(jax.ShapeDtypeStruct((length, width), jnp.bfloat16), part, part, part),
        compiler_params=pltpu.CompilerParams(vmem_limit_bytes=VMEM_BYTES),
        cost_estimate=pl.CostEstimate(
            flops=length * width * lanes * 6, bytes_accessed=length * width * 4, transcendentals=0
        ),
        name="norm_mix",
    )(core, own, other, gain[None], shift[None], weight, bias[None])


def mlp_kernel(
    own_ref,
    other_ref,
    gm_own_ref,
    gm_other_ref,
    bias_ref,
    up_ref,
    down_ref,
    up_grad_ref,
    down_grad_ref,
    m_own_ref,
    m_other_ref,
    gh_own_ref,
    gh_other_ref,
    bias_grad_ref,
    h_ref,
    gm_ref,
    turned_ref,
):
    tile = pl.program_id(0)
    rows, width = own_ref.shape
    chips = up_grad_ref.shape[0]
    up_rows = width // chips
    units = bias_ref.shape[1]
    folds = width // units

    @pl.when(tile == 0)
    def clear():
        for ref in (m_own_ref, m_other_ref, gh_own_ref, gh_other_ref):
            ref[...] = jnp.zeros_like(ref)
        h_ref[:rows] = own_ref[...]
        h_ref[rows:] = other_ref[...]
        gm_ref[:rows] = gm_own_ref[...]
        gm_ref[rows:] = gm_other_ref[...]
        turned_ref[...] = h_ref[...].T

    weight_up = up_ref[...].reshape(width, units)
    weight_down = down_ref[...].reshape(units, width)
    gm = gm_ref[...]
    upward = plain_product(h_ref[...], weight_up) + bias_ref[...]
    normal = 0.5 * (1.0 + lax.erf(upward * 0.5**0.5))
    slope = normal + upward * jnp.exp(upward * upward * -0.5) * (0.5 / jnp.pi) ** 0.5
    active = (upward * normal).astype(jnp.bfloat16)
    grad_up = (inner_cols(gm, weight_down) * slope).astype(jnp.bfloat16)
    bias_grad_ref[...] = jnp.sum(grad_up.astype(jnp.float32), axis=0, keepdims=True)
    branch = plain_product(active, weight_down)
    m_own_ref[...] += branch[:rows]
    m_other_ref[...] += branch[rows:]
    grad_norm = inner_cols(grad_up, weight_up)
    gh_own_ref[...] += grad_norm[:rows]
    gh_other_ref[...] += grad_norm[rows:]
    up_grad = plain_product(turned_ref[...], grad_up).astype(jnp.bfloat16)
    row = pl.multiple_of(tile // folds * up_rows, up_rows)
    column = pl.multiple_of(lax.rem(tile, folds) * units, units)
    up_grad = up_grad.reshape(chips, up_rows, units)
    up_grad_ref[:, pl.ds(row, up_rows), pl.ds(column, units)] = up_grad
    down_grad = inner_rows(active, gm).astype(jnp.bfloat16)
    down_grad_ref[...] = down_grad.reshape(down_grad_ref.shape)


def mlp(own, other, gm_own, gm_other, up, down, bias, chips):
    rows, width = own.shape
    up_rows = width // chips
    half = bias.shape[0]
    units = 256
    folds = width // units
    once = dict(pipeline_mode=pl.Buffered(1))
    fixed = pl.BlockSpec((rows, width), lambda j: (0, 0), **once)
    if up.ndim == 3:
        pieces = units * chips // half
        up_spec = pl.BlockSpec((chips, up_rows, units), lambda j: (0, j // folds, lax.rem(j, folds)))
        down_spec = pl.BlockSpec((pieces, units // pieces, width), lambda j: (j, 0, 0))
        up_shape, down_shape = (chips, half // chips, width), (chips, half // chips, width)
        down_grad_spec = down_spec
    else:
        up_spec = pl.BlockSpec((width, units), lambda j: (0, j))
        down_spec = pl.BlockSpec((units, width), lambda j: (j, 0))
        up_shape, down_shape = (1, half // width * width, width), (1, half, width)
        down_grad_spec = pl.BlockSpec((1, units, width), lambda j: (0, j, 0))
    total = jax.ShapeDtypeStruct((rows, width), jnp.float32)
    outs = pl.pallas_call(
        mlp_kernel,
        grid=(half // units,),
        in_specs=[fixed] * 4 + [pl.BlockSpec((1, units), lambda j: (0, j)), up_spec, down_spec],
        out_specs=[
            pl.BlockSpec(up_shape, lambda j: (0, 0, 0), **once),
            down_grad_spec,
            *[fixed] * 4,
            pl.BlockSpec((1, units), lambda j: (0, j)),
        ],
        out_shape=(
            jax.ShapeDtypeStruct(up_shape, jnp.bfloat16),
            jax.ShapeDtypeStruct(down_shape, jnp.bfloat16),
            *[total] * 4,
            jax.ShapeDtypeStruct((1, half), jnp.float32),
        ),
        scratch_shapes=[
            pltpu.VMEM((2 * rows, width), jnp.bfloat16),
            pltpu.VMEM((2 * rows, width), jnp.bfloat16),
            pltpu.VMEM((width, 2 * rows), jnp.bfloat16),
        ],
        compiler_params=pltpu.CompilerParams(vmem_limit_bytes=VMEM_BYTES),
        cost_estimate=pl.CostEstimate(
            flops=2 * rows * width * half * 12,
            bytes_accessed=half * width * 8 + rows * width * 24,
            transcendentals=rows * half * 4,
        ),
        name="mlp_both_ways",
    )(own, other, gm_own, gm_other, bias[None], up, down)
    up_grad, down_grad = outs[0], outs[1]
    if up.ndim == 2:
        up_grad = up_grad.reshape(half // width, chips, up_rows, width).swapaxes(0, 1)
        up_grad = up_grad.reshape(chips, -1, width)
        down_grad = down_grad.reshape(chips, -1, width)
    return (up_grad, down_grad, *outs[2:])


def finish_kernel(
    grad_ref, weight_ref, x_ref, gx_ref, gain_ref, out_ref, gain_grad_ref, shift_grad_ref, sums_ref, acc_ref
):
    step = pl.program_id(0)
    parts = [grad_ref[slot] for slot in range(grad_ref.shape[0])]
    grad = jnp.concatenate(parts, axis=1)
    width = x_ref.shape[1]
    product = inner_cols(grad, weight_ref[...].reshape(width, width))
    sums_ref[...] = jnp.sum(grad.astype(jnp.float32), axis=0, keepdims=True)[None]

    @pl.when(step == 0)
    def begin():
        acc_ref[...] = product

    @pl.when(step > 0)
    def further():
        acc_ref[...] += product

    @pl.when(step == pl.num_programs(0) - 1)
    def end():
        values = x_ref[...].astype(jnp.float32)
        centered = values - jnp.mean(values, axis=1, keepdims=True)
        scale = lax.rsqrt(jnp.mean(centered * centered, axis=1, keepdims=True) + 1e-06)
        unit = centered * scale
        grad_norm = acc_ref[...]
        gain_grad_ref[...] = jnp.sum(grad_norm * unit, axis=0, keepdims=True)
        shift_grad_ref[...] = jnp.sum(grad_norm, axis=0, keepdims=True)
        grad_unit = grad_norm * gain_ref[...]
        mean = jnp.mean(grad_unit, axis=1, keepdims=True)
        slant = jnp.mean(grad_unit * unit, axis=1, keepdims=True)
        out_ref[...] = gx_ref[...] + scale * (grad_unit - mean - unit * slant)


def finish(grads, weights, inputs, gx, gain):
    rows, width = inputs.shape
    group, lanes = grads.shape[0], grads.shape[2] // 3
    if lanes % 128:
        grads = grads.reshape(group, rows, 3, lanes).transpose(2, 0, 1, 3)
        grads = grads.reshape(3 * group, rows, lanes)
        grad_spec = pl.BlockSpec((group, rows, lanes), lambda k: (k, 0, 0))
    else:
        grad_spec = pl.BlockSpec((group, rows, lanes), lambda k: (0, 0, k))
    if weights.ndim == 3:
        share = width // weights.shape[0]
        first = weights.shape[1] // share - 3
        weight_spec = pl.BlockSpec((weights.shape[0], share, width), lambda k: (0, first + k, 0))
    else:
        weight_spec = pl.BlockSpec((width, width), lambda k: (0, k))
    fixed = lambda *shape: pl.BlockSpec(shape, lambda k: (0, 0))
    vector = jax.ShapeDtypeStruct((1, width), jnp.float32)
    return pl.pallas_call(
        finish_kernel,
        grid=(3,),
        in_specs=[
            grad_spec,
            weight_spec,
            fixed(rows, width),
            fixed(rows, width),
            fixed(1, width),
        ],
        out_specs=[
            fixed(rows, width),
            fixed(1, width),
            fixed(1, width),
            pl.BlockSpec((1, 1, width), lambda k: (k, 0, 0)),
        ],
        out_shape=(
            jax.ShapeDtypeStruct((rows, width), jnp.float32),
            vector,
            vector,
            jax.ShapeDtypeStruct((3, 1, width), jnp.float32),
        ),
        scratch_shapes=[pltpu.VMEM((rows, width), jnp.float32)],
        compiler_params=pltpu.CompilerParams(vmem_limit_bytes=VMEM_BYTES),
        cost_estimate=pl.CostEstimate(
            flops=rows * width * width * 6, bytes_accessed=width * width * 16, transcendentals=0
        ),
        name="finish_input",
    )(grads, weights, inputs, gx, gain[None])


def swap_cores(value):
    return lax.ppermute(value, "core", [(0, 1), (1, 0)])


def line_pieces(value, axis):
    size = lax.axis_size(axis)
    if size == 2:
        other = lax.ppermute(value, axis, [(0, 1), (1, 0)])
        return [(None, other)]
    pieces = []
    for sign in (-1, 1):
        moving = value
        for step in range(1, size):
            pairs = [(i, i - sign) for i in range(size) if 0 <= i - sign < size]
            pairs = [(i, j) for i, j in pairs if 0 <= i + sign * (step - 1) < size]
            moving = lax.ppermute(moving, axis, pairs)
            pieces.append((sign * step, moving))
    return pieces


def line_pieces_two(first, second, axis):
    size = lax.axis_size(axis)
    pieces = ([], [])
    moving = {-1: (first, second), 1: (first, second)}
    for step in range(1, size):
        arrived = []
        for sign in (-1, 1):
            pairs = [(i, i - sign) for i in range(size) if 0 <= i - sign < size]
            pairs = [(i, j) for i, j in pairs if 0 <= i + sign * (step - 1) < size]
            arrived.append((sign, pairs, lax.ppermute(moving[sign][0], axis, pairs)))
        tied = lax.optimization_barrier(
            tuple(item[2] for item in arrived) + tuple(moving[item[0]][1] for item in arrived)
        )
        for n, (sign, pairs, _) in enumerate(arrived):
            later = lax.ppermute(tied[2 + n], axis, pairs)
            moving[sign] = (tied[n], later)
            pieces[0].append((sign * step, tied[n]))
            pieces[1].append((sign * step, later))
    return pieces


def line_order(value, pieces, axis):
    place = lax.axis_index(axis)
    size = lax.axis_size(axis)
    if size == 2:
        other = pieces[0][1]
        return jnp.where(place == 0, jnp.stack([value, other]), jnp.stack([other, value]))
    whole = jnp.zeros((size, *value.shape), value.dtype)
    for distance, piece in sorted(pieces, key=lambda item: -abs(item[0])) + [(0, value)]:
        slot = jnp.clip(place + distance, 0, size - 1)
        whole = lax.dynamic_update_index_in_dim(whole, piece, slot, 0)
    return whole


def gather_line(value, axis):
    return line_order(value, line_pieces(value, axis), axis)


def rounded_sum(*terms):
    return sum(term.astype(jnp.float32) for term in terms).astype(jnp.bfloat16)


def scatter_line(value, axis, dim):
    place = lax.axis_index(axis)
    size = lax.axis_size(axis)
    pick = lambda slot: lax.dynamic_index_in_dim(
        value, jnp.clip(slot, 0, size - 1), dim, keepdims=False
    )
    if size == 2:
        return rounded_sum(pick(place), lax.ppermute(pick(1 - place), axis, [(0, 1), (1, 0)]))
    sums = []
    for sign in (-1, 1):
        moving = None
        for step in range(1, size):
            start = 0 if sign < 0 else size - 1
            pairs = [(i, i - sign) for i in range(size) if 0 <= i - sign < size]
            pairs = [(i, j) for i, j in pairs if abs(i - start) <= step - 1]
            own = pick(place - sign * (size - step))
            payload = own if moving is None else rounded_sum(own, moving)
            moving = lax.ppermute(payload, axis, pairs)
        sums.append(moving)
    return rounded_sum(pick(place), *sums)


def on_device(
    tokens,
    cotangent,
    segment_ids,
    valid,
    project_in,
    project_out,
    hidden_up,
    hidden_down,
    gains_biases,
    moment_in,
    moment_out,
    moment_up,
    moment_down,
    moment_gains,
    square_in,
    square_out,
    square_up,
    square_down,
    square_gains,
):
    rows = tokens.shape[0]
    width = tokens.shape[1]
    everyone = ("outer", "inner", "line", "core")
    planes = ("outer", "inner")
    seq = ("line", "core")
    streams, line = lax.axis_size(planes), lax.axis_size("line")
    group = 2 * line
    count = streams * group
    chips = streams * line
    share = width // count
    lanes = width // group
    length = rows * group
    images = length // IMG_LEN
    core = lax.axis_index("core")
    first_core = core == 0

    def in_order(own, other, axis):
        return jnp.concatenate(
            [jnp.where(first_core, own, other), jnp.where(first_core, other, own)], axis=axis
        )

    half = FF // 2
    unit_block = FF // count
    folds = half // width
    up_end = 2 * share * folds
    low = lambda value: value.astype(jnp.bfloat16)
    direct = share % 16 == 0 and unit_block == 128
    if direct:
        up_blocks = low(hidden_up).reshape(share, chips, 2, unit_block)
        up_first = up_blocks[:, :, 0].reshape(share, half)
        up_second = up_blocks[:, :, 1].reshape(share, half)
        out_rows = low(project_out)
        received = swap_cores(
            jnp.concatenate(
                [jnp.where(first_core, up_second, up_first).reshape(-1, width), out_rows], axis=0
            )
        )
        up_rows = in_order(
            jnp.where(first_core, up_first, up_second),
            received[: share * folds].reshape(share, half),
            0,
        )
        packed = jnp.concatenate(
            [
                up_rows.reshape(2 * share, folds, width).transpose(1, 0, 2).reshape(-1, width),
                in_order(out_rows, received[share * folds :], 0),
                low(hidden_down),
            ],
            axis=0,
        )
        weight_pieces, pieces = line_pieces_two(packed, tokens, "line")
        line_packed = line_order(packed, weight_pieces, "line")
        middle = up_end + share
        inner_first, outer_first = line_packed[:, :middle], line_packed[:, middle:]
        inner_first = gather_line(inner_first, "inner")
        outer_first = gather_line(outer_first, "outer")
    else:
        pieces = line_pieces(tokens, "line")

    own_tokens = line_order(tokens, pieces, "line").reshape(-1, width)
    swapped = [(distance, swap_cores(piece)) for distance, piece in pieces]
    other_tokens = line_order(swap_cores(tokens), swapped, "line").reshape(-1, width)
    if direct:
        inner_first, outer_first, own_tokens = lax.optimization_barrier(
            (inner_first, outer_first, own_tokens)
        )
        inner_first = gather_line(inner_first, "outer").reshape(chips, -1, width)
        outer_first = gather_line(outer_first, "inner").swapaxes(0, 1).reshape(chips, -1, width)

    owned = project_in.astype(jnp.bfloat16).reshape(share, 3, group, lanes)
    owned = owned.transpose(2, 0, 1, 3).reshape(group, share, 3 * lanes)
    position = lax.broadcasted_iota(jnp.int32, (images, rows), 1)
    found = (segment_ids[None, :] == lax.broadcasted_iota(jnp.int32, (images, rows), 0)) & (
        valid[None, :] == 1
    )
    first = jnp.min(jnp.where(found, position, rows), axis=1)
    small = jnp.concatenate(
        [
            gains_biases.astype(jnp.bfloat16).reshape(-1),
            (first // 32).astype(jnp.bfloat16),
            (first % 32).astype(jnp.bfloat16),
        ]
    )
    vector_size = gains_biases.size
    extra = -(-small.shape[0] // (3 * lanes))
    small = jnp.pad(small, (0, extra * 3 * lanes - small.shape[0])).reshape(1, extra, 3 * lanes)
    blocks = jnp.concatenate([owned, jnp.broadcast_to(small, (group, extra, 3 * lanes))], axis=1)
    blocks = lax.all_to_all(blocks, seq, split_axis=0, concat_axis=0, tiled=True)
    blocks = gather_line(gather_line(blocks, "inner"), "outer")
    blocks = blocks.reshape(count, share + extra, 3 * lanes)
    mine_in = blocks[:, :share].reshape(width, 3 * lanes)
    small = blocks[:, share:].reshape(count, -1)
    vectors = small[:, :vector_size].reshape(count, -1, share).transpose(1, 0, 2)
    vectors = vectors.reshape(-1, width).astype(jnp.float32)
    first = small[:, vector_size : vector_size + 2 * images].astype(jnp.int32)
    first = first[:, :images] * 32 + first[:, images:]
    first = lax.dynamic_slice_in_dim(first, lax.axis_index(planes) * group, group, 0)
    offsets = lax.broadcasted_iota(jnp.int32, (group, images), 0) * rows
    starts = jnp.min(jnp.where(first < rows, first + offsets, length), axis=0)

    gain_one, shift_one, bias_query, bias_value, bias_out = (
        vectors[0],
        vectors[1],
        vectors[2],
        vectors[3],
        vectors[4],
    )
    scale_one, gain_two, shift_two, bias_down, scale_two = (
        vectors[5],
        vectors[6],
        vectors[7],
        vectors[8],
        vectors[9],
    )
    bias_up = lax.dynamic_index_in_dim(
        vectors[10:].reshape(chips, 2, unit_block), core, axis=1, keepdims=False
    ).reshape(half)
    column = lax.axis_index(seq) * lanes
    bias_in = jnp.concatenate(
        [
            lax.dynamic_slice_in_dim(bias_query, column, lanes, 0),
            jnp.zeros((lanes,), jnp.float32),
            lax.dynamic_slice_in_dim(bias_value, column, lanes, 0),
        ]
    )
    grad_rows = cotangent.astype(jnp.float32) * valid.astype(jnp.float32)[:, None]
    grad_branch = (scale_two * grad_rows).astype(jnp.bfloat16)

    normed_one, query, keys, values = norm_mix(
        core.reshape(1),
        own_tokens,
        other_tokens,
        rows,
        gain_one,
        shift_one,
        mine_in,
        bias_in,
    )
    wide, attended, logs = attend(starts, query, keys, values)
    if direct:
        inner_first, outer_first, attended = lax.optimization_barrier(
            (inner_first, outer_first, attended)
        )
        mlp_up, mlp_down = inner_first, outer_first[:, share:]
        whole_out = jnp.concatenate([inner_first[:, up_end:], outer_first[:, :share]], axis=1)
        whole_out = whole_out.reshape(width, width)
    else:
        whole_out, whole_up, whole_down = (
            lax.all_gather(low(value), everyone, axis=0, tiled=True)
            for value in (project_out, hidden_up, hidden_down)
        )
        block = jnp.arange(half) // unit_block * 2 + core
        index = block * unit_block + lax.rem(jnp.arange(half), unit_block)
        mlp_up, mlp_down = jnp.take(whole_up, index, axis=1), jnp.take(whole_down, index, axis=0)
    returned = lax.all_to_all(
        attended.reshape(group, rows, lanes), seq, split_axis=0, concat_axis=0, tiled=True
    )
    in_rows, returned = lax.optimization_barrier((low(project_in), returned))
    if direct:
        in_rows = in_rows.reshape(share, 3, width).swapaxes(0, 1).reshape(-1, width)
    whole_in = lax.all_gather(in_rows, everyone, axis=0, tiled=not direct)
    attended_rows = returned.transpose(1, 0, 2).reshape(rows, width)
    inputs = tokens.astype(jnp.float32)
    projected = plain_product(attended_rows, whole_out) + bias_out
    second = inputs + scale_one * projected
    norm_two, norm_two_back = jax.vjp(layer_norm, second, gain_two, shift_two)
    normed_two = norm_two.astype(jnp.bfloat16)
    grad_up, grad_down, branch, branch_other, grad_norm_two, grad_norm_other, grad_bias_up = mlp(
        normed_two,
        swap_cores(normed_two),
        grad_branch,
        swap_cores(grad_branch),
        mlp_up,
        mlp_down,
        bias_up,
        chips,
    )
    grad_norm_two = grad_norm_two + swap_cores(grad_norm_other)
    branch = branch + swap_cores(branch_other) + bias_down
    block_output = (second + scale_two * branch).astype(jnp.bfloat16)
    grad_scale_two = jnp.sum(grad_rows * branch, axis=0)
    grad_bias_down = jnp.sum(grad_branch.astype(jnp.float32), axis=0)
    second_part, grad_gain_two, grad_shift_two = norm_two_back(grad_norm_two)
    grad_second = grad_rows + second_part
    grad_scale_one = jnp.sum(grad_second * projected, axis=0)
    grad_projected = (scale_one * grad_second).astype(jnp.bfloat16)
    grad_bias_out = jnp.sum(grad_projected.astype(jnp.float32), axis=0)
    grad_attended = inner_cols(grad_projected, whole_out).astype(jnp.bfloat16)
    grad_stream = lax.all_to_all(
        grad_attended.reshape(rows, group, lanes).transpose(1, 0, 2),
        seq,
        split_axis=0,
        concat_axis=0,
        tiled=True,
    ).reshape(length, lanes)
    grad_out = inner_rows(attended_rows, grad_projected).astype(jnp.bfloat16)
    grad_out = grad_out.reshape(chips, 2 * share, width)
    outer, inner = lax.axis_size("outer"), lax.axis_size("inner")
    grad_up, grad_out, grad_down = (
        value.reshape(outer, inner, line, -1, width) for value in (grad_up, grad_out, grad_down)
    )
    grad_down = scatter_line(scatter_line(grad_down, "outer", 0), "inner", 0)
    grad_up = scatter_line(scatter_line(grad_up, "inner", 1), "outer", 0)
    grad_out = scatter_line(scatter_line(grad_out, "inner", 1), "outer", 0)

    grad_mixed_stream = attend_back(starts, query, keys, values, wide, logs, grad_stream)
    grad_mixed = lax.all_to_all(
        grad_mixed_stream.reshape(group, rows, 3 * lanes), seq, split_axis=0, concat_axis=0, tiled=True
    )
    plane_sums = jnp.concatenate([grad_up, grad_out, grad_down], axis=1)
    summed = scatter_line(plane_sums, "line", 0)
    grad_in = inner_rows(normed_one, grad_mixed_stream).astype(jnp.bfloat16)
    parts = grad_in.reshape(outer, inner, group * share, 3 * lanes)
    parts = scatter_line(scatter_line(parts, "inner", 1), "outer", 0)
    parts, grad_mixed = lax.optimization_barrier((parts, grad_mixed))
    parts = parts.reshape(group, share, 3 * lanes)
    parts = lax.all_to_all(parts, seq, split_axis=0, concat_axis=0, tiled=True)
    parts = parts.astype(jnp.float32)
    summed_in = parts.reshape(group, share, 3, lanes).transpose(1, 2, 0, 3).reshape(share, 3 * width)

    input_grad, grad_gain_one, grad_shift_one, mixed_sums = finish(
        grad_mixed, whole_in, tokens, grad_second, gain_one
    )
    up_sums = grad_bias_up.reshape(chips, unit_block)
    up_sums = jnp.where(
        (lax.broadcasted_iota(jnp.int32, (1, 2, 1), 1) == core), up_sums[:, None, :], 0.0
    )
    grad_small = jnp.concatenate(
        [
            jnp.stack(
                [
                    grad_gain_one[0],
                    grad_shift_one[0],
                    mixed_sums[0, 0],
                    mixed_sums[2, 0],
                    grad_bias_out,
                    grad_scale_one,
                    grad_gain_two,
                    grad_shift_two,
                    grad_bias_down,
                    grad_scale_two,
                ]
            ),
            up_sums.reshape(-1, width),
        ],
        axis=0,
    )
    small_rows = grad_small.shape[0]
    parts = grad_small.reshape(small_rows, count, share).transpose(1, 0, 2)
    parts = lax.all_to_all(
        parts.reshape(count, small_rows * share), everyone, split_axis=0, concat_axis=0, tiled=True
    )
    summed_gains = jnp.sum(parts, axis=0).reshape(small_rows, share)

    up_sum = summed[:up_end].reshape(folds, 2, share, width)
    out_sum = summed[up_end : up_end + 2 * share].reshape(1, 2, share, width)
    both_sums = jnp.concatenate([up_sum, out_sum], axis=0)
    own_sums = jnp.where(first_core, both_sums[:, 0], both_sums[:, 1])
    other_sums = swap_cores(jnp.where(first_core, both_sums[:, 1], both_sums[:, 0]))
    summed_down = summed[up_end + 2 * share :].astype(jnp.float32)
    summed_out = own_sums[folds].astype(jnp.float32) + other_sums[folds].astype(jnp.float32)
    own_up = own_sums[:folds].transpose(1, 0, 2).reshape(share, chips, 1, unit_block)
    other_up = other_sums[:folds].transpose(1, 0, 2).reshape(share, chips, 1, unit_block)
    summed_up = in_order(own_up, other_up, 2).reshape(share, FF).astype(jnp.float32)
    rate_out = max(1, 4 * D // IMG_LEN) ** (-0.5)
    new_in, new_moment_in, new_square_in = adamw(
        project_in, moment_in, square_in, summed_in, D ** (-0.5), 0.04
    )
    new_out, new_moment_out, new_square_out = adamw(
        project_out, moment_out, square_out, summed_out, rate_out, 0.04
    )
    new_up, new_moment_up, new_square_up = adamw(
        hidden_up, moment_up, square_up, summed_up, D ** (-0.5), 0.04
    )
    new_down, new_moment_down, new_square_down = adamw(
        hidden_down, moment_down, square_down, summed_down, FF ** (-0.5), 0.04
    )
    new_gains, new_moment_gains, new_square_gains = adamw(
        gains_biases, moment_gains, square_gains, summed_gains, 0.2, 0.0
    )
    return (
        block_output,
        input_grad,
        new_in,
        new_out,
        new_up,
        new_down,
        new_gains,
        new_moment_in,
        new_moment_out,
        new_moment_up,
        new_moment_down,
        new_moment_gains,
        new_square_in,
        new_square_out,
        new_square_up,
        new_square_down,
        new_square_gains,
        summed_gains[8],
    )


def solution(mesh):
    streams, group = mesh.shape["fsdp"], mesh.shape["seq"]
    outer = math.isqrt(streams)
    fine = jax.sharding.Mesh(
        mesh.devices.reshape(outer, streams // outer, group // 2, 2),
        ("outer", "inner", "line", "core"),
    )
    return jax.shard_map(
        on_device,
        mesh=fine,
        in_specs=(
            P(("outer", "inner", "line", "core"), None),
            P(("outer", "inner", "line", "core"), None),
            P(("outer", "inner", "line", "core")),
            P(("outer", "inner", "line", "core")),
            P(("outer", "inner", "line", "core"), None),
            P(("outer", "inner", "line", "core"), None),
            P(("outer", "inner", "line", "core"), None),
            P(("outer", "inner", "line", "core"), None),
            P(None, ("outer", "inner", "line", "core")),
            P(("outer", "inner", "line", "core"), None),
            P(("outer", "inner", "line", "core"), None),
            P(("outer", "inner", "line", "core"), None),
            P(("outer", "inner", "line", "core"), None),
            P(None, ("outer", "inner", "line", "core")),
            P(("outer", "inner", "line", "core"), None),
            P(("outer", "inner", "line", "core"), None),
            P(("outer", "inner", "line", "core"), None),
            P(("outer", "inner", "line", "core"), None),
            P(None, ("outer", "inner", "line", "core")),
        ),
        out_specs=(
            P(("outer", "inner", "line", "core"), None),
            P(("outer", "inner", "line", "core"), None),
            P(("outer", "inner", "line", "core"), None),
            P(("outer", "inner", "line", "core"), None),
            P(("outer", "inner", "line", "core"), None),
            P(("outer", "inner", "line", "core"), None),
            P(None, ("outer", "inner", "line", "core")),
            P(("outer", "inner", "line", "core"), None),
            P(("outer", "inner", "line", "core"), None),
            P(("outer", "inner", "line", "core"), None),
            P(("outer", "inner", "line", "core"), None),
            P(None, ("outer", "inner", "line", "core")),
            P(("outer", "inner", "line", "core"), None),
            P(("outer", "inner", "line", "core"), None),
            P(("outer", "inner", "line", "core"), None),
            P(("outer", "inner", "line", "core"), None),
            P(None, ("outer", "inner", "line", "core")),
            P(("outer", "inner", "line", "core")),
        ),
        check_vma=False,
    )
```

```python
import functools
import math

import jax
import jax.numpy as jnp
from jax import lax
from jax.experimental import pallas as pl
from jax.experimental.pallas import tpu as pltpu
from jax.sharding import PartitionSpec as P

D = 1024
FF = 4096
HEADS = 16
HEAD_DIM = 64
IMG_LEN = 1370
WINDOW = 1408
TILE = 352
VMEM_BYTES = 56 * 1024 * 1024
STEP = 10


masked_score = -1e30


def layer_norm(values, gain, shift):
    average = jnp.mean(values, axis=-1, keepdims=True)
    centered = values - average
    variance = jnp.mean(centered * centered, axis=-1, keepdims=True)
    return centered * lax.rsqrt(variance + 1e-06) * gain + shift


def exact_gelu(values):
    return jax.nn.gelu(values, approximate=False)


def plain_product(left, right):
    return jnp.dot(left, right, preferred_element_type=jnp.float32)


def inner_rows(left, right):
    return lax.dot_general(
        left, right, (((0,), (0,)), ((), ())), preferred_element_type=jnp.float32
    )


def inner_cols(left, right):
    return lax.dot_general(
        left, right, (((1,), (1,)), ((), ())), preferred_element_type=jnp.float32
    )


def adamw(param, moment, square, grad, rate, decay):
    new_moment = 0.9 * moment + 0.1 * grad
    new_square = 0.999 * square + 0.001 * grad * grad
    corrected = new_moment / (1.0 - 0.9**STEP)
    scaled = jnp.sqrt(new_square / (1.0 - 0.999**STEP)) + 1e-08
    return (param - rate * (corrected / scaled + decay * param), new_moment, new_square)


def head_lanes(shape):
    return lax.broadcasted_iota(jnp.int32, shape, 1) // HEAD_DIM


def window_of(starts_ref, image, length):
    start = starts_ref[image]
    base = jnp.clip(start // 16 * 16, 0, length - WINDOW)
    return (pl.multiple_of(base, 16), start - base)


def image_mask(position, offset):
    return (position >= offset) & (position < offset + IMG_LEN)


def attend_kernel(starts_ref, q_ref, k_ref, v_ref, wide_ref, out_ref, log_ref):
    image, tile = pl.program_id(0), pl.program_id(1)
    length, lanes = q_ref.shape
    base, offset = window_of(starts_ref, image, length)
    rows = pl.ds(pl.multiple_of(base + tile * TILE, 16), TILE)

    @pl.when((image == 0) & (tile == 0))
    def clear():
        wide_ref[...] = jnp.zeros_like(wide_ref)
        out_ref[...] = jnp.zeros_like(out_ref)
        log_ref[...] = jnp.zeros_like(log_ref)

    query = q_ref[rows, :].astype(jnp.float32) * HEAD_DIM ** (-0.5)
    keys = k_ref[pl.ds(base, WINDOW), :]
    values = v_ref[pl.ds(base, WINDOW), :]
    key_ok = image_mask(lax.broadcasted_iota(jnp.int32, (1, WINDOW), 1), offset)
    bias = jnp.where(key_ok, 0.0, masked_score)
    row_ok = image_mask(lax.broadcasted_iota(jnp.int32, (TILE, 1), 0) + tile * TILE, offset)
    head_of = head_lanes((TILE, lanes))
    total_out = jnp.zeros((TILE, lanes), jnp.float32)
    total_log = jnp.zeros((TILE, lanes), jnp.float32)
    for head in range(lanes // HEAD_DIM):
        mine = head_of == head
        part = jnp.where(mine, query, 0.0).astype(jnp.bfloat16)
        scores = inner_cols(part, keys) + bias
        top = jnp.max(scores, axis=1, keepdims=True)
        weights = jnp.exp(scores - top)
        total = jnp.sum(weights, axis=1, keepdims=True)
        probs = (weights * (1.0 / total)).astype(jnp.bfloat16)
        total_out = jnp.where(mine, plain_product(probs, values), total_out)
        total_log = jnp.where(mine, top + jnp.log(total), total_log)
    merged = jnp.where(row_ok, total_out, wide_ref[rows, :])
    wide_ref[rows, :] = merged
    out_ref[rows, :] = merged.astype(jnp.bfloat16)
    log_ref[rows, :] = jnp.where(row_ok, total_log, log_ref[rows, :])


def attend(starts, query, keys, values):
    length, lanes = query.shape
    whole = pl.BlockSpec((length, lanes), lambda image, tile, starts: (0, 0))
    wide = jax.ShapeDtypeStruct((length, lanes), jnp.float32)
    images = length // IMG_LEN
    return pl.pallas_call(
        attend_kernel,
        grid_spec=pltpu.PrefetchScalarGridSpec(
            num_scalar_prefetch=1,
            grid=(images, WINDOW // TILE),
            in_specs=[whole] * 3,
            out_specs=[whole] * 3,
        ),
        out_shape=(wide, jax.ShapeDtypeStruct((length, lanes), jnp.bfloat16), wide),
        compiler_params=pltpu.CompilerParams(
            vmem_limit_bytes=VMEM_BYTES, dimension_semantics=("arbitrary", "arbitrary")
        ),
        cost_estimate=pl.CostEstimate(
            flops=images * WINDOW * WINDOW * lanes * 8,
            bytes_accessed=length * lanes * 16,
            transcendentals=images * WINDOW * WINDOW * lanes // HEAD_DIM,
        ),
        name="attend_forward",
    )(starts, query, keys, values)


def attend_back_kernel(
    starts_ref, q_ref, k_ref, v_ref, wide_ref, log_ref, go_ref, grad_ref, key_acc, value_acc
):
    image, tile = pl.program_id(0), pl.program_id(1)
    length, lanes = q_ref.shape
    base, offset = window_of(starts_ref, image, length)
    rows = pl.ds(pl.multiple_of(base + tile * TILE, 16), TILE)
    window = pl.ds(base, WINDOW)

    @pl.when((image == 0) & (tile == 0))
    def clear():
        grad_ref[...] = jnp.zeros_like(grad_ref)

    @pl.when(tile == 0)
    def clear_sums():
        key_acc[...] = jnp.zeros_like(key_acc)
        value_acc[...] = jnp.zeros_like(value_acc)

    query = q_ref[rows, :].astype(jnp.float32) * HEAD_DIM ** (-0.5)
    keys = k_ref[window, :]
    values = v_ref[window, :]
    key_ok = image_mask(lax.broadcasted_iota(jnp.int32, (1, WINDOW), 1), offset)
    bias = jnp.where(key_ok, 0.0, masked_score)
    row_ok = image_mask(lax.broadcasted_iota(jnp.int32, (TILE, 1), 0) + tile * TILE, offset)
    head_of = head_lanes((TILE, lanes))
    grad_out = jnp.where(row_ok, go_ref[rows, :].astype(jnp.float32), 0.0)
    centre_parts = grad_out * wide_ref[rows, :]
    logs = jnp.where(row_ok, log_ref[rows, :], -masked_score)
    query_grad = jnp.zeros((TILE, lanes), jnp.float32)
    for head in range(lanes // HEAD_DIM):
        mine = head_of == head
        part = jnp.where(mine, query, 0.0).astype(jnp.bfloat16)
        grad_part = jnp.where(mine, grad_out, 0.0).astype(jnp.bfloat16)
        centre = jnp.sum(jnp.where(mine, centre_parts, 0.0), axis=1, keepdims=True)
        log_total = jnp.max(jnp.where(mine, logs, masked_score), axis=1, keepdims=True)
        probs = jnp.exp(inner_cols(part, keys) + bias - log_total)
        grad_probs = inner_cols(grad_part, values)
        grad_scores = (probs * (grad_probs - centre)).astype(jnp.bfloat16)
        query_grad = jnp.where(mine, plain_product(grad_scores, keys), query_grad)
        key_acc[...] += inner_rows(part, grad_scores)
        value_acc[...] += inner_rows(grad_part, probs.astype(jnp.bfloat16))
    old = grad_ref[rows, 0:lanes].astype(jnp.float32)
    merged = jnp.where(row_ok, query_grad * HEAD_DIM ** (-0.5), old)
    grad_ref[rows, 0:lanes] = merged.astype(jnp.bfloat16)

    @pl.when(tile == pl.num_programs(1) - 1)
    def flush():
        inside = image_mask(lax.broadcasted_iota(jnp.int32, (WINDOW, 1), 0), offset)
        for slot, sums in ((1, key_acc), (2, value_acc)):
            columns = slice(slot * lanes, (slot + 1) * lanes)
            old = grad_ref[window, columns].astype(jnp.float32)
            merged = jnp.where(inside, sums[...].T, old)
            grad_ref[window, columns] = merged.astype(jnp.bfloat16)


def attend_back(starts, query, keys, values, wide, logs, grad_out):
    length, lanes = query.shape
    whole = pl.BlockSpec((length, lanes), lambda image, tile, starts: (0, 0))
    images = length // IMG_LEN
    return pl.pallas_call(
        attend_back_kernel,
        grid_spec=pltpu.PrefetchScalarGridSpec(
            num_scalar_prefetch=1,
            grid=(images, WINDOW // TILE),
            in_specs=[whole] * 6,
            out_specs=pl.BlockSpec((length, 3 * lanes), lambda image, tile, starts: (0, 0)),
            scratch_shapes=[pltpu.VMEM((lanes, WINDOW), jnp.float32)] * 2,
        ),
        out_shape=jax.ShapeDtypeStruct((length, 3 * lanes), jnp.bfloat16),
        compiler_params=pltpu.CompilerParams(
            vmem_limit_bytes=VMEM_BYTES, dimension_semantics=("arbitrary", "arbitrary")
        ),
        cost_estimate=pl.CostEstimate(
            flops=images * WINDOW * WINDOW * lanes * 20,
            bytes_accessed=length * lanes * 22,
            transcendentals=images * WINDOW * WINDOW * lanes // HEAD_DIM,
        ),
        name="attend_backward",
    )(starts, query, keys, values, wide, logs, grad_out)


def norm_mix_kernel(
    core_ref, own_ref, other_ref, gain_ref, shift_ref, weight_ref, bias_ref, a_ref, q_ref, k_ref, v_ref
):
    lanes = q_ref.shape[1]
    mine = lax.rem(pl.program_id(0), 2) == core_ref[0]
    own, other = own_ref[...].astype(jnp.float32), other_ref[...].astype(jnp.float32)
    normed = layer_norm(jnp.where(mine, own, other), gain_ref[...], shift_ref[...])
    normed = normed.astype(jnp.bfloat16)
    a_ref[...] = normed
    mixed = (plain_product(normed, weight_ref[...]) + bias_ref[...]).astype(jnp.bfloat16)
    q_ref[...] = mixed[:, :lanes]
    k_ref[...] = mixed[:, lanes : 2 * lanes]
    v_ref[...] = mixed[:, 2 * lanes :]


def norm_mix(core, own, other, block, gain, shift, weight, bias):
    length, width = own.shape[0] * 2, own.shape[1]
    lanes = weight.shape[1] // 3
    row = lambda size: pl.BlockSpec((block, size), lambda i, core: (i, 0))
    half = pl.BlockSpec((block, width), lambda i, core: (i // 2, 0))
    fixed = lambda *shape: pl.BlockSpec(shape, lambda i, core: (0, 0))
    part = jax.ShapeDtypeStruct((length, lanes), jnp.bfloat16)
    return pl.pallas_call(
        norm_mix_kernel,
        grid_spec=pltpu.PrefetchScalarGridSpec(
            num_scalar_prefetch=1,
            grid=(length // block,),
            in_specs=[
                half,
                half,
                fixed(1, width),
                fixed(1, width),
                fixed(width, 3 * lanes),
                fixed(1, 3 * lanes),
            ],
            out_specs=[row(width), row(lanes), row(lanes), row(lanes)],
        ),
        out_shape=(jax.ShapeDtypeStruct((length, width), jnp.bfloat16), part, part, part),
        compiler_params=pltpu.CompilerParams(vmem_limit_bytes=VMEM_BYTES),
        cost_estimate=pl.CostEstimate(
            flops=length * width * lanes * 6, bytes_accessed=length * width * 4, transcendentals=0
        ),
        name="norm_mix",
    )(core, own, other, gain[None], shift[None], weight, bias[None])


def mlp_kernel(pieces, core_ref, own_ref, other_ref, gm_own_ref, gm_other_ref, bias_ref, *refs):
    up_refs, down_refs = refs[:pieces], refs[pieces : 2 * pieces]
    up_grad_ref, down_grad_ref, m_own_ref, m_other_ref, gh_own_ref, gh_other_ref = refs[
        2 * pieces : 2 * pieces + 6
    ]
    bias_grad_ref, h_ref, gm_ref, turned_ref = refs[2 * pieces + 6 :]
    tile = pl.program_id(0)
    rows, width = own_ref.shape
    chips = up_grad_ref.shape[0]
    up_rows = width // chips
    units = bias_ref.shape[1]
    folds = width // units

    @pl.when(tile == 0)
    def clear():
        for ref in (m_own_ref, m_other_ref, gh_own_ref, gh_other_ref):
            ref[...] = jnp.zeros_like(ref)
        h_ref[:rows] = own_ref[...]
        h_ref[rows:] = other_ref[...]
        gm_ref[:rows] = gm_own_ref[...]
        gm_ref[rows:] = gm_other_ref[...]
        turned_ref[...] = h_ref[...].T

    weight_up = jnp.concatenate([ref[...].reshape(width, -1) for ref in up_refs], axis=1)
    weight_down = jnp.concatenate([ref[...].reshape(-1, width) for ref in down_refs], axis=0)
    gm = gm_ref[...]
    upward = plain_product(h_ref[...], weight_up) + bias_ref[...]
    normal = 0.5 * (1.0 + lax.erf(upward * 0.5**0.5))
    slope = normal + upward * jnp.exp(upward * upward * -0.5) * (0.5 / jnp.pi) ** 0.5
    active = (upward * normal).astype(jnp.bfloat16)
    grad_up = (inner_cols(gm, weight_down) * slope).astype(jnp.bfloat16)
    bias_grad_ref[...] = jnp.sum(grad_up.astype(jnp.float32), axis=0, keepdims=True)
    branch = plain_product(active, weight_down)
    m_own_ref[...] += branch[:rows]
    m_other_ref[...] += branch[rows:]
    grad_norm = inner_cols(grad_up, weight_up)
    gh_own_ref[...] += grad_norm[:rows]
    gh_other_ref[...] += grad_norm[rows:]
    up_grad = plain_product(turned_ref[...], grad_up).astype(jnp.bfloat16)
    row = pl.multiple_of(tile // folds * up_rows, up_rows)
    column = pl.multiple_of(lax.rem(tile, folds) * units, units)
    up_grad = up_grad.reshape(chips, up_rows, units)
    up_grad_ref[:, pl.ds(row, up_rows), pl.ds(column, units)] = up_grad
    down_grad = inner_rows(active, gm).astype(jnp.bfloat16)
    down_grad_ref[...] = down_grad.reshape(down_grad_ref.shape)


def mlp(core, own, other, gm_own, gm_other, weights, bias, chips):
    rows, width = own.shape
    half = bias.shape[0]
    unit_block = half // chips
    units = 256
    folds = width // units
    once = dict(pipeline_mode=pl.Buffered(1))
    fixed = pl.BlockSpec((rows, width), lambda j, core: (0, 0), **once)
    if len(weights) == 1:
        count = 2 * chips
        share = width // count
        pieces = units // unit_block
        lane_blocks = width // unit_block

        def up_spec(piece):
            def place(j, core):
                block = 2 * (j * pieces + piece) + core[0]
                return (0, block // lane_blocks, lax.rem(block, lane_blocks))

            return pl.BlockSpec((count, share, unit_block), place)

        def down_spec(piece):
            return pl.BlockSpec(
                (1, unit_block, width), lambda j, core: (2 * (j * pieces + piece) + core[0], 1, 0)
            )

        weights = list(weights) * (2 * pieces)
        weight_specs = [up_spec(n) for n in range(pieces)] + [down_spec(n) for n in range(pieces)]
        up_shape, down_shape = (chips, half // chips, width), (chips, half // chips, width)
        down_grad_spec = pl.BlockSpec((pieces, unit_block, width), lambda j, core: (j, 0, 0))
    else:
        pieces = 1
        weight_specs = [
            pl.BlockSpec((width, units), lambda j, core: (0, j)),
            pl.BlockSpec((units, width), lambda j, core: (j, 0)),
        ]
        up_shape, down_shape = (1, half // width * width, width), (1, half, width)
        down_grad_spec = pl.BlockSpec((1, units, width), lambda j, core: (0, j, 0))
    total = jax.ShapeDtypeStruct((rows, width), jnp.float32)
    outs = pl.pallas_call(
        functools.partial(mlp_kernel, pieces),
        grid_spec=pltpu.PrefetchScalarGridSpec(
            num_scalar_prefetch=1,
            grid=(half // units,),
            in_specs=[fixed] * 4 + [pl.BlockSpec((1, units), lambda j, core: (0, j)), *weight_specs],
            out_specs=[
                pl.BlockSpec(up_shape, lambda j, core: (0, 0, 0), **once),
                down_grad_spec,
                *[fixed] * 4,
                pl.BlockSpec((1, units), lambda j, core: (0, j)),
            ],
            scratch_shapes=[
                pltpu.VMEM((2 * rows, width), jnp.bfloat16),
                pltpu.VMEM((2 * rows, width), jnp.bfloat16),
                pltpu.VMEM((width, 2 * rows), jnp.bfloat16),
            ],
        ),
        out_shape=(
            jax.ShapeDtypeStruct(up_shape, jnp.bfloat16),
            jax.ShapeDtypeStruct(down_shape, jnp.bfloat16),
            *[total] * 4,
            jax.ShapeDtypeStruct((1, half), jnp.float32),
        ),
        compiler_params=pltpu.CompilerParams(vmem_limit_bytes=VMEM_BYTES),
        cost_estimate=pl.CostEstimate(
            flops=2 * rows * width * half * 12,
            bytes_accessed=half * width * 8 + rows * width * 24,
            transcendentals=rows * half * 4,
        ),
        name="mlp_both_ways",
    )(core, own, other, gm_own, gm_other, bias[None], *weights)
    up_grad, down_grad = outs[0], outs[1]
    if pieces == 1:
        up_grad = up_grad.reshape(half // width, chips, width // chips, width).swapaxes(0, 1)
        up_grad = up_grad.reshape(chips, -1, width)
        down_grad = down_grad.reshape(chips, -1, width)
    return (up_grad, down_grad, *outs[2:])


def finish_kernel(
    grad_ref, weight_ref, x_ref, gx_ref, gain_ref, out_ref, gain_grad_ref, shift_grad_ref, sums_ref, acc_ref
):
    step = pl.program_id(0)
    parts = [grad_ref[slot] for slot in range(grad_ref.shape[0])]
    grad = jnp.concatenate(parts, axis=1)
    width = x_ref.shape[1]
    product = inner_cols(grad, weight_ref[...].reshape(width, width))
    sums_ref[...] = jnp.sum(grad.astype(jnp.float32), axis=0, keepdims=True)[None]

    @pl.when(step == 0)
    def begin():
        acc_ref[...] = product

    @pl.when(step > 0)
    def further():
        acc_ref[...] += product

    @pl.when(step == pl.num_programs(0) - 1)
    def end():
        values = x_ref[...].astype(jnp.float32)
        centered = values - jnp.mean(values, axis=1, keepdims=True)
        scale = lax.rsqrt(jnp.mean(centered * centered, axis=1, keepdims=True) + 1e-06)
        unit = centered * scale
        grad_norm = acc_ref[...]
        gain_grad_ref[...] = jnp.sum(grad_norm * unit, axis=0, keepdims=True)
        shift_grad_ref[...] = jnp.sum(grad_norm, axis=0, keepdims=True)
        grad_unit = grad_norm * gain_ref[...]
        mean = jnp.mean(grad_unit, axis=1, keepdims=True)
        slant = jnp.mean(grad_unit * unit, axis=1, keepdims=True)
        out_ref[...] = gx_ref[...] + scale * (grad_unit - mean - unit * slant)


def finish(grads, weights, inputs, gx, gain):
    rows, width = inputs.shape
    group, lanes = grads.shape[0], grads.shape[2] // 3
    if lanes % 128:
        grads = grads.reshape(group, rows, 3, lanes).transpose(2, 0, 1, 3)
        grads = grads.reshape(3 * group, rows, lanes)
        grad_spec = pl.BlockSpec((group, rows, lanes), lambda k: (k, 0, 0))
    else:
        grad_spec = pl.BlockSpec((group, rows, lanes), lambda k: (0, 0, k))
    if weights.ndim == 3:
        share = width // weights.shape[0]
        first = weights.shape[1] // share - 3
        weight_spec = pl.BlockSpec((weights.shape[0], share, width), lambda k: (0, first + k, 0))
    else:
        weight_spec = pl.BlockSpec((width, width), lambda k: (0, k))
    fixed = lambda *shape: pl.BlockSpec(shape, lambda k: (0, 0))
    vector = jax.ShapeDtypeStruct((1, width), jnp.float32)
    return pl.pallas_call(
        finish_kernel,
        grid=(3,),
        in_specs=[
            grad_spec,
            weight_spec,
            fixed(rows, width),
            fixed(rows, width),
            fixed(1, width),
        ],
        out_specs=[
            fixed(rows, width),
            fixed(1, width),
            fixed(1, width),
            pl.BlockSpec((1, 1, width), lambda k: (k, 0, 0)),
        ],
        out_shape=(
            jax.ShapeDtypeStruct((rows, width), jnp.float32),
            vector,
            vector,
            jax.ShapeDtypeStruct((3, 1, width), jnp.float32),
        ),
        scratch_shapes=[pltpu.VMEM((rows, width), jnp.float32)],
        compiler_params=pltpu.CompilerParams(vmem_limit_bytes=VMEM_BYTES),
        cost_estimate=pl.CostEstimate(
            flops=rows * width * width * 6, bytes_accessed=width * width * 16, transcendentals=0
        ),
        name="finish_input",
    )(grads, weights, inputs, gx, gain[None])


def swap_cores(value):
    return lax.ppermute(value, "core", [(0, 1), (1, 0)])


def line_pieces(value, axis):
    size = lax.axis_size(axis)
    if size == 2:
        other = lax.ppermute(value, axis, [(0, 1), (1, 0)])
        return [(None, other)]
    pieces = []
    for sign in (-1, 1):
        moving = value
        for step in range(1, size):
            pairs = [(i, i - sign) for i in range(size) if 0 <= i - sign < size]
            pairs = [(i, j) for i, j in pairs if 0 <= i + sign * (step - 1) < size]
            moving = lax.ppermute(moving, axis, pairs)
            pieces.append((sign * step, moving))
    return pieces


def line_order(value, pieces, axis):
    place = lax.axis_index(axis)
    size = lax.axis_size(axis)
    if size == 2:
        other = pieces[0][1]
        return jnp.where(place == 0, jnp.stack([value, other]), jnp.stack([other, value]))
    whole = jnp.zeros((size, *value.shape), value.dtype)
    for distance, piece in sorted(pieces, key=lambda item: -abs(item[0])) + [(0, value)]:
        slot = jnp.clip(place + distance, 0, size - 1)
        whole = lax.dynamic_update_index_in_dim(whole, piece, slot, 0)
    return whole


def gather_line(value, axis):
    return line_order(value, line_pieces(value, axis), axis)


def rounded_sum(*terms):
    return sum(term.astype(jnp.float32) for term in terms).astype(jnp.bfloat16)


def scatter_terms(value, axis, dim):
    if lax.axis_size(axis) != 2:
        return (scatter_line(value, axis, dim),)
    place = lax.axis_index(axis)
    pick = lambda slot: lax.dynamic_index_in_dim(value, slot, dim, keepdims=False)
    return (pick(place), lax.ppermute(pick(1 - place), axis, [(0, 1), (1, 0)]))


def scatter_direct(value, axis, dim):
    place = lax.axis_index(axis)
    size = lax.axis_size(axis)
    pick = lambda slot: lax.dynamic_index_in_dim(
        value, jnp.clip(slot, 0, size - 1), dim, keepdims=False
    )
    terms = [pick(place)]
    for distance in range(size - 1, 0, -1):
        for move in (-distance, distance):
            pairs = [(i, i + move) for i in range(size) if 0 <= i + move < size]
            terms.append(lax.ppermute(pick(place + move), axis, pairs))
    return rounded_sum(*terms)


def scatter_line(value, axis, dim):
    place = lax.axis_index(axis)
    size = lax.axis_size(axis)
    pick = lambda slot: lax.dynamic_index_in_dim(
        value, jnp.clip(slot, 0, size - 1), dim, keepdims=False
    )
    if size == 2:
        return rounded_sum(pick(place), lax.ppermute(pick(1 - place), axis, [(0, 1), (1, 0)]))
    sums = []
    for sign in (-1, 1):
        moving = None
        for step in range(1, size):
            start = 0 if sign < 0 else size - 1
            pairs = [(i, i - sign) for i in range(size) if 0 <= i - sign < size]
            pairs = [(i, j) for i, j in pairs if abs(i - start) <= step - 1]
            own = pick(place - sign * (size - step))
            payload = own if moving is None else rounded_sum(own, moving)
            moving = lax.ppermute(payload, axis, pairs)
        sums.append(moving)
    return rounded_sum(pick(place), *sums)


def on_device(
    tokens,
    cotangent,
    segment_ids,
    valid,
    project_in,
    project_out,
    hidden_up,
    hidden_down,
    gains_biases,
    moment_in,
    moment_out,
    moment_up,
    moment_down,
    moment_gains,
    square_in,
    square_out,
    square_up,
    square_down,
    square_gains,
):
    rows = tokens.shape[0]
    width = tokens.shape[1]
    everyone = ("outer", "inner", "line", "core")
    planes = ("outer", "inner")
    seq = ("line", "core")
    streams, line = lax.axis_size(planes), lax.axis_size("line")
    group = 2 * line
    count = streams * group
    chips = streams * line
    share = width // count
    lanes = width // group
    length = rows * group
    images = length // IMG_LEN
    core = lax.axis_index("core")
    first_core = core == 0

    def in_order(own, other, axis):
        return jnp.concatenate(
            [jnp.where(first_core, own, other), jnp.where(first_core, other, own)], axis=axis
        )

    half = FF // 2
    unit_block = FF // count
    folds = half // width
    up_end = 2 * share * folds
    low = lambda value: value.astype(jnp.bfloat16)
    direct = share % 16 == 0 and unit_block == 128
    pieces = line_pieces(tokens, "line")
    if direct:
        fold = lambda value: low(value).reshape(share, -1, width).swapaxes(0, 1).reshape(-1, width)
        packed = jnp.concatenate([fold(hidden_up), low(hidden_down), low(project_out)], axis=0)
        pieces = dict(pieces)
        begun = sorted(pieces, key=abs)[:4]
        packed, *tied = lax.optimization_barrier((packed, *[pieces[n] for n in begun]))
        pieces = list((pieces | dict(zip(begun, tied))).items())
        gathered = lax.all_gather(packed, everyone, axis=0, tiled=False)
        whole_out = gathered[:, packed.shape[0] - share :].reshape(width, width)
        mlp_weights = (gathered,)
    own_tokens = line_order(tokens, pieces, "line").reshape(-1, width)
    swapped = [(distance, swap_cores(piece)) for distance, piece in pieces]
    other_tokens = line_order(swap_cores(tokens), swapped, "line").reshape(-1, width)

    owned = project_in.astype(jnp.bfloat16).reshape(share, 3, group, lanes)
    owned = owned.transpose(2, 0, 1, 3).reshape(group, share, 3 * lanes)
    position = lax.broadcasted_iota(jnp.int32, (images, rows), 1)
    found = (segment_ids[None, :] == lax.broadcasted_iota(jnp.int32, (images, rows), 0)) & (
        valid[None, :] == 1
    )
    first = jnp.min(jnp.where(found, position, rows), axis=1)
    small = jnp.concatenate(
        [
            gains_biases.astype(jnp.bfloat16).reshape(-1),
            (first // 32).astype(jnp.bfloat16),
            (first % 32).astype(jnp.bfloat16),
        ]
    )
    vector_size = gains_biases.size
    extra = -(-small.shape[0] // (3 * lanes))
    small = jnp.pad(small, (0, extra * 3 * lanes - small.shape[0])).reshape(1, extra, 3 * lanes)
    blocks = jnp.concatenate([owned, jnp.broadcast_to(small, (group, extra, 3 * lanes))], axis=1)
    blocks = lax.all_to_all(blocks, seq, split_axis=0, concat_axis=0, tiled=True)
    blocks = gather_line(gather_line(blocks, "inner"), "outer")
    blocks = blocks.reshape(count, share + extra, 3 * lanes)
    mine_in = blocks[:, :share].reshape(width, 3 * lanes)
    small = blocks[:, share:].reshape(count, -1)
    vectors = small[:, :vector_size].reshape(count, -1, share).transpose(1, 0, 2)
    vectors = vectors.reshape(-1, width).astype(jnp.float32)
    first = small[:, vector_size : vector_size + 2 * images].astype(jnp.int32)
    first = first[:, :images] * 32 + first[:, images:]
    first = lax.dynamic_slice_in_dim(first, lax.axis_index(planes) * group, group, 0)
    offsets = lax.broadcasted_iota(jnp.int32, (group, images), 0) * rows
    starts = jnp.min(jnp.where(first < rows, first + offsets, length), axis=0)

    gain_one, shift_one, bias_query, bias_value, bias_out = (
        vectors[0],
        vectors[1],
        vectors[2],
        vectors[3],
        vectors[4],
    )
    scale_one, gain_two, shift_two, bias_down, scale_two = (
        vectors[5],
        vectors[6],
        vectors[7],
        vectors[8],
        vectors[9],
    )
    bias_up = lax.dynamic_index_in_dim(
        vectors[10:].reshape(chips, 2, unit_block), core, axis=1, keepdims=False
    ).reshape(half)
    column = lax.axis_index(seq) * lanes
    bias_in = jnp.concatenate(
        [
            lax.dynamic_slice_in_dim(bias_query, column, lanes, 0),
            jnp.zeros((lanes,), jnp.float32),
            lax.dynamic_slice_in_dim(bias_value, column, lanes, 0),
        ]
    )
    grad_rows = cotangent.astype(jnp.float32) * valid.astype(jnp.float32)[:, None]
    grad_branch = (scale_two * grad_rows).astype(jnp.bfloat16)

    normed_one, query, keys, values = norm_mix(
        core.reshape(1),
        own_tokens,
        other_tokens,
        rows,
        gain_one,
        shift_one,
        mine_in,
        bias_in,
    )
    wide, attended, logs = attend(starts, query, keys, values)
    if not direct:
        whole_out, whole_up, whole_down = (
            lax.all_gather(low(value), everyone, axis=0, tiled=True)
            for value in (project_out, hidden_up, hidden_down)
        )
        block = jnp.arange(half) // unit_block * 2 + core
        index = block * unit_block + lax.rem(jnp.arange(half), unit_block)
        mlp_weights = (jnp.take(whole_up, index, axis=1), jnp.take(whole_down, index, axis=0))
    returned = lax.all_to_all(
        attended.reshape(group, rows, lanes), seq, split_axis=0, concat_axis=0, tiled=True
    )
    in_rows, returned = lax.optimization_barrier((low(project_in), returned))
    if direct:
        in_rows = in_rows.reshape(share, 3, width).swapaxes(0, 1).reshape(-1, width)
    whole_in = lax.all_gather(in_rows, everyone, axis=0, tiled=not direct)
    attended_rows = returned.transpose(1, 0, 2).reshape(rows, width)
    inputs = tokens.astype(jnp.float32)
    projected = plain_product(attended_rows, whole_out) + bias_out
    second = inputs + scale_one * projected
    norm_two, norm_two_back = jax.vjp(layer_norm, second, gain_two, shift_two)
    normed_two = norm_two.astype(jnp.bfloat16)
    grad_up, grad_down, branch, branch_other, grad_norm_two, grad_norm_other, grad_bias_up = mlp(
        core.reshape(1),
        normed_two,
        swap_cores(normed_two),
        grad_branch,
        swap_cores(grad_branch),
        mlp_weights,
        bias_up,
        chips,
    )
    grad_norm_two = grad_norm_two + swap_cores(grad_norm_other)
    branch = branch + swap_cores(branch_other) + bias_down
    block_output = (second + scale_two * branch).astype(jnp.bfloat16)
    grad_scale_two = jnp.sum(grad_rows * branch, axis=0)
    grad_bias_down = jnp.sum(grad_branch.astype(jnp.float32), axis=0)
    second_part, grad_gain_two, grad_shift_two = norm_two_back(grad_norm_two)
    grad_second = grad_rows + second_part
    grad_scale_one = jnp.sum(grad_second * projected, axis=0)
    grad_projected = (scale_one * grad_second).astype(jnp.bfloat16)
    grad_bias_out = jnp.sum(grad_projected.astype(jnp.float32), axis=0)
    grad_attended = inner_cols(grad_projected, whole_out).astype(jnp.bfloat16)
    grad_stream = lax.all_to_all(
        grad_attended.reshape(rows, group, lanes).transpose(1, 0, 2),
        seq,
        split_axis=0,
        concat_axis=0,
        tiled=True,
    ).reshape(length, lanes)
    grad_out = inner_rows(attended_rows, grad_projected).astype(jnp.bfloat16)
    grad_out = grad_out.reshape(chips, 2 * share, width)
    outer, inner = lax.axis_size("outer"), lax.axis_size("inner")
    grad_up, grad_out, grad_down = (
        value.reshape(outer, inner, line, -1, width) for value in (grad_up, grad_out, grad_down)
    )
    begun = (
        scatter_terms(grad_up, "inner", 1),
        scatter_terms(grad_out, "inner", 1),
        scatter_terms(grad_down, "outer", 0),
    )

    grad_mixed_stream = attend_back(starts, query, keys, values, wide, logs, grad_stream)
    grad_mixed = lax.all_to_all(
        grad_mixed_stream.reshape(group, rows, 3 * lanes), seq, split_axis=0, concat_axis=0, tiled=True
    )
    begun, grad_mixed_stream = lax.optimization_barrier((begun, grad_mixed_stream))
    grad_up, grad_out, grad_down = (rounded_sum(*terms) for terms in begun)
    grad_down = scatter_line(grad_down, "inner", 0)
    grad_up, grad_out = (scatter_line(value, "outer", 0) for value in (grad_up, grad_out))
    plane_sums = jnp.concatenate([grad_up, grad_out, grad_down], axis=1)
    plane_sums, grad_mixed = lax.optimization_barrier((plane_sums, grad_mixed))
    summed = scatter_direct(plane_sums, "line", 0)
    grad_in = inner_rows(normed_one, grad_mixed_stream).astype(jnp.bfloat16)
    parts = grad_in.reshape(outer, inner, group * share, 3 * lanes)
    parts = scatter_line(scatter_line(parts, "inner", 1), "outer", 0)
    input_grad, grad_gain_one, grad_shift_one, mixed_sums = finish(
        grad_mixed, whole_in, tokens, grad_second, gain_one
    )
    parts, grad_gain_one = lax.optimization_barrier((parts, grad_gain_one))
    parts = parts.reshape(group, share, 3 * lanes)
    parts = lax.all_to_all(parts, seq, split_axis=0, concat_axis=0, tiled=True)
    parts = parts.astype(jnp.float32)
    summed_in = parts.reshape(group, share, 3, lanes).transpose(1, 2, 0, 3).reshape(share, 3 * width)
    up_sums = grad_bias_up.reshape(chips, unit_block)
    up_sums = jnp.where(
        (lax.broadcasted_iota(jnp.int32, (1, 2, 1), 1) == core), up_sums[:, None, :], 0.0
    )
    grad_small = jnp.concatenate(
        [
            jnp.stack(
                [
                    grad_gain_one[0],
                    grad_shift_one[0],
                    mixed_sums[0, 0],
                    mixed_sums[2, 0],
                    grad_bias_out,
                    grad_scale_one,
                    grad_gain_two,
                    grad_shift_two,
                    grad_bias_down,
                    grad_scale_two,
                ]
            ),
            up_sums.reshape(-1, width),
        ],
        axis=0,
    )
    small_rows = grad_small.shape[0]
    parts = grad_small.reshape(small_rows, count, share).transpose(1, 0, 2)
    parts = lax.all_to_all(
        parts.reshape(count, small_rows * share), everyone, split_axis=0, concat_axis=0, tiled=True
    )
    summed_gains = jnp.sum(parts, axis=0).reshape(small_rows, share)

    up_sum = summed[:up_end].reshape(folds, 2, share, width)
    out_sum = summed[up_end : up_end + 2 * share].reshape(1, 2, share, width)
    both_sums = jnp.concatenate([up_sum, out_sum], axis=0)
    own_sums = jnp.where(first_core, both_sums[:, 0], both_sums[:, 1])
    other_sums = swap_cores(jnp.where(first_core, both_sums[:, 1], both_sums[:, 0]))
    summed_down = summed[up_end + 2 * share :].astype(jnp.float32)
    summed_out = own_sums[folds].astype(jnp.float32) + other_sums[folds].astype(jnp.float32)
    own_up = own_sums[:folds].transpose(1, 0, 2).reshape(share, chips, 1, unit_block)
    other_up = other_sums[:folds].transpose(1, 0, 2).reshape(share, chips, 1, unit_block)
    summed_up = in_order(own_up, other_up, 2).reshape(share, FF).astype(jnp.float32)
    rate_out = max(1, 4 * D // IMG_LEN) ** (-0.5)
    new_in, new_moment_in, new_square_in = adamw(
        project_in, moment_in, square_in, summed_in, D ** (-0.5), 0.04
    )
    new_out, new_moment_out, new_square_out = adamw(
        project_out, moment_out, square_out, summed_out, rate_out, 0.04
    )
    new_up, new_moment_up, new_square_up = adamw(
        hidden_up, moment_up, square_up, summed_up, D ** (-0.5), 0.04
    )
    new_down, new_moment_down, new_square_down = adamw(
        hidden_down, moment_down, square_down, summed_down, FF ** (-0.5), 0.04
    )
    new_gains, new_moment_gains, new_square_gains = adamw(
        gains_biases, moment_gains, square_gains, summed_gains, 0.2, 0.0
    )
    return (
        block_output,
        input_grad,
        new_in,
        new_out,
        new_up,
        new_down,
        new_gains,
        new_moment_in,
        new_moment_out,
        new_moment_up,
        new_moment_down,
        new_moment_gains,
        new_square_in,
        new_square_out,
        new_square_up,
        new_square_down,
        new_square_gains,
        summed_gains[8],
    )


def solution(mesh):
    streams, group = mesh.shape["fsdp"], mesh.shape["seq"]
    outer = math.isqrt(streams)
    fine = jax.sharding.Mesh(
        mesh.devices.reshape(outer, streams // outer, group // 2, 2),
        ("outer", "inner", "line", "core"),
    )
    return jax.shard_map(
        on_device,
        mesh=fine,
        in_specs=(
            P(("outer", "inner", "line", "core"), None),
            P(("outer", "inner", "line", "core"), None),
            P(("outer", "inner", "line", "core")),
            P(("outer", "inner", "line", "core")),
            P(("outer", "inner", "line", "core"), None),
            P(("outer", "inner", "line", "core"), None),
            P(("outer", "inner", "line", "core"), None),
            P(("outer", "inner", "line", "core"), None),
            P(None, ("outer", "inner", "line", "core")),
            P(("outer", "inner", "line", "core"), None),
            P(("outer", "inner", "line", "core"), None),
            P(("outer", "inner", "line", "core"), None),
            P(("outer", "inner", "line", "core"), None),
            P(None, ("outer", "inner", "line", "core")),
            P(("outer", "inner", "line", "core"), None),
            P(("outer", "inner", "line", "core"), None),
            P(("outer", "inner", "line", "core"), None),
            P(("outer", "inner", "line", "core"), None),
            P(None, ("outer", "inner", "line", "core")),
        ),
        out_specs=(
            P(("outer", "inner", "line", "core"), None),
            P(("outer", "inner", "line", "core"), None),
            P(("outer", "inner", "line", "core"), None),
            P(("outer", "inner", "line", "core"), None),
            P(("outer", "inner", "line", "core"), None),
            P(("outer", "inner", "line", "core"), None),
            P(None, ("outer", "inner", "line", "core")),
            P(("outer", "inner", "line", "core"), None),
            P(("outer", "inner", "line", "core"), None),
            P(("outer", "inner", "line", "core"), None),
            P(("outer", "inner", "line", "core"), None),
            P(None, ("outer", "inner", "line", "core")),
            P(("outer", "inner", "line", "core"), None),
            P(("outer", "inner", "line", "core"), None),
            P(("outer", "inner", "line", "core"), None),
            P(("outer", "inner", "line", "core"), None),
            P(None, ("outer", "inner", "line", "core")),
            P(("outer", "inner", "line", "core")),
        ),
        check_vma=False,
    )
```

```python
import functools
import math

import jax
import jax.numpy as jnp
from jax import lax
from jax.experimental import pallas as pl
from jax.experimental.pallas import tpu as pltpu
from jax.sharding import PartitionSpec as P

D = 1024
FF = 4096
HEADS = 16
HEAD_DIM = 64
IMG_LEN = 1370
WINDOW = 1408
TILE = 352
VMEM_BYTES = 56 * 1024 * 1024
STEP = 10


masked_score = -1e30


def layer_norm(values, gain, shift):
    average = jnp.mean(values, axis=-1, keepdims=True)
    centered = values - average
    variance = jnp.mean(centered * centered, axis=-1, keepdims=True)
    return centered * lax.rsqrt(variance + 1e-06) * gain + shift


def exact_gelu(values):
    return jax.nn.gelu(values, approximate=False)


def plain_product(left, right):
    return jnp.dot(left, right, preferred_element_type=jnp.float32)


def inner_rows(left, right):
    return lax.dot_general(
        left, right, (((0,), (0,)), ((), ())), preferred_element_type=jnp.float32
    )


def inner_cols(left, right):
    return lax.dot_general(
        left, right, (((1,), (1,)), ((), ())), preferred_element_type=jnp.float32
    )


def adamw(param, moment, square, grad, rate, decay):
    new_moment = 0.9 * moment + 0.1 * grad
    new_square = 0.999 * square + 0.001 * grad * grad
    corrected = new_moment / (1.0 - 0.9**STEP)
    scaled = jnp.sqrt(new_square / (1.0 - 0.999**STEP)) + 1e-08
    return (param - rate * (corrected / scaled + decay * param), new_moment, new_square)


def head_lanes(shape):
    return lax.broadcasted_iota(jnp.int32, shape, 1) // HEAD_DIM


def window_of(starts_ref, image, length):
    start = starts_ref[image]
    base = jnp.clip(start // 16 * 16, 0, length - WINDOW)
    return (pl.multiple_of(base, 16), start - base)


def image_mask(position, offset):
    return (position >= offset) & (position < offset + IMG_LEN)


def attend_kernel(starts_ref, q_ref, k_ref, v_ref, wide_ref, out_ref, log_ref):
    image, tile = pl.program_id(0), pl.program_id(1)
    length, lanes = q_ref.shape
    base, offset = window_of(starts_ref, image, length)
    rows = pl.ds(pl.multiple_of(base + tile * TILE, 16), TILE)

    @pl.when((image == 0) & (tile == 0))
    def clear():
        wide_ref[...] = jnp.zeros_like(wide_ref)
        out_ref[...] = jnp.zeros_like(out_ref)
        log_ref[...] = jnp.zeros_like(log_ref)

    query = q_ref[rows, :].astype(jnp.float32) * HEAD_DIM ** (-0.5)
    keys = k_ref[pl.ds(base, WINDOW), :]
    values = v_ref[pl.ds(base, WINDOW), :]
    key_ok = image_mask(lax.broadcasted_iota(jnp.int32, (1, WINDOW), 1), offset)
    bias = jnp.where(key_ok, 0.0, masked_score)
    row_ok = image_mask(lax.broadcasted_iota(jnp.int32, (TILE, 1), 0) + tile * TILE, offset)
    head_of = head_lanes((TILE, lanes))
    total_out = jnp.zeros((TILE, lanes), jnp.float32)
    total_log = jnp.zeros((TILE, lanes), jnp.float32)
    for head in range(lanes // HEAD_DIM):
        mine = head_of == head
        part = jnp.where(mine, query, 0.0).astype(jnp.bfloat16)
        scores = inner_cols(part, keys) + bias
        top = jnp.max(scores, axis=1, keepdims=True)
        weights = jnp.exp(scores - top)
        total = jnp.sum(weights, axis=1, keepdims=True)
        probs = (weights * (1.0 / total)).astype(jnp.bfloat16)
        total_out = jnp.where(mine, plain_product(probs, values), total_out)
        total_log = jnp.where(mine, top + jnp.log(total), total_log)
    merged = jnp.where(row_ok, total_out, wide_ref[rows, :])
    wide_ref[rows, :] = merged
    out_ref[rows, :] = merged.astype(jnp.bfloat16)
    log_ref[rows, :] = jnp.where(row_ok, total_log, log_ref[rows, :])


def attend(starts, query, keys, values):
    length, lanes = query.shape
    whole = pl.BlockSpec((length, lanes), lambda image, tile, starts: (0, 0))
    wide = jax.ShapeDtypeStruct((length, lanes), jnp.float32)
    images = length // IMG_LEN
    return pl.pallas_call(
        attend_kernel,
        grid_spec=pltpu.PrefetchScalarGridSpec(
            num_scalar_prefetch=1,
            grid=(images, WINDOW // TILE),
            in_specs=[whole] * 3,
            out_specs=[whole] * 3,
        ),
        out_shape=(wide, jax.ShapeDtypeStruct((length, lanes), jnp.bfloat16), wide),
        compiler_params=pltpu.CompilerParams(
            vmem_limit_bytes=VMEM_BYTES, dimension_semantics=("arbitrary", "arbitrary")
        ),
        cost_estimate=pl.CostEstimate(
            flops=images * WINDOW * WINDOW * lanes * 8,
            bytes_accessed=length * lanes * 16,
            transcendentals=images * WINDOW * WINDOW * lanes // HEAD_DIM,
        ),
        name="attend_forward",
    )(starts, query, keys, values)


def attend_back_kernel(
    starts_ref, q_ref, k_ref, v_ref, wide_ref, log_ref, go_ref, grad_ref, key_acc, value_acc
):
    image, tile = pl.program_id(0), pl.program_id(1)
    length, lanes = q_ref.shape
    base, offset = window_of(starts_ref, image, length)
    rows = pl.ds(pl.multiple_of(base + tile * TILE, 16), TILE)
    window = pl.ds(base, WINDOW)

    @pl.when((image == 0) & (tile == 0))
    def clear():
        grad_ref[...] = jnp.zeros_like(grad_ref)

    @pl.when(tile == 0)
    def clear_sums():
        key_acc[...] = jnp.zeros_like(key_acc)
        value_acc[...] = jnp.zeros_like(value_acc)

    query = q_ref[rows, :].astype(jnp.float32) * HEAD_DIM ** (-0.5)
    keys = k_ref[window, :]
    values = v_ref[window, :]
    key_ok = image_mask(lax.broadcasted_iota(jnp.int32, (1, WINDOW), 1), offset)
    bias = jnp.where(key_ok, 0.0, masked_score)
    row_ok = image_mask(lax.broadcasted_iota(jnp.int32, (TILE, 1), 0) + tile * TILE, offset)
    head_of = head_lanes((TILE, lanes))
    grad_out = jnp.where(row_ok, go_ref[rows, :].astype(jnp.float32), 0.0)
    centre_parts = grad_out * wide_ref[rows, :]
    logs = jnp.where(row_ok, log_ref[rows, :], -masked_score)
    query_grad = jnp.zeros((TILE, lanes), jnp.float32)
    for head in range(lanes // HEAD_DIM):
        mine = head_of == head
        part = jnp.where(mine, query, 0.0).astype(jnp.bfloat16)
        grad_part = jnp.where(mine, grad_out, 0.0).astype(jnp.bfloat16)
        centre = jnp.sum(jnp.where(mine, centre_parts, 0.0), axis=1, keepdims=True)
        log_total = jnp.max(jnp.where(mine, logs, masked_score), axis=1, keepdims=True)
        probs = jnp.exp(inner_cols(part, keys) + bias - log_total)
        grad_probs = inner_cols(grad_part, values)
        grad_scores = (probs * (grad_probs - centre)).astype(jnp.bfloat16)
        query_grad = jnp.where(mine, plain_product(grad_scores, keys), query_grad)
        key_acc[...] += inner_rows(part, grad_scores)
        value_acc[...] += inner_rows(grad_part, probs.astype(jnp.bfloat16))
    old = grad_ref[rows, 0:lanes].astype(jnp.float32)
    merged = jnp.where(row_ok, query_grad * HEAD_DIM ** (-0.5), old)
    grad_ref[rows, 0:lanes] = merged.astype(jnp.bfloat16)

    @pl.when(tile == pl.num_programs(1) - 1)
    def flush():
        inside = image_mask(lax.broadcasted_iota(jnp.int32, (WINDOW, 1), 0), offset)
        for slot, sums in ((1, key_acc), (2, value_acc)):
            columns = slice(slot * lanes, (slot + 1) * lanes)
            old = grad_ref[window, columns].astype(jnp.float32)
            merged = jnp.where(inside, sums[...].T, old)
            grad_ref[window, columns] = merged.astype(jnp.bfloat16)


def attend_back(starts, query, keys, values, wide, logs, grad_out):
    length, lanes = query.shape
    whole = pl.BlockSpec((length, lanes), lambda image, tile, starts: (0, 0))
    images = length // IMG_LEN
    return pl.pallas_call(
        attend_back_kernel,
        grid_spec=pltpu.PrefetchScalarGridSpec(
            num_scalar_prefetch=1,
            grid=(images, WINDOW // TILE),
            in_specs=[whole] * 6,
            out_specs=pl.BlockSpec((length, 3 * lanes), lambda image, tile, starts: (0, 0)),
            scratch_shapes=[pltpu.VMEM((lanes, WINDOW), jnp.float32)] * 2,
        ),
        out_shape=jax.ShapeDtypeStruct((length, 3 * lanes), jnp.bfloat16),
        compiler_params=pltpu.CompilerParams(
            vmem_limit_bytes=VMEM_BYTES, dimension_semantics=("arbitrary", "arbitrary")
        ),
        cost_estimate=pl.CostEstimate(
            flops=images * WINDOW * WINDOW * lanes * 20,
            bytes_accessed=length * lanes * 22,
            transcendentals=images * WINDOW * WINDOW * lanes // HEAD_DIM,
        ),
        name="attend_backward",
    )(starts, query, keys, values, wide, logs, grad_out)


def norm_mix_kernel(pieces, place_ref, own_ref, other_ref, gain_ref, shift_ref, bias_ref, *refs):
    weight = jnp.concatenate(
        [ref[...].reshape(own_ref.shape[1], -1) for ref in refs[:pieces]], axis=1
    )
    a_ref, q_ref, k_ref, v_ref = refs[pieces:]
    lanes = q_ref.shape[1]
    mine = lax.rem(pl.program_id(0), 2) == lax.rem(place_ref[0], 2)
    own, other = own_ref[...].astype(jnp.float32), other_ref[...].astype(jnp.float32)
    normed = layer_norm(jnp.where(mine, own, other), gain_ref[...], shift_ref[...])
    normed = normed.astype(jnp.bfloat16)
    a_ref[...] = normed
    mixed = (plain_product(normed, weight) + bias_ref[...]).astype(jnp.bfloat16)
    q_ref[...] = mixed[:, :lanes]
    k_ref[...] = mixed[:, lanes : 2 * lanes]
    v_ref[...] = mixed[:, 2 * lanes :]


def norm_mix(place, own, other, block, gain, shift, weight, bias):
    length, width = own.shape[0] * 2, own.shape[1]
    lanes = bias.shape[0] // 3
    row = lambda size: pl.BlockSpec((block, size), lambda i, place: (i, 0))
    half = pl.BlockSpec((block, width), lambda i, place: (i // 2, 0))
    fixed = lambda *shape: pl.BlockSpec(shape, lambda i, place: (0, 0))
    part = jax.ShapeDtypeStruct((length, lanes), jnp.bfloat16)
    if weight.ndim == 3:
        count = weight.shape[0]
        columns = lambda k: pl.BlockSpec(
            (count, width // count, lanes), lambda i, place: (0, k, place[0])
        )
        weights, weight_specs = [weight] * 3, [columns(k) for k in range(3)]
    else:
        weights, weight_specs = [weight], [fixed(width, 3 * lanes)]
    return pl.pallas_call(
        functools.partial(norm_mix_kernel, len(weights)),
        grid_spec=pltpu.PrefetchScalarGridSpec(
            num_scalar_prefetch=1,
            grid=(length // block,),
            in_specs=[
                half,
                half,
                fixed(1, width),
                fixed(1, width),
                fixed(1, 3 * lanes),
                *weight_specs,
            ],
            out_specs=[row(width), row(lanes), row(lanes), row(lanes)],
        ),
        out_shape=(jax.ShapeDtypeStruct((length, width), jnp.bfloat16), part, part, part),
        compiler_params=pltpu.CompilerParams(vmem_limit_bytes=VMEM_BYTES),
        cost_estimate=pl.CostEstimate(
            flops=length * width * lanes * 6, bytes_accessed=length * width * 4, transcendentals=0
        ),
        name="norm_mix",
    )(place, own, other, gain[None], shift[None], bias[None], *weights)


def mlp_kernel(pieces, core_ref, own_ref, other_ref, gm_own_ref, gm_other_ref, bias_ref, *refs):
    up_refs, down_refs = refs[:pieces], refs[pieces : 2 * pieces]
    up_grad_ref, down_grad_ref, m_own_ref, m_other_ref, gh_own_ref, gh_other_ref = refs[
        2 * pieces : 2 * pieces + 6
    ]
    bias_grad_ref, h_ref, gm_ref, turned_ref = refs[2 * pieces + 6 :]
    tile = pl.program_id(0)
    rows, width = own_ref.shape
    chips = up_grad_ref.shape[0]
    up_rows = width // chips
    units = bias_ref.shape[1]
    folds = width // units

    @pl.when(tile == 0)
    def clear():
        for ref in (m_own_ref, m_other_ref, gh_own_ref, gh_other_ref):
            ref[...] = jnp.zeros_like(ref)
        h_ref[:rows] = own_ref[...]
        h_ref[rows:] = other_ref[...]
        gm_ref[:rows] = gm_own_ref[...]
        gm_ref[rows:] = gm_other_ref[...]
        turned_ref[...] = h_ref[...].T

    weight_up = jnp.concatenate([ref[...].reshape(width, -1) for ref in up_refs], axis=1)
    weight_down = jnp.concatenate([ref[...].reshape(-1, width) for ref in down_refs], axis=0)
    gm = gm_ref[...]
    upward = plain_product(h_ref[...], weight_up) + bias_ref[...]
    normal = 0.5 * (1.0 + lax.erf(upward * 0.5**0.5))
    slope = normal + upward * jnp.exp(upward * upward * -0.5) * (0.5 / jnp.pi) ** 0.5
    active = (upward * normal).astype(jnp.bfloat16)
    grad_up = (inner_cols(gm, weight_down) * slope).astype(jnp.bfloat16)
    bias_grad_ref[...] = jnp.sum(grad_up.astype(jnp.float32), axis=0, keepdims=True)
    branch = plain_product(active, weight_down)
    m_own_ref[...] += branch[:rows]
    m_other_ref[...] += branch[rows:]
    grad_norm = inner_cols(grad_up, weight_up)
    gh_own_ref[...] += grad_norm[:rows]
    gh_other_ref[...] += grad_norm[rows:]
    up_grad = plain_product(turned_ref[...], grad_up).astype(jnp.bfloat16)
    row = pl.multiple_of(tile // folds * up_rows, up_rows)
    column = pl.multiple_of(lax.rem(tile, folds) * units, units)
    up_grad = up_grad.reshape(chips, up_rows, units)
    up_grad_ref[:, pl.ds(row, up_rows), pl.ds(column, units)] = up_grad
    down_grad = inner_rows(active, gm).astype(jnp.bfloat16)
    down_grad_ref[...] = down_grad.reshape(down_grad_ref.shape)


def mlp(core, own, other, gm_own, gm_other, weights, bias, chips):
    rows, width = own.shape
    half = bias.shape[0]
    unit_block = half // chips
    units = 256
    folds = width // units
    once = dict(pipeline_mode=pl.Buffered(1))
    fixed = pl.BlockSpec((rows, width), lambda j, core: (0, 0), **once)
    if len(weights) == 1:
        count = 2 * chips
        share = width // count
        pieces = units // unit_block
        lane_blocks = width // unit_block

        def up_spec(piece):
            def place(j, core):
                block = 2 * (j * pieces + piece) + core[0]
                return (0, block // lane_blocks, lax.rem(block, lane_blocks))

            return pl.BlockSpec((count, share, unit_block), place)

        def down_spec(piece):
            return pl.BlockSpec(
                (1, unit_block, width), lambda j, core: (2 * (j * pieces + piece) + core[0], 1, 0)
            )

        weights = list(weights) * (2 * pieces)
        weight_specs = [up_spec(n) for n in range(pieces)] + [down_spec(n) for n in range(pieces)]
        up_shape, down_shape = (chips, half // chips, width), (chips, half // chips, width)
        down_grad_spec = pl.BlockSpec((pieces, unit_block, width), lambda j, core: (j, 0, 0))
    else:
        pieces = 1
        weight_specs = [
            pl.BlockSpec((width, units), lambda j, core: (0, j)),
            pl.BlockSpec((units, width), lambda j, core: (j, 0)),
        ]
        up_shape, down_shape = (1, half // width * width, width), (1, half, width)
        down_grad_spec = pl.BlockSpec((1, units, width), lambda j, core: (0, j, 0))
    total = jax.ShapeDtypeStruct((rows, width), jnp.float32)
    outs = pl.pallas_call(
        functools.partial(mlp_kernel, pieces),
        grid_spec=pltpu.PrefetchScalarGridSpec(
            num_scalar_prefetch=1,
            grid=(half // units,),
            in_specs=[fixed] * 4 + [pl.BlockSpec((1, units), lambda j, core: (0, j)), *weight_specs],
            out_specs=[
                pl.BlockSpec(up_shape, lambda j, core: (0, 0, 0), **once),
                down_grad_spec,
                *[fixed] * 4,
                pl.BlockSpec((1, units), lambda j, core: (0, j)),
            ],
            scratch_shapes=[
                pltpu.VMEM((2 * rows, width), jnp.bfloat16),
                pltpu.VMEM((2 * rows, width), jnp.bfloat16),
                pltpu.VMEM((width, 2 * rows), jnp.bfloat16),
            ],
        ),
        out_shape=(
            jax.ShapeDtypeStruct(up_shape, jnp.bfloat16),
            jax.ShapeDtypeStruct(down_shape, jnp.bfloat16),
            *[total] * 4,
            jax.ShapeDtypeStruct((1, half), jnp.float32),
        ),
        compiler_params=pltpu.CompilerParams(vmem_limit_bytes=VMEM_BYTES),
        cost_estimate=pl.CostEstimate(
            flops=2 * rows * width * half * 12,
            bytes_accessed=half * width * 8 + rows * width * 24,
            transcendentals=rows * half * 4,
        ),
        name="mlp_both_ways",
    )(core, own, other, gm_own, gm_other, bias[None], *weights)
    up_grad, down_grad = outs[0], outs[1]
    if pieces == 1:
        up_grad = up_grad.reshape(half // width, chips, width // chips, width).swapaxes(0, 1)
        up_grad = up_grad.reshape(chips, -1, width)
        down_grad = down_grad.reshape(chips, -1, width)
    return (up_grad, down_grad, *outs[2:])


def finish_kernel(
    grad_ref, weight_ref, x_ref, gx_ref, gain_ref, out_ref, gain_grad_ref, shift_grad_ref, sums_ref, acc_ref
):
    step = pl.program_id(0)
    parts = [grad_ref[slot] for slot in range(grad_ref.shape[0])]
    grad = jnp.concatenate(parts, axis=1)
    width = x_ref.shape[1]
    product = inner_cols(grad, weight_ref[...].reshape(width, width))
    sums_ref[...] = jnp.sum(grad.astype(jnp.float32), axis=0, keepdims=True)[None]

    @pl.when(step == 0)
    def begin():
        acc_ref[...] = product

    @pl.when(step > 0)
    def further():
        acc_ref[...] += product

    @pl.when(step == pl.num_programs(0) - 1)
    def end():
        values = x_ref[...].astype(jnp.float32)
        centered = values - jnp.mean(values, axis=1, keepdims=True)
        scale = lax.rsqrt(jnp.mean(centered * centered, axis=1, keepdims=True) + 1e-06)
        unit = centered * scale
        grad_norm = acc_ref[...]
        gain_grad_ref[...] = jnp.sum(grad_norm * unit, axis=0, keepdims=True)
        shift_grad_ref[...] = jnp.sum(grad_norm, axis=0, keepdims=True)
        grad_unit = grad_norm * gain_ref[...]
        mean = jnp.mean(grad_unit, axis=1, keepdims=True)
        slant = jnp.mean(grad_unit * unit, axis=1, keepdims=True)
        out_ref[...] = gx_ref[...] + scale * (grad_unit - mean - unit * slant)


def finish(grads, weights, inputs, gx, gain):
    rows, width = inputs.shape
    group, lanes = grads.shape[0], grads.shape[2] // 3
    if lanes % 128:
        grads = grads.reshape(group, rows, 3, lanes).transpose(2, 0, 1, 3)
        grads = grads.reshape(3 * group, rows, lanes)
        grad_spec = pl.BlockSpec((group, rows, lanes), lambda k: (k, 0, 0))
    else:
        grad_spec = pl.BlockSpec((group, rows, lanes), lambda k: (0, 0, k))
    if weights.ndim == 3:
        share = width // weights.shape[0]
        first = weights.shape[1] // share - 3
        weight_spec = pl.BlockSpec((weights.shape[0], share, width), lambda k: (0, first + k, 0))
    else:
        weight_spec = pl.BlockSpec((width, width), lambda k: (0, k))
    fixed = lambda *shape: pl.BlockSpec(shape, lambda k: (0, 0))
    vector = jax.ShapeDtypeStruct((1, width), jnp.float32)
    return pl.pallas_call(
        finish_kernel,
        grid=(3,),
        in_specs=[
            grad_spec,
            weight_spec,
            fixed(rows, width),
            fixed(rows, width),
            fixed(1, width),
        ],
        out_specs=[
            fixed(rows, width),
            fixed(1, width),
            fixed(1, width),
            pl.BlockSpec((1, 1, width), lambda k: (k, 0, 0)),
        ],
        out_shape=(
            jax.ShapeDtypeStruct((rows, width), jnp.float32),
            vector,
            vector,
            jax.ShapeDtypeStruct((3, 1, width), jnp.float32),
        ),
        scratch_shapes=[pltpu.VMEM((rows, width), jnp.float32)],
        compiler_params=pltpu.CompilerParams(vmem_limit_bytes=VMEM_BYTES),
        cost_estimate=pl.CostEstimate(
            flops=rows * width * width * 6, bytes_accessed=width * width * 16, transcendentals=0
        ),
        name="finish_input",
    )(grads, weights, inputs, gx, gain[None])


def swap_cores(value):
    return lax.ppermute(value, "core", [(0, 1), (1, 0)])


def line_pieces(value, axis):
    size = lax.axis_size(axis)
    if size == 2:
        other = lax.ppermute(value, axis, [(0, 1), (1, 0)])
        return [(None, other)]
    pieces = []
    for sign in (-1, 1):
        moving = value
        for step in range(1, size):
            pairs = [(i, i - sign) for i in range(size) if 0 <= i - sign < size]
            pairs = [(i, j) for i, j in pairs if 0 <= i + sign * (step - 1) < size]
            moving = lax.ppermute(moving, axis, pairs)
            pieces.append((sign * step, moving))
    return pieces


def line_order(value, pieces, axis):
    place = lax.axis_index(axis)
    size = lax.axis_size(axis)
    if size == 2:
        other = pieces[0][1]
        return jnp.where(place == 0, jnp.stack([value, other]), jnp.stack([other, value]))
    whole = jnp.zeros((size, *value.shape), value.dtype)
    for distance, piece in sorted(pieces, key=lambda item: -abs(item[0])) + [(0, value)]:
        slot = jnp.clip(place + distance, 0, size - 1)
        whole = lax.dynamic_update_index_in_dim(whole, piece, slot, 0)
    return whole


def gather_line(value, axis):
    return line_order(value, line_pieces(value, axis), axis)


def rounded_sum(*terms):
    return sum(term.astype(jnp.float32) for term in terms).astype(jnp.bfloat16)


def scatter_terms(value, axis, dim):
    if lax.axis_size(axis) != 2:
        return (scatter_line(value, axis, dim),)
    place = lax.axis_index(axis)
    pick = lambda slot: lax.dynamic_index_in_dim(value, slot, dim, keepdims=False)
    return (pick(place), lax.ppermute(pick(1 - place), axis, [(0, 1), (1, 0)]))


def scatter_step(value, axis, moving, step):
    place = lax.axis_index(axis)
    size = lax.axis_size(axis)
    sums = []
    for n, sign in enumerate((-1, 1)):
        start = 0 if sign < 0 else size - 1
        pairs = [(i, i - sign) for i in range(size) if 0 <= i - sign < size]
        pairs = [(i, j) for i, j in pairs if abs(i - start) <= step - 1]
        slot = jnp.clip(place - sign * (size - step), 0, size - 1)
        own = lax.dynamic_index_in_dim(value, slot, 0, keepdims=False)
        payload = own if moving is None else rounded_sum(own, moving[n])
        sums.append(lax.ppermute(payload, axis, pairs))
    return tuple(sums)


def scatter_line(value, axis, dim):
    place = lax.axis_index(axis)
    size = lax.axis_size(axis)
    pick = lambda slot: lax.dynamic_index_in_dim(
        value, jnp.clip(slot, 0, size - 1), dim, keepdims=False
    )
    if size == 2:
        return rounded_sum(pick(place), lax.ppermute(pick(1 - place), axis, [(0, 1), (1, 0)]))
    sums = []
    for sign in (-1, 1):
        moving = None
        for step in range(1, size):
            start = 0 if sign < 0 else size - 1
            pairs = [(i, i - sign) for i in range(size) if 0 <= i - sign < size]
            pairs = [(i, j) for i, j in pairs if abs(i - start) <= step - 1]
            own = pick(place - sign * (size - step))
            payload = own if moving is None else rounded_sum(own, moving)
            moving = lax.ppermute(payload, axis, pairs)
        sums.append(moving)
    return rounded_sum(pick(place), *sums)


def on_device(
    tokens,
    cotangent,
    segment_ids,
    valid,
    project_in,
    project_out,
    hidden_up,
    hidden_down,
    gains_biases,
    moment_in,
    moment_out,
    moment_up,
    moment_down,
    moment_gains,
    square_in,
    square_out,
    square_up,
    square_down,
    square_gains,
):
    rows = tokens.shape[0]
    width = tokens.shape[1]
    everyone = ("outer", "inner", "line", "core")
    planes = ("outer", "inner")
    seq = ("line", "core")
    streams, line = lax.axis_size(planes), lax.axis_size("line")
    group = 2 * line
    count = streams * group
    chips = streams * line
    share = width // count
    lanes = width // group
    length = rows * group
    images = length // IMG_LEN
    core = lax.axis_index("core")
    first_core = core == 0

    def in_order(own, other, axis):
        return jnp.concatenate(
            [jnp.where(first_core, own, other), jnp.where(first_core, other, own)], axis=axis
        )

    half = FF // 2
    unit_block = FF // count
    folds = half // width
    up_end = 2 * share * folds
    low = lambda value: value.astype(jnp.bfloat16)
    direct = share % 16 == 0 and unit_block == 128
    position = lax.broadcasted_iota(jnp.int32, (images, rows), 1)
    found = (segment_ids[None, :] == lax.broadcasted_iota(jnp.int32, (images, rows), 0)) & (
        valid[None, :] == 1
    )
    first = jnp.min(jnp.where(found, position, rows), axis=1)
    small = jnp.concatenate([low(gains_biases).reshape(-1), low(first // 32), low(first % 32)])
    fold = lambda value: low(value).reshape(share, -1, width).swapaxes(0, 1).reshape(-1, width)
    if direct:
        small = jnp.pad(small, (0, 16 * width - small.shape[0])).reshape(16, width)
        whole_in = lax.all_gather(
            jnp.concatenate([fold(project_in), small], axis=0), everyone, axis=0, tiled=False
        )
        small = whole_in[:, 3 * share]
    else:
        whole_in = lax.all_gather(low(project_in), everyone, axis=0, tiled=True)
        small = lax.all_gather(small, everyone, axis=0, tiled=False)
    vector_size = gains_biases.size
    vectors = small[:, :vector_size].reshape(count, -1, share).transpose(1, 0, 2)
    vectors = vectors.reshape(-1, width).astype(jnp.float32)
    first = small[:, vector_size : vector_size + 2 * images].astype(jnp.int32)
    first = first[:, :images] * 32 + first[:, images:]
    first = lax.dynamic_slice_in_dim(first, lax.axis_index(planes) * group, group, 0)
    offsets = lax.broadcasted_iota(jnp.int32, (group, images), 0) * rows
    starts = jnp.min(jnp.where(first < rows, first + offsets, length), axis=0)

    pieces = line_pieces(tokens, "line")
    if direct:
        packed = jnp.concatenate([fold(hidden_up), low(hidden_down), low(project_out)], axis=0)
        packed, pieces_in = lax.optimization_barrier((packed, tuple(piece for _, piece in pieces)))
        pieces = [(distance, piece) for (distance, _), piece in zip(pieces, pieces_in)]
        gathered = lax.all_gather(packed, everyone, axis=0, tiled=False)
        whole_out = gathered[:, packed.shape[0] - share :].reshape(width, width)
        mlp_weights = (gathered,)
    own_tokens = line_order(tokens, pieces, "line").reshape(-1, width)
    swapped = [(distance, swap_cores(piece)) for distance, piece in pieces]
    other_tokens = line_order(swap_cores(tokens), swapped, "line").reshape(-1, width)

    gain_one, shift_one, bias_query, bias_value, bias_out = (
        vectors[0],
        vectors[1],
        vectors[2],
        vectors[3],
        vectors[4],
    )
    scale_one, gain_two, shift_two, bias_down, scale_two = (
        vectors[5],
        vectors[6],
        vectors[7],
        vectors[8],
        vectors[9],
    )
    bias_up = lax.dynamic_index_in_dim(
        vectors[10:].reshape(chips, 2, unit_block), core, axis=1, keepdims=False
    ).reshape(half)
    column = lax.axis_index(seq) * lanes
    bias_in = jnp.concatenate(
        [
            lax.dynamic_slice_in_dim(bias_query, column, lanes, 0),
            jnp.zeros((lanes,), jnp.float32),
            lax.dynamic_slice_in_dim(bias_value, column, lanes, 0),
        ]
    )
    grad_rows = cotangent.astype(jnp.float32) * valid.astype(jnp.float32)[:, None]
    grad_branch = (scale_two * grad_rows).astype(jnp.bfloat16)

    place = lax.axis_index(seq)
    if direct:
        mine_in = whole_in
    else:
        mine_in = lax.dynamic_index_in_dim(
            whole_in.reshape(width, 3, group, lanes), place, axis=2, keepdims=False
        ).reshape(width, 3 * lanes)
    normed_one, query, keys, values = norm_mix(
        place.reshape(1), own_tokens, other_tokens, rows, gain_one, shift_one, mine_in, bias_in
    )
    wide, attended, logs = attend(starts, query, keys, values)
    if not direct:
        whole_out, whole_up, whole_down = (
            lax.all_gather(low(value), everyone, axis=0, tiled=True)
            for value in (project_out, hidden_up, hidden_down)
        )
        block = jnp.arange(half) // unit_block * 2 + core
        index = block * unit_block + lax.rem(jnp.arange(half), unit_block)
        mlp_weights = (jnp.take(whole_up, index, axis=1), jnp.take(whole_down, index, axis=0))
    returned = lax.all_to_all(
        attended.reshape(group, rows, lanes), seq, split_axis=0, concat_axis=0, tiled=True
    )
    attended_rows = returned.transpose(1, 0, 2).reshape(rows, width)
    inputs = tokens.astype(jnp.float32)
    projected = plain_product(attended_rows, whole_out) + bias_out
    second = inputs + scale_one * projected
    norm_two, norm_two_back = jax.vjp(layer_norm, second, gain_two, shift_two)
    normed_two = norm_two.astype(jnp.bfloat16)
    grad_up, grad_down, branch, branch_other, grad_norm_two, grad_norm_other, grad_bias_up = mlp(
        core.reshape(1),
        normed_two,
        swap_cores(normed_two),
        grad_branch,
        swap_cores(grad_branch),
        mlp_weights,
        bias_up,
        chips,
    )
    grad_norm_two = grad_norm_two + swap_cores(grad_norm_other)
    branch = branch + swap_cores(branch_other) + bias_down
    block_output = (second + scale_two * branch).astype(jnp.bfloat16)
    grad_scale_two = jnp.sum(grad_rows * branch, axis=0)
    grad_bias_down = jnp.sum(grad_branch.astype(jnp.float32), axis=0)
    second_part, grad_gain_two, grad_shift_two = norm_two_back(grad_norm_two)
    grad_second = grad_rows + second_part
    grad_scale_one = jnp.sum(grad_second * projected, axis=0)
    grad_projected = (scale_one * grad_second).astype(jnp.bfloat16)
    grad_bias_out = jnp.sum(grad_projected.astype(jnp.float32), axis=0)
    grad_attended = inner_cols(grad_projected, whole_out).astype(jnp.bfloat16)
    grad_stream = lax.all_to_all(
        grad_attended.reshape(rows, group, lanes).transpose(1, 0, 2),
        seq,
        split_axis=0,
        concat_axis=0,
        tiled=True,
    ).reshape(length, lanes)
    grad_out = inner_rows(attended_rows, grad_projected).astype(jnp.bfloat16)
    grad_out = grad_out.reshape(chips, 2 * share, width)
    outer, inner = lax.axis_size("outer"), lax.axis_size("inner")
    grad_up, grad_out, grad_down = (
        value.reshape(outer, inner, line, -1, width) for value in (grad_up, grad_out, grad_down)
    )
    begun = (
        scatter_terms(grad_up, "inner", 1),
        scatter_terms(grad_out, "inner", 1),
        scatter_terms(grad_down, "outer", 0),
    )
    out_terms, grad_stream = lax.optimization_barrier((begun[1], grad_stream))
    begun = (begun[0], out_terms, begun[2])
    grad_mixed_stream = attend_back(starts, query, keys, values, wide, logs, grad_stream)
    grad_mixed = lax.all_to_all(
        grad_mixed_stream.reshape(group, rows, 3 * lanes), seq, split_axis=0, concat_axis=0, tiled=True
    )
    begun, grad_mixed_stream = lax.optimization_barrier((begun, grad_mixed_stream))
    grad_up, grad_out, grad_down = (rounded_sum(*terms) for terms in begun)
    grad_down = scatter_line(grad_down, "inner", 0)
    grad_up = scatter_line(jnp.concatenate([grad_up, grad_out], axis=2), "outer", 0)
    plane_sums = jnp.concatenate([grad_up, grad_down], axis=1)
    moving = scatter_step(plane_sums, "line", None, 1)
    moving, grad_mixed = lax.optimization_barrier((moving, grad_mixed))
    grad_in = inner_rows(normed_one, grad_mixed_stream).astype(jnp.bfloat16)
    parts = grad_in.reshape(outer, inner, group * share, 3 * lanes)
    parts = scatter_line(scatter_line(parts, "inner", 1), "outer", 0)
    input_grad, grad_gain_one, grad_shift_one, mixed_sums = finish(
        grad_mixed, whole_in, tokens, grad_second, gain_one
    )
    for step in range(2, line):
        moving = scatter_step(plane_sums, "line", moving, step)
        if step == 2:
            moving, parts, grad_gain_one = lax.optimization_barrier((moving, parts, grad_gain_one))
    summed = rounded_sum(
        lax.dynamic_index_in_dim(plane_sums, lax.axis_index("line"), 0, keepdims=False), *moving
    )
    parts = parts.reshape(group, share, 3 * lanes)
    parts = lax.all_to_all(parts, seq, split_axis=0, concat_axis=0, tiled=True)
    parts = parts.astype(jnp.float32)
    summed_in = parts.reshape(group, share, 3, lanes).transpose(1, 2, 0, 3).reshape(share, 3 * width)
    up_sums = grad_bias_up.reshape(chips, unit_block)
    up_sums = jnp.where(
        (lax.broadcasted_iota(jnp.int32, (1, 2, 1), 1) == core), up_sums[:, None, :], 0.0
    )
    grad_small = jnp.concatenate(
        [
            jnp.stack(
                [
                    grad_gain_one[0],
                    grad_shift_one[0],
                    mixed_sums[0, 0],
                    mixed_sums[2, 0],
                    grad_bias_out,
                    grad_scale_one,
                    grad_gain_two,
                    grad_shift_two,
                    grad_bias_down,
                    grad_scale_two,
                ]
            ),
            up_sums.reshape(-1, width),
        ],
        axis=0,
    )
    small_rows = grad_small.shape[0]
    parts = grad_small.reshape(small_rows, count, share).transpose(1, 0, 2)
    parts = lax.all_to_all(
        parts.reshape(count, small_rows * share), everyone, split_axis=0, concat_axis=0, tiled=True
    )
    summed_gains = jnp.sum(parts, axis=0).reshape(small_rows, share)

    up_sum = summed[:up_end].reshape(folds, 2, share, width)
    out_sum = summed[up_end : up_end + 2 * share].reshape(1, 2, share, width)
    both_sums = jnp.concatenate([up_sum, out_sum], axis=0)
    own_sums = jnp.where(first_core, both_sums[:, 0], both_sums[:, 1])
    other_sums = swap_cores(jnp.where(first_core, both_sums[:, 1], both_sums[:, 0]))
    summed_down = summed[up_end + 2 * share :].astype(jnp.float32)
    summed_out = own_sums[folds].astype(jnp.float32) + other_sums[folds].astype(jnp.float32)
    own_up = own_sums[:folds].transpose(1, 0, 2).reshape(share, chips, 1, unit_block)
    other_up = other_sums[:folds].transpose(1, 0, 2).reshape(share, chips, 1, unit_block)
    summed_up = in_order(own_up, other_up, 2).reshape(share, FF).astype(jnp.float32)
    rate_out = max(1, 4 * D // IMG_LEN) ** (-0.5)
    new_in, new_moment_in, new_square_in = adamw(
        project_in, moment_in, square_in, summed_in, D ** (-0.5), 0.04
    )
    new_out, new_moment_out, new_square_out = adamw(
        project_out, moment_out, square_out, summed_out, rate_out, 0.04
    )
    new_up, new_moment_up, new_square_up = adamw(
        hidden_up, moment_up, square_up, summed_up, D ** (-0.5), 0.04
    )
    new_down, new_moment_down, new_square_down = adamw(
        hidden_down, moment_down, square_down, summed_down, FF ** (-0.5), 0.04
    )
    new_gains, new_moment_gains, new_square_gains = adamw(
        gains_biases, moment_gains, square_gains, summed_gains, 0.2, 0.0
    )
    return (
        block_output,
        input_grad,
        new_in,
        new_out,
        new_up,
        new_down,
        new_gains,
        new_moment_in,
        new_moment_out,
        new_moment_up,
        new_moment_down,
        new_moment_gains,
        new_square_in,
        new_square_out,
        new_square_up,
        new_square_down,
        new_square_gains,
        summed_gains[8],
    )


def solution(mesh):
    streams, group = mesh.shape["fsdp"], mesh.shape["seq"]
    outer = math.isqrt(streams)
    fine = jax.sharding.Mesh(
        mesh.devices.reshape(outer, streams // outer, group // 2, 2),
        ("outer", "inner", "line", "core"),
    )
    return jax.shard_map(
        on_device,
        mesh=fine,
        in_specs=(
            P(("outer", "inner", "line", "core"), None),
            P(("outer", "inner", "line", "core"), None),
            P(("outer", "inner", "line", "core")),
            P(("outer", "inner", "line", "core")),
            P(("outer", "inner", "line", "core"), None),
            P(("outer", "inner", "line", "core"), None),
            P(("outer", "inner", "line", "core"), None),
            P(("outer", "inner", "line", "core"), None),
            P(None, ("outer", "inner", "line", "core")),
            P(("outer", "inner", "line", "core"), None),
            P(("outer", "inner", "line", "core"), None),
            P(("outer", "inner", "line", "core"), None),
            P(("outer", "inner", "line", "core"), None),
            P(None, ("outer", "inner", "line", "core")),
            P(("outer", "inner", "line", "core"), None),
            P(("outer", "inner", "line", "core"), None),
            P(("outer", "inner", "line", "core"), None),
            P(("outer", "inner", "line", "core"), None),
            P(None, ("outer", "inner", "line", "core")),
        ),
        out_specs=(
            P(("outer", "inner", "line", "core"), None),
            P(("outer", "inner", "line", "core"), None),
            P(("outer", "inner", "line", "core"), None),
            P(("outer", "inner", "line", "core"), None),
            P(("outer", "inner", "line", "core"), None),
            P(("outer", "inner", "line", "core"), None),
            P(None, ("outer", "inner", "line", "core")),
            P(("outer", "inner", "line", "core"), None),
            P(("outer", "inner", "line", "core"), None),
            P(("outer", "inner", "line", "core"), None),
            P(("outer", "inner", "line", "core"), None),
            P(None, ("outer", "inner", "line", "core")),
            P(("outer", "inner", "line", "core"), None),
            P(("outer", "inner", "line", "core"), None),
            P(("outer", "inner", "line", "core"), None),
            P(("outer", "inner", "line", "core"), None),
            P(None, ("outer", "inner", "line", "core")),
            P(("outer", "inner", "line", "core")),
        ),
        check_vma=False,
    )
```

```python
import functools
import math

import jax
import jax.numpy as jnp
from jax import lax
from jax.experimental import pallas as pl
from jax.experimental.pallas import tpu as pltpu
from jax.sharding import PartitionSpec as P

D = 1024
FF = 4096
HEADS = 16
HEAD_DIM = 64
IMG_LEN = 1370
WINDOW = 1408
TILE = 352
VMEM_BYTES = 56 * 1024 * 1024
STEP = 10


masked_score = -1e30


def layer_norm(values, gain, shift):
    average = jnp.mean(values, axis=-1, keepdims=True)
    centered = values - average
    variance = jnp.mean(centered * centered, axis=-1, keepdims=True)
    return centered * lax.rsqrt(variance + 1e-06) * gain + shift


def exact_gelu(values):
    return jax.nn.gelu(values, approximate=False)


def plain_product(left, right):
    return jnp.dot(left, right, preferred_element_type=jnp.float32)


def inner_rows(left, right):
    return lax.dot_general(
        left, right, (((0,), (0,)), ((), ())), preferred_element_type=jnp.float32
    )


def inner_cols(left, right):
    return lax.dot_general(
        left, right, (((1,), (1,)), ((), ())), preferred_element_type=jnp.float32
    )


def adamw(param, moment, square, grad, rate, decay):
    new_moment = 0.9 * moment + 0.1 * grad
    new_square = 0.999 * square + 0.001 * grad * grad
    corrected = new_moment / (1.0 - 0.9**STEP)
    scaled = jnp.sqrt(new_square / (1.0 - 0.999**STEP)) + 1e-08
    return (param - rate * (corrected / scaled + decay * param), new_moment, new_square)


def head_lanes(shape):
    return lax.broadcasted_iota(jnp.int32, shape, 1) // HEAD_DIM


def window_of(starts_ref, image, length):
    start = starts_ref[image]
    base = jnp.clip(start // 16 * 16, 0, length - WINDOW)
    return (pl.multiple_of(base, 16), start - base)


def image_mask(position, offset):
    return (position >= offset) & (position < offset + IMG_LEN)


def attend_kernel(starts_ref, q_ref, k_ref, v_ref, wide_ref, out_ref, log_ref):
    image, tile = pl.program_id(0), pl.program_id(1)
    length, lanes = q_ref.shape
    base, offset = window_of(starts_ref, image, length)
    rows = pl.ds(pl.multiple_of(base + tile * TILE, 16), TILE)

    @pl.when((image == 0) & (tile == 0))
    def clear():
        wide_ref[...] = jnp.zeros_like(wide_ref)
        out_ref[...] = jnp.zeros_like(out_ref)
        log_ref[...] = jnp.zeros_like(log_ref)

    query = q_ref[rows, :].astype(jnp.float32) * HEAD_DIM ** (-0.5)
    keys = k_ref[pl.ds(base, WINDOW), :]
    values = v_ref[pl.ds(base, WINDOW), :]
    key_ok = image_mask(lax.broadcasted_iota(jnp.int32, (1, WINDOW), 1), offset)
    bias = jnp.where(key_ok, 0.0, masked_score)
    row_ok = image_mask(lax.broadcasted_iota(jnp.int32, (TILE, 1), 0) + tile * TILE, offset)
    head_of = head_lanes((TILE, lanes))
    total_out = jnp.zeros((TILE, lanes), jnp.float32)
    total_log = jnp.zeros((TILE, lanes), jnp.float32)
    for head in range(lanes // HEAD_DIM):
        mine = head_of == head
        part = jnp.where(mine, query, 0.0).astype(jnp.bfloat16)
        scores = inner_cols(part, keys) + bias
        top = jnp.max(scores, axis=1, keepdims=True)
        weights = jnp.exp(scores - top)
        total = jnp.sum(weights, axis=1, keepdims=True)
        probs = (weights * (1.0 / total)).astype(jnp.bfloat16)
        total_out = jnp.where(mine, plain_product(probs, values), total_out)
        total_log = jnp.where(mine, top + jnp.log(total), total_log)
    merged = jnp.where(row_ok, total_out, wide_ref[rows, :])
    wide_ref[rows, :] = merged
    out_ref[rows, :] = merged.astype(jnp.bfloat16)
    log_ref[rows, :] = jnp.where(row_ok, total_log, log_ref[rows, :])


def attend(starts, query, keys, values):
    length, lanes = query.shape
    whole = pl.BlockSpec((length, lanes), lambda image, tile, starts: (0, 0))
    wide = jax.ShapeDtypeStruct((length, lanes), jnp.float32)
    images = length // IMG_LEN
    return pl.pallas_call(
        attend_kernel,
        grid_spec=pltpu.PrefetchScalarGridSpec(
            num_scalar_prefetch=1,
            grid=(images, WINDOW // TILE),
            in_specs=[whole] * 3,
            out_specs=[whole] * 3,
        ),
        out_shape=(wide, jax.ShapeDtypeStruct((length, lanes), jnp.bfloat16), wide),
        compiler_params=pltpu.CompilerParams(
            vmem_limit_bytes=VMEM_BYTES, dimension_semantics=("arbitrary", "arbitrary")
        ),
        cost_estimate=pl.CostEstimate(
            flops=images * WINDOW * WINDOW * lanes * 8,
            bytes_accessed=length * lanes * 16,
            transcendentals=images * WINDOW * WINDOW * lanes // HEAD_DIM,
        ),
        name="attend_forward",
    )(starts, query, keys, values)


def attend_back_kernel(
    starts_ref, q_ref, k_ref, v_ref, wide_ref, log_ref, go_ref, grad_ref, key_acc, value_acc
):
    image, tile = pl.program_id(0), pl.program_id(1)
    length, lanes = q_ref.shape
    base, offset = window_of(starts_ref, image, length)
    rows = pl.ds(pl.multiple_of(base + tile * TILE, 16), TILE)
    window = pl.ds(base, WINDOW)

    @pl.when((image == 0) & (tile == 0))
    def clear():
        grad_ref[...] = jnp.zeros_like(grad_ref)

    @pl.when(tile == 0)
    def clear_sums():
        key_acc[...] = jnp.zeros_like(key_acc)
        value_acc[...] = jnp.zeros_like(value_acc)

    query = q_ref[rows, :].astype(jnp.float32) * HEAD_DIM ** (-0.5)
    keys = k_ref[window, :]
    values = v_ref[window, :]
    key_ok = image_mask(lax.broadcasted_iota(jnp.int32, (1, WINDOW), 1), offset)
    bias = jnp.where(key_ok, 0.0, masked_score)
    row_ok = image_mask(lax.broadcasted_iota(jnp.int32, (TILE, 1), 0) + tile * TILE, offset)
    head_of = head_lanes((TILE, lanes))
    grad_out = jnp.where(row_ok, go_ref[rows, :].astype(jnp.float32), 0.0)
    centre_parts = grad_out * wide_ref[rows, :]
    logs = jnp.where(row_ok, log_ref[rows, :], -masked_score)
    query_grad = jnp.zeros((TILE, lanes), jnp.float32)
    for head in range(lanes // HEAD_DIM):
        mine = head_of == head
        part = jnp.where(mine, query, 0.0).astype(jnp.bfloat16)
        grad_part = jnp.where(mine, grad_out, 0.0).astype(jnp.bfloat16)
        centre = jnp.sum(jnp.where(mine, centre_parts, 0.0), axis=1, keepdims=True)
        log_total = jnp.max(jnp.where(mine, logs, masked_score), axis=1, keepdims=True)
        probs = jnp.exp(inner_cols(part, keys) + bias - log_total)
        grad_probs = inner_cols(grad_part, values)
        grad_scores = (probs * (grad_probs - centre)).astype(jnp.bfloat16)
        query_grad = jnp.where(mine, plain_product(grad_scores, keys), query_grad)
        key_acc[...] += inner_rows(part, grad_scores)
        value_acc[...] += inner_rows(grad_part, probs.astype(jnp.bfloat16))
    old = grad_ref[rows, 0:lanes].astype(jnp.float32)
    merged = jnp.where(row_ok, query_grad * HEAD_DIM ** (-0.5), old)
    grad_ref[rows, 0:lanes] = merged.astype(jnp.bfloat16)

    @pl.when(tile == pl.num_programs(1) - 1)
    def flush():
        inside = image_mask(lax.broadcasted_iota(jnp.int32, (WINDOW, 1), 0), offset)
        for slot, sums in ((1, key_acc), (2, value_acc)):
            columns = slice(slot * lanes, (slot + 1) * lanes)
            old = grad_ref[window, columns].astype(jnp.float32)
            merged = jnp.where(inside, sums[...].T, old)
            grad_ref[window, columns] = merged.astype(jnp.bfloat16)


def attend_back(starts, query, keys, values, wide, logs, grad_out):
    length, lanes = query.shape
    whole = pl.BlockSpec((length, lanes), lambda image, tile, starts: (0, 0))
    images = length // IMG_LEN
    return pl.pallas_call(
        attend_back_kernel,
        grid_spec=pltpu.PrefetchScalarGridSpec(
            num_scalar_prefetch=1,
            grid=(images, WINDOW // TILE),
            in_specs=[whole] * 6,
            out_specs=pl.BlockSpec((length, 3 * lanes), lambda image, tile, starts: (0, 0)),
            scratch_shapes=[pltpu.VMEM((lanes, WINDOW), jnp.float32)] * 2,
        ),
        out_shape=jax.ShapeDtypeStruct((length, 3 * lanes), jnp.bfloat16),
        compiler_params=pltpu.CompilerParams(
            vmem_limit_bytes=VMEM_BYTES, dimension_semantics=("arbitrary", "arbitrary")
        ),
        cost_estimate=pl.CostEstimate(
            flops=images * WINDOW * WINDOW * lanes * 20,
            bytes_accessed=length * lanes * 22,
            transcendentals=images * WINDOW * WINDOW * lanes // HEAD_DIM,
        ),
        name="attend_backward",
    )(starts, query, keys, values, wide, logs, grad_out)


def norm_mix_kernel(pieces, place_ref, own_ref, other_ref, gain_ref, shift_ref, bias_ref, *refs):
    weight = jnp.concatenate(
        [ref[...].reshape(own_ref.shape[1], -1) for ref in refs[:pieces]], axis=1
    )
    a_ref, q_ref, k_ref, v_ref = refs[pieces:]
    lanes = q_ref.shape[1]
    mine = lax.rem(pl.program_id(0), 2) == lax.rem(place_ref[0], 2)
    own, other = own_ref[...].astype(jnp.float32), other_ref[...].astype(jnp.float32)
    normed = layer_norm(jnp.where(mine, own, other), gain_ref[...], shift_ref[...])
    normed = normed.astype(jnp.bfloat16)
    a_ref[...] = normed
    mixed = (plain_product(normed, weight) + bias_ref[...]).astype(jnp.bfloat16)
    q_ref[...] = mixed[:, :lanes]
    k_ref[...] = mixed[:, lanes : 2 * lanes]
    v_ref[...] = mixed[:, 2 * lanes :]


def norm_mix(place, own, other, block, gain, shift, weight, bias):
    length, width = own.shape[0] * 2, own.shape[1]
    lanes = bias.shape[0] // 3
    row = lambda size: pl.BlockSpec((block, size), lambda i, place: (i, 0))
    half = pl.BlockSpec((block, width), lambda i, place: (i // 2, 0))
    fixed = lambda *shape: pl.BlockSpec(shape, lambda i, place: (0, 0))
    part = jax.ShapeDtypeStruct((length, lanes), jnp.bfloat16)
    weights, weight_specs = [weight], [fixed(width, 3 * lanes)]
    return pl.pallas_call(
        functools.partial(norm_mix_kernel, len(weights)),
        grid_spec=pltpu.PrefetchScalarGridSpec(
            num_scalar_prefetch=1,
            grid=(length // block,),
            in_specs=[
                half,
                half,
                fixed(1, width),
                fixed(1, width),
                fixed(1, 3 * lanes),
                *weight_specs,
            ],
            out_specs=[row(width), row(lanes), row(lanes), row(lanes)],
        ),
        out_shape=(jax.ShapeDtypeStruct((length, width), jnp.bfloat16), part, part, part),
        compiler_params=pltpu.CompilerParams(vmem_limit_bytes=VMEM_BYTES),
        cost_estimate=pl.CostEstimate(
            flops=length * width * lanes * 6, bytes_accessed=length * width * 4, transcendentals=0
        ),
        name="norm_mix",
    )(place, own, other, gain[None], shift[None], bias[None], *weights)


def mlp_kernel(pieces, core_ref, own_ref, other_ref, gm_own_ref, gm_other_ref, bias_ref, *refs):
    up_refs, down_refs = refs[:pieces], refs[pieces : 2 * pieces]
    up_grad_ref, down_grad_ref, m_own_ref, m_other_ref, gh_own_ref, gh_other_ref = refs[
        2 * pieces : 2 * pieces + 6
    ]
    bias_grad_ref, h_ref, gm_ref, turned_ref = refs[2 * pieces + 6 :]
    tile = pl.program_id(0)
    rows, width = own_ref.shape
    chips = up_grad_ref.shape[0]
    up_rows = width // chips
    units = bias_ref.shape[1]
    folds = width // units

    @pl.when(tile == 0)
    def clear():
        for ref in (m_own_ref, m_other_ref, gh_own_ref, gh_other_ref):
            ref[...] = jnp.zeros_like(ref)
        h_ref[:rows] = own_ref[...]
        h_ref[rows:] = other_ref[...]
        gm_ref[:rows] = gm_own_ref[...]
        gm_ref[rows:] = gm_other_ref[...]
        turned_ref[...] = h_ref[...].T

    weight_up = jnp.concatenate([ref[...].reshape(width, -1) for ref in up_refs], axis=1)
    weight_down = jnp.concatenate([ref[...].reshape(-1, width) for ref in down_refs], axis=0)
    gm = gm_ref[...]
    upward = plain_product(h_ref[...], weight_up) + bias_ref[...]
    normal = 0.5 * (1.0 + lax.erf(upward * 0.5**0.5))
    slope = normal + upward * jnp.exp(upward * upward * -0.5) * (0.5 / jnp.pi) ** 0.5
    active = (upward * normal).astype(jnp.bfloat16)
    grad_up = (inner_cols(gm, weight_down) * slope).astype(jnp.bfloat16)
    bias_grad_ref[...] = jnp.sum(grad_up.astype(jnp.float32), axis=0, keepdims=True)
    branch = plain_product(active, weight_down)
    m_own_ref[...] += branch[:rows]
    m_other_ref[...] += branch[rows:]
    grad_norm = inner_cols(grad_up, weight_up)
    gh_own_ref[...] += grad_norm[:rows]
    gh_other_ref[...] += grad_norm[rows:]
    up_grad = plain_product(turned_ref[...], grad_up).astype(jnp.bfloat16)
    row = pl.multiple_of(tile // folds * up_rows, up_rows)
    column = pl.multiple_of(lax.rem(tile, folds) * units, units)
    up_grad = up_grad.reshape(chips, up_rows, units)
    up_grad_ref[:, pl.ds(row, up_rows), pl.ds(column, units)] = up_grad
    down_grad = inner_rows(active, gm).astype(jnp.bfloat16)
    down_grad_ref[...] = down_grad.reshape(down_grad_ref.shape)


def mlp(core, own, other, gm_own, gm_other, weights, bias, chips):
    rows, width = own.shape
    half = bias.shape[0]
    unit_block = half // chips
    units = 256
    folds = width // units
    once = dict(pipeline_mode=pl.Buffered(1))
    fixed = pl.BlockSpec((rows, width), lambda j, core: (0, 0), **once)
    if len(weights) == 1:
        count = 2 * chips
        share = width // count
        pieces = units // unit_block
        lane_blocks = width // unit_block

        def up_spec(piece):
            def place(j, core):
                block = 2 * (j * pieces + piece) + core[0]
                return (0, block // lane_blocks, lax.rem(block, lane_blocks))

            return pl.BlockSpec((count, share, unit_block), place)

        def down_spec(piece):
            return pl.BlockSpec(
                (1, unit_block, width), lambda j, core: (2 * (j * pieces + piece) + core[0], 1, 0)
            )

        weights = list(weights) * (2 * pieces)
        weight_specs = [up_spec(n) for n in range(pieces)] + [down_spec(n) for n in range(pieces)]
        up_shape, down_shape = (chips, half // chips, width), (chips, half // chips, width)
        down_grad_spec = pl.BlockSpec((pieces, unit_block, width), lambda j, core: (j, 0, 0))
    else:
        pieces = 1
        weight_specs = [
            pl.BlockSpec((width, units), lambda j, core: (0, j)),
            pl.BlockSpec((units, width), lambda j, core: (j, 0)),
        ]
        up_shape, down_shape = (1, half // width * width, width), (1, half, width)
        down_grad_spec = pl.BlockSpec((1, units, width), lambda j, core: (0, j, 0))
    total = jax.ShapeDtypeStruct((rows, width), jnp.float32)
    outs = pl.pallas_call(
        functools.partial(mlp_kernel, pieces),
        grid_spec=pltpu.PrefetchScalarGridSpec(
            num_scalar_prefetch=1,
            grid=(half // units,),
            in_specs=[fixed] * 4 + [pl.BlockSpec((1, units), lambda j, core: (0, j)), *weight_specs],
            out_specs=[
                pl.BlockSpec(up_shape, lambda j, core: (0, 0, 0), **once),
                down_grad_spec,
                *[fixed] * 4,
                pl.BlockSpec((1, units), lambda j, core: (0, j)),
            ],
            scratch_shapes=[
                pltpu.VMEM((2 * rows, width), jnp.bfloat16),
                pltpu.VMEM((2 * rows, width), jnp.bfloat16),
                pltpu.VMEM((width, 2 * rows), jnp.bfloat16),
            ],
        ),
        out_shape=(
            jax.ShapeDtypeStruct(up_shape, jnp.bfloat16),
            jax.ShapeDtypeStruct(down_shape, jnp.bfloat16),
            *[total] * 4,
            jax.ShapeDtypeStruct((1, half), jnp.float32),
        ),
        compiler_params=pltpu.CompilerParams(vmem_limit_bytes=VMEM_BYTES),
        cost_estimate=pl.CostEstimate(
            flops=2 * rows * width * half * 12,
            bytes_accessed=half * width * 8 + rows * width * 24,
            transcendentals=rows * half * 4,
        ),
        name="mlp_both_ways",
    )(core, own, other, gm_own, gm_other, bias[None], *weights)
    up_grad, down_grad = outs[0], outs[1]
    if pieces == 1:
        up_grad = up_grad.reshape(half // width, chips, width // chips, width).swapaxes(0, 1)
        up_grad = up_grad.reshape(chips, -1, width)
        down_grad = down_grad.reshape(chips, -1, width)
    return (up_grad, down_grad, *outs[2:])


def finish_kernel(
    grad_ref, weight_ref, x_ref, gx_ref, gain_ref, out_ref, gain_grad_ref, shift_grad_ref, sums_ref, acc_ref
):
    step = pl.program_id(0)
    parts = [grad_ref[slot] for slot in range(grad_ref.shape[0])]
    grad = jnp.concatenate(parts, axis=1)
    width = x_ref.shape[1]
    product = inner_cols(grad, weight_ref[...].reshape(width, width))
    sums_ref[...] = jnp.sum(grad.astype(jnp.float32), axis=0, keepdims=True)[None]

    @pl.when(step == 0)
    def begin():
        acc_ref[...] = product

    @pl.when(step > 0)
    def further():
        acc_ref[...] += product

    @pl.when(step == pl.num_programs(0) - 1)
    def end():
        values = x_ref[...].astype(jnp.float32)
        centered = values - jnp.mean(values, axis=1, keepdims=True)
        scale = lax.rsqrt(jnp.mean(centered * centered, axis=1, keepdims=True) + 1e-06)
        unit = centered * scale
        grad_norm = acc_ref[...]
        gain_grad_ref[...] = jnp.sum(grad_norm * unit, axis=0, keepdims=True)
        shift_grad_ref[...] = jnp.sum(grad_norm, axis=0, keepdims=True)
        grad_unit = grad_norm * gain_ref[...]
        mean = jnp.mean(grad_unit, axis=1, keepdims=True)
        slant = jnp.mean(grad_unit * unit, axis=1, keepdims=True)
        out_ref[...] = gx_ref[...] + scale * (grad_unit - mean - unit * slant)


def finish(grads, weights, inputs, gx, gain):
    rows, width = inputs.shape
    group, lanes = grads.shape[0], grads.shape[2] // 3
    if lanes % 128:
        grads = grads.reshape(group, rows, 3, lanes).transpose(2, 0, 1, 3)
        grads = grads.reshape(3 * group, rows, lanes)
        grad_spec = pl.BlockSpec((group, rows, lanes), lambda k: (k, 0, 0))
    else:
        grad_spec = pl.BlockSpec((group, rows, lanes), lambda k: (0, 0, k))
    if weights.ndim == 3:
        share = width // weights.shape[0]
        first = weights.shape[1] // share - 3
        weight_spec = pl.BlockSpec((weights.shape[0], share, width), lambda k: (0, first + k, 0))
    else:
        weight_spec = pl.BlockSpec((width, width), lambda k: (0, k))
    fixed = lambda *shape: pl.BlockSpec(shape, lambda k: (0, 0))
    vector = jax.ShapeDtypeStruct((1, width), jnp.float32)
    return pl.pallas_call(
        finish_kernel,
        grid=(3,),
        in_specs=[
            grad_spec,
            weight_spec,
            fixed(rows, width),
            fixed(rows, width),
            fixed(1, width),
        ],
        out_specs=[
            fixed(rows, width),
            fixed(1, width),
            fixed(1, width),
            pl.BlockSpec((1, 1, width), lambda k: (k, 0, 0)),
        ],
        out_shape=(
            jax.ShapeDtypeStruct((rows, width), jnp.float32),
            vector,
            vector,
            jax.ShapeDtypeStruct((3, 1, width), jnp.float32),
        ),
        scratch_shapes=[pltpu.VMEM((rows, width), jnp.float32)],
        compiler_params=pltpu.CompilerParams(vmem_limit_bytes=VMEM_BYTES),
        cost_estimate=pl.CostEstimate(
            flops=rows * width * width * 6, bytes_accessed=width * width * 16, transcendentals=0
        ),
        name="finish_input",
    )(grads, weights, inputs, gx, gain[None])


def swap_cores(value):
    return lax.ppermute(value, "core", [(0, 1), (1, 0)])


def line_pieces(value, axis):
    size = lax.axis_size(axis)
    if size == 2:
        other = lax.ppermute(value, axis, [(0, 1), (1, 0)])
        return [(None, other)]
    pieces = []
    for sign in (-1, 1):
        moving = value
        for step in range(1, size):
            pairs = [(i, i - sign) for i in range(size) if 0 <= i - sign < size]
            pairs = [(i, j) for i, j in pairs if 0 <= i + sign * (step - 1) < size]
            moving = lax.ppermute(moving, axis, pairs)
            pieces.append((sign * step, moving))
    return pieces


def line_order(value, pieces, axis):
    place = lax.axis_index(axis)
    size = lax.axis_size(axis)
    if size == 2:
        other = pieces[0][1]
        return jnp.where(place == 0, jnp.stack([value, other]), jnp.stack([other, value]))
    whole = jnp.zeros((size, *value.shape), value.dtype)
    for distance, piece in sorted(pieces, key=lambda item: -abs(item[0])) + [(0, value)]:
        slot = jnp.clip(place + distance, 0, size - 1)
        whole = lax.dynamic_update_index_in_dim(whole, piece, slot, 0)
    return whole


def gather_line(value, axis):
    return line_order(value, line_pieces(value, axis), axis)


def exchange_line(value, axis):
    place = lax.axis_index(axis)
    size = lax.axis_size(axis)
    pick = lambda slot: lax.dynamic_index_in_dim(
        value, jnp.clip(slot, 0, size - 1), 0, keepdims=False
    )
    pieces = []
    for distance in range(1, size):
        for move in (-distance, distance):
            pairs = [(i, i + move) for i in range(size) if 0 <= i + move < size]
            pieces.append((-move, lax.ppermute(pick(place + move), axis, pairs)))
    if size == 2:
        pieces = [(None, pieces[0][1] + pieces[1][1])]
    return line_order(pick(place), pieces, axis)


def rounded_sum(*terms):
    return sum(term.astype(jnp.float32) for term in terms).astype(jnp.bfloat16)


def scatter_terms(value, axis, dim):
    if lax.axis_size(axis) != 2:
        return (scatter_line(value, axis, dim),)
    place = lax.axis_index(axis)
    pick = lambda slot: lax.dynamic_index_in_dim(value, slot, dim, keepdims=False)
    return (pick(place), lax.ppermute(pick(1 - place), axis, [(0, 1), (1, 0)]))


def scatter_payload(value, axis, moving, step):
    place = lax.axis_index(axis)
    size = lax.axis_size(axis)
    payload = []
    for n, sign in enumerate((-1, 1)):
        slot = jnp.clip(place - sign * (size - step), 0, size - 1)
        own = lax.dynamic_index_in_dim(value, slot, 0, keepdims=False)
        payload.append(own if moving is None else rounded_sum(own, moving[n]))
    return tuple(payload)


def scatter_send(payload, axis, step):
    size = lax.axis_size(axis)
    sums = []
    for value, sign in zip(payload, (-1, 1)):
        start = 0 if sign < 0 else size - 1
        pairs = [(i, i - sign) for i in range(size) if 0 <= i - sign < size]
        pairs = [(i, j) for i, j in pairs if abs(i - start) <= step - 1]
        sums.append(lax.ppermute(value, axis, pairs))
    return tuple(sums)


def scatter_line(value, axis, dim):
    place = lax.axis_index(axis)
    size = lax.axis_size(axis)
    pick = lambda slot: lax.dynamic_index_in_dim(
        value, jnp.clip(slot, 0, size - 1), dim, keepdims=False
    )
    if size == 2:
        return rounded_sum(pick(place), lax.ppermute(pick(1 - place), axis, [(0, 1), (1, 0)]))
    sums = []
    for sign in (-1, 1):
        moving = None
        for step in range(1, size):
            start = 0 if sign < 0 else size - 1
            pairs = [(i, i - sign) for i in range(size) if 0 <= i - sign < size]
            pairs = [(i, j) for i, j in pairs if abs(i - start) <= step - 1]
            own = pick(place - sign * (size - step))
            payload = own if moving is None else rounded_sum(own, moving)
            moving = lax.ppermute(payload, axis, pairs)
        sums.append(moving)
    return rounded_sum(pick(place), *sums)


def on_device(
    tokens,
    cotangent,
    segment_ids,
    valid,
    project_in,
    project_out,
    hidden_up,
    hidden_down,
    gains_biases,
    moment_in,
    moment_out,
    moment_up,
    moment_down,
    moment_gains,
    square_in,
    square_out,
    square_up,
    square_down,
    square_gains,
):
    rows = tokens.shape[0]
    width = tokens.shape[1]
    everyone = ("outer", "inner", "line", "core")
    planes = ("outer", "inner")
    seq = ("line", "core")
    streams, line = lax.axis_size(planes), lax.axis_size("line")
    group = 2 * line
    count = streams * group
    chips = streams * line
    share = width // count
    lanes = width // group
    length = rows * group
    images = length // IMG_LEN
    core = lax.axis_index("core")
    first_core = core == 0

    def in_order(own, other, axis):
        return jnp.concatenate(
            [jnp.where(first_core, own, other), jnp.where(first_core, other, own)], axis=axis
        )

    half = FF // 2
    unit_block = FF // count
    folds = half // width
    up_end = 2 * share * folds
    low = lambda value: value.astype(jnp.bfloat16)
    direct = share % 16 == 0 and unit_block == 128
    position = lax.broadcasted_iota(jnp.int32, (images, rows), 1)
    found = (segment_ids[None, :] == lax.broadcasted_iota(jnp.int32, (images, rows), 0)) & (
        valid[None, :] == 1
    )
    first = jnp.min(jnp.where(found, position, rows), axis=1)
    small = jnp.concatenate([low(gains_biases).reshape(-1), low(first // 32), low(first % 32)])
    fold = lambda value: low(value).reshape(share, -1, width).swapaxes(0, 1).reshape(-1, width)
    if direct:
        extra = 16
        small = jnp.pad(small, (0, extra * 3 * lanes - small.shape[0]))
        small = jnp.broadcast_to(small.reshape(1, extra, 3 * lanes), (group, extra, 3 * lanes))
        owned = low(project_in).reshape(share, 3, group, lanes).transpose(2, 0, 1, 3)
        blocks = jnp.concatenate([owned.reshape(group, share, 3 * lanes), small], axis=1)
        blocks = blocks.reshape(line, 2, share + extra, 3 * lanes)
        keep = jnp.where(first_core, blocks[:, 0], blocks[:, 1])
        sent = swap_cores(jnp.where(first_core, blocks[:, 1], blocks[:, 0]))
        blocks = exchange_line(in_order(keep[:, None], sent[:, None], 1), "line")
        blocks = gather_line(gather_line(blocks, "inner"), "outer")
        blocks = blocks.reshape(count, share + extra, 3 * lanes)
        mine_in = blocks[:, :share].reshape(width, 3 * lanes)
        small = blocks[:, share:].reshape(count, -1)
    else:
        whole_in = lax.all_gather(low(project_in), everyone, axis=0, tiled=True)
        mine_in = lax.dynamic_index_in_dim(
            whole_in.reshape(width, 3, group, lanes), lax.axis_index(seq), axis=2, keepdims=False
        ).reshape(width, 3 * lanes)
        small = lax.all_gather(small, everyone, axis=0, tiled=False)
    vector_size = gains_biases.size
    vectors = small[:, :vector_size].reshape(count, -1, share).transpose(1, 0, 2)
    vectors = vectors.reshape(-1, width).astype(jnp.float32)
    first = small[:, vector_size : vector_size + 2 * images].astype(jnp.int32)
    first = first[:, :images] * 32 + first[:, images:]
    first = lax.dynamic_slice_in_dim(first, lax.axis_index(planes) * group, group, 0)
    offsets = lax.broadcasted_iota(jnp.int32, (group, images), 0) * rows
    starts = jnp.min(jnp.where(first < rows, first + offsets, length), axis=0)

    pieces = line_pieces(tokens, "line")
    if direct:
        packed = jnp.concatenate([fold(hidden_up), low(hidden_down), low(project_out)], axis=0)
        packed, pieces_in = lax.optimization_barrier((packed, tuple(piece for _, piece in pieces)))
        pieces = [(distance, piece) for (distance, _), piece in zip(pieces, pieces_in)]
        gathered = lax.all_gather(packed, everyone, axis=0, tiled=False)
        whole_out = gathered[:, packed.shape[0] - share :].reshape(width, width)
        mlp_weights = (gathered,)
        whole_in = lax.all_gather(fold(project_in), everyone, axis=0, tiled=False)
    own_tokens = line_order(tokens, pieces, "line").reshape(-1, width)
    swapped = [(distance, swap_cores(piece)) for distance, piece in pieces]
    other_tokens = line_order(swap_cores(tokens), swapped, "line").reshape(-1, width)

    gain_one, shift_one, bias_query, bias_value, bias_out = (
        vectors[0],
        vectors[1],
        vectors[2],
        vectors[3],
        vectors[4],
    )
    scale_one, gain_two, shift_two, bias_down, scale_two = (
        vectors[5],
        vectors[6],
        vectors[7],
        vectors[8],
        vectors[9],
    )
    bias_up = lax.dynamic_index_in_dim(
        vectors[10:].reshape(chips, 2, unit_block), core, axis=1, keepdims=False
    ).reshape(half)
    column = lax.axis_index(seq) * lanes
    bias_in = jnp.concatenate(
        [
            lax.dynamic_slice_in_dim(bias_query, column, lanes, 0),
            jnp.zeros((lanes,), jnp.float32),
            lax.dynamic_slice_in_dim(bias_value, column, lanes, 0),
        ]
    )
    grad_rows = cotangent.astype(jnp.float32) * valid.astype(jnp.float32)[:, None]
    grad_branch = (scale_two * grad_rows).astype(jnp.bfloat16)

    place = lax.axis_index(seq)
    normed_one, query, keys, values = norm_mix(
        place.reshape(1), own_tokens, other_tokens, rows, gain_one, shift_one, mine_in, bias_in
    )
    wide, attended, logs = attend(starts, query, keys, values)
    if not direct:
        whole_out, whole_up, whole_down = (
            lax.all_gather(low(value), everyone, axis=0, tiled=True)
            for value in (project_out, hidden_up, hidden_down)
        )
        block = jnp.arange(half) // unit_block * 2 + core
        index = block * unit_block + lax.rem(jnp.arange(half), unit_block)
        mlp_weights = (jnp.take(whole_up, index, axis=1), jnp.take(whole_down, index, axis=0))
    returned = lax.all_to_all(
        attended.reshape(group, rows, lanes), seq, split_axis=0, concat_axis=0, tiled=True
    )
    attended_rows = returned.transpose(1, 0, 2).reshape(rows, width)
    inputs = tokens.astype(jnp.float32)
    projected = plain_product(attended_rows, whole_out) + bias_out
    second = inputs + scale_one * projected
    norm_two, norm_two_back = jax.vjp(layer_norm, second, gain_two, shift_two)
    normed_two = norm_two.astype(jnp.bfloat16)
    grad_up, grad_down, branch, branch_other, grad_norm_two, grad_norm_other, grad_bias_up = mlp(
        core.reshape(1),
        normed_two,
        swap_cores(normed_two),
        grad_branch,
        swap_cores(grad_branch),
        mlp_weights,
        bias_up,
        chips,
    )
    grad_norm_two = grad_norm_two + swap_cores(grad_norm_other)
    branch = branch + swap_cores(branch_other) + bias_down
    block_output = (second + scale_two * branch).astype(jnp.bfloat16)
    grad_scale_two = jnp.sum(grad_rows * branch, axis=0)
    grad_bias_down = jnp.sum(grad_branch.astype(jnp.float32), axis=0)
    second_part, grad_gain_two, grad_shift_two = norm_two_back(grad_norm_two)
    grad_second = grad_rows + second_part
    grad_scale_one = jnp.sum(grad_second * projected, axis=0)
    grad_projected = (scale_one * grad_second).astype(jnp.bfloat16)
    grad_bias_out = jnp.sum(grad_projected.astype(jnp.float32), axis=0)
    grad_attended = inner_cols(grad_projected, whole_out).astype(jnp.bfloat16)
    grad_stream = lax.all_to_all(
        grad_attended.reshape(rows, group, lanes).transpose(1, 0, 2),
        seq,
        split_axis=0,
        concat_axis=0,
        tiled=True,
    ).reshape(length, lanes)
    grad_out = inner_rows(attended_rows, grad_projected).astype(jnp.bfloat16)
    grad_out = grad_out.reshape(chips, 2 * share, width)
    outer, inner = lax.axis_size("outer"), lax.axis_size("inner")
    grad_up, grad_out, grad_down = (
        value.reshape(outer, inner, line, -1, width) for value in (grad_up, grad_out, grad_down)
    )
    begun = (
        scatter_terms(grad_up, "inner", 1),
        scatter_terms(grad_out, "inner", 1),
        scatter_terms(grad_down, "outer", 0),
    )
    out_terms, whole_in, grad_stream = lax.optimization_barrier((begun[1], whole_in, grad_stream))
    begun = (begun[0], out_terms, begun[2])
    grad_mixed_stream = attend_back(starts, query, keys, values, wide, logs, grad_stream)
    grad_mixed = lax.all_to_all(
        grad_mixed_stream.reshape(group, rows, 3 * lanes), seq, split_axis=0, concat_axis=0, tiled=True
    )
    begun, grad_mixed_stream = lax.optimization_barrier((begun, grad_mixed_stream))
    grad_up, grad_out, grad_down = (rounded_sum(*terms) for terms in begun)
    grad_down = scatter_line(grad_down, "inner", 0)
    grad_up = scatter_line(jnp.concatenate([grad_up, grad_out], axis=2), "outer", 0)
    plane_sums = jnp.concatenate([grad_up, grad_down], axis=1)
    moving = scatter_send(scatter_payload(plane_sums, "line", None, 1), "line", 1)
    moving, grad_mixed = lax.optimization_barrier((moving, grad_mixed))
    grad_in = inner_rows(normed_one, grad_mixed_stream).astype(jnp.bfloat16)
    parts = grad_in.reshape(outer, inner, group * share, 3 * lanes)
    parts = scatter_line(scatter_line(parts, "inner", 1), "outer", 0)
    input_grad, grad_gain_one, grad_shift_one, mixed_sums = finish(
        grad_mixed, whole_in, tokens, grad_second, gain_one
    )
    for step in range(2, line):
        payload = scatter_payload(plane_sums, "line", moving, step)
        if step == 3:
            payload, parts, grad_gain_one = lax.optimization_barrier((payload, parts, grad_gain_one))
        moving = scatter_send(payload, "line", step)
    summed = rounded_sum(
        lax.dynamic_index_in_dim(plane_sums, lax.axis_index("line"), 0, keepdims=False), *moving
    )
    parts = parts.reshape(group, share, 3 * lanes)
    parts = lax.all_to_all(parts, seq, split_axis=0, concat_axis=0, tiled=True)
    parts = parts.astype(jnp.float32)
    summed_in = parts.reshape(group, share, 3, lanes).transpose(1, 2, 0, 3).reshape(share, 3 * width)
    up_sums = grad_bias_up.reshape(chips, unit_block)
    up_sums = jnp.where(
        (lax.broadcasted_iota(jnp.int32, (1, 2, 1), 1) == core), up_sums[:, None, :], 0.0
    )
    grad_small = jnp.concatenate(
        [
            jnp.stack(
                [
                    grad_gain_one[0],
                    grad_shift_one[0],
                    mixed_sums[0, 0],
                    mixed_sums[2, 0],
                    grad_bias_out,
                    grad_scale_one,
                    grad_gain_two,
                    grad_shift_two,
                    grad_bias_down,
                    grad_scale_two,
                ]
            ),
            up_sums.reshape(-1, width),
        ],
        axis=0,
    )
    small_rows = grad_small.shape[0]
    parts = grad_small.reshape(small_rows, count, share).transpose(1, 0, 2)
    parts = lax.all_to_all(
        parts.reshape(count, small_rows * share), everyone, split_axis=0, concat_axis=0, tiled=True
    )
    summed_gains = jnp.sum(parts, axis=0).reshape(small_rows, share)

    up_sum = summed[:up_end].reshape(folds, 2, share, width)
    out_sum = summed[up_end : up_end + 2 * share].reshape(1, 2, share, width)
    both_sums = jnp.concatenate([up_sum, out_sum], axis=0)
    own_sums = jnp.where(first_core, both_sums[:, 0], both_sums[:, 1])
    other_sums = swap_cores(jnp.where(first_core, both_sums[:, 1], both_sums[:, 0]))
    summed_down = summed[up_end + 2 * share :].astype(jnp.float32)
    summed_out = own_sums[folds].astype(jnp.float32) + other_sums[folds].astype(jnp.float32)
    own_up = own_sums[:folds].transpose(1, 0, 2).reshape(share, chips, 1, unit_block)
    other_up = other_sums[:folds].transpose(1, 0, 2).reshape(share, chips, 1, unit_block)
    summed_up = in_order(own_up, other_up, 2).reshape(share, FF).astype(jnp.float32)
    rate_out = max(1, 4 * D // IMG_LEN) ** (-0.5)
    new_in, new_moment_in, new_square_in = adamw(
        project_in, moment_in, square_in, summed_in, D ** (-0.5), 0.04
    )
    new_out, new_moment_out, new_square_out = adamw(
        project_out, moment_out, square_out, summed_out, rate_out, 0.04
    )
    new_up, new_moment_up, new_square_up = adamw(
        hidden_up, moment_up, square_up, summed_up, D ** (-0.5), 0.04
    )
    new_down, new_moment_down, new_square_down = adamw(
        hidden_down, moment_down, square_down, summed_down, FF ** (-0.5), 0.04
    )
    new_gains, new_moment_gains, new_square_gains = adamw(
        gains_biases, moment_gains, square_gains, summed_gains, 0.2, 0.0
    )
    return (
        block_output,
        input_grad,
        new_in,
        new_out,
        new_up,
        new_down,
        new_gains,
        new_moment_in,
        new_moment_out,
        new_moment_up,
        new_moment_down,
        new_moment_gains,
        new_square_in,
        new_square_out,
        new_square_up,
        new_square_down,
        new_square_gains,
        summed_gains[8],
    )


def solution(mesh):
    streams, group = mesh.shape["fsdp"], mesh.shape["seq"]
    outer = math.isqrt(streams)
    fine = jax.sharding.Mesh(
        mesh.devices.reshape(outer, streams // outer, group // 2, 2),
        ("outer", "inner", "line", "core"),
    )
    return jax.shard_map(
        on_device,
        mesh=fine,
        in_specs=(
            P(("outer", "inner", "line", "core"), None),
            P(("outer", "inner", "line", "core"), None),
            P(("outer", "inner", "line", "core")),
            P(("outer", "inner", "line", "core")),
            P(("outer", "inner", "line", "core"), None),
            P(("outer", "inner", "line", "core"), None),
            P(("outer", "inner", "line", "core"), None),
            P(("outer", "inner", "line", "core"), None),
            P(None, ("outer", "inner", "line", "core")),
            P(("outer", "inner", "line", "core"), None),
            P(("outer", "inner", "line", "core"), None),
            P(("outer", "inner", "line", "core"), None),
            P(("outer", "inner", "line", "core"), None),
            P(None, ("outer", "inner", "line", "core")),
            P(("outer", "inner", "line", "core"), None),
            P(("outer", "inner", "line", "core"), None),
            P(("outer", "inner", "line", "core"), None),
            P(("outer", "inner", "line", "core"), None),
            P(None, ("outer", "inner", "line", "core")),
        ),
        out_specs=(
            P(("outer", "inner", "line", "core"), None),
            P(("outer", "inner", "line", "core"), None),
            P(("outer", "inner", "line", "core"), None),
            P(("outer", "inner", "line", "core"), None),
            P(("outer", "inner", "line", "core"), None),
            P(("outer", "inner", "line", "core"), None),
            P(None, ("outer", "inner", "line", "core")),
            P(("outer", "inner", "line", "core"), None),
            P(("outer", "inner", "line", "core"), None),
            P(("outer", "inner", "line", "core"), None),
            P(("outer", "inner", "line", "core"), None),
            P(None, ("outer", "inner", "line", "core")),
            P(("outer", "inner", "line", "core"), None),
            P(("outer", "inner", "line", "core"), None),
            P(("outer", "inner", "line", "core"), None),
            P(("outer", "inner", "line", "core"), None),
            P(None, ("outer", "inner", "line", "core")),
            P(("outer", "inner", "line", "core")),
        ),
        check_vma=False,
    )
```

```python
import functools
import math

import jax
import jax.numpy as jnp
from jax import lax
from jax.experimental import pallas as pl
from jax.experimental.pallas import tpu as pltpu
from jax.sharding import PartitionSpec as P

D = 1024
FF = 4096
HEADS = 16
HEAD_DIM = 64
IMG_LEN = 1370
WINDOW = 1408
TILE = 352
VMEM_BYTES = 56 * 1024 * 1024
STEP = 10


masked_score = -1e30


def layer_norm(values, gain, shift):
    average = jnp.mean(values, axis=-1, keepdims=True)
    centered = values - average
    variance = jnp.mean(centered * centered, axis=-1, keepdims=True)
    return centered * lax.rsqrt(variance + 1e-06) * gain + shift


def exact_gelu(values):
    return jax.nn.gelu(values, approximate=False)


def plain_product(left, right):
    return jnp.dot(left, right, preferred_element_type=jnp.float32)


def inner_rows(left, right):
    return lax.dot_general(
        left, right, (((0,), (0,)), ((), ())), preferred_element_type=jnp.float32
    )


def inner_cols(left, right):
    return lax.dot_general(
        left, right, (((1,), (1,)), ((), ())), preferred_element_type=jnp.float32
    )


def adamw(param, moment, square, grad, rate, decay):
    new_moment = 0.9 * moment + 0.1 * grad
    new_square = 0.999 * square + 0.001 * grad * grad
    corrected = new_moment / (1.0 - 0.9**STEP)
    scaled = jnp.sqrt(new_square / (1.0 - 0.999**STEP)) + 1e-08
    return (param - rate * (corrected / scaled + decay * param), new_moment, new_square)


def head_lanes(shape):
    return lax.broadcasted_iota(jnp.int32, shape, 1) // HEAD_DIM


def window_of(starts_ref, image, length):
    start = starts_ref[image]
    base = jnp.clip(start // 16 * 16, 0, length - WINDOW)
    return (pl.multiple_of(base, 16), start - base)


def image_mask(position, offset):
    return (position >= offset) & (position < offset + IMG_LEN)


def attend_kernel(starts_ref, q_ref, k_ref, v_ref, wide_ref, out_ref, log_ref):
    image, tile = pl.program_id(0), pl.program_id(1)
    length, lanes = q_ref.shape
    base, offset = window_of(starts_ref, image, length)
    rows = pl.ds(pl.multiple_of(base + tile * TILE, 16), TILE)

    @pl.when((image == 0) & (tile == 0))
    def clear():
        wide_ref[...] = jnp.zeros_like(wide_ref)
        out_ref[...] = jnp.zeros_like(out_ref)
        log_ref[...] = jnp.zeros_like(log_ref)

    query = q_ref[rows, :].astype(jnp.float32) * HEAD_DIM ** (-0.5)
    keys = k_ref[pl.ds(base, WINDOW), :]
    values = v_ref[pl.ds(base, WINDOW), :]
    key_ok = image_mask(lax.broadcasted_iota(jnp.int32, (1, WINDOW), 1), offset)
    bias = jnp.where(key_ok, 0.0, masked_score)
    row_ok = image_mask(lax.broadcasted_iota(jnp.int32, (TILE, 1), 0) + tile * TILE, offset)
    head_of = head_lanes((TILE, lanes))
    total_out = jnp.zeros((TILE, lanes), jnp.float32)
    total_log = jnp.zeros((TILE, lanes), jnp.float32)
    for head in range(lanes // HEAD_DIM):
        mine = head_of == head
        part = jnp.where(mine, query, 0.0).astype(jnp.bfloat16)
        scores = inner_cols(part, keys) + bias
        top = jnp.max(scores, axis=1, keepdims=True)
        weights = jnp.exp(scores - top)
        total = jnp.sum(weights, axis=1, keepdims=True)
        probs = (weights * (1.0 / total)).astype(jnp.bfloat16)
        total_out = jnp.where(mine, plain_product(probs, values), total_out)
        total_log = jnp.where(mine, top + jnp.log(total), total_log)
    merged = jnp.where(row_ok, total_out, wide_ref[rows, :])
    wide_ref[rows, :] = merged
    out_ref[rows, :] = merged.astype(jnp.bfloat16)
    log_ref[rows, :] = jnp.where(row_ok, total_log, log_ref[rows, :])


def attend(starts, query, keys, values):
    length, lanes = query.shape
    whole = pl.BlockSpec((length, lanes), lambda image, tile, starts: (0, 0))
    wide = jax.ShapeDtypeStruct((length, lanes), jnp.float32)
    images = length // IMG_LEN
    return pl.pallas_call(
        attend_kernel,
        grid_spec=pltpu.PrefetchScalarGridSpec(
            num_scalar_prefetch=1,
            grid=(images, WINDOW // TILE),
            in_specs=[whole] * 3,
            out_specs=[whole] * 3,
        ),
        out_shape=(wide, jax.ShapeDtypeStruct((length, lanes), jnp.bfloat16), wide),
        compiler_params=pltpu.CompilerParams(
            vmem_limit_bytes=VMEM_BYTES, dimension_semantics=("arbitrary", "arbitrary")
        ),
        cost_estimate=pl.CostEstimate(
            flops=images * WINDOW * WINDOW * lanes * 8,
            bytes_accessed=length * lanes * 16,
            transcendentals=images * WINDOW * WINDOW * lanes // HEAD_DIM,
        ),
        name="attend_forward",
    )(starts, query, keys, values)


def attend_back_kernel(
    starts_ref, q_ref, k_ref, v_ref, wide_ref, log_ref, go_ref, grad_ref, key_acc, value_acc
):
    image, tile = pl.program_id(0), pl.program_id(1)
    length, lanes = q_ref.shape
    base, offset = window_of(starts_ref, image, length)
    rows = pl.ds(pl.multiple_of(base + tile * TILE, 16), TILE)
    window = pl.ds(base, WINDOW)

    @pl.when((image == 0) & (tile == 0))
    def clear():
        grad_ref[...] = jnp.zeros_like(grad_ref)

    @pl.when(tile == 0)
    def clear_sums():
        key_acc[...] = jnp.zeros_like(key_acc)
        value_acc[...] = jnp.zeros_like(value_acc)

    query = q_ref[rows, :].astype(jnp.float32) * HEAD_DIM ** (-0.5)
    keys = k_ref[window, :]
    values = v_ref[window, :]
    key_ok = image_mask(lax.broadcasted_iota(jnp.int32, (1, WINDOW), 1), offset)
    bias = jnp.where(key_ok, 0.0, masked_score)
    row_ok = image_mask(lax.broadcasted_iota(jnp.int32, (TILE, 1), 0) + tile * TILE, offset)
    head_of = head_lanes((TILE, lanes))
    grad_out = jnp.where(row_ok, go_ref[rows, :].astype(jnp.float32), 0.0)
    centre_parts = grad_out * wide_ref[rows, :]
    logs = jnp.where(row_ok, log_ref[rows, :], -masked_score)
    query_grad = jnp.zeros((TILE, lanes), jnp.float32)
    for head in range(lanes // HEAD_DIM):
        mine = head_of == head
        part = jnp.where(mine, query, 0.0).astype(jnp.bfloat16)
        grad_part = jnp.where(mine, grad_out, 0.0).astype(jnp.bfloat16)
        centre = jnp.sum(jnp.where(mine, centre_parts, 0.0), axis=1, keepdims=True)
        log_total = jnp.max(jnp.where(mine, logs, masked_score), axis=1, keepdims=True)
        probs = jnp.exp(inner_cols(part, keys) + bias - log_total)
        grad_probs = inner_cols(grad_part, values)
        grad_scores = (probs * (grad_probs - centre)).astype(jnp.bfloat16)
        query_grad = jnp.where(mine, plain_product(grad_scores, keys), query_grad)
        key_acc[...] += inner_rows(part, grad_scores)
        value_acc[...] += inner_rows(grad_part, probs.astype(jnp.bfloat16))
    old = grad_ref[rows, 0:lanes].astype(jnp.float32)
    merged = jnp.where(row_ok, query_grad * HEAD_DIM ** (-0.5), old)
    grad_ref[rows, 0:lanes] = merged.astype(jnp.bfloat16)

    @pl.when(tile == pl.num_programs(1) - 1)
    def flush():
        inside = image_mask(lax.broadcasted_iota(jnp.int32, (WINDOW, 1), 0), offset)
        for slot, sums in ((1, key_acc), (2, value_acc)):
            columns = slice(slot * lanes, (slot + 1) * lanes)
            old = grad_ref[window, columns].astype(jnp.float32)
            merged = jnp.where(inside, sums[...].T, old)
            grad_ref[window, columns] = merged.astype(jnp.bfloat16)


def attend_back(starts, query, keys, values, wide, logs, grad_out):
    length, lanes = query.shape
    whole = pl.BlockSpec((length, lanes), lambda image, tile, starts: (0, 0))
    images = length // IMG_LEN
    return pl.pallas_call(
        attend_back_kernel,
        grid_spec=pltpu.PrefetchScalarGridSpec(
            num_scalar_prefetch=1,
            grid=(images, WINDOW // TILE),
            in_specs=[whole] * 6,
            out_specs=pl.BlockSpec((length, 3 * lanes), lambda image, tile, starts: (0, 0)),
            scratch_shapes=[pltpu.VMEM((lanes, WINDOW), jnp.float32)] * 2,
        ),
        out_shape=jax.ShapeDtypeStruct((length, 3 * lanes), jnp.bfloat16),
        compiler_params=pltpu.CompilerParams(
            vmem_limit_bytes=VMEM_BYTES, dimension_semantics=("arbitrary", "arbitrary")
        ),
        cost_estimate=pl.CostEstimate(
            flops=images * WINDOW * WINDOW * lanes * 20,
            bytes_accessed=length * lanes * 22,
            transcendentals=images * WINDOW * WINDOW * lanes // HEAD_DIM,
        ),
        name="attend_backward",
    )(starts, query, keys, values, wide, logs, grad_out)


def norm_mix_kernel(pieces, place_ref, own_ref, other_ref, gain_ref, shift_ref, bias_ref, *refs):
    weight = jnp.concatenate(
        [ref[...].reshape(own_ref.shape[1], -1) for ref in refs[:pieces]], axis=1
    )
    a_ref, q_ref, k_ref, v_ref = refs[pieces:]
    lanes = q_ref.shape[1]
    mine = lax.rem(pl.program_id(0), 2) == lax.rem(place_ref[0], 2)
    own, other = own_ref[...].astype(jnp.float32), other_ref[...].astype(jnp.float32)
    normed = layer_norm(jnp.where(mine, own, other), gain_ref[...], shift_ref[...])
    normed = normed.astype(jnp.bfloat16)
    a_ref[...] = normed
    mixed = (plain_product(normed, weight) + bias_ref[...]).astype(jnp.bfloat16)
    q_ref[...] = mixed[:, :lanes]
    k_ref[...] = mixed[:, lanes : 2 * lanes]
    v_ref[...] = mixed[:, 2 * lanes :]


def norm_mix(place, own, other, block, gain, shift, weight, bias):
    length, width = own.shape[0] * 2, own.shape[1]
    lanes = bias.shape[0] // 3
    row = lambda size: pl.BlockSpec((block, size), lambda i, place: (i, 0))
    half = pl.BlockSpec((block, width), lambda i, place: (i // 2, 0))
    fixed = lambda *shape: pl.BlockSpec(shape, lambda i, place: (0, 0))
    part = jax.ShapeDtypeStruct((length, lanes), jnp.bfloat16)
    weights, weight_specs = [weight], [fixed(width, 3 * lanes)]
    return pl.pallas_call(
        functools.partial(norm_mix_kernel, len(weights)),
        grid_spec=pltpu.PrefetchScalarGridSpec(
            num_scalar_prefetch=1,
            grid=(length // block,),
            in_specs=[
                half,
                half,
                fixed(1, width),
                fixed(1, width),
                fixed(1, 3 * lanes),
                *weight_specs,
            ],
            out_specs=[row(width), row(lanes), row(lanes), row(lanes)],
        ),
        out_shape=(jax.ShapeDtypeStruct((length, width), jnp.bfloat16), part, part, part),
        compiler_params=pltpu.CompilerParams(vmem_limit_bytes=VMEM_BYTES),
        cost_estimate=pl.CostEstimate(
            flops=length * width * lanes * 6, bytes_accessed=length * width * 4, transcendentals=0
        ),
        name="norm_mix",
    )(place, own, other, gain[None], shift[None], bias[None], *weights)


def mlp_kernel(pieces, core_ref, own_ref, other_ref, gm_own_ref, gm_other_ref, bias_ref, *refs):
    up_refs, down_refs = refs[:pieces], refs[pieces : 2 * pieces]
    up_grad_ref, down_grad_ref, m_own_ref, m_other_ref, gh_own_ref, gh_other_ref = refs[
        2 * pieces : 2 * pieces + 6
    ]
    bias_grad_ref, h_ref, gm_ref, turned_ref = refs[2 * pieces + 6 :]
    tile = pl.program_id(0)
    rows, width = own_ref.shape
    chips = up_grad_ref.shape[0]
    up_rows = width // chips
    units = bias_ref.shape[1]
    folds = width // units

    @pl.when(tile == 0)
    def clear():
        for ref in (m_own_ref, m_other_ref, gh_own_ref, gh_other_ref):
            ref[...] = jnp.zeros_like(ref)
        h_ref[:rows] = own_ref[...]
        h_ref[rows:] = other_ref[...]
        gm_ref[:rows] = gm_own_ref[...]
        gm_ref[rows:] = gm_other_ref[...]
        turned_ref[...] = h_ref[...].T

    weight_up = jnp.concatenate([ref[...].reshape(width, -1) for ref in up_refs], axis=1)
    weight_down = jnp.concatenate([ref[...].reshape(-1, width) for ref in down_refs], axis=0)
    gm = gm_ref[...]
    upward = plain_product(h_ref[...], weight_up) + bias_ref[...]
    normal = 0.5 * (1.0 + lax.erf(upward * 0.5**0.5))
    slope = normal + upward * jnp.exp(upward * upward * -0.5) * (0.5 / jnp.pi) ** 0.5
    active = (upward * normal).astype(jnp.bfloat16)
    grad_up = (inner_cols(gm, weight_down) * slope).astype(jnp.bfloat16)
    bias_grad_ref[...] = jnp.sum(grad_up.astype(jnp.float32), axis=0, keepdims=True)
    branch = plain_product(active, weight_down)
    m_own_ref[...] += branch[:rows]
    m_other_ref[...] += branch[rows:]
    grad_norm = inner_cols(grad_up, weight_up)
    gh_own_ref[...] += grad_norm[:rows]
    gh_other_ref[...] += grad_norm[rows:]
    up_grad = plain_product(turned_ref[...], grad_up).astype(jnp.bfloat16)
    row = pl.multiple_of(tile // folds * up_rows, up_rows)
    column = pl.multiple_of(lax.rem(tile, folds) * units, units)
    up_grad = up_grad.reshape(chips, up_rows, units)
    up_grad_ref[:, pl.ds(row, up_rows), pl.ds(column, units)] = up_grad
    down_grad = inner_rows(active, gm).astype(jnp.bfloat16)
    down_grad_ref[...] = down_grad.reshape(down_grad_ref.shape)


def mlp(core, own, other, gm_own, gm_other, weights, bias, chips):
    rows, width = own.shape
    half = bias.shape[0]
    unit_block = half // chips
    units = 256
    folds = width // units
    once = dict(pipeline_mode=pl.Buffered(1))
    fixed = pl.BlockSpec((rows, width), lambda j, core: (0, 0), **once)
    if len(weights) == 1:
        up_rows = width // chips
        pieces = 1
        owners = units // unit_block
        weights = list(weights) * 2
        weight_specs = [
            pl.BlockSpec((chips, up_rows, units), lambda j, core: (0, j // folds, lax.rem(j, folds))),
            pl.BlockSpec(
                (owners, unit_block, width), lambda j, core: (j, half // width * up_rows // unit_block, 0)
            ),
        ]
        up_shape, down_shape = (chips, half // chips, width), (chips, half // chips, width)
        down_grad_spec = pl.BlockSpec((owners, unit_block, width), lambda j, core: (j, 0, 0))
    else:
        pieces = 1
        weight_specs = [
            pl.BlockSpec((width, units), lambda j, core: (0, j)),
            pl.BlockSpec((units, width), lambda j, core: (j, 0)),
        ]
        up_shape, down_shape = (1, half // width * width, width), (1, half, width)
        down_grad_spec = pl.BlockSpec((1, units, width), lambda j, core: (0, j, 0))
    total = jax.ShapeDtypeStruct((rows, width), jnp.float32)
    outs = pl.pallas_call(
        functools.partial(mlp_kernel, pieces),
        grid_spec=pltpu.PrefetchScalarGridSpec(
            num_scalar_prefetch=1,
            grid=(half // units,),
            in_specs=[fixed] * 4 + [pl.BlockSpec((1, units), lambda j, core: (0, j)), *weight_specs],
            out_specs=[
                pl.BlockSpec(up_shape, lambda j, core: (0, 0, 0), **once),
                down_grad_spec,
                *[fixed] * 4,
                pl.BlockSpec((1, units), lambda j, core: (0, j)),
            ],
            scratch_shapes=[
                pltpu.VMEM((2 * rows, width), jnp.bfloat16),
                pltpu.VMEM((2 * rows, width), jnp.bfloat16),
                pltpu.VMEM((width, 2 * rows), jnp.bfloat16),
            ],
        ),
        out_shape=(
            jax.ShapeDtypeStruct(up_shape, jnp.bfloat16),
            jax.ShapeDtypeStruct(down_shape, jnp.bfloat16),
            *[total] * 4,
            jax.ShapeDtypeStruct((1, half), jnp.float32),
        ),
        compiler_params=pltpu.CompilerParams(vmem_limit_bytes=VMEM_BYTES),
        cost_estimate=pl.CostEstimate(
            flops=2 * rows * width * half * 12,
            bytes_accessed=half * width * 8 + rows * width * 24,
            transcendentals=rows * half * 4,
        ),
        name="mlp_both_ways",
    )(core, own, other, gm_own, gm_other, bias[None], *weights)
    up_grad, down_grad = outs[0], outs[1]
    if up_shape[0] == 1:
        up_grad = up_grad.reshape(half // width, chips, width // chips, width).swapaxes(0, 1)
        up_grad = up_grad.reshape(chips, -1, width)
        down_grad = down_grad.reshape(chips, -1, width)
    return (up_grad, down_grad, *outs[2:])


def finish_kernel(
    grad_ref, weight_ref, x_ref, gx_ref, gain_ref, out_ref, gain_grad_ref, shift_grad_ref, sums_ref, acc_ref
):
    step = pl.program_id(0)
    parts = [grad_ref[slot] for slot in range(grad_ref.shape[0])]
    grad = jnp.concatenate(parts, axis=1)
    width = x_ref.shape[1]
    product = inner_cols(grad, weight_ref[...].reshape(width, width))
    sums_ref[...] = jnp.sum(grad.astype(jnp.float32), axis=0, keepdims=True)[None]

    @pl.when(step == 0)
    def begin():
        acc_ref[...] = product

    @pl.when(step > 0)
    def further():
        acc_ref[...] += product

    @pl.when(step == pl.num_programs(0) - 1)
    def end():
        values = x_ref[...].astype(jnp.float32)
        centered = values - jnp.mean(values, axis=1, keepdims=True)
        scale = lax.rsqrt(jnp.mean(centered * centered, axis=1, keepdims=True) + 1e-06)
        unit = centered * scale
        grad_norm = acc_ref[...]
        gain_grad_ref[...] = jnp.sum(grad_norm * unit, axis=0, keepdims=True)
        shift_grad_ref[...] = jnp.sum(grad_norm, axis=0, keepdims=True)
        grad_unit = grad_norm * gain_ref[...]
        mean = jnp.mean(grad_unit, axis=1, keepdims=True)
        slant = jnp.mean(grad_unit * unit, axis=1, keepdims=True)
        out_ref[...] = gx_ref[...] + scale * (grad_unit - mean - unit * slant)


def finish(grads, weights, inputs, gx, gain):
    rows, width = inputs.shape
    group, lanes = grads.shape[0], grads.shape[2] // 3
    if lanes % 128:
        grads = grads.reshape(group, rows, 3, lanes).transpose(2, 0, 1, 3)
        grads = grads.reshape(3 * group, rows, lanes)
        grad_spec = pl.BlockSpec((group, rows, lanes), lambda k: (k, 0, 0))
    else:
        grad_spec = pl.BlockSpec((group, rows, lanes), lambda k: (0, 0, k))
    if weights.ndim == 3:
        share = width // weights.shape[0]
        first = weights.shape[1] // share - 3
        weight_spec = pl.BlockSpec((weights.shape[0], share, width), lambda k: (0, first + k, 0))
    else:
        weight_spec = pl.BlockSpec((width, width), lambda k: (0, k))
    fixed = lambda *shape: pl.BlockSpec(shape, lambda k: (0, 0))
    vector = jax.ShapeDtypeStruct((1, width), jnp.float32)
    return pl.pallas_call(
        finish_kernel,
        grid=(3,),
        in_specs=[
            grad_spec,
            weight_spec,
            fixed(rows, width),
            fixed(rows, width),
            fixed(1, width),
        ],
        out_specs=[
            fixed(rows, width),
            fixed(1, width),
            fixed(1, width),
            pl.BlockSpec((1, 1, width), lambda k: (k, 0, 0)),
        ],
        out_shape=(
            jax.ShapeDtypeStruct((rows, width), jnp.float32),
            vector,
            vector,
            jax.ShapeDtypeStruct((3, 1, width), jnp.float32),
        ),
        scratch_shapes=[pltpu.VMEM((rows, width), jnp.float32)],
        compiler_params=pltpu.CompilerParams(vmem_limit_bytes=VMEM_BYTES),
        cost_estimate=pl.CostEstimate(
            flops=rows * width * width * 6, bytes_accessed=width * width * 16, transcendentals=0
        ),
        name="finish_input",
    )(grads, weights, inputs, gx, gain[None])


def swap_cores(value):
    return lax.ppermute(value, "core", [(0, 1), (1, 0)])


def line_pairs(size, sign, step):
    pairs = [(i, i - sign) for i in range(size) if 0 <= i - sign < size]
    return [(i, j) for i, j in pairs if 0 <= i + sign * (step - 1) < size]


def line_pieces(value, axis):
    size = lax.axis_size(axis)
    if size == 2:
        other = lax.ppermute(value, axis, [(0, 1), (1, 0)])
        return [(None, other)]
    pieces = []
    for sign in (-1, 1):
        moving = value
        for step in range(1, size):
            moving = lax.ppermute(moving, axis, line_pairs(size, sign, step))
            pieces.append((sign * step, moving))
    return pieces


def line_order(value, pieces, axis):
    place = lax.axis_index(axis)
    size = lax.axis_size(axis)
    if size == 2:
        other = pieces[0][1]
        return jnp.where(place == 0, jnp.stack([value, other]), jnp.stack([other, value]))
    whole = jnp.zeros((size, *value.shape), value.dtype)
    for distance, piece in sorted(pieces, key=lambda item: -abs(item[0])) + [(0, value)]:
        slot = jnp.clip(place + distance, 0, size - 1)
        whole = lax.dynamic_update_index_in_dim(whole, piece, slot, 0)
    return whole


def gather_line(value, axis):
    return line_order(value, line_pieces(value, axis), axis)


def exchange_line(value, axis):
    place = lax.axis_index(axis)
    size = lax.axis_size(axis)
    pick = lambda slot: lax.dynamic_index_in_dim(
        value, jnp.clip(slot, 0, size - 1), 0, keepdims=False
    )
    pieces = []
    for distance in range(1, size):
        for move in (-distance, distance):
            pairs = [(i, i + move) for i in range(size) if 0 <= i + move < size]
            pieces.append((-move, lax.ppermute(pick(place + move), axis, pairs)))
    if size == 2:
        pieces = [(None, pieces[0][1] + pieces[1][1])]
    return line_order(pick(place), pieces, axis)


def rounded_sum(*terms):
    return sum(term.astype(jnp.float32) for term in terms).astype(jnp.bfloat16)


def scatter_terms(value, axis, dim):
    if lax.axis_size(axis) != 2:
        return (scatter_line(value, axis, dim),)
    place = lax.axis_index(axis)
    pick = lambda slot: lax.dynamic_index_in_dim(value, slot, dim, keepdims=False)
    return (pick(place), lax.ppermute(pick(1 - place), axis, [(0, 1), (1, 0)]))


def scatter_payload(value, axis, moving, step):
    place = lax.axis_index(axis)
    size = lax.axis_size(axis)
    payload = []
    for n, sign in enumerate((-1, 1)):
        slot = jnp.clip(place - sign * (size - step), 0, size - 1)
        own = lax.dynamic_index_in_dim(value, slot, 0, keepdims=False)
        payload.append(own if moving is None else rounded_sum(own, moving[n]))
    return tuple(payload)


def scatter_send(payload, axis, step):
    size = lax.axis_size(axis)
    sums = []
    for value, sign in zip(payload, (-1, 1)):
        start = 0 if sign < 0 else size - 1
        pairs = [(i, i - sign) for i in range(size) if 0 <= i - sign < size]
        pairs = [(i, j) for i, j in pairs if abs(i - start) <= step - 1]
        sums.append(lax.ppermute(value, axis, pairs))
    return tuple(sums)


def scatter_line(value, axis, dim):
    place = lax.axis_index(axis)
    size = lax.axis_size(axis)
    pick = lambda slot: lax.dynamic_index_in_dim(
        value, jnp.clip(slot, 0, size - 1), dim, keepdims=False
    )
    if size == 2:
        return rounded_sum(pick(place), lax.ppermute(pick(1 - place), axis, [(0, 1), (1, 0)]))
    sums = []
    for sign in (-1, 1):
        moving = None
        for step in range(1, size):
            start = 0 if sign < 0 else size - 1
            pairs = [(i, i - sign) for i in range(size) if 0 <= i - sign < size]
            pairs = [(i, j) for i, j in pairs if abs(i - start) <= step - 1]
            own = pick(place - sign * (size - step))
            payload = own if moving is None else rounded_sum(own, moving)
            moving = lax.ppermute(payload, axis, pairs)
        sums.append(moving)
    return rounded_sum(pick(place), *sums)


def on_device(
    tokens,
    cotangent,
    segment_ids,
    valid,
    project_in,
    project_out,
    hidden_up,
    hidden_down,
    gains_biases,
    moment_in,
    moment_out,
    moment_up,
    moment_down,
    moment_gains,
    square_in,
    square_out,
    square_up,
    square_down,
    square_gains,
):
    rows = tokens.shape[0]
    width = tokens.shape[1]
    everyone = ("outer", "inner", "line", "core")
    planes = ("outer", "inner")
    seq = ("line", "core")
    streams, line = lax.axis_size(planes), lax.axis_size("line")
    group = 2 * line
    count = streams * group
    chips = streams * line
    share = width // count
    lanes = width // group
    length = rows * group
    images = length // IMG_LEN
    core = lax.axis_index("core")
    first_core = core == 0

    def in_order(own, other, axis):
        return jnp.concatenate(
            [jnp.where(first_core, own, other), jnp.where(first_core, other, own)], axis=axis
        )

    half = FF // 2
    unit_block = FF // count
    folds = half // width
    up_end = 2 * share * folds
    low = lambda value: value.astype(jnp.bfloat16)
    direct = share % 16 == 0 and unit_block == 128 and line > 3
    position = lax.broadcasted_iota(jnp.int32, (images, rows), 1)
    found = (segment_ids[None, :] == lax.broadcasted_iota(jnp.int32, (images, rows), 0)) & (
        valid[None, :] == 1
    )
    first = jnp.min(jnp.where(found, position, rows), axis=1)
    small = jnp.concatenate([low(gains_biases).reshape(-1), low(first // 32), low(first % 32)])
    fold = lambda value: low(value).reshape(share, -1, width).swapaxes(0, 1).reshape(-1, width)
    if direct:
        extra = 16
        small = jnp.pad(small, (0, extra * 3 * lanes - small.shape[0]))
        small = jnp.broadcast_to(small.reshape(1, extra, 3 * lanes), (group, extra, 3 * lanes))
        owned = low(project_in).reshape(share, 3, group, lanes).transpose(2, 0, 1, 3)
        blocks = jnp.concatenate([owned.reshape(group, share, 3 * lanes), small], axis=1)
        blocks = blocks.reshape(line, 2, share + extra, 3 * lanes)
        keep = jnp.where(first_core, blocks[:, 0], blocks[:, 1])
        sent = swap_cores(jnp.where(first_core, blocks[:, 1], blocks[:, 0]))
        blocks = in_order(keep[:, None], sent[:, None], 1)

        up_blocks = low(hidden_up).reshape(share, chips, 2, unit_block)
        up_first = up_blocks[:, :, 0].reshape(share, half)
        up_second = up_blocks[:, :, 1].reshape(share, half)
        out_rows = low(project_out)
        received = swap_cores(
            jnp.concatenate(
                [jnp.where(first_core, up_second, up_first).reshape(-1, width), out_rows], axis=0
            )
        )
        up_rows = in_order(
            jnp.where(first_core, up_first, up_second),
            received[: share * folds].reshape(share, half),
            0,
        )
        packed = jnp.concatenate(
            [
                up_rows.reshape(2 * share, folds, width).transpose(1, 0, 2).reshape(-1, width),
                low(hidden_down),
                in_order(out_rows, received[share * folds :], 0),
            ],
            axis=0,
        )
        gathered = lax.all_gather(packed, ("outer", "inner", "line"), axis=0, tiled=False)
        whole_out = gathered[:, packed.shape[0] - 2 * share :].reshape(width, width)
        mlp_weights = (gathered,)
        whole_in = lax.all_gather(fold(project_in), everyone, axis=0, tiled=False)

        pieces, swapped = [], []
        moving = [tokens, tokens]
        for step in range(1, line):
            moving = [
                lax.ppermute(value, "line", line_pairs(line, sign, step))
                for sign, value in zip((-1, 1), moving)
            ]
            if step == 1:
                blocks = exchange_line(blocks, "line")
            elif step == 2:
                blocks = gather_line(gather_line(blocks, "inner"), "outer")
            moving, blocks, swapped = lax.optimization_barrier((moving, blocks, swapped))
            pieces += [(sign * step, value) for sign, value in zip((-1, 1), moving)]
            swapped = swapped + [swap_cores(value) for value in moving]
        swapped = [(distance, value) for (distance, _), value in zip(pieces, swapped)]
        blocks = blocks.reshape(count, share + extra, 3 * lanes)
        mine_in = blocks[:, :share].reshape(width, 3 * lanes)
        small = blocks[:, share:].reshape(count, -1)
    else:
        whole_in = lax.all_gather(low(project_in), everyone, axis=0, tiled=True)
        mine_in = lax.dynamic_index_in_dim(
            whole_in.reshape(width, 3, group, lanes), lax.axis_index(seq), axis=2, keepdims=False
        ).reshape(width, 3 * lanes)
        small = lax.all_gather(small, everyone, axis=0, tiled=False)
    vector_size = gains_biases.size
    vectors = small[:, :vector_size].reshape(count, -1, share).transpose(1, 0, 2)
    vectors = vectors.reshape(-1, width).astype(jnp.float32)
    first = small[:, vector_size : vector_size + 2 * images].astype(jnp.int32)
    first = first[:, :images] * 32 + first[:, images:]
    first = lax.dynamic_slice_in_dim(first, lax.axis_index(planes) * group, group, 0)
    offsets = lax.broadcasted_iota(jnp.int32, (group, images), 0) * rows
    starts = jnp.min(jnp.where(first < rows, first + offsets, length), axis=0)

    if not direct:
        pieces = line_pieces(tokens, "line")
        swapped = [(distance, swap_cores(piece)) for distance, piece in pieces]
    own_tokens = line_order(tokens, pieces, "line").reshape(-1, width)
    other_tokens = line_order(swap_cores(tokens), swapped, "line").reshape(-1, width)

    gain_one, shift_one, bias_query, bias_value, bias_out = (
        vectors[0],
        vectors[1],
        vectors[2],
        vectors[3],
        vectors[4],
    )
    scale_one, gain_two, shift_two, bias_down, scale_two = (
        vectors[5],
        vectors[6],
        vectors[7],
        vectors[8],
        vectors[9],
    )
    bias_up = lax.dynamic_index_in_dim(
        vectors[10:].reshape(chips, 2, unit_block), core, axis=1, keepdims=False
    ).reshape(half)
    column = lax.axis_index(seq) * lanes
    bias_in = jnp.concatenate(
        [
            lax.dynamic_slice_in_dim(bias_query, column, lanes, 0),
            jnp.zeros((lanes,), jnp.float32),
            lax.dynamic_slice_in_dim(bias_value, column, lanes, 0),
        ]
    )
    grad_rows = cotangent.astype(jnp.float32) * valid.astype(jnp.float32)[:, None]
    grad_branch = (scale_two * grad_rows).astype(jnp.bfloat16)

    place = lax.axis_index(seq)
    normed_one, query, keys, values = norm_mix(
        place.reshape(1), own_tokens, other_tokens, rows, gain_one, shift_one, mine_in, bias_in
    )
    wide, attended, logs = attend(starts, query, keys, values)
    if not direct:
        whole_out, whole_up, whole_down = (
            lax.all_gather(low(value), everyone, axis=0, tiled=True)
            for value in (project_out, hidden_up, hidden_down)
        )
        block = jnp.arange(half) // unit_block * 2 + core
        index = block * unit_block + lax.rem(jnp.arange(half), unit_block)
        mlp_weights = (jnp.take(whole_up, index, axis=1), jnp.take(whole_down, index, axis=0))
    returned = lax.all_to_all(
        attended.reshape(group, rows, lanes), seq, split_axis=0, concat_axis=0, tiled=True
    )
    attended_rows = returned.transpose(1, 0, 2).reshape(rows, width)
    inputs = tokens.astype(jnp.float32)
    projected = plain_product(attended_rows, whole_out) + bias_out
    second = inputs + scale_one * projected
    norm_two, norm_two_back = jax.vjp(layer_norm, second, gain_two, shift_two)
    normed_two = norm_two.astype(jnp.bfloat16)
    grad_up, grad_down, branch, branch_other, grad_norm_two, grad_norm_other, grad_bias_up = mlp(
        core.reshape(1),
        normed_two,
        swap_cores(normed_two),
        grad_branch,
        swap_cores(grad_branch),
        mlp_weights,
        bias_up,
        chips,
    )
    grad_norm_two = grad_norm_two + swap_cores(grad_norm_other)
    branch = branch + swap_cores(branch_other) + bias_down
    block_output = (second + scale_two * branch).astype(jnp.bfloat16)
    grad_scale_two = jnp.sum(grad_rows * branch, axis=0)
    grad_bias_down = jnp.sum(grad_branch.astype(jnp.float32), axis=0)
    second_part, grad_gain_two, grad_shift_two = norm_two_back(grad_norm_two)
    grad_second = grad_rows + second_part
    grad_scale_one = jnp.sum(grad_second * projected, axis=0)
    grad_projected = (scale_one * grad_second).astype(jnp.bfloat16)
    grad_bias_out = jnp.sum(grad_projected.astype(jnp.float32), axis=0)
    grad_attended = inner_cols(grad_projected, whole_out).astype(jnp.bfloat16)
    grad_stream = lax.all_to_all(
        grad_attended.reshape(rows, group, lanes).transpose(1, 0, 2),
        seq,
        split_axis=0,
        concat_axis=0,
        tiled=True,
    ).reshape(length, lanes)
    grad_out = inner_rows(attended_rows, grad_projected).astype(jnp.bfloat16)
    grad_out = grad_out.reshape(chips, 2 * share, width)
    outer, inner = lax.axis_size("outer"), lax.axis_size("inner")
    grad_up, grad_out, grad_down = (
        value.reshape(outer, inner, line, -1, width) for value in (grad_up, grad_out, grad_down)
    )
    begun = (
        scatter_terms(grad_up, "inner", 1),
        scatter_terms(grad_out, "inner", 1),
        scatter_terms(grad_down, "outer", 0),
    )
    out_terms, whole_in, grad_stream = lax.optimization_barrier((begun[1], whole_in, grad_stream))
    begun = (begun[0], out_terms, begun[2])
    grad_mixed_stream = attend_back(starts, query, keys, values, wide, logs, grad_stream)
    grad_mixed = lax.all_to_all(
        grad_mixed_stream.reshape(group, rows, 3 * lanes), seq, split_axis=0, concat_axis=0, tiled=True
    )
    begun, grad_mixed_stream = lax.optimization_barrier((begun, grad_mixed_stream))
    grad_up, grad_out, grad_down = (rounded_sum(*terms) for terms in begun)
    grad_down = scatter_line(grad_down, "inner", 0)
    grad_up = scatter_line(jnp.concatenate([grad_up, grad_out], axis=2), "outer", 0)
    plane_sums = jnp.concatenate([grad_up, grad_down], axis=1)
    moving = scatter_send(scatter_payload(plane_sums, "line", None, 1), "line", 1)
    moving, grad_mixed = lax.optimization_barrier((moving, grad_mixed))
    grad_in = inner_rows(normed_one, grad_mixed_stream).astype(jnp.bfloat16)
    parts = grad_in.reshape(outer, inner, group * share, 3 * lanes)
    parts = scatter_line(scatter_line(parts, "inner", 1), "outer", 0)
    input_grad, grad_gain_one, grad_shift_one, mixed_sums = finish(
        grad_mixed, whole_in, tokens, grad_second, gain_one
    )
    for step in range(2, line):
        payload = scatter_payload(plane_sums, "line", moving, step)
        if step == 3:
            payload, parts, grad_gain_one = lax.optimization_barrier((payload, parts, grad_gain_one))
        moving = scatter_send(payload, "line", step)
    summed = rounded_sum(
        lax.dynamic_index_in_dim(plane_sums, lax.axis_index("line"), 0, keepdims=False), *moving
    )
    parts = parts.reshape(group, share, 3 * lanes)
    parts = lax.all_to_all(parts, seq, split_axis=0, concat_axis=0, tiled=True)
    parts = parts.astype(jnp.float32)
    summed_in = parts.reshape(group, share, 3, lanes).transpose(1, 2, 0, 3).reshape(share, 3 * width)
    up_sums = grad_bias_up.reshape(chips, unit_block)
    up_sums = jnp.where(
        (lax.broadcasted_iota(jnp.int32, (1, 2, 1), 1) == core), up_sums[:, None, :], 0.0
    )
    grad_small = jnp.concatenate(
        [
            jnp.stack(
                [
                    grad_gain_one[0],
                    grad_shift_one[0],
                    mixed_sums[0, 0],
                    mixed_sums[2, 0],
                    grad_bias_out,
                    grad_scale_one,
                    grad_gain_two,
                    grad_shift_two,
                    grad_bias_down,
                    grad_scale_two,
                ]
            ),
            up_sums.reshape(-1, width),
        ],
        axis=0,
    )
    small_rows = grad_small.shape[0]
    parts = grad_small.reshape(small_rows, count, share).transpose(1, 0, 2)
    parts = lax.all_to_all(
        parts.reshape(count, small_rows * share), everyone, split_axis=0, concat_axis=0, tiled=True
    )
    summed_gains = jnp.sum(parts, axis=0).reshape(small_rows, share)

    up_sum = summed[:up_end].reshape(folds, 2, share, width)
    out_sum = summed[up_end : up_end + 2 * share].reshape(1, 2, share, width)
    both_sums = jnp.concatenate([up_sum, out_sum], axis=0)
    own_sums = jnp.where(first_core, both_sums[:, 0], both_sums[:, 1])
    other_sums = swap_cores(jnp.where(first_core, both_sums[:, 1], both_sums[:, 0]))
    summed_down = summed[up_end + 2 * share :].astype(jnp.float32)
    summed_out = own_sums[folds].astype(jnp.float32) + other_sums[folds].astype(jnp.float32)
    own_up = own_sums[:folds].transpose(1, 0, 2).reshape(share, chips, 1, unit_block)
    other_up = other_sums[:folds].transpose(1, 0, 2).reshape(share, chips, 1, unit_block)
    summed_up = in_order(own_up, other_up, 2).reshape(share, FF).astype(jnp.float32)
    rate_out = max(1, 4 * D // IMG_LEN) ** (-0.5)
    new_in, new_moment_in, new_square_in = adamw(
        project_in, moment_in, square_in, summed_in, D ** (-0.5), 0.04
    )
    new_out, new_moment_out, new_square_out = adamw(
        project_out, moment_out, square_out, summed_out, rate_out, 0.04
    )
    new_up, new_moment_up, new_square_up = adamw(
        hidden_up, moment_up, square_up, summed_up, D ** (-0.5), 0.04
    )
    new_down, new_moment_down, new_square_down = adamw(
        hidden_down, moment_down, square_down, summed_down, FF ** (-0.5), 0.04
    )
    new_gains, new_moment_gains, new_square_gains = adamw(
        gains_biases, moment_gains, square_gains, summed_gains, 0.2, 0.0
    )
    return (
        block_output,
        input_grad,
        new_in,
        new_out,
        new_up,
        new_down,
        new_gains,
        new_moment_in,
        new_moment_out,
        new_moment_up,
        new_moment_down,
        new_moment_gains,
        new_square_in,
        new_square_out,
        new_square_up,
        new_square_down,
        new_square_gains,
        summed_gains[8],
    )


def solution(mesh):
    streams, group = mesh.shape["fsdp"], mesh.shape["seq"]
    outer = math.isqrt(streams)
    fine = jax.sharding.Mesh(
        mesh.devices.reshape(outer, streams // outer, group // 2, 2),
        ("outer", "inner", "line", "core"),
    )
    return jax.shard_map(
        on_device,
        mesh=fine,
        in_specs=(
            P(("outer", "inner", "line", "core"), None),
            P(("outer", "inner", "line", "core"), None),
            P(("outer", "inner", "line", "core")),
            P(("outer", "inner", "line", "core")),
            P(("outer", "inner", "line", "core"), None),
            P(("outer", "inner", "line", "core"), None),
            P(("outer", "inner", "line", "core"), None),
            P(("outer", "inner", "line", "core"), None),
            P(None, ("outer", "inner", "line", "core")),
            P(("outer", "inner", "line", "core"), None),
            P(("outer", "inner", "line", "core"), None),
            P(("outer", "inner", "line", "core"), None),
            P(("outer", "inner", "line", "core"), None),
            P(None, ("outer", "inner", "line", "core")),
            P(("outer", "inner", "line", "core"), None),
            P(("outer", "inner", "line", "core"), None),
            P(("outer", "inner", "line", "core"), None),
            P(("outer", "inner", "line", "core"), None),
            P(None, ("outer", "inner", "line", "core")),
        ),
        out_specs=(
            P(("outer", "inner", "line", "core"), None),
            P(("outer", "inner", "line", "core"), None),
            P(("outer", "inner", "line", "core"), None),
            P(("outer", "inner", "line", "core"), None),
            P(("outer", "inner", "line", "core"), None),
            P(("outer", "inner", "line", "core"), None),
            P(None, ("outer", "inner", "line", "core")),
            P(("outer", "inner", "line", "core"), None),
            P(("outer", "inner", "line", "core"), None),
            P(("outer", "inner", "line", "core"), None),
            P(("outer", "inner", "line", "core"), None),
            P(None, ("outer", "inner", "line", "core")),
            P(("outer", "inner", "line", "core"), None),
            P(("outer", "inner", "line", "core"), None),
            P(("outer", "inner", "line", "core"), None),
            P(("outer", "inner", "line", "core"), None),
            P(None, ("outer", "inner", "line", "core")),
            P(("outer", "inner", "line", "core")),
        ),
        check_vma=False,
    )
```

```python
import functools
import math

import jax
import jax.numpy as jnp
from jax import lax
from jax.experimental import pallas as pl
from jax.experimental.pallas import tpu as pltpu
from jax.sharding import PartitionSpec as P

D = 1024
FF = 4096
HEADS = 16
HEAD_DIM = 64
IMG_LEN = 1370
WINDOW = 1408
TILE = 352
VMEM_BYTES = 56 * 1024 * 1024
STEP = 10


masked_score = -1e30


def layer_norm(values, gain, shift):
    average = jnp.mean(values, axis=-1, keepdims=True)
    centered = values - average
    variance = jnp.mean(centered * centered, axis=-1, keepdims=True)
    return centered * lax.rsqrt(variance + 1e-06) * gain + shift


def exact_gelu(values):
    return jax.nn.gelu(values, approximate=False)


def plain_product(left, right):
    return jnp.dot(left, right, preferred_element_type=jnp.float32)


def inner_rows(left, right):
    return lax.dot_general(
        left, right, (((0,), (0,)), ((), ())), preferred_element_type=jnp.float32
    )


def inner_cols(left, right):
    return lax.dot_general(
        left, right, (((1,), (1,)), ((), ())), preferred_element_type=jnp.float32
    )


def adamw(param, moment, square, grad, rate, decay):
    new_moment = 0.9 * moment + 0.1 * grad
    new_square = 0.999 * square + 0.001 * grad * grad
    corrected = new_moment / (1.0 - 0.9**STEP)
    scaled = jnp.sqrt(new_square / (1.0 - 0.999**STEP)) + 1e-08
    return (param - rate * (corrected / scaled + decay * param), new_moment, new_square)


def head_lanes(shape):
    return lax.broadcasted_iota(jnp.int32, shape, 1) // HEAD_DIM


def window_of(starts_ref, image, length):
    start = starts_ref[image]
    base = jnp.clip(start // 16 * 16, 0, length - WINDOW)
    return (pl.multiple_of(base, 16), start - base)


def image_mask(position, offset):
    return (position >= offset) & (position < offset + IMG_LEN)


def attend_kernel(starts_ref, q_ref, k_ref, v_ref, wide_ref, out_ref, log_ref):
    image, tile = pl.program_id(0), pl.program_id(1)
    length, lanes = q_ref.shape
    base, offset = window_of(starts_ref, image, length)
    rows = pl.ds(pl.multiple_of(base + tile * TILE, 16), TILE)

    @pl.when((image == 0) & (tile == 0))
    def clear():
        wide_ref[...] = jnp.zeros_like(wide_ref)
        out_ref[...] = jnp.zeros_like(out_ref)
        log_ref[...] = jnp.zeros_like(log_ref)

    query = q_ref[rows, :].astype(jnp.float32) * HEAD_DIM ** (-0.5)
    keys = k_ref[pl.ds(base, WINDOW), :]
    values = v_ref[pl.ds(base, WINDOW), :]
    key_ok = image_mask(lax.broadcasted_iota(jnp.int32, (1, WINDOW), 1), offset)
    bias = jnp.where(key_ok, 0.0, masked_score)
    row_ok = image_mask(lax.broadcasted_iota(jnp.int32, (TILE, 1), 0) + tile * TILE, offset)
    head_of = head_lanes((TILE, lanes))
    total_out = jnp.zeros((TILE, lanes), jnp.float32)
    total_log = jnp.zeros((TILE, lanes), jnp.float32)
    for head in range(lanes // HEAD_DIM):
        mine = head_of == head
        part = jnp.where(mine, query, 0.0).astype(jnp.bfloat16)
        scores = inner_cols(part, keys) + bias
        top = jnp.max(scores, axis=1, keepdims=True)
        weights = jnp.exp(scores - top)
        total = jnp.sum(weights, axis=1, keepdims=True)
        probs = (weights * (1.0 / total)).astype(jnp.bfloat16)
        total_out = jnp.where(mine, plain_product(probs, values), total_out)
        total_log = jnp.where(mine, top + jnp.log(total), total_log)
    merged = jnp.where(row_ok, total_out, wide_ref[rows, :])
    wide_ref[rows, :] = merged
    out_ref[rows, :] = merged.astype(jnp.bfloat16)
    log_ref[rows, :] = jnp.where(row_ok, total_log, log_ref[rows, :])


def attend(starts, query, keys, values):
    length, lanes = query.shape
    whole = pl.BlockSpec((length, lanes), lambda image, tile, starts: (0, 0))
    wide = jax.ShapeDtypeStruct((length, lanes), jnp.float32)
    images = length // IMG_LEN
    return pl.pallas_call(
        attend_kernel,
        grid_spec=pltpu.PrefetchScalarGridSpec(
            num_scalar_prefetch=1,
            grid=(images, WINDOW // TILE),
            in_specs=[whole] * 3,
            out_specs=[whole] * 3,
        ),
        out_shape=(wide, jax.ShapeDtypeStruct((length, lanes), jnp.bfloat16), wide),
        compiler_params=pltpu.CompilerParams(
            vmem_limit_bytes=VMEM_BYTES, dimension_semantics=("arbitrary", "arbitrary")
        ),
        cost_estimate=pl.CostEstimate(
            flops=images * WINDOW * WINDOW * lanes * 8,
            bytes_accessed=length * lanes * 16,
            transcendentals=images * WINDOW * WINDOW * lanes // HEAD_DIM,
        ),
        name="attend_forward",
    )(starts, query, keys, values)


def attend_back_kernel(
    starts_ref, q_ref, k_ref, v_ref, wide_ref, log_ref, go_ref, grad_ref, key_acc, value_acc
):
    image, tile = pl.program_id(0), pl.program_id(1)
    length, lanes = q_ref.shape
    base, offset = window_of(starts_ref, image, length)
    rows = pl.ds(pl.multiple_of(base + tile * TILE, 16), TILE)
    window = pl.ds(base, WINDOW)

    @pl.when((image == 0) & (tile == 0))
    def clear():
        grad_ref[...] = jnp.zeros_like(grad_ref)

    @pl.when(tile == 0)
    def clear_sums():
        key_acc[...] = jnp.zeros_like(key_acc)
        value_acc[...] = jnp.zeros_like(value_acc)

    query = q_ref[rows, :].astype(jnp.float32) * HEAD_DIM ** (-0.5)
    keys = k_ref[window, :]
    values = v_ref[window, :]
    key_ok = image_mask(lax.broadcasted_iota(jnp.int32, (1, WINDOW), 1), offset)
    bias = jnp.where(key_ok, 0.0, masked_score)
    row_ok = image_mask(lax.broadcasted_iota(jnp.int32, (TILE, 1), 0) + tile * TILE, offset)
    head_of = head_lanes((TILE, lanes))
    grad_out = jnp.where(row_ok, go_ref[rows, :].astype(jnp.float32), 0.0)
    centre_parts = grad_out * wide_ref[rows, :]
    logs = jnp.where(row_ok, log_ref[rows, :], -masked_score)
    query_grad = jnp.zeros((TILE, lanes), jnp.float32)
    for head in range(lanes // HEAD_DIM):
        mine = head_of == head
        part = jnp.where(mine, query, 0.0).astype(jnp.bfloat16)
        grad_part = jnp.where(mine, grad_out, 0.0).astype(jnp.bfloat16)
        centre = jnp.sum(jnp.where(mine, centre_parts, 0.0), axis=1, keepdims=True)
        log_total = jnp.max(jnp.where(mine, logs, masked_score), axis=1, keepdims=True)
        probs = jnp.exp(inner_cols(part, keys) + bias - log_total)
        grad_probs = inner_cols(grad_part, values)
        grad_scores = (probs * (grad_probs - centre)).astype(jnp.bfloat16)
        query_grad = jnp.where(mine, plain_product(grad_scores, keys), query_grad)
        key_acc[...] += inner_rows(part, grad_scores)
        value_acc[...] += inner_rows(grad_part, probs.astype(jnp.bfloat16))
    old = grad_ref[rows, 0:lanes].astype(jnp.float32)
    merged = jnp.where(row_ok, query_grad * HEAD_DIM ** (-0.5), old)
    grad_ref[rows, 0:lanes] = merged.astype(jnp.bfloat16)

    @pl.when(tile == pl.num_programs(1) - 1)
    def flush():
        inside = image_mask(lax.broadcasted_iota(jnp.int32, (WINDOW, 1), 0), offset)
        for slot, sums in ((1, key_acc), (2, value_acc)):
            columns = slice(slot * lanes, (slot + 1) * lanes)
            old = grad_ref[window, columns].astype(jnp.float32)
            merged = jnp.where(inside, sums[...].T, old)
            grad_ref[window, columns] = merged.astype(jnp.bfloat16)


def attend_back(starts, query, keys, values, wide, logs, grad_out):
    length, lanes = query.shape
    whole = pl.BlockSpec((length, lanes), lambda image, tile, starts: (0, 0))
    images = length // IMG_LEN
    return pl.pallas_call(
        attend_back_kernel,
        grid_spec=pltpu.PrefetchScalarGridSpec(
            num_scalar_prefetch=1,
            grid=(images, WINDOW // TILE),
            in_specs=[whole] * 6,
            out_specs=pl.BlockSpec((length, 3 * lanes), lambda image, tile, starts: (0, 0)),
            scratch_shapes=[pltpu.VMEM((lanes, WINDOW), jnp.float32)] * 2,
        ),
        out_shape=jax.ShapeDtypeStruct((length, 3 * lanes), jnp.bfloat16),
        compiler_params=pltpu.CompilerParams(
            vmem_limit_bytes=VMEM_BYTES, dimension_semantics=("arbitrary", "arbitrary")
        ),
        cost_estimate=pl.CostEstimate(
            flops=images * WINDOW * WINDOW * lanes * 20,
            bytes_accessed=length * lanes * 22,
            transcendentals=images * WINDOW * WINDOW * lanes // HEAD_DIM,
        ),
        name="attend_backward",
    )(starts, query, keys, values, wide, logs, grad_out)


def norm_mix_kernel(pieces, place_ref, own_ref, other_ref, gain_ref, shift_ref, bias_ref, *refs):
    weight = jnp.concatenate(
        [ref[...].reshape(own_ref.shape[1], -1) for ref in refs[:pieces]], axis=1
    )
    a_ref, q_ref, k_ref, v_ref = refs[pieces:]
    lanes = q_ref.shape[1]
    mine = lax.rem(pl.program_id(0), 2) == lax.rem(place_ref[0], 2)
    own, other = own_ref[...].astype(jnp.float32), other_ref[...].astype(jnp.float32)
    normed = layer_norm(jnp.where(mine, own, other), gain_ref[...], shift_ref[...])
    normed = normed.astype(jnp.bfloat16)
    a_ref[...] = normed
    mixed = (plain_product(normed, weight) + bias_ref[...]).astype(jnp.bfloat16)
    q_ref[...] = mixed[:, :lanes]
    k_ref[...] = mixed[:, lanes : 2 * lanes]
    v_ref[...] = mixed[:, 2 * lanes :]


def norm_mix(place, own, other, block, gain, shift, weight, bias):
    length, width = own.shape[0] * 2, own.shape[1]
    lanes = bias.shape[0] // 3
    row = lambda size: pl.BlockSpec((block, size), lambda i, place: (i, 0))
    half = pl.BlockSpec((block, width), lambda i, place: (i // 2, 0))
    fixed = lambda *shape: pl.BlockSpec(shape, lambda i, place: (0, 0))
    part = jax.ShapeDtypeStruct((length, lanes), jnp.bfloat16)
    weights, weight_specs = [weight], [fixed(width, 3 * lanes)]
    return pl.pallas_call(
        functools.partial(norm_mix_kernel, len(weights)),
        grid_spec=pltpu.PrefetchScalarGridSpec(
            num_scalar_prefetch=1,
            grid=(length // block,),
            in_specs=[
                half,
                half,
                fixed(1, width),
                fixed(1, width),
                fixed(1, 3 * lanes),
                *weight_specs,
            ],
            out_specs=[row(width), row(lanes), row(lanes), row(lanes)],
        ),
        out_shape=(jax.ShapeDtypeStruct((length, width), jnp.bfloat16), part, part, part),
        compiler_params=pltpu.CompilerParams(vmem_limit_bytes=VMEM_BYTES),
        cost_estimate=pl.CostEstimate(
            flops=length * width * lanes * 6, bytes_accessed=length * width * 4, transcendentals=0
        ),
        name="norm_mix",
    )(place, own, other, gain[None], shift[None], bias[None], *weights)


def mlp_kernel(pieces, core_ref, own_ref, other_ref, gm_own_ref, gm_other_ref, bias_ref, *refs):
    up_refs, down_refs = refs[:pieces], refs[pieces : 2 * pieces]
    up_grad_ref, down_grad_ref, m_own_ref, m_other_ref, gh_own_ref, gh_other_ref = refs[
        2 * pieces : 2 * pieces + 6
    ]
    bias_grad_ref, h_ref, gm_ref, turned_ref = refs[2 * pieces + 6 :]
    tile = pl.program_id(0)
    rows, width = own_ref.shape
    chips = up_grad_ref.shape[0]
    up_rows = width // chips
    units = bias_ref.shape[1]
    folds = width // units

    @pl.when(tile == 0)
    def clear():
        for ref in (m_own_ref, m_other_ref, gh_own_ref, gh_other_ref):
            ref[...] = jnp.zeros_like(ref)
        h_ref[:rows] = own_ref[...]
        h_ref[rows:] = other_ref[...]
        gm_ref[:rows] = gm_own_ref[...]
        gm_ref[rows:] = gm_other_ref[...]
        turned_ref[...] = h_ref[...].T

    weight_up = jnp.concatenate([ref[...].reshape(width, -1) for ref in up_refs], axis=1)
    weight_down = jnp.concatenate([ref[...].reshape(-1, width) for ref in down_refs], axis=0)
    gm = gm_ref[...]
    upward = plain_product(h_ref[...], weight_up) + bias_ref[...]
    normal = 0.5 * (1.0 + lax.erf(upward * 0.5**0.5))
    slope = normal + upward * jnp.exp(upward * upward * -0.5) * (0.5 / jnp.pi) ** 0.5
    active = (upward * normal).astype(jnp.bfloat16)
    grad_up = (inner_cols(gm, weight_down) * slope).astype(jnp.bfloat16)
    bias_grad_ref[...] = jnp.sum(grad_up.astype(jnp.float32), axis=0, keepdims=True)
    branch = plain_product(active, weight_down)
    m_own_ref[...] += branch[:rows]
    m_other_ref[...] += branch[rows:]
    grad_norm = inner_cols(grad_up, weight_up)
    gh_own_ref[...] += grad_norm[:rows]
    gh_other_ref[...] += grad_norm[rows:]
    up_grad = plain_product(turned_ref[...], grad_up).astype(jnp.bfloat16)
    row = pl.multiple_of(tile // folds * up_rows, up_rows)
    column = pl.multiple_of(lax.rem(tile, folds) * units, units)
    up_grad = up_grad.reshape(chips, up_rows, units)
    up_grad_ref[:, pl.ds(row, up_rows), pl.ds(column, units)] = up_grad
    down_grad = inner_rows(active, gm).astype(jnp.bfloat16)
    down_grad_ref[...] = down_grad.reshape(down_grad_ref.shape)


def mlp(core, own, other, gm_own, gm_other, weights, bias, chips):
    rows, width = own.shape
    half = bias.shape[0]
    unit_block = half // chips
    units = 256
    folds = width // units
    once = dict(pipeline_mode=pl.Buffered(1))
    fixed = pl.BlockSpec((rows, width), lambda j, core: (0, 0), **once)
    if len(weights) == 1:
        count = 2 * chips
        share = width // count
        pieces = units // unit_block
        lane_blocks = width // unit_block

        def up_spec(piece):
            def place(j, core):
                block = 2 * (j * pieces + piece) + core[0]
                return (0, block // lane_blocks, lax.rem(block, lane_blocks))

            return pl.BlockSpec((count, share, unit_block), place)

        def down_spec(piece):
            return pl.BlockSpec(
                (1, unit_block, width), lambda j, core: (2 * (j * pieces + piece) + core[0], 1, 0)
            )

        weights = list(weights) * (2 * pieces)
        weight_specs = [up_spec(n) for n in range(pieces)] + [down_spec(n) for n in range(pieces)]
        up_shape, down_shape = (chips, half // chips, width), (chips, half // chips, width)
        down_grad_spec = pl.BlockSpec((pieces, unit_block, width), lambda j, core: (j, 0, 0))
    else:
        pieces = 1
        weight_specs = [
            pl.BlockSpec((width, units), lambda j, core: (0, j)),
            pl.BlockSpec((units, width), lambda j, core: (j, 0)),
        ]
        up_shape, down_shape = (1, half // width * width, width), (1, half, width)
        down_grad_spec = pl.BlockSpec((1, units, width), lambda j, core: (0, j, 0))
    total = jax.ShapeDtypeStruct((rows, width), jnp.float32)
    outs = pl.pallas_call(
        functools.partial(mlp_kernel, pieces),
        grid_spec=pltpu.PrefetchScalarGridSpec(
            num_scalar_prefetch=1,
            grid=(half // units,),
            in_specs=[fixed] * 4 + [pl.BlockSpec((1, units), lambda j, core: (0, j)), *weight_specs],
            out_specs=[
                pl.BlockSpec(up_shape, lambda j, core: (0, 0, 0), **once),
                down_grad_spec,
                *[fixed] * 4,
                pl.BlockSpec((1, units), lambda j, core: (0, j)),
            ],
            scratch_shapes=[
                pltpu.VMEM((2 * rows, width), jnp.bfloat16),
                pltpu.VMEM((2 * rows, width), jnp.bfloat16),
                pltpu.VMEM((width, 2 * rows), jnp.bfloat16),
            ],
        ),
        out_shape=(
            jax.ShapeDtypeStruct(up_shape, jnp.bfloat16),
            jax.ShapeDtypeStruct(down_shape, jnp.bfloat16),
            *[total] * 4,
            jax.ShapeDtypeStruct((1, half), jnp.float32),
        ),
        compiler_params=pltpu.CompilerParams(vmem_limit_bytes=VMEM_BYTES),
        cost_estimate=pl.CostEstimate(
            flops=2 * rows * width * half * 12,
            bytes_accessed=half * width * 8 + rows * width * 24,
            transcendentals=rows * half * 4,
        ),
        name="mlp_both_ways",
    )(core, own, other, gm_own, gm_other, bias[None], *weights)
    up_grad, down_grad = outs[0], outs[1]
    if pieces == 1:
        up_grad = up_grad.reshape(half // width, chips, width // chips, width).swapaxes(0, 1)
        up_grad = up_grad.reshape(chips, -1, width)
        down_grad = down_grad.reshape(chips, -1, width)
    return (up_grad, down_grad, *outs[2:])


def finish_kernel(
    grad_ref, weight_ref, x_ref, gx_ref, gain_ref, out_ref, gain_grad_ref, shift_grad_ref, sums_ref, acc_ref
):
    step = pl.program_id(0)
    parts = [grad_ref[slot] for slot in range(grad_ref.shape[0])]
    grad = jnp.concatenate(parts, axis=1)
    width = x_ref.shape[1]
    product = inner_cols(grad, weight_ref[...].reshape(width, width))
    sums_ref[...] = jnp.sum(grad.astype(jnp.float32), axis=0, keepdims=True)[None]

    @pl.when(step == 0)
    def begin():
        acc_ref[...] = product

    @pl.when(step > 0)
    def further():
        acc_ref[...] += product

    @pl.when(step == pl.num_programs(0) - 1)
    def end():
        values = x_ref[...].astype(jnp.float32)
        centered = values - jnp.mean(values, axis=1, keepdims=True)
        scale = lax.rsqrt(jnp.mean(centered * centered, axis=1, keepdims=True) + 1e-06)
        unit = centered * scale
        grad_norm = acc_ref[...]
        gain_grad_ref[...] = jnp.sum(grad_norm * unit, axis=0, keepdims=True)
        shift_grad_ref[...] = jnp.sum(grad_norm, axis=0, keepdims=True)
        grad_unit = grad_norm * gain_ref[...]
        mean = jnp.mean(grad_unit, axis=1, keepdims=True)
        slant = jnp.mean(grad_unit * unit, axis=1, keepdims=True)
        out_ref[...] = gx_ref[...] + scale * (grad_unit - mean - unit * slant)


def finish(grads, weights, inputs, gx, gain):
    rows, width = inputs.shape
    group, lanes = grads.shape[0], grads.shape[2] // 3
    if lanes % 128:
        grads = grads.reshape(group, rows, 3, lanes).transpose(2, 0, 1, 3)
        grads = grads.reshape(3 * group, rows, lanes)
        grad_spec = pl.BlockSpec((group, rows, lanes), lambda k: (k, 0, 0))
    else:
        grad_spec = pl.BlockSpec((group, rows, lanes), lambda k: (0, 0, k))
    if weights.ndim == 3:
        share = width // weights.shape[0]
        first = weights.shape[1] // share - 3
        weight_spec = pl.BlockSpec((weights.shape[0], share, width), lambda k: (0, first + k, 0))
    else:
        weight_spec = pl.BlockSpec((width, width), lambda k: (0, k))
    fixed = lambda *shape: pl.BlockSpec(shape, lambda k: (0, 0))
    vector = jax.ShapeDtypeStruct((1, width), jnp.float32)
    return pl.pallas_call(
        finish_kernel,
        grid=(3,),
        in_specs=[
            grad_spec,
            weight_spec,
            fixed(rows, width),
            fixed(rows, width),
            fixed(1, width),
        ],
        out_specs=[
            fixed(rows, width),
            fixed(1, width),
            fixed(1, width),
            pl.BlockSpec((1, 1, width), lambda k: (k, 0, 0)),
        ],
        out_shape=(
            jax.ShapeDtypeStruct((rows, width), jnp.float32),
            vector,
            vector,
            jax.ShapeDtypeStruct((3, 1, width), jnp.float32),
        ),
        scratch_shapes=[pltpu.VMEM((rows, width), jnp.float32)],
        compiler_params=pltpu.CompilerParams(vmem_limit_bytes=VMEM_BYTES),
        cost_estimate=pl.CostEstimate(
            flops=rows * width * width * 6, bytes_accessed=width * width * 16, transcendentals=0
        ),
        name="finish_input",
    )(grads, weights, inputs, gx, gain[None])


def swap_cores(value):
    return lax.ppermute(value, "core", [(0, 1), (1, 0)])


def line_pairs(size, sign, step):
    pairs = [(i, i - sign) for i in range(size) if 0 <= i - sign < size]
    return [(i, j) for i, j in pairs if 0 <= i + sign * (step - 1) < size]


def line_pieces(value, axis):
    size = lax.axis_size(axis)
    if size == 2:
        other = lax.ppermute(value, axis, [(0, 1), (1, 0)])
        return [(None, other)]
    pieces = []
    for sign in (-1, 1):
        moving = value
        for step in range(1, size):
            moving = lax.ppermute(moving, axis, line_pairs(size, sign, step))
            pieces.append((sign * step, moving))
    return pieces


def line_order(value, pieces, axis):
    place = lax.axis_index(axis)
    size = lax.axis_size(axis)
    if size == 2:
        other = pieces[0][1]
        return jnp.where(place == 0, jnp.stack([value, other]), jnp.stack([other, value]))
    whole = jnp.zeros((size, *value.shape), value.dtype)
    for distance, piece in sorted(pieces, key=lambda item: -abs(item[0])) + [(0, value)]:
        slot = jnp.clip(place + distance, 0, size - 1)
        whole = lax.dynamic_update_index_in_dim(whole, piece, slot, 0)
    return whole


def gather_line(value, axis):
    return line_order(value, line_pieces(value, axis), axis)


def exchange_line(value, axis):
    place = lax.axis_index(axis)
    size = lax.axis_size(axis)
    pick = lambda slot: lax.dynamic_index_in_dim(
        value, jnp.clip(slot, 0, size - 1), 0, keepdims=False
    )
    pieces = []
    for distance in range(1, size):
        for move in (-distance, distance):
            pairs = [(i, i + move) for i in range(size) if 0 <= i + move < size]
            pieces.append((-move, lax.ppermute(pick(place + move), axis, pairs)))
    if size == 2:
        pieces = [(None, pieces[0][1] + pieces[1][1])]
    return line_order(pick(place), pieces, axis)


def rounded_sum(*terms):
    return sum(term.astype(jnp.float32) for term in terms).astype(jnp.bfloat16)


def scatter_terms(value, axis, dim):
    if lax.axis_size(axis) != 2:
        return (scatter_line(value, axis, dim),)
    place = lax.axis_index(axis)
    pick = lambda slot: lax.dynamic_index_in_dim(value, slot, dim, keepdims=False)
    return (pick(place), lax.ppermute(pick(1 - place), axis, [(0, 1), (1, 0)]))


def scatter_payload(value, axis, moving, step):
    place = lax.axis_index(axis)
    size = lax.axis_size(axis)
    payload = []
    for n, sign in enumerate((-1, 1)):
        slot = jnp.clip(place - sign * (size - step), 0, size - 1)
        own = lax.dynamic_index_in_dim(value, slot, 0, keepdims=False)
        payload.append(own if moving is None else rounded_sum(own, moving[n]))
    return tuple(payload)


def scatter_send(payload, axis, step):
    size = lax.axis_size(axis)
    sums = []
    for value, sign in zip(payload, (-1, 1)):
        start = 0 if sign < 0 else size - 1
        pairs = [(i, i - sign) for i in range(size) if 0 <= i - sign < size]
        pairs = [(i, j) for i, j in pairs if abs(i - start) <= step - 1]
        sums.append(lax.ppermute(value, axis, pairs))
    return tuple(sums)


def scatter_line(value, axis, dim):
    place = lax.axis_index(axis)
    size = lax.axis_size(axis)
    pick = lambda slot: lax.dynamic_index_in_dim(
        value, jnp.clip(slot, 0, size - 1), dim, keepdims=False
    )
    if size == 2:
        return rounded_sum(pick(place), lax.ppermute(pick(1 - place), axis, [(0, 1), (1, 0)]))
    sums = []
    for sign in (-1, 1):
        moving = None
        for step in range(1, size):
            start = 0 if sign < 0 else size - 1
            pairs = [(i, i - sign) for i in range(size) if 0 <= i - sign < size]
            pairs = [(i, j) for i, j in pairs if abs(i - start) <= step - 1]
            own = pick(place - sign * (size - step))
            payload = own if moving is None else rounded_sum(own, moving)
            moving = lax.ppermute(payload, axis, pairs)
        sums.append(moving)
    return rounded_sum(pick(place), *sums)


def on_device(
    tokens,
    cotangent,
    segment_ids,
    valid,
    project_in,
    project_out,
    hidden_up,
    hidden_down,
    gains_biases,
    moment_in,
    moment_out,
    moment_up,
    moment_down,
    moment_gains,
    square_in,
    square_out,
    square_up,
    square_down,
    square_gains,
):
    rows = tokens.shape[0]
    width = tokens.shape[1]
    everyone = ("outer", "inner", "line", "core")
    planes = ("outer", "inner")
    seq = ("line", "core")
    streams, line = lax.axis_size(planes), lax.axis_size("line")
    group = 2 * line
    count = streams * group
    chips = streams * line
    share = width // count
    lanes = width // group
    length = rows * group
    images = length // IMG_LEN
    core = lax.axis_index("core")
    first_core = core == 0

    def in_order(own, other, axis):
        return jnp.concatenate(
            [jnp.where(first_core, own, other), jnp.where(first_core, other, own)], axis=axis
        )

    half = FF // 2
    unit_block = FF // count
    folds = half // width
    up_end = 2 * share * folds
    low = lambda value: value.astype(jnp.bfloat16)
    direct = share % 16 == 0 and unit_block == 128 and line > 3
    position = lax.broadcasted_iota(jnp.int32, (images, rows), 1)
    found = (segment_ids[None, :] == lax.broadcasted_iota(jnp.int32, (images, rows), 0)) & (
        valid[None, :] == 1
    )
    first = jnp.min(jnp.where(found, position, rows), axis=1)
    small = jnp.concatenate([low(gains_biases).reshape(-1), low(first // 32), low(first % 32)])
    fold = lambda value: low(value).reshape(share, -1, width).swapaxes(0, 1).reshape(-1, width)
    if direct:
        extra = 16
        small = jnp.pad(small, (0, extra * 3 * lanes - small.shape[0]))
        small = jnp.broadcast_to(small.reshape(1, extra, 3 * lanes), (group, extra, 3 * lanes))
        owned = low(project_in).reshape(share, 3, group, lanes).transpose(2, 0, 1, 3)
        blocks = jnp.concatenate([owned.reshape(group, share, 3 * lanes), small], axis=1)
        blocks = blocks.reshape(line, 2, share + extra, 3 * lanes)
        keep = jnp.where(first_core, blocks[:, 0], blocks[:, 1])
        sent = swap_cores(jnp.where(first_core, blocks[:, 1], blocks[:, 0]))
        blocks = in_order(keep[:, None], sent[:, None], 1)

        pieces, swapped = [], []
        moving = [tokens, tokens]
        for step in range(1, line):
            moving = [
                lax.ppermute(value, "line", line_pairs(line, sign, step))
                for sign, value in zip((-1, 1), moving)
            ]
            if step == 1:
                blocks = exchange_line(blocks, "line")
            elif step == 2:
                blocks = gather_line(gather_line(blocks, "inner"), "outer")
            moving, blocks, swapped = lax.optimization_barrier((moving, blocks, swapped))
            pieces += [(sign * step, value) for sign, value in zip((-1, 1), moving)]
            if step == line - 1:
                packed = jnp.concatenate([fold(hidden_up), low(hidden_down), low(project_out)], axis=0)
                packed, moving = lax.optimization_barrier((packed, moving))
                gathered = lax.all_gather(packed, everyone, axis=0, tiled=False)
            swapped = swapped + [swap_cores(value) for value in moving]
        swapped = [(distance, value) for (distance, _), value in zip(pieces, swapped)]
        whole_out = gathered[:, packed.shape[0] - share :].reshape(width, width)
        mlp_weights = (gathered,)
        whole_in = lax.all_gather(fold(project_in), everyone, axis=0, tiled=False)
        blocks = blocks.reshape(count, share + extra, 3 * lanes)
        mine_in = blocks[:, :share].reshape(width, 3 * lanes)
        small = blocks[:, share:].reshape(count, -1)
    else:
        whole_in = lax.all_gather(low(project_in), everyone, axis=0, tiled=True)
        mine_in = lax.dynamic_index_in_dim(
            whole_in.reshape(width, 3, group, lanes), lax.axis_index(seq), axis=2, keepdims=False
        ).reshape(width, 3 * lanes)
        small = lax.all_gather(small, everyone, axis=0, tiled=False)
    vector_size = gains_biases.size
    vectors = small[:, :vector_size].reshape(count, -1, share).transpose(1, 0, 2)
    vectors = vectors.reshape(-1, width).astype(jnp.float32)
    first = small[:, vector_size : vector_size + 2 * images].astype(jnp.int32)
    first = first[:, :images] * 32 + first[:, images:]
    first = lax.dynamic_slice_in_dim(first, lax.axis_index(planes) * group, group, 0)
    offsets = lax.broadcasted_iota(jnp.int32, (group, images), 0) * rows
    starts = jnp.min(jnp.where(first < rows, first + offsets, length), axis=0)

    if not direct:
        pieces = line_pieces(tokens, "line")
        swapped = [(distance, swap_cores(piece)) for distance, piece in pieces]
    own_tokens = line_order(tokens, pieces, "line").reshape(-1, width)
    other_tokens = line_order(swap_cores(tokens), swapped, "line").reshape(-1, width)

    gain_one, shift_one, bias_query, bias_value, bias_out = (
        vectors[0],
        vectors[1],
        vectors[2],
        vectors[3],
        vectors[4],
    )
    scale_one, gain_two, shift_two, bias_down, scale_two = (
        vectors[5],
        vectors[6],
        vectors[7],
        vectors[8],
        vectors[9],
    )
    bias_up = lax.dynamic_index_in_dim(
        vectors[10:].reshape(chips, 2, unit_block), core, axis=1, keepdims=False
    ).reshape(half)
    column = lax.axis_index(seq) * lanes
    bias_in = jnp.concatenate(
        [
            lax.dynamic_slice_in_dim(bias_query, column, lanes, 0),
            jnp.zeros((lanes,), jnp.float32),
            lax.dynamic_slice_in_dim(bias_value, column, lanes, 0),
        ]
    )
    grad_rows = cotangent.astype(jnp.float32) * valid.astype(jnp.float32)[:, None]
    grad_branch = (scale_two * grad_rows).astype(jnp.bfloat16)

    place = lax.axis_index(seq)
    normed_one, query, keys, values = norm_mix(
        place.reshape(1), own_tokens, other_tokens, rows, gain_one, shift_one, mine_in, bias_in
    )
    wide, attended, logs = attend(starts, query, keys, values)
    if not direct:
        whole_out, whole_up, whole_down = (
            lax.all_gather(low(value), everyone, axis=0, tiled=True)
            for value in (project_out, hidden_up, hidden_down)
        )
        block = jnp.arange(half) // unit_block * 2 + core
        index = block * unit_block + lax.rem(jnp.arange(half), unit_block)
        mlp_weights = (jnp.take(whole_up, index, axis=1), jnp.take(whole_down, index, axis=0))
    returned = lax.all_to_all(
        attended.reshape(group, rows, lanes), seq, split_axis=0, concat_axis=0, tiled=True
    )
    attended_rows = returned.transpose(1, 0, 2).reshape(rows, width)
    inputs = tokens.astype(jnp.float32)
    projected = plain_product(attended_rows, whole_out) + bias_out
    second = inputs + scale_one * projected
    norm_two, norm_two_back = jax.vjp(layer_norm, second, gain_two, shift_two)
    normed_two = norm_two.astype(jnp.bfloat16)
    grad_up, grad_down, branch, branch_other, grad_norm_two, grad_norm_other, grad_bias_up = mlp(
        core.reshape(1),
        normed_two,
        swap_cores(normed_two),
        grad_branch,
        swap_cores(grad_branch),
        mlp_weights,
        bias_up,
        chips,
    )
    grad_norm_two = grad_norm_two + swap_cores(grad_norm_other)
    branch = branch + swap_cores(branch_other) + bias_down
    block_output = (second + scale_two * branch).astype(jnp.bfloat16)
    grad_scale_two = jnp.sum(grad_rows * branch, axis=0)
    grad_bias_down = jnp.sum(grad_branch.astype(jnp.float32), axis=0)
    second_part, grad_gain_two, grad_shift_two = norm_two_back(grad_norm_two)
    grad_second = grad_rows + second_part
    grad_scale_one = jnp.sum(grad_second * projected, axis=0)
    grad_projected = (scale_one * grad_second).astype(jnp.bfloat16)
    grad_bias_out = jnp.sum(grad_projected.astype(jnp.float32), axis=0)
    grad_attended = inner_cols(grad_projected, whole_out).astype(jnp.bfloat16)
    grad_stream = lax.all_to_all(
        grad_attended.reshape(rows, group, lanes).transpose(1, 0, 2),
        seq,
        split_axis=0,
        concat_axis=0,
        tiled=True,
    ).reshape(length, lanes)
    grad_out = inner_rows(attended_rows, grad_projected).astype(jnp.bfloat16)
    grad_out = grad_out.reshape(chips, 2 * share, width)
    outer, inner = lax.axis_size("outer"), lax.axis_size("inner")
    grad_up, grad_out, grad_down = (
        value.reshape(outer, inner, line, -1, width) for value in (grad_up, grad_out, grad_down)
    )
    begun = (
        scatter_terms(grad_up, "inner", 1),
        scatter_terms(grad_out, "inner", 1),
        scatter_terms(grad_down, "outer", 0),
    )
    out_terms, whole_in, grad_stream = lax.optimization_barrier((begun[1], whole_in, grad_stream))
    begun = (begun[0], out_terms, begun[2])
    grad_mixed_stream = attend_back(starts, query, keys, values, wide, logs, grad_stream)
    grad_mixed = lax.all_to_all(
        grad_mixed_stream.reshape(group, rows, 3 * lanes), seq, split_axis=0, concat_axis=0, tiled=True
    )
    begun, grad_mixed_stream = lax.optimization_barrier((begun, grad_mixed_stream))
    grad_up, grad_out, grad_down = (rounded_sum(*terms) for terms in begun)
    grad_down = scatter_line(grad_down, "inner", 0)
    grad_up = scatter_line(jnp.concatenate([grad_up, grad_out], axis=2), "outer", 0)
    plane_sums = jnp.concatenate([grad_up, grad_down], axis=1)
    moving = scatter_send(scatter_payload(plane_sums, "line", None, 1), "line", 1)
    moving, grad_mixed = lax.optimization_barrier((moving, grad_mixed))
    grad_in = inner_rows(normed_one, grad_mixed_stream).astype(jnp.bfloat16)
    parts = grad_in.reshape(outer, inner, group * share, 3 * lanes)
    parts = scatter_line(scatter_line(parts, "inner", 1), "outer", 0)
    input_grad, grad_gain_one, grad_shift_one, mixed_sums = finish(
        grad_mixed, whole_in, tokens, grad_second, gain_one
    )
    for step in range(2, line):
        payload = scatter_payload(plane_sums, "line", moving, step)
        if step == 3:
            payload, parts, grad_gain_one = lax.optimization_barrier((payload, parts, grad_gain_one))
        moving = scatter_send(payload, "line", step)
    summed = rounded_sum(
        lax.dynamic_index_in_dim(plane_sums, lax.axis_index("line"), 0, keepdims=False), *moving
    )
    parts = parts.reshape(group, share, 3 * lanes)
    parts = lax.all_to_all(parts, seq, split_axis=0, concat_axis=0, tiled=True)
    parts = parts.astype(jnp.float32)
    summed_in = parts.reshape(group, share, 3, lanes).transpose(1, 2, 0, 3).reshape(share, 3 * width)
    up_sums = grad_bias_up.reshape(chips, unit_block)
    up_sums = jnp.where(
        (lax.broadcasted_iota(jnp.int32, (1, 2, 1), 1) == core), up_sums[:, None, :], 0.0
    )
    grad_small = jnp.concatenate(
        [
            jnp.stack(
                [
                    grad_gain_one[0],
                    grad_shift_one[0],
                    mixed_sums[0, 0],
                    mixed_sums[2, 0],
                    grad_bias_out,
                    grad_scale_one,
                    grad_gain_two,
                    grad_shift_two,
                    grad_bias_down,
                    grad_scale_two,
                ]
            ),
            up_sums.reshape(-1, width),
        ],
        axis=0,
    )
    small_rows = grad_small.shape[0]
    parts = grad_small.reshape(small_rows, count, share).transpose(1, 0, 2)
    parts = lax.all_to_all(
        parts.reshape(count, small_rows * share), everyone, split_axis=0, concat_axis=0, tiled=True
    )
    summed_gains = jnp.sum(parts, axis=0).reshape(small_rows, share)

    up_sum = summed[:up_end].reshape(folds, 2, share, width)
    out_sum = summed[up_end : up_end + 2 * share].reshape(1, 2, share, width)
    both_sums = jnp.concatenate([up_sum, out_sum], axis=0)
    own_sums = jnp.where(first_core, both_sums[:, 0], both_sums[:, 1])
    other_sums = swap_cores(jnp.where(first_core, both_sums[:, 1], both_sums[:, 0]))
    summed_down = summed[up_end + 2 * share :].astype(jnp.float32)
    summed_out = own_sums[folds].astype(jnp.float32) + other_sums[folds].astype(jnp.float32)
    own_up = own_sums[:folds].transpose(1, 0, 2).reshape(share, chips, 1, unit_block)
    other_up = other_sums[:folds].transpose(1, 0, 2).reshape(share, chips, 1, unit_block)
    summed_up = in_order(own_up, other_up, 2).reshape(share, FF).astype(jnp.float32)
    rate_out = max(1, 4 * D // IMG_LEN) ** (-0.5)
    new_in, new_moment_in, new_square_in = adamw(
        project_in, moment_in, square_in, summed_in, D ** (-0.5), 0.04
    )
    new_out, new_moment_out, new_square_out = adamw(
        project_out, moment_out, square_out, summed_out, rate_out, 0.04
    )
    new_up, new_moment_up, new_square_up = adamw(
        hidden_up, moment_up, square_up, summed_up, D ** (-0.5), 0.04
    )
    new_down, new_moment_down, new_square_down = adamw(
        hidden_down, moment_down, square_down, summed_down, FF ** (-0.5), 0.04
    )
    new_gains, new_moment_gains, new_square_gains = adamw(
        gains_biases, moment_gains, square_gains, summed_gains, 0.2, 0.0
    )
    return (
        block_output,
        input_grad,
        new_in,
        new_out,
        new_up,
        new_down,
        new_gains,
        new_moment_in,
        new_moment_out,
        new_moment_up,
        new_moment_down,
        new_moment_gains,
        new_square_in,
        new_square_out,
        new_square_up,
        new_square_down,
        new_square_gains,
        summed_gains[8],
    )


def solution(mesh):
    streams, group = mesh.shape["fsdp"], mesh.shape["seq"]
    outer = math.isqrt(streams)
    fine = jax.sharding.Mesh(
        mesh.devices.reshape(outer, streams // outer, group // 2, 2),
        ("outer", "inner", "line", "core"),
    )
    return jax.shard_map(
        on_device,
        mesh=fine,
        in_specs=(
            P(("outer", "inner", "line", "core"), None),
            P(("outer", "inner", "line", "core"), None),
            P(("outer", "inner", "line", "core")),
            P(("outer", "inner", "line", "core")),
            P(("outer", "inner", "line", "core"), None),
            P(("outer", "inner", "line", "core"), None),
            P(("outer", "inner", "line", "core"), None),
            P(("outer", "inner", "line", "core"), None),
            P(None, ("outer", "inner", "line", "core")),
            P(("outer", "inner", "line", "core"), None),
            P(("outer", "inner", "line", "core"), None),
            P(("outer", "inner", "line", "core"), None),
            P(("outer", "inner", "line", "core"), None),
            P(None, ("outer", "inner", "line", "core")),
            P(("outer", "inner", "line", "core"), None),
            P(("outer", "inner", "line", "core"), None),
            P(("outer", "inner", "line", "core"), None),
            P(("outer", "inner", "line", "core"), None),
            P(None, ("outer", "inner", "line", "core")),
        ),
        out_specs=(
            P(("outer", "inner", "line", "core"), None),
            P(("outer", "inner", "line", "core"), None),
            P(("outer", "inner", "line", "core"), None),
            P(("outer", "inner", "line", "core"), None),
            P(("outer", "inner", "line", "core"), None),
            P(("outer", "inner", "line", "core"), None),
            P(None, ("outer", "inner", "line", "core")),
            P(("outer", "inner", "line", "core"), None),
            P(("outer", "inner", "line", "core"), None),
            P(("outer", "inner", "line", "core"), None),
            P(("outer", "inner", "line", "core"), None),
            P(None, ("outer", "inner", "line", "core")),
            P(("outer", "inner", "line", "core"), None),
            P(("outer", "inner", "line", "core"), None),
            P(("outer", "inner", "line", "core"), None),
            P(("outer", "inner", "line", "core"), None),
            P(None, ("outer", "inner", "line", "core")),
            P(("outer", "inner", "line", "core")),
        ),
        check_vma=False,
    )
```

```python
import functools
import math

import jax
import jax.numpy as jnp
from jax import lax
from jax.experimental import pallas as pl
from jax.experimental.pallas import tpu as pltpu
from jax.sharding import PartitionSpec as P

D = 1024
FF = 4096
HEADS = 16
HEAD_DIM = 64
IMG_LEN = 1370
WINDOW = 1408
TILE = 352
VMEM_BYTES = 56 * 1024 * 1024
STEP = 10


masked_score = -1e30


def layer_norm(values, gain, shift):
    average = jnp.mean(values, axis=-1, keepdims=True)
    centered = values - average
    variance = jnp.mean(centered * centered, axis=-1, keepdims=True)
    return centered * lax.rsqrt(variance + 1e-06) * gain + shift


def exact_gelu(values):
    return jax.nn.gelu(values, approximate=False)


def plain_product(left, right):
    return jnp.dot(left, right, preferred_element_type=jnp.float32)


def inner_rows(left, right):
    return lax.dot_general(
        left, right, (((0,), (0,)), ((), ())), preferred_element_type=jnp.float32
    )


def inner_cols(left, right):
    return lax.dot_general(
        left, right, (((1,), (1,)), ((), ())), preferred_element_type=jnp.float32
    )


def adamw(param, moment, square, grad, rate, decay):
    new_moment = 0.9 * moment + 0.1 * grad
    new_square = 0.999 * square + 0.001 * grad * grad
    corrected = new_moment / (1.0 - 0.9**STEP)
    scaled = jnp.sqrt(new_square / (1.0 - 0.999**STEP)) + 1e-08
    return (param - rate * (corrected / scaled + decay * param), new_moment, new_square)


def head_lanes(shape):
    return lax.broadcasted_iota(jnp.int32, shape, 1) // HEAD_DIM


def window_of(starts_ref, image, length):
    start = starts_ref[image]
    base = jnp.clip(start // 16 * 16, 0, length - WINDOW)
    return (pl.multiple_of(base, 16), start - base)


def image_mask(position, offset):
    return (position >= offset) & (position < offset + IMG_LEN)


def attend_kernel(starts_ref, q_ref, k_ref, v_ref, wide_ref, out_ref, log_ref):
    image, tile = pl.program_id(0), pl.program_id(1)
    length, lanes = q_ref.shape
    base, offset = window_of(starts_ref, image, length)
    rows = pl.ds(pl.multiple_of(base + tile * TILE, 16), TILE)

    @pl.when((image == 0) & (tile == 0))
    def clear():
        wide_ref[...] = jnp.zeros_like(wide_ref)
        out_ref[...] = jnp.zeros_like(out_ref)
        log_ref[...] = jnp.zeros_like(log_ref)

    query = q_ref[rows, :].astype(jnp.float32) * HEAD_DIM ** (-0.5)
    keys = k_ref[pl.ds(base, WINDOW), :]
    values = v_ref[pl.ds(base, WINDOW), :]
    key_ok = image_mask(lax.broadcasted_iota(jnp.int32, (1, WINDOW), 1), offset)
    bias = jnp.where(key_ok, 0.0, masked_score)
    row_ok = image_mask(lax.broadcasted_iota(jnp.int32, (TILE, 1), 0) + tile * TILE, offset)
    head_of = head_lanes((TILE, lanes))
    total_out = jnp.zeros((TILE, lanes), jnp.float32)
    total_log = jnp.zeros((TILE, lanes), jnp.float32)
    for head in range(lanes // HEAD_DIM):
        mine = head_of == head
        part = jnp.where(mine, query, 0.0).astype(jnp.bfloat16)
        scores = inner_cols(part, keys) + bias
        top = jnp.max(scores, axis=1, keepdims=True)
        weights = jnp.exp(scores - top)
        total = jnp.sum(weights, axis=1, keepdims=True)
        probs = (weights * (1.0 / total)).astype(jnp.bfloat16)
        total_out = jnp.where(mine, plain_product(probs, values), total_out)
        total_log = jnp.where(mine, top + jnp.log(total), total_log)
    merged = jnp.where(row_ok, total_out, wide_ref[rows, :])
    wide_ref[rows, :] = merged
    out_ref[rows, :] = merged.astype(jnp.bfloat16)
    log_ref[rows, :] = jnp.where(row_ok, total_log, log_ref[rows, :])


def attend(starts, query, keys, values):
    length, lanes = query.shape
    whole = pl.BlockSpec((length, lanes), lambda image, tile, starts: (0, 0))
    wide = jax.ShapeDtypeStruct((length, lanes), jnp.float32)
    images = length // IMG_LEN
    return pl.pallas_call(
        attend_kernel,
        grid_spec=pltpu.PrefetchScalarGridSpec(
            num_scalar_prefetch=1,
            grid=(images, WINDOW // TILE),
            in_specs=[whole] * 3,
            out_specs=[whole] * 3,
        ),
        out_shape=(wide, jax.ShapeDtypeStruct((length, lanes), jnp.bfloat16), wide),
        compiler_params=pltpu.CompilerParams(
            vmem_limit_bytes=VMEM_BYTES, dimension_semantics=("arbitrary", "arbitrary")
        ),
        cost_estimate=pl.CostEstimate(
            flops=images * WINDOW * WINDOW * lanes * 8,
            bytes_accessed=length * lanes * 16,
            transcendentals=images * WINDOW * WINDOW * lanes // HEAD_DIM,
        ),
        name="attend_forward",
    )(starts, query, keys, values)


def attend_back_kernel(
    starts_ref, q_ref, k_ref, v_ref, wide_ref, log_ref, go_ref, grad_ref, key_acc, value_acc
):
    image, tile = pl.program_id(0), pl.program_id(1)
    length, lanes = q_ref.shape
    base, offset = window_of(starts_ref, image, length)
    rows = pl.ds(pl.multiple_of(base + tile * TILE, 16), TILE)
    window = pl.ds(base, WINDOW)

    @pl.when((image == 0) & (tile == 0))
    def clear():
        grad_ref[...] = jnp.zeros_like(grad_ref)

    @pl.when(tile == 0)
    def clear_sums():
        key_acc[...] = jnp.zeros_like(key_acc)
        value_acc[...] = jnp.zeros_like(value_acc)

    query = q_ref[rows, :].astype(jnp.float32) * HEAD_DIM ** (-0.5)
    keys = k_ref[window, :]
    values = v_ref[window, :]
    key_ok = image_mask(lax.broadcasted_iota(jnp.int32, (1, WINDOW), 1), offset)
    bias = jnp.where(key_ok, 0.0, masked_score)
    row_ok = image_mask(lax.broadcasted_iota(jnp.int32, (TILE, 1), 0) + tile * TILE, offset)
    head_of = head_lanes((TILE, lanes))
    grad_out = jnp.where(row_ok, go_ref[rows, :].astype(jnp.float32), 0.0)
    centre_parts = grad_out * wide_ref[rows, :]
    logs = jnp.where(row_ok, log_ref[rows, :], -masked_score)
    query_grad = jnp.zeros((TILE, lanes), jnp.float32)
    for head in range(lanes // HEAD_DIM):
        mine = head_of == head
        part = jnp.where(mine, query, 0.0).astype(jnp.bfloat16)
        grad_part = jnp.where(mine, grad_out, 0.0).astype(jnp.bfloat16)
        centre = jnp.sum(jnp.where(mine, centre_parts, 0.0), axis=1, keepdims=True)
        log_total = jnp.max(jnp.where(mine, logs, masked_score), axis=1, keepdims=True)
        probs = jnp.exp(inner_cols(part, keys) + bias - log_total)
        grad_probs = inner_cols(grad_part, values)
        grad_scores = (probs * (grad_probs - centre)).astype(jnp.bfloat16)
        query_grad = jnp.where(mine, plain_product(grad_scores, keys), query_grad)
        key_acc[...] += inner_rows(part, grad_scores)
        value_acc[...] += inner_rows(grad_part, probs.astype(jnp.bfloat16))
    old = grad_ref[rows, 0:lanes].astype(jnp.float32)
    merged = jnp.where(row_ok, query_grad * HEAD_DIM ** (-0.5), old)
    grad_ref[rows, 0:lanes] = merged.astype(jnp.bfloat16)

    @pl.when(tile == pl.num_programs(1) - 1)
    def flush():
        inside = image_mask(lax.broadcasted_iota(jnp.int32, (WINDOW, 1), 0), offset)
        for slot, sums in ((1, key_acc), (2, value_acc)):
            columns = slice(slot * lanes, (slot + 1) * lanes)
            old = grad_ref[window, columns].astype(jnp.float32)
            merged = jnp.where(inside, sums[...].T, old)
            grad_ref[window, columns] = merged.astype(jnp.bfloat16)


def attend_back(starts, query, keys, values, wide, logs, grad_out):
    length, lanes = query.shape
    whole = pl.BlockSpec((length, lanes), lambda image, tile, starts: (0, 0))
    images = length // IMG_LEN
    return pl.pallas_call(
        attend_back_kernel,
        grid_spec=pltpu.PrefetchScalarGridSpec(
            num_scalar_prefetch=1,
            grid=(images, WINDOW // TILE),
            in_specs=[whole] * 6,
            out_specs=pl.BlockSpec((length, 3 * lanes), lambda image, tile, starts: (0, 0)),
            scratch_shapes=[pltpu.VMEM((lanes, WINDOW), jnp.float32)] * 2,
        ),
        out_shape=jax.ShapeDtypeStruct((length, 3 * lanes), jnp.bfloat16),
        compiler_params=pltpu.CompilerParams(
            vmem_limit_bytes=VMEM_BYTES, dimension_semantics=("arbitrary", "arbitrary")
        ),
        cost_estimate=pl.CostEstimate(
            flops=images * WINDOW * WINDOW * lanes * 20,
            bytes_accessed=length * lanes * 22,
            transcendentals=images * WINDOW * WINDOW * lanes // HEAD_DIM,
        ),
        name="attend_backward",
    )(starts, query, keys, values, wide, logs, grad_out)


def norm_mix_kernel(pieces, place_ref, own_ref, other_ref, gain_ref, shift_ref, bias_ref, *refs):
    weight = jnp.concatenate(
        [ref[...].reshape(own_ref.shape[1], -1) for ref in refs[:pieces]], axis=1
    )
    a_ref, q_ref, k_ref, v_ref = refs[pieces:]
    lanes = q_ref.shape[1]
    mine = lax.rem(pl.program_id(0), 2) == lax.rem(place_ref[0], 2)
    own, other = own_ref[...].astype(jnp.float32), other_ref[...].astype(jnp.float32)
    normed = layer_norm(jnp.where(mine, own, other), gain_ref[...], shift_ref[...])
    normed = normed.astype(jnp.bfloat16)
    a_ref[...] = normed
    mixed = (plain_product(normed, weight) + bias_ref[...]).astype(jnp.bfloat16)
    q_ref[...] = mixed[:, :lanes]
    k_ref[...] = mixed[:, lanes : 2 * lanes]
    v_ref[...] = mixed[:, 2 * lanes :]


def norm_mix(place, own, other, block, gain, shift, weight, bias):
    length, width = own.shape[0] * 2, own.shape[1]
    lanes = bias.shape[0] // 3
    row = lambda size: pl.BlockSpec((block, size), lambda i, place: (i, 0))
    half = pl.BlockSpec((block, width), lambda i, place: (i // 2, 0))
    fixed = lambda *shape: pl.BlockSpec(shape, lambda i, place: (0, 0))
    part = jax.ShapeDtypeStruct((length, lanes), jnp.bfloat16)
    weights, weight_specs = [weight], [fixed(width, 3 * lanes)]
    return pl.pallas_call(
        functools.partial(norm_mix_kernel, len(weights)),
        grid_spec=pltpu.PrefetchScalarGridSpec(
            num_scalar_prefetch=1,
            grid=(length // block,),
            in_specs=[
                half,
                half,
                fixed(1, width),
                fixed(1, width),
                fixed(1, 3 * lanes),
                *weight_specs,
            ],
            out_specs=[row(width), row(lanes), row(lanes), row(lanes)],
        ),
        out_shape=(jax.ShapeDtypeStruct((length, width), jnp.bfloat16), part, part, part),
        compiler_params=pltpu.CompilerParams(vmem_limit_bytes=VMEM_BYTES),
        cost_estimate=pl.CostEstimate(
            flops=length * width * lanes * 6, bytes_accessed=length * width * 4, transcendentals=0
        ),
        name="norm_mix",
    )(place, own, other, gain[None], shift[None], bias[None], *weights)


def mlp_kernel(pieces, core_ref, own_ref, other_ref, gm_own_ref, gm_other_ref, bias_ref, *refs):
    up_refs, down_refs = refs[:pieces], refs[pieces : 2 * pieces]
    up_grad_ref, down_grad_ref, m_own_ref, m_other_ref, gh_own_ref, gh_other_ref = refs[
        2 * pieces : 2 * pieces + 6
    ]
    bias_grad_ref, h_ref, gm_ref, turned_ref = refs[2 * pieces + 6 :]
    tile = pl.program_id(0)
    rows, width = own_ref.shape
    chips = up_grad_ref.shape[0]
    up_rows = width // chips
    units = bias_ref.shape[1]
    folds = width // units

    @pl.when(tile == 0)
    def clear():
        for ref in (m_own_ref, m_other_ref, gh_own_ref, gh_other_ref):
            ref[...] = jnp.zeros_like(ref)
        h_ref[:rows] = own_ref[...]
        h_ref[rows:] = other_ref[...]
        gm_ref[:rows] = gm_own_ref[...]
        gm_ref[rows:] = gm_other_ref[...]
        turned_ref[...] = h_ref[...].T

    weight_up = jnp.concatenate([ref[...].reshape(width, -1) for ref in up_refs], axis=1)
    weight_down = jnp.concatenate([ref[...].reshape(-1, width) for ref in down_refs], axis=0)
    gm = gm_ref[...]
    upward = plain_product(h_ref[...], weight_up) + bias_ref[...]
    normal = 0.5 * (1.0 + lax.erf(upward * 0.5**0.5))
    slope = normal + upward * jnp.exp(upward * upward * -0.5) * (0.5 / jnp.pi) ** 0.5
    active = (upward * normal).astype(jnp.bfloat16)
    grad_up = (inner_cols(gm, weight_down) * slope).astype(jnp.bfloat16)
    bias_grad_ref[...] = jnp.sum(grad_up.astype(jnp.float32), axis=0, keepdims=True)
    branch = plain_product(active, weight_down)
    m_own_ref[...] += branch[:rows]
    m_other_ref[...] += branch[rows:]
    grad_norm = inner_cols(grad_up, weight_up)
    gh_own_ref[...] += grad_norm[:rows]
    gh_other_ref[...] += grad_norm[rows:]
    up_grad = plain_product(turned_ref[...], grad_up).astype(jnp.bfloat16)
    row = pl.multiple_of(tile // folds * up_rows, up_rows)
    column = pl.multiple_of(lax.rem(tile, folds) * units, units)
    up_grad = up_grad.reshape(chips, up_rows, units)
    up_grad_ref[:, pl.ds(row, up_rows), pl.ds(column, units)] = up_grad
    down_grad = inner_rows(active, gm).astype(jnp.bfloat16)
    down_grad_ref[...] = down_grad.reshape(down_grad_ref.shape)


def mlp(core, own, other, gm_own, gm_other, weights, bias, chips):
    rows, width = own.shape
    half = bias.shape[0]
    unit_block = half // chips
    units = 256
    folds = width // units
    once = dict(pipeline_mode=pl.Buffered(1))
    fixed = pl.BlockSpec((rows, width), lambda j, core: (0, 0), **once)
    if len(weights) == 1:
        count = 2 * chips
        share = width // count
        pieces = units // unit_block
        lane_blocks = width // unit_block

        def up_spec(piece):
            def place(j, core):
                block = 2 * (j * pieces + piece) + core[0]
                return (0, block // lane_blocks, lax.rem(block, lane_blocks))

            return pl.BlockSpec((count, share, unit_block), place)

        def down_spec(piece):
            return pl.BlockSpec(
                (1, unit_block, width), lambda j, core: (2 * (j * pieces + piece) + core[0], 1, 0)
            )

        weights = list(weights) * (2 * pieces)
        weight_specs = [up_spec(n) for n in range(pieces)] + [down_spec(n) for n in range(pieces)]
        up_shape, down_shape = (chips, half // chips, width), (chips, half // chips, width)
        down_grad_spec = pl.BlockSpec((pieces, unit_block, width), lambda j, core: (j, 0, 0))
    else:
        pieces = 1
        weight_specs = [
            pl.BlockSpec((width, units), lambda j, core: (0, j)),
            pl.BlockSpec((units, width), lambda j, core: (j, 0)),
        ]
        up_shape, down_shape = (1, half // width * width, width), (1, half, width)
        down_grad_spec = pl.BlockSpec((1, units, width), lambda j, core: (0, j, 0))
    total = jax.ShapeDtypeStruct((rows, width), jnp.float32)
    outs = pl.pallas_call(
        functools.partial(mlp_kernel, pieces),
        grid_spec=pltpu.PrefetchScalarGridSpec(
            num_scalar_prefetch=1,
            grid=(half // units,),
            in_specs=[fixed] * 4 + [pl.BlockSpec((1, units), lambda j, core: (0, j)), *weight_specs],
            out_specs=[
                pl.BlockSpec(up_shape, lambda j, core: (0, 0, 0), **once),
                down_grad_spec,
                *[fixed] * 4,
                pl.BlockSpec((1, units), lambda j, core: (0, j)),
            ],
            scratch_shapes=[
                pltpu.VMEM((2 * rows, width), jnp.bfloat16),
                pltpu.VMEM((2 * rows, width), jnp.bfloat16),
                pltpu.VMEM((width, 2 * rows), jnp.bfloat16),
            ],
        ),
        out_shape=(
            jax.ShapeDtypeStruct(up_shape, jnp.bfloat16),
            jax.ShapeDtypeStruct(down_shape, jnp.bfloat16),
            *[total] * 4,
            jax.ShapeDtypeStruct((1, half), jnp.float32),
        ),
        compiler_params=pltpu.CompilerParams(vmem_limit_bytes=VMEM_BYTES),
        cost_estimate=pl.CostEstimate(
            flops=2 * rows * width * half * 12,
            bytes_accessed=half * width * 8 + rows * width * 24,
            transcendentals=rows * half * 4,
        ),
        name="mlp_both_ways",
    )(core, own, other, gm_own, gm_other, bias[None], *weights)
    up_grad, down_grad = outs[0], outs[1]
    if pieces == 1:
        up_grad = up_grad.reshape(half // width, chips, width // chips, width).swapaxes(0, 1)
        up_grad = up_grad.reshape(chips, -1, width)
        down_grad = down_grad.reshape(chips, -1, width)
    return (up_grad, down_grad, *outs[2:])


def finish_kernel(
    grad_ref, weight_ref, x_ref, gx_ref, gain_ref, out_ref, gain_grad_ref, shift_grad_ref, sums_ref, acc_ref
):
    step = pl.program_id(0)
    parts = [grad_ref[slot] for slot in range(grad_ref.shape[0])]
    grad = jnp.concatenate(parts, axis=1)
    width = x_ref.shape[1]
    product = inner_cols(grad, weight_ref[...].reshape(width, width))
    sums_ref[...] = jnp.sum(grad.astype(jnp.float32), axis=0, keepdims=True)[None]

    @pl.when(step == 0)
    def begin():
        acc_ref[...] = product

    @pl.when(step > 0)
    def further():
        acc_ref[...] += product

    @pl.when(step == pl.num_programs(0) - 1)
    def end():
        values = x_ref[...].astype(jnp.float32)
        centered = values - jnp.mean(values, axis=1, keepdims=True)
        scale = lax.rsqrt(jnp.mean(centered * centered, axis=1, keepdims=True) + 1e-06)
        unit = centered * scale
        grad_norm = acc_ref[...]
        gain_grad_ref[...] = jnp.sum(grad_norm * unit, axis=0, keepdims=True)
        shift_grad_ref[...] = jnp.sum(grad_norm, axis=0, keepdims=True)
        grad_unit = grad_norm * gain_ref[...]
        mean = jnp.mean(grad_unit, axis=1, keepdims=True)
        slant = jnp.mean(grad_unit * unit, axis=1, keepdims=True)
        out_ref[...] = gx_ref[...] + scale * (grad_unit - mean - unit * slant)


def finish(grads, weights, inputs, gx, gain):
    rows, width = inputs.shape
    group, lanes = grads.shape[0], grads.shape[2] // 3
    if lanes % 128:
        grads = grads.reshape(group, rows, 3, lanes).transpose(2, 0, 1, 3)
        grads = grads.reshape(3 * group, rows, lanes)
        grad_spec = pl.BlockSpec((group, rows, lanes), lambda k: (k, 0, 0))
    else:
        grad_spec = pl.BlockSpec((group, rows, lanes), lambda k: (0, 0, k))
    if weights.ndim == 3:
        share = width // weights.shape[0]
        first = weights.shape[1] // share - 3
        weight_spec = pl.BlockSpec((weights.shape[0], share, width), lambda k: (0, first + k, 0))
    else:
        weight_spec = pl.BlockSpec((width, width), lambda k: (0, k))
    fixed = lambda *shape: pl.BlockSpec(shape, lambda k: (0, 0))
    vector = jax.ShapeDtypeStruct((1, width), jnp.float32)
    return pl.pallas_call(
        finish_kernel,
        grid=(3,),
        in_specs=[
            grad_spec,
            weight_spec,
            fixed(rows, width),
            fixed(rows, width),
            fixed(1, width),
        ],
        out_specs=[
            fixed(rows, width),
            fixed(1, width),
            fixed(1, width),
            pl.BlockSpec((1, 1, width), lambda k: (k, 0, 0)),
        ],
        out_shape=(
            jax.ShapeDtypeStruct((rows, width), jnp.float32),
            vector,
            vector,
            jax.ShapeDtypeStruct((3, 1, width), jnp.float32),
        ),
        scratch_shapes=[pltpu.VMEM((rows, width), jnp.float32)],
        compiler_params=pltpu.CompilerParams(vmem_limit_bytes=VMEM_BYTES),
        cost_estimate=pl.CostEstimate(
            flops=rows * width * width * 6, bytes_accessed=width * width * 16, transcendentals=0
        ),
        name="finish_input",
    )(grads, weights, inputs, gx, gain[None])


def swap_cores(value):
    return lax.ppermute(value, "core", [(0, 1), (1, 0)])


def line_pairs(size, sign, step):
    pairs = [(i, i - sign) for i in range(size) if 0 <= i - sign < size]
    return [(i, j) for i, j in pairs if 0 <= i + sign * (step - 1) < size]


def line_pieces(value, axis):
    size = lax.axis_size(axis)
    if size == 2:
        other = lax.ppermute(value, axis, [(0, 1), (1, 0)])
        return [(None, other)]
    pieces = []
    for sign in (-1, 1):
        moving = value
        for step in range(1, size):
            moving = lax.ppermute(moving, axis, line_pairs(size, sign, step))
            pieces.append((sign * step, moving))
    return pieces


def line_order(value, pieces, axis):
    place = lax.axis_index(axis)
    size = lax.axis_size(axis)
    if size == 2:
        other = pieces[0][1]
        return jnp.where(place == 0, jnp.stack([value, other]), jnp.stack([other, value]))
    whole = jnp.zeros((size, *value.shape), value.dtype)
    for distance, piece in sorted(pieces, key=lambda item: -abs(item[0])) + [(0, value)]:
        slot = jnp.clip(place + distance, 0, size - 1)
        whole = lax.dynamic_update_index_in_dim(whole, piece, slot, 0)
    return whole


def gather_line(value, axis):
    return line_order(value, line_pieces(value, axis), axis)


def rounded_sum(*terms):
    return sum(term.astype(jnp.float32) for term in terms).astype(jnp.bfloat16)


def scatter_terms(value, axis, dim):
    if lax.axis_size(axis) != 2:
        return (scatter_line(value, axis, dim),)
    place = lax.axis_index(axis)
    pick = lambda slot: lax.dynamic_index_in_dim(value, slot, dim, keepdims=False)
    return (pick(place), lax.ppermute(pick(1 - place), axis, [(0, 1), (1, 0)]))


def scatter_payload(value, axis, moving, step):
    place = lax.axis_index(axis)
    size = lax.axis_size(axis)
    payload = []
    for n, sign in enumerate((-1, 1)):
        slot = jnp.clip(place - sign * (size - step), 0, size - 1)
        own = lax.dynamic_index_in_dim(value, slot, 0, keepdims=False)
        payload.append(own if moving is None else rounded_sum(own, moving[n]))
    return tuple(payload)


def scatter_send(payload, axis, step):
    size = lax.axis_size(axis)
    sums = []
    for value, sign in zip(payload, (-1, 1)):
        start = 0 if sign < 0 else size - 1
        pairs = [(i, i - sign) for i in range(size) if 0 <= i - sign < size]
        pairs = [(i, j) for i, j in pairs if abs(i - start) <= step - 1]
        sums.append(lax.ppermute(value, axis, pairs))
    return tuple(sums)


def scatter_line(value, axis, dim):
    place = lax.axis_index(axis)
    size = lax.axis_size(axis)
    pick = lambda slot: lax.dynamic_index_in_dim(
        value, jnp.clip(slot, 0, size - 1), dim, keepdims=False
    )
    if size == 2:
        return rounded_sum(pick(place), lax.ppermute(pick(1 - place), axis, [(0, 1), (1, 0)]))
    sums = []
    for sign in (-1, 1):
        moving = None
        for step in range(1, size):
            start = 0 if sign < 0 else size - 1
            pairs = [(i, i - sign) for i in range(size) if 0 <= i - sign < size]
            pairs = [(i, j) for i, j in pairs if abs(i - start) <= step - 1]
            own = pick(place - sign * (size - step))
            payload = own if moving is None else rounded_sum(own, moving)
            moving = lax.ppermute(payload, axis, pairs)
        sums.append(moving)
    return rounded_sum(pick(place), *sums)


def on_device(
    tokens,
    cotangent,
    segment_ids,
    valid,
    project_in,
    project_out,
    hidden_up,
    hidden_down,
    gains_biases,
    moment_in,
    moment_out,
    moment_up,
    moment_down,
    moment_gains,
    square_in,
    square_out,
    square_up,
    square_down,
    square_gains,
):
    rows = tokens.shape[0]
    width = tokens.shape[1]
    everyone = ("outer", "inner", "line", "core")
    planes = ("outer", "inner")
    seq = ("line", "core")
    streams, line = lax.axis_size(planes), lax.axis_size("line")
    group = 2 * line
    count = streams * group
    chips = streams * line
    share = width // count
    lanes = width // group
    length = rows * group
    images = length // IMG_LEN
    core = lax.axis_index("core")
    first_core = core == 0

    def in_order(own, other, axis):
        return jnp.concatenate(
            [jnp.where(first_core, own, other), jnp.where(first_core, other, own)], axis=axis
        )

    half = FF // 2
    unit_block = FF // count
    folds = half // width
    up_end = 2 * share * folds
    low = lambda value: value.astype(jnp.bfloat16)
    direct = share % 16 == 0 and unit_block == 128 and line > 3
    position = lax.broadcasted_iota(jnp.int32, (images, rows), 1)
    found = (segment_ids[None, :] == lax.broadcasted_iota(jnp.int32, (images, rows), 0)) & (
        valid[None, :] == 1
    )
    first = jnp.min(jnp.where(found, position, rows), axis=1)
    small = jnp.concatenate([low(gains_biases).reshape(-1), low(first // 32), low(first % 32)])
    fold = lambda value: low(value).reshape(share, -1, width).swapaxes(0, 1).reshape(-1, width)
    if direct:
        extra = 16
        small = jnp.pad(small, (0, extra * 3 * lanes - small.shape[0]))
        small = jnp.broadcast_to(small.reshape(1, extra, 3 * lanes), (group, extra, 3 * lanes))
        owned = low(project_in).reshape(share, 3, group, lanes).transpose(2, 0, 1, 3)
        blocks = jnp.concatenate([owned.reshape(group, share, 3 * lanes), small], axis=1)
        pieces, swapped = [], []
        moving = [tokens, tokens]
        for step in range(1, line):
            moving = [
                lax.ppermute(value, "line", line_pairs(line, sign, step))
                for sign, value in zip((-1, 1), moving)
            ]
            if step == 1:
                blocks = lax.all_to_all(blocks, seq, split_axis=0, concat_axis=0, tiled=True)
            elif step == 2:
                blocks = gather_line(gather_line(blocks, "inner"), "outer")
            moving, blocks, swapped = lax.optimization_barrier((moving, blocks, swapped))
            pieces += [(sign * step, value) for sign, value in zip((-1, 1), moving)]
            if step == line - 2:
                packed = jnp.concatenate([fold(hidden_up), low(hidden_down), low(project_out)], axis=0)
                packed, moving = lax.optimization_barrier((packed, moving))
                gathered = lax.all_gather(packed, everyone, axis=0, tiled=False)
            swapped = swapped + [swap_cores(value) for value in moving]
        swapped = [(distance, value) for (distance, _), value in zip(pieces, swapped)]
        whole_out = gathered[:, packed.shape[0] - share :].reshape(width, width)
        mlp_weights = (gathered,)
        whole_in = lax.all_gather(fold(project_in), everyone, axis=0, tiled=False)
        blocks = blocks.reshape(count, share + extra, 3 * lanes)
        mine_in = blocks[:, :share].reshape(width, 3 * lanes)
        small = blocks[:, share:].reshape(count, -1)
    else:
        whole_in = lax.all_gather(low(project_in), everyone, axis=0, tiled=True)
        mine_in = lax.dynamic_index_in_dim(
            whole_in.reshape(width, 3, group, lanes), lax.axis_index(seq), axis=2, keepdims=False
        ).reshape(width, 3 * lanes)
        small = lax.all_gather(small, everyone, axis=0, tiled=False)
    vector_size = gains_biases.size
    vectors = small[:, :vector_size].reshape(count, -1, share).transpose(1, 0, 2)
    vectors = vectors.reshape(-1, width).astype(jnp.float32)
    first = small[:, vector_size : vector_size + 2 * images].astype(jnp.int32)
    first = first[:, :images] * 32 + first[:, images:]
    first = lax.dynamic_slice_in_dim(first, lax.axis_index(planes) * group, group, 0)
    offsets = lax.broadcasted_iota(jnp.int32, (group, images), 0) * rows
    starts = jnp.min(jnp.where(first < rows, first + offsets, length), axis=0)

    if not direct:
        pieces = line_pieces(tokens, "line")
        swapped = [(distance, swap_cores(piece)) for distance, piece in pieces]
    own_tokens = line_order(tokens, pieces, "line").reshape(-1, width)
    other_tokens = line_order(swap_cores(tokens), swapped, "line").reshape(-1, width)

    gain_one, shift_one, bias_query, bias_value, bias_out = (
        vectors[0],
        vectors[1],
        vectors[2],
        vectors[3],
        vectors[4],
    )
    scale_one, gain_two, shift_two, bias_down, scale_two = (
        vectors[5],
        vectors[6],
        vectors[7],
        vectors[8],
        vectors[9],
    )
    bias_up = lax.dynamic_index_in_dim(
        vectors[10:].reshape(chips, 2, unit_block), core, axis=1, keepdims=False
    ).reshape(half)
    column = lax.axis_index(seq) * lanes
    bias_in = jnp.concatenate(
        [
            lax.dynamic_slice_in_dim(bias_query, column, lanes, 0),
            jnp.zeros((lanes,), jnp.float32),
            lax.dynamic_slice_in_dim(bias_value, column, lanes, 0),
        ]
    )
    grad_rows = cotangent.astype(jnp.float32) * valid.astype(jnp.float32)[:, None]
    grad_branch = (scale_two * grad_rows).astype(jnp.bfloat16)

    place = lax.axis_index(seq)
    normed_one, query, keys, values = norm_mix(
        place.reshape(1), own_tokens, other_tokens, rows, gain_one, shift_one, mine_in, bias_in
    )
    wide, attended, logs = attend(starts, query, keys, values)
    if not direct:
        whole_out, whole_up, whole_down = (
            lax.all_gather(low(value), everyone, axis=0, tiled=True)
            for value in (project_out, hidden_up, hidden_down)
        )
        block = jnp.arange(half) // unit_block * 2 + core
        index = block * unit_block + lax.rem(jnp.arange(half), unit_block)
        mlp_weights = (jnp.take(whole_up, index, axis=1), jnp.take(whole_down, index, axis=0))
    returned = lax.all_to_all(
        attended.reshape(group, rows, lanes), seq, split_axis=0, concat_axis=0, tiled=True
    )
    attended_rows = returned.transpose(1, 0, 2).reshape(rows, width)
    inputs = tokens.astype(jnp.float32)
    projected = plain_product(attended_rows, whole_out) + bias_out
    second = inputs + scale_one * projected
    norm_two, norm_two_back = jax.vjp(layer_norm, second, gain_two, shift_two)
    normed_two = norm_two.astype(jnp.bfloat16)
    grad_up, grad_down, branch, branch_other, grad_norm_two, grad_norm_other, grad_bias_up = mlp(
        core.reshape(1),
        normed_two,
        swap_cores(normed_two),
        grad_branch,
        swap_cores(grad_branch),
        mlp_weights,
        bias_up,
        chips,
    )
    grad_norm_two = grad_norm_two + swap_cores(grad_norm_other)
    branch = branch + swap_cores(branch_other) + bias_down
    block_output = (second + scale_two * branch).astype(jnp.bfloat16)
    grad_scale_two = jnp.sum(grad_rows * branch, axis=0)
    grad_bias_down = jnp.sum(grad_branch.astype(jnp.float32), axis=0)
    second_part, grad_gain_two, grad_shift_two = norm_two_back(grad_norm_two)
    grad_second = grad_rows + second_part
    grad_scale_one = jnp.sum(grad_second * projected, axis=0)
    grad_projected = (scale_one * grad_second).astype(jnp.bfloat16)
    grad_bias_out = jnp.sum(grad_projected.astype(jnp.float32), axis=0)
    grad_attended = inner_cols(grad_projected, whole_out).astype(jnp.bfloat16)
    grad_stream = lax.all_to_all(
        grad_attended.reshape(rows, group, lanes).transpose(1, 0, 2),
        seq,
        split_axis=0,
        concat_axis=0,
        tiled=True,
    ).reshape(length, lanes)
    grad_out = inner_rows(attended_rows, grad_projected).astype(jnp.bfloat16)
    grad_out = grad_out.reshape(chips, 2 * share, width)
    outer, inner = lax.axis_size("outer"), lax.axis_size("inner")
    grad_up, grad_out, grad_down = (
        value.reshape(outer, inner, line, -1, width) for value in (grad_up, grad_out, grad_down)
    )
    begun = (
        scatter_terms(grad_up, "inner", 1),
        scatter_terms(grad_out, "inner", 1),
        scatter_terms(grad_down, "outer", 0),
    )
    out_terms, whole_in, grad_stream = lax.optimization_barrier((begun[1], whole_in, grad_stream))
    begun = (begun[0], out_terms, begun[2])
    grad_mixed_stream = attend_back(starts, query, keys, values, wide, logs, grad_stream)
    grad_mixed = lax.all_to_all(
        grad_mixed_stream.reshape(group, rows, 3 * lanes), seq, split_axis=0, concat_axis=0, tiled=True
    )
    begun, grad_mixed_stream = lax.optimization_barrier((begun, grad_mixed_stream))
    grad_up, grad_out, grad_down = (rounded_sum(*terms) for terms in begun)
    grad_down = scatter_line(grad_down, "inner", 0)
    grad_up = scatter_line(jnp.concatenate([grad_up, grad_out], axis=2), "outer", 0)
    plane_sums = jnp.concatenate([grad_up, grad_down], axis=1)
    moving = scatter_send(scatter_payload(plane_sums, "line", None, 1), "line", 1)
    moving, grad_mixed = lax.optimization_barrier((moving, grad_mixed))
    grad_in = inner_rows(normed_one, grad_mixed_stream).astype(jnp.bfloat16)
    parts = grad_in.reshape(outer, inner, group * share, 3 * lanes)
    parts = scatter_line(scatter_line(parts, "inner", 1), "outer", 0)
    input_grad, grad_gain_one, grad_shift_one, mixed_sums = finish(
        grad_mixed, whole_in, tokens, grad_second, gain_one
    )
    for step in range(2, line):
        payload = scatter_payload(plane_sums, "line", moving, step)
        if step == 3:
            payload, parts, grad_gain_one = lax.optimization_barrier((payload, parts, grad_gain_one))
        moving = scatter_send(payload, "line", step)
    summed = rounded_sum(
        lax.dynamic_index_in_dim(plane_sums, lax.axis_index("line"), 0, keepdims=False), *moving
    )
    parts = parts.reshape(group, share, 3 * lanes)
    parts = lax.all_to_all(parts, seq, split_axis=0, concat_axis=0, tiled=True)
    parts = parts.astype(jnp.float32)
    summed_in = parts.reshape(group, share, 3, lanes).transpose(1, 2, 0, 3).reshape(share, 3 * width)
    up_sums = grad_bias_up.reshape(chips, unit_block)
    up_sums = jnp.where(
        (lax.broadcasted_iota(jnp.int32, (1, 2, 1), 1) == core), up_sums[:, None, :], 0.0
    )
    grad_small = jnp.concatenate(
        [
            jnp.stack(
                [
                    grad_gain_one[0],
                    grad_shift_one[0],
                    mixed_sums[0, 0],
                    mixed_sums[2, 0],
                    grad_bias_out,
                    grad_scale_one,
                    grad_gain_two,
                    grad_shift_two,
                    grad_bias_down,
                    grad_scale_two,
                ]
            ),
            up_sums.reshape(-1, width),
        ],
        axis=0,
    )
    small_rows = grad_small.shape[0]
    parts = grad_small.reshape(small_rows, count, share).transpose(1, 0, 2)
    parts = lax.all_to_all(
        parts.reshape(count, small_rows * share), everyone, split_axis=0, concat_axis=0, tiled=True
    )
    summed_gains = jnp.sum(parts, axis=0).reshape(small_rows, share)

    up_sum = summed[:up_end].reshape(folds, 2, share, width)
    out_sum = summed[up_end : up_end + 2 * share].reshape(1, 2, share, width)
    both_sums = jnp.concatenate([up_sum, out_sum], axis=0)
    own_sums = jnp.where(first_core, both_sums[:, 0], both_sums[:, 1])
    other_sums = swap_cores(jnp.where(first_core, both_sums[:, 1], both_sums[:, 0]))
    summed_down = summed[up_end + 2 * share :].astype(jnp.float32)
    summed_out = own_sums[folds].astype(jnp.float32) + other_sums[folds].astype(jnp.float32)
    own_up = own_sums[:folds].transpose(1, 0, 2).reshape(share, chips, 1, unit_block)
    other_up = other_sums[:folds].transpose(1, 0, 2).reshape(share, chips, 1, unit_block)
    summed_up = in_order(own_up, other_up, 2).reshape(share, FF).astype(jnp.float32)
    rate_out = max(1, 4 * D // IMG_LEN) ** (-0.5)
    new_in, new_moment_in, new_square_in = adamw(
        project_in, moment_in, square_in, summed_in, D ** (-0.5), 0.04
    )
    new_out, new_moment_out, new_square_out = adamw(
        project_out, moment_out, square_out, summed_out, rate_out, 0.04
    )
    new_up, new_moment_up, new_square_up = adamw(
        hidden_up, moment_up, square_up, summed_up, D ** (-0.5), 0.04
    )
    new_down, new_moment_down, new_square_down = adamw(
        hidden_down, moment_down, square_down, summed_down, FF ** (-0.5), 0.04
    )
    new_gains, new_moment_gains, new_square_gains = adamw(
        gains_biases, moment_gains, square_gains, summed_gains, 0.2, 0.0
    )
    return (
        block_output,
        input_grad,
        new_in,
        new_out,
        new_up,
        new_down,
        new_gains,
        new_moment_in,
        new_moment_out,
        new_moment_up,
        new_moment_down,
        new_moment_gains,
        new_square_in,
        new_square_out,
        new_square_up,
        new_square_down,
        new_square_gains,
        summed_gains[8],
    )


def solution(mesh):
    streams, group = mesh.shape["fsdp"], mesh.shape["seq"]
    outer = math.isqrt(streams)
    fine = jax.sharding.Mesh(
        mesh.devices.reshape(outer, streams // outer, group // 2, 2),
        ("outer", "inner", "line", "core"),
    )
    return jax.shard_map(
        on_device,
        mesh=fine,
        in_specs=(
            P(("outer", "inner", "line", "core"), None),
            P(("outer", "inner", "line", "core"), None),
            P(("outer", "inner", "line", "core")),
            P(("outer", "inner", "line", "core")),
            P(("outer", "inner", "line", "core"), None),
            P(("outer", "inner", "line", "core"), None),
            P(("outer", "inner", "line", "core"), None),
            P(("outer", "inner", "line", "core"), None),
            P(None, ("outer", "inner", "line", "core")),
            P(("outer", "inner", "line", "core"), None),
            P(("outer", "inner", "line", "core"), None),
            P(("outer", "inner", "line", "core"), None),
            P(("outer", "inner", "line", "core"), None),
            P(None, ("outer", "inner", "line", "core")),
            P(("outer", "inner", "line", "core"), None),
            P(("outer", "inner", "line", "core"), None),
            P(("outer", "inner", "line", "core"), None),
            P(("outer", "inner", "line", "core"), None),
            P(None, ("outer", "inner", "line", "core")),
        ),
        out_specs=(
            P(("outer", "inner", "line", "core"), None),
            P(("outer", "inner", "line", "core"), None),
            P(("outer", "inner", "line", "core"), None),
            P(("outer", "inner", "line", "core"), None),
            P(("outer", "inner", "line", "core"), None),
            P(("outer", "inner", "line", "core"), None),
            P(None, ("outer", "inner", "line", "core")),
            P(("outer", "inner", "line", "core"), None),
            P(("outer", "inner", "line", "core"), None),
            P(("outer", "inner", "line", "core"), None),
            P(("outer", "inner", "line", "core"), None),
            P(None, ("outer", "inner", "line", "core")),
            P(("outer", "inner", "line", "core"), None),
            P(("outer", "inner", "line", "core"), None),
            P(("outer", "inner", "line", "core"), None),
            P(("outer", "inner", "line", "core"), None),
            P(None, ("outer", "inner", "line", "core")),
            P(("outer", "inner", "line", "core")),
        ),
        check_vma=False,
    )
```

```python
import functools
import math

import jax
import jax.numpy as jnp
from jax import lax
from jax.experimental import pallas as pl
from jax.experimental.pallas import tpu as pltpu
from jax.sharding import PartitionSpec as P

D = 1024
FF = 4096
HEADS = 16
HEAD_DIM = 64
IMG_LEN = 1370
WINDOW = 1408
TILE = 352
VMEM_BYTES = 56 * 1024 * 1024
STEP = 10


masked_score = -1e30


def layer_norm(values, gain, shift):
    average = jnp.mean(values, axis=-1, keepdims=True)
    centered = values - average
    variance = jnp.mean(centered * centered, axis=-1, keepdims=True)
    return centered * lax.rsqrt(variance + 1e-06) * gain + shift


def exact_gelu(values):
    return jax.nn.gelu(values, approximate=False)


def plain_product(left, right):
    return jnp.dot(left, right, preferred_element_type=jnp.float32)


def inner_rows(left, right):
    return lax.dot_general(
        left, right, (((0,), (0,)), ((), ())), preferred_element_type=jnp.float32
    )


def inner_cols(left, right):
    return lax.dot_general(
        left, right, (((1,), (1,)), ((), ())), preferred_element_type=jnp.float32
    )


def adamw(param, moment, square, grad, rate, decay):
    new_moment = 0.9 * moment + 0.1 * grad
    new_square = 0.999 * square + 0.001 * grad * grad
    corrected = new_moment / (1.0 - 0.9**STEP)
    scaled = jnp.sqrt(new_square / (1.0 - 0.999**STEP)) + 1e-08
    return (param - rate * (corrected / scaled + decay * param), new_moment, new_square)


def head_lanes(shape):
    return lax.broadcasted_iota(jnp.int32, shape, 1) // HEAD_DIM


def window_of(starts_ref, image, length):
    start = starts_ref[image]
    base = jnp.clip(start // 16 * 16, 0, length - WINDOW)
    return (pl.multiple_of(base, 16), start - base)


def image_mask(position, offset):
    return (position >= offset) & (position < offset + IMG_LEN)


def attend_kernel(starts_ref, q_ref, k_ref, v_ref, wide_ref, out_ref, log_ref):
    image, tile = pl.program_id(0), pl.program_id(1)
    length, lanes = q_ref.shape
    base, offset = window_of(starts_ref, image, length)
    rows = pl.ds(pl.multiple_of(base + tile * TILE, 16), TILE)

    @pl.when((image == 0) & (tile == 0))
    def clear():
        wide_ref[...] = jnp.zeros_like(wide_ref)
        out_ref[...] = jnp.zeros_like(out_ref)
        log_ref[...] = jnp.zeros_like(log_ref)

    query = q_ref[rows, :].astype(jnp.float32) * HEAD_DIM ** (-0.5)
    keys = k_ref[pl.ds(base, WINDOW), :]
    values = v_ref[pl.ds(base, WINDOW), :]
    key_ok = image_mask(lax.broadcasted_iota(jnp.int32, (1, WINDOW), 1), offset)
    bias = jnp.where(key_ok, 0.0, masked_score)
    row_ok = image_mask(lax.broadcasted_iota(jnp.int32, (TILE, 1), 0) + tile * TILE, offset)
    head_of = head_lanes((TILE, lanes))
    total_out = jnp.zeros((TILE, lanes), jnp.float32)
    total_log = jnp.zeros((TILE, lanes), jnp.float32)
    for head in range(lanes // HEAD_DIM):
        mine = head_of == head
        part = jnp.where(mine, query, 0.0).astype(jnp.bfloat16)
        scores = inner_cols(part, keys) + bias
        top = jnp.max(scores, axis=1, keepdims=True)
        weights = jnp.exp(scores - top)
        total = jnp.sum(weights, axis=1, keepdims=True)
        probs = (weights * (1.0 / total)).astype(jnp.bfloat16)
        total_out = jnp.where(mine, plain_product(probs, values), total_out)
        total_log = jnp.where(mine, top + jnp.log(total), total_log)
    merged = jnp.where(row_ok, total_out, wide_ref[rows, :])
    wide_ref[rows, :] = merged
    out_ref[rows, :] = merged.astype(jnp.bfloat16)
    log_ref[rows, :] = jnp.where(row_ok, total_log, log_ref[rows, :])


def attend(starts, query, keys, values):
    length, lanes = query.shape
    whole = pl.BlockSpec((length, lanes), lambda image, tile, starts: (0, 0))
    wide = jax.ShapeDtypeStruct((length, lanes), jnp.float32)
    images = length // IMG_LEN
    return pl.pallas_call(
        attend_kernel,
        grid_spec=pltpu.PrefetchScalarGridSpec(
            num_scalar_prefetch=1,
            grid=(images, WINDOW // TILE),
            in_specs=[whole] * 3,
            out_specs=[whole] * 3,
        ),
        out_shape=(wide, jax.ShapeDtypeStruct((length, lanes), jnp.bfloat16), wide),
        compiler_params=pltpu.CompilerParams(
            vmem_limit_bytes=VMEM_BYTES, dimension_semantics=("arbitrary", "arbitrary")
        ),
        cost_estimate=pl.CostEstimate(
            flops=images * WINDOW * WINDOW * lanes * 8,
            bytes_accessed=length * lanes * 16,
            transcendentals=images * WINDOW * WINDOW * lanes // HEAD_DIM,
        ),
        name="attend_forward",
    )(starts, query, keys, values)


def attend_back_kernel(
    starts_ref, q_ref, k_ref, v_ref, wide_ref, log_ref, go_ref, grad_ref, key_acc, value_acc
):
    image, tile = pl.program_id(0), pl.program_id(1)
    length, lanes = q_ref.shape
    base, offset = window_of(starts_ref, image, length)
    rows = pl.ds(pl.multiple_of(base + tile * TILE, 16), TILE)
    window = pl.ds(base, WINDOW)

    @pl.when((image == 0) & (tile == 0))
    def clear():
        grad_ref[...] = jnp.zeros_like(grad_ref)

    @pl.when(tile == 0)
    def clear_sums():
        key_acc[...] = jnp.zeros_like(key_acc)
        value_acc[...] = jnp.zeros_like(value_acc)

    query = q_ref[rows, :].astype(jnp.float32) * HEAD_DIM ** (-0.5)
    keys = k_ref[window, :]
    values = v_ref[window, :]
    key_ok = image_mask(lax.broadcasted_iota(jnp.int32, (1, WINDOW), 1), offset)
    bias = jnp.where(key_ok, 0.0, masked_score)
    row_ok = image_mask(lax.broadcasted_iota(jnp.int32, (TILE, 1), 0) + tile * TILE, offset)
    head_of = head_lanes((TILE, lanes))
    grad_out = jnp.where(row_ok, go_ref[rows, :].astype(jnp.float32), 0.0)
    centre_parts = grad_out * wide_ref[rows, :]
    logs = jnp.where(row_ok, log_ref[rows, :], -masked_score)
    query_grad = jnp.zeros((TILE, lanes), jnp.float32)
    for head in range(lanes // HEAD_DIM):
        mine = head_of == head
        part = jnp.where(mine, query, 0.0).astype(jnp.bfloat16)
        grad_part = jnp.where(mine, grad_out, 0.0).astype(jnp.bfloat16)
        centre = jnp.sum(jnp.where(mine, centre_parts, 0.0), axis=1, keepdims=True)
        log_total = jnp.max(jnp.where(mine, logs, masked_score), axis=1, keepdims=True)
        probs = jnp.exp(inner_cols(part, keys) + bias - log_total)
        grad_probs = inner_cols(grad_part, values)
        grad_scores = (probs * (grad_probs - centre)).astype(jnp.bfloat16)
        query_grad = jnp.where(mine, plain_product(grad_scores, keys), query_grad)
        key_acc[...] += inner_rows(part, grad_scores)
        value_acc[...] += inner_rows(grad_part, probs.astype(jnp.bfloat16))
    old = grad_ref[rows, 0:lanes].astype(jnp.float32)
    merged = jnp.where(row_ok, query_grad * HEAD_DIM ** (-0.5), old)
    grad_ref[rows, 0:lanes] = merged.astype(jnp.bfloat16)

    @pl.when(tile == pl.num_programs(1) - 1)
    def flush():
        inside = image_mask(lax.broadcasted_iota(jnp.int32, (WINDOW, 1), 0), offset)
        for slot, sums in ((1, key_acc), (2, value_acc)):
            columns = slice(slot * lanes, (slot + 1) * lanes)
            old = grad_ref[window, columns].astype(jnp.float32)
            merged = jnp.where(inside, sums[...].T, old)
            grad_ref[window, columns] = merged.astype(jnp.bfloat16)


def attend_back(starts, query, keys, values, wide, logs, grad_out):
    length, lanes = query.shape
    whole = pl.BlockSpec((length, lanes), lambda image, tile, starts: (0, 0))
    images = length // IMG_LEN
    return pl.pallas_call(
        attend_back_kernel,
        grid_spec=pltpu.PrefetchScalarGridSpec(
            num_scalar_prefetch=1,
            grid=(images, WINDOW // TILE),
            in_specs=[whole] * 6,
            out_specs=pl.BlockSpec((length, 3 * lanes), lambda image, tile, starts: (0, 0)),
            scratch_shapes=[pltpu.VMEM((lanes, WINDOW), jnp.float32)] * 2,
        ),
        out_shape=jax.ShapeDtypeStruct((length, 3 * lanes), jnp.bfloat16),
        compiler_params=pltpu.CompilerParams(
            vmem_limit_bytes=VMEM_BYTES, dimension_semantics=("arbitrary", "arbitrary")
        ),
        cost_estimate=pl.CostEstimate(
            flops=images * WINDOW * WINDOW * lanes * 20,
            bytes_accessed=length * lanes * 22,
            transcendentals=images * WINDOW * WINDOW * lanes // HEAD_DIM,
        ),
        name="attend_backward",
    )(starts, query, keys, values, wide, logs, grad_out)


def norm_mix_kernel(pieces, place_ref, own_ref, other_ref, gain_ref, shift_ref, bias_ref, *refs):
    weight = jnp.concatenate(
        [ref[...].reshape(own_ref.shape[1], -1) for ref in refs[:pieces]], axis=1
    )
    a_ref, q_ref, k_ref, v_ref = refs[pieces:]
    lanes = q_ref.shape[1]
    mine = lax.rem(pl.program_id(0), 2) == lax.rem(place_ref[0], 2)
    own, other = own_ref[...].astype(jnp.float32), other_ref[...].astype(jnp.float32)
    normed = layer_norm(jnp.where(mine, own, other), gain_ref[...], shift_ref[...])
    normed = normed.astype(jnp.bfloat16)
    a_ref[...] = normed
    mixed = (plain_product(normed, weight) + bias_ref[...]).astype(jnp.bfloat16)
    q_ref[...] = mixed[:, :lanes]
    k_ref[...] = mixed[:, lanes : 2 * lanes]
    v_ref[...] = mixed[:, 2 * lanes :]


def norm_mix(place, own, other, length, block, gain, shift, weight, bias):
    width = own.shape[1]
    lanes = bias.shape[0] // 3
    row = lambda size: pl.BlockSpec((block, size), lambda i, place: (i, 0))
    half = pl.BlockSpec((block, width), lambda i, place: (i // 2, 0))
    fixed = lambda *shape: pl.BlockSpec(shape, lambda i, place: (0, 0))
    part = jax.ShapeDtypeStruct((length, lanes), jnp.bfloat16)
    weights, weight_specs = [weight], [fixed(width, 3 * lanes)]
    return pl.pallas_call(
        functools.partial(norm_mix_kernel, len(weights)),
        grid_spec=pltpu.PrefetchScalarGridSpec(
            num_scalar_prefetch=1,
            grid=(length // block,),
            in_specs=[
                half,
                half,
                fixed(1, width),
                fixed(1, width),
                fixed(1, 3 * lanes),
                *weight_specs,
            ],
            out_specs=[row(width), row(lanes), row(lanes), row(lanes)],
        ),
        out_shape=(jax.ShapeDtypeStruct((length, width), jnp.bfloat16), part, part, part),
        compiler_params=pltpu.CompilerParams(vmem_limit_bytes=VMEM_BYTES),
        cost_estimate=pl.CostEstimate(
            flops=length * width * lanes * 6, bytes_accessed=length * width * 4, transcendentals=0
        ),
        name="norm_mix",
    )(place, own, other, gain[None], shift[None], bias[None], *weights)


def mlp_kernel(pieces, core_ref, own_ref, other_ref, gm_own_ref, gm_other_ref, bias_ref, *refs):
    up_refs, down_refs = refs[:pieces], refs[pieces : 2 * pieces]
    up_grad_ref, down_grad_ref, m_own_ref, m_other_ref, gh_own_ref, gh_other_ref = refs[
        2 * pieces : 2 * pieces + 6
    ]
    bias_grad_ref, h_ref, gm_ref, turned_ref = refs[2 * pieces + 6 :]
    tile = pl.program_id(0)
    rows, width = own_ref.shape
    chips = up_grad_ref.shape[0]
    up_rows = width // chips
    units = bias_ref.shape[1]
    folds = width // units

    @pl.when(tile == 0)
    def clear():
        for ref in (m_own_ref, m_other_ref, gh_own_ref, gh_other_ref):
            ref[...] = jnp.zeros_like(ref)
        h_ref[:rows] = own_ref[...]
        h_ref[rows:] = other_ref[...]
        gm_ref[:rows] = gm_own_ref[...]
        gm_ref[rows:] = gm_other_ref[...]
        turned_ref[...] = h_ref[...].T

    weight_up = jnp.concatenate([ref[...].reshape(width, -1) for ref in up_refs], axis=1)
    weight_down = jnp.concatenate([ref[...].reshape(-1, width) for ref in down_refs], axis=0)
    gm = gm_ref[...]
    upward = plain_product(h_ref[...], weight_up) + bias_ref[...]
    normal = 0.5 * (1.0 + lax.erf(upward * 0.5**0.5))
    slope = normal + upward * jnp.exp(upward * upward * -0.5) * (0.5 / jnp.pi) ** 0.5
    active = (upward * normal).astype(jnp.bfloat16)
    grad_up = (inner_cols(gm, weight_down) * slope).astype(jnp.bfloat16)
    bias_grad_ref[...] = jnp.sum(grad_up.astype(jnp.float32), axis=0, keepdims=True)
    branch = plain_product(active, weight_down)
    m_own_ref[...] += branch[:rows]
    m_other_ref[...] += branch[rows:]
    grad_norm = inner_cols(grad_up, weight_up)
    gh_own_ref[...] += grad_norm[:rows]
    gh_other_ref[...] += grad_norm[rows:]
    up_grad = plain_product(turned_ref[...], grad_up).astype(jnp.bfloat16)
    row = pl.multiple_of(tile // folds * up_rows, up_rows)
    column = pl.multiple_of(lax.rem(tile, folds) * units, units)
    up_grad = up_grad.reshape(chips, up_rows, units)
    up_grad_ref[:, pl.ds(row, up_rows), pl.ds(column, units)] = up_grad
    down_grad = inner_rows(active, gm).astype(jnp.bfloat16)
    down_grad_ref[...] = down_grad.reshape(down_grad_ref.shape)


def mlp(core, own, other, gm_own, gm_other, weights, bias, chips):
    rows, width = own.shape
    half = bias.shape[0]
    unit_block = half // chips
    units = 256
    folds = width // units
    once = dict(pipeline_mode=pl.Buffered(1))
    fixed = pl.BlockSpec((rows, width), lambda j, core: (0, 0), **once)
    if len(weights) == 1:
        count = 2 * chips
        share = width // count
        pieces = units // unit_block
        lane_blocks = width // unit_block

        def up_spec(piece):
            def place(j, core):
                block = 2 * (j * pieces + piece) + core[0]
                return (0, block // lane_blocks, lax.rem(block, lane_blocks))

            return pl.BlockSpec((count, share, unit_block), place)

        def down_spec(piece):
            return pl.BlockSpec(
                (1, unit_block, width), lambda j, core: (2 * (j * pieces + piece) + core[0], 1, 0)
            )

        weights = list(weights) * (2 * pieces)
        weight_specs = [up_spec(n) for n in range(pieces)] + [down_spec(n) for n in range(pieces)]
        up_shape, down_shape = (chips, half // chips, width), (chips, half // chips, width)
        down_grad_spec = pl.BlockSpec((pieces, unit_block, width), lambda j, core: (j, 0, 0))
    else:
        pieces = 1
        weight_specs = [
            pl.BlockSpec((width, units), lambda j, core: (0, j)),
            pl.BlockSpec((units, width), lambda j, core: (j, 0)),
        ]
        up_shape, down_shape = (1, half // width * width, width), (1, half, width)
        down_grad_spec = pl.BlockSpec((1, units, width), lambda j, core: (0, j, 0))
    total = jax.ShapeDtypeStruct((rows, width), jnp.float32)
    outs = pl.pallas_call(
        functools.partial(mlp_kernel, pieces),
        grid_spec=pltpu.PrefetchScalarGridSpec(
            num_scalar_prefetch=1,
            grid=(half // units,),
            in_specs=[fixed] * 4 + [pl.BlockSpec((1, units), lambda j, core: (0, j)), *weight_specs],
            out_specs=[
                pl.BlockSpec(up_shape, lambda j, core: (0, 0, 0), **once),
                down_grad_spec,
                *[fixed] * 4,
                pl.BlockSpec((1, units), lambda j, core: (0, j)),
            ],
            scratch_shapes=[
                pltpu.VMEM((2 * rows, width), jnp.bfloat16),
                pltpu.VMEM((2 * rows, width), jnp.bfloat16),
                pltpu.VMEM((width, 2 * rows), jnp.bfloat16),
            ],
        ),
        out_shape=(
            jax.ShapeDtypeStruct(up_shape, jnp.bfloat16),
            jax.ShapeDtypeStruct(down_shape, jnp.bfloat16),
            *[total] * 4,
            jax.ShapeDtypeStruct((1, half), jnp.float32),
        ),
        compiler_params=pltpu.CompilerParams(vmem_limit_bytes=VMEM_BYTES),
        cost_estimate=pl.CostEstimate(
            flops=2 * rows * width * half * 12,
            bytes_accessed=half * width * 8 + rows * width * 24,
            transcendentals=rows * half * 4,
        ),
        name="mlp_both_ways",
    )(core, own, other, gm_own, gm_other, bias[None], *weights)
    up_grad, down_grad = outs[0], outs[1]
    if pieces == 1:
        up_grad = up_grad.reshape(half // width, chips, width // chips, width).swapaxes(0, 1)
        up_grad = up_grad.reshape(chips, -1, width)
        down_grad = down_grad.reshape(chips, -1, width)
    return (up_grad, down_grad, *outs[2:])


def finish_kernel(
    grad_ref, weight_ref, x_ref, gx_ref, gain_ref, out_ref, gain_grad_ref, shift_grad_ref, sums_ref, acc_ref
):
    step = pl.program_id(0)
    parts = [grad_ref[slot] for slot in range(grad_ref.shape[0])]
    grad = jnp.concatenate(parts, axis=1)
    width = x_ref.shape[1]
    product = inner_cols(grad, weight_ref[...].reshape(width, width))
    sums_ref[...] = jnp.sum(grad.astype(jnp.float32), axis=0, keepdims=True)[None]

    @pl.when(step == 0)
    def begin():
        acc_ref[...] = product

    @pl.when(step > 0)
    def further():
        acc_ref[...] += product

    @pl.when(step == pl.num_programs(0) - 1)
    def end():
        values = x_ref[...].astype(jnp.float32)
        centered = values - jnp.mean(values, axis=1, keepdims=True)
        scale = lax.rsqrt(jnp.mean(centered * centered, axis=1, keepdims=True) + 1e-06)
        unit = centered * scale
        grad_norm = acc_ref[...]
        gain_grad_ref[...] = jnp.sum(grad_norm * unit, axis=0, keepdims=True)
        shift_grad_ref[...] = jnp.sum(grad_norm, axis=0, keepdims=True)
        grad_unit = grad_norm * gain_ref[...]
        mean = jnp.mean(grad_unit, axis=1, keepdims=True)
        slant = jnp.mean(grad_unit * unit, axis=1, keepdims=True)
        out_ref[...] = gx_ref[...] + scale * (grad_unit - mean - unit * slant)


def finish(grads, weights, inputs, gx, gain):
    rows, width = inputs.shape
    group, lanes = grads.shape[0], grads.shape[2] // 3
    if lanes % 128:
        grads = grads.reshape(group, rows, 3, lanes).transpose(2, 0, 1, 3)
        grads = grads.reshape(3 * group, rows, lanes)
        grad_spec = pl.BlockSpec((group, rows, lanes), lambda k: (k, 0, 0))
    else:
        grad_spec = pl.BlockSpec((group, rows, lanes), lambda k: (0, 0, k))
    if weights.ndim == 3:
        share = width // weights.shape[0]
        first = weights.shape[1] // share - 3
        weight_spec = pl.BlockSpec((weights.shape[0], share, width), lambda k: (0, first + k, 0))
    else:
        weight_spec = pl.BlockSpec((width, width), lambda k: (0, k))
    fixed = lambda *shape: pl.BlockSpec(shape, lambda k: (0, 0))
    vector = jax.ShapeDtypeStruct((1, width), jnp.float32)
    return pl.pallas_call(
        finish_kernel,
        grid=(3,),
        in_specs=[
            grad_spec,
            weight_spec,
            fixed(rows, width),
            fixed(rows, width),
            fixed(1, width),
        ],
        out_specs=[
            fixed(rows, width),
            fixed(1, width),
            fixed(1, width),
            pl.BlockSpec((1, 1, width), lambda k: (k, 0, 0)),
        ],
        out_shape=(
            jax.ShapeDtypeStruct((rows, width), jnp.float32),
            vector,
            vector,
            jax.ShapeDtypeStruct((3, 1, width), jnp.float32),
        ),
        scratch_shapes=[pltpu.VMEM((rows, width), jnp.float32)],
        compiler_params=pltpu.CompilerParams(vmem_limit_bytes=VMEM_BYTES),
        cost_estimate=pl.CostEstimate(
            flops=rows * width * width * 6, bytes_accessed=width * width * 16, transcendentals=0
        ),
        name="finish_input",
    )(grads, weights, inputs, gx, gain[None])


def swap_cores(value):
    return lax.ppermute(value, "core", [(0, 1), (1, 0)])


def line_pairs(size, sign, step):
    pairs = [(i, i - sign) for i in range(size) if 0 <= i - sign < size]
    return [(i, j) for i, j in pairs if 0 <= i + sign * (step - 1) < size]


def line_pieces(value, axis):
    size = lax.axis_size(axis)
    if size == 2:
        other = lax.ppermute(value, axis, [(0, 1), (1, 0)])
        return [(None, other)]
    pieces = []
    for sign in (-1, 1):
        moving = value
        for step in range(1, size):
            moving = lax.ppermute(moving, axis, line_pairs(size, sign, step))
            pieces.append((sign * step, moving))
    return pieces


def line_order(value, pieces, axis, spare=False):
    place = lax.axis_index(axis)
    size = lax.axis_size(axis)
    if size == 2:
        other = pieces[0][1]
        return jnp.where(place == 0, jnp.stack([value, other]), jnp.stack([other, value]))
    whole = jnp.zeros((size + 1, *value.shape), value.dtype)
    for distance, piece in [(0, value)] + sorted(pieces, key=lambda item: abs(item[0])):
        slot = place + distance
        slot = jnp.where((slot >= 0) & (slot < size), slot, size)
        whole = lax.dynamic_update_index_in_dim(whole, piece, slot, 0)
    return whole if spare else whole[:size]


def gather_line(value, axis):
    return line_order(value, line_pieces(value, axis), axis)


def rounded_sum(*terms):
    return sum(term.astype(jnp.float32) for term in terms).astype(jnp.bfloat16)


def scatter_terms(value, axis, dim):
    if lax.axis_size(axis) != 2:
        return (scatter_line(value, axis, dim),)
    place = lax.axis_index(axis)
    pick = lambda slot: lax.dynamic_index_in_dim(value, slot, dim, keepdims=False)
    return (pick(place), lax.ppermute(pick(1 - place), axis, [(0, 1), (1, 0)]))


def scatter_payload(value, axis, moving, step):
    place = lax.axis_index(axis)
    size = lax.axis_size(axis)
    payload = []
    for n, sign in enumerate((-1, 1)):
        slot = jnp.clip(place - sign * (size - step), 0, size - 1)
        own = lax.dynamic_index_in_dim(value, slot, 0, keepdims=False)
        payload.append(own if moving is None else rounded_sum(own, moving[n]))
    return tuple(payload)


def scatter_send(payload, axis, step):
    size = lax.axis_size(axis)
    sums = []
    for value, sign in zip(payload, (-1, 1)):
        start = 0 if sign < 0 else size - 1
        pairs = [(i, i - sign) for i in range(size) if 0 <= i - sign < size]
        pairs = [(i, j) for i, j in pairs if abs(i - start) <= step - 1]
        sums.append(lax.ppermute(value, axis, pairs))
    return tuple(sums)


def scatter_line(value, axis, dim):
    place = lax.axis_index(axis)
    size = lax.axis_size(axis)
    pick = lambda slot: lax.dynamic_index_in_dim(
        value, jnp.clip(slot, 0, size - 1), dim, keepdims=False
    )
    if size == 2:
        return rounded_sum(pick(place), lax.ppermute(pick(1 - place), axis, [(0, 1), (1, 0)]))
    sums = []
    for sign in (-1, 1):
        moving = None
        for step in range(1, size):
            start = 0 if sign < 0 else size - 1
            pairs = [(i, i - sign) for i in range(size) if 0 <= i - sign < size]
            pairs = [(i, j) for i, j in pairs if abs(i - start) <= step - 1]
            own = pick(place - sign * (size - step))
            payload = own if moving is None else rounded_sum(own, moving)
            moving = lax.ppermute(payload, axis, pairs)
        sums.append(moving)
    return rounded_sum(pick(place), *sums)


def on_device(
    tokens,
    cotangent,
    segment_ids,
    valid,
    project_in,
    project_out,
    hidden_up,
    hidden_down,
    gains_biases,
    moment_in,
    moment_out,
    moment_up,
    moment_down,
    moment_gains,
    square_in,
    square_out,
    square_up,
    square_down,
    square_gains,
):
    rows = tokens.shape[0]
    width = tokens.shape[1]
    everyone = ("outer", "inner", "line", "core")
    planes = ("outer", "inner")
    seq = ("line", "core")
    streams, line = lax.axis_size(planes), lax.axis_size("line")
    group = 2 * line
    count = streams * group
    chips = streams * line
    share = width // count
    lanes = width // group
    length = rows * group
    images = length // IMG_LEN
    core = lax.axis_index("core")
    first_core = core == 0

    def in_order(own, other, axis):
        return jnp.concatenate(
            [jnp.where(first_core, own, other), jnp.where(first_core, other, own)], axis=axis
        )

    half = FF // 2
    unit_block = FF // count
    folds = half // width
    up_end = 2 * share * folds
    low = lambda value: value.astype(jnp.bfloat16)
    direct = share % 16 == 0 and unit_block == 128 and line > 3
    position = lax.broadcasted_iota(jnp.int32, (images, rows), 1)
    found = (segment_ids[None, :] == lax.broadcasted_iota(jnp.int32, (images, rows), 0)) & (
        valid[None, :] == 1
    )
    first = jnp.min(jnp.where(found, position, rows), axis=1)
    small = jnp.concatenate([low(gains_biases).reshape(-1), low(first // 32), low(first % 32)])
    fold = lambda value: low(value).reshape(share, -1, width).swapaxes(0, 1).reshape(-1, width)
    if direct:
        extra = 16
        small = jnp.pad(small, (0, extra * 3 * lanes - small.shape[0]))
        small = jnp.broadcast_to(small.reshape(1, extra, 3 * lanes), (group, extra, 3 * lanes))
        owned = low(project_in).reshape(share, 3, group, lanes).transpose(2, 0, 1, 3)
        blocks = jnp.concatenate([owned.reshape(group, share, 3 * lanes), small], axis=1)
        pieces, swapped = [], []
        moving = [tokens, tokens]
        for step in range(1, line):
            moving = [
                lax.ppermute(value, "line", line_pairs(line, sign, step))
                for sign, value in zip((-1, 1), moving)
            ]
            if step == 1:
                blocks = lax.all_to_all(blocks, seq, split_axis=0, concat_axis=0, tiled=True)
            elif step == 2:
                blocks = gather_line(gather_line(blocks, "inner"), "outer")
            moving, blocks, swapped = lax.optimization_barrier((moving, blocks, swapped))
            pieces += [(sign * step, value) for sign, value in zip((-1, 1), moving)]
            if step == line - 2:
                packed = jnp.concatenate([fold(hidden_up), low(hidden_down), low(project_out)], axis=0)
                packed, moving = lax.optimization_barrier((packed, moving))
                gathered = lax.all_gather(packed, everyone, axis=0, tiled=False)
            swapped = swapped + [swap_cores(value) for value in moving]
        swapped = [(distance, value) for (distance, _), value in zip(pieces, swapped)]
        whole_out = gathered[:, packed.shape[0] - share :].reshape(width, width)
        mlp_weights = (gathered,)
        whole_in = lax.all_gather(fold(project_in), everyone, axis=0, tiled=False)
        blocks = blocks.reshape(count, share + extra, 3 * lanes)
        mine_in = blocks[:, :share].reshape(width, 3 * lanes)
        small = blocks[:, share:].reshape(count, -1)
    else:
        whole_in = lax.all_gather(low(project_in), everyone, axis=0, tiled=True)
        mine_in = lax.dynamic_index_in_dim(
            whole_in.reshape(width, 3, group, lanes), lax.axis_index(seq), axis=2, keepdims=False
        ).reshape(width, 3 * lanes)
        small = lax.all_gather(small, everyone, axis=0, tiled=False)
    vector_size = gains_biases.size
    vectors = small[:, :vector_size].reshape(count, -1, share).transpose(1, 0, 2)
    vectors = vectors.reshape(-1, width).astype(jnp.float32)
    first = small[:, vector_size : vector_size + 2 * images].astype(jnp.int32)
    first = first[:, :images] * 32 + first[:, images:]
    first = lax.dynamic_slice_in_dim(first, lax.axis_index(planes) * group, group, 0)
    offsets = lax.broadcasted_iota(jnp.int32, (group, images), 0) * rows
    starts = jnp.min(jnp.where(first < rows, first + offsets, length), axis=0)

    if not direct:
        pieces = line_pieces(tokens, "line")
        swapped = [(distance, swap_cores(piece)) for distance, piece in pieces]
    own_tokens = line_order(tokens, pieces, "line", True).reshape(-1, width)
    other_tokens = line_order(swap_cores(tokens), swapped, "line", True).reshape(-1, width)

    gain_one, shift_one, bias_query, bias_value, bias_out = (
        vectors[0],
        vectors[1],
        vectors[2],
        vectors[3],
        vectors[4],
    )
    scale_one, gain_two, shift_two, bias_down, scale_two = (
        vectors[5],
        vectors[6],
        vectors[7],
        vectors[8],
        vectors[9],
    )
    bias_up = lax.dynamic_index_in_dim(
        vectors[10:].reshape(chips, 2, unit_block), core, axis=1, keepdims=False
    ).reshape(half)
    column = lax.axis_index(seq) * lanes
    bias_in = jnp.concatenate(
        [
            lax.dynamic_slice_in_dim(bias_query, column, lanes, 0),
            jnp.zeros((lanes,), jnp.float32),
            lax.dynamic_slice_in_dim(bias_value, column, lanes, 0),
        ]
    )
    grad_rows = cotangent.astype(jnp.float32) * valid.astype(jnp.float32)[:, None]
    grad_branch = (scale_two * grad_rows).astype(jnp.bfloat16)

    place = lax.axis_index(seq)
    normed_one, query, keys, values = norm_mix(
        place.reshape(1), own_tokens, other_tokens, length, rows, gain_one, shift_one, mine_in, bias_in
    )
    wide, attended, logs = attend(starts, query, keys, values)
    if not direct:
        whole_out, whole_up, whole_down = (
            lax.all_gather(low(value), everyone, axis=0, tiled=True)
            for value in (project_out, hidden_up, hidden_down)
        )
        block = jnp.arange(half) // unit_block * 2 + core
        index = block * unit_block + lax.rem(jnp.arange(half), unit_block)
        mlp_weights = (jnp.take(whole_up, index, axis=1), jnp.take(whole_down, index, axis=0))
    returned = lax.all_to_all(
        attended.reshape(group, rows, lanes), seq, split_axis=0, concat_axis=0, tiled=True
    )
    attended_rows = returned.transpose(1, 0, 2).reshape(rows, width)
    inputs = tokens.astype(jnp.float32)
    projected = plain_product(attended_rows, whole_out) + bias_out
    second = inputs + scale_one * projected
    norm_two, norm_two_back = jax.vjp(layer_norm, second, gain_two, shift_two)
    normed_two = norm_two.astype(jnp.bfloat16)
    grad_up, grad_down, branch, branch_other, grad_norm_two, grad_norm_other, grad_bias_up = mlp(
        core.reshape(1),
        normed_two,
        swap_cores(normed_two),
        grad_branch,
        swap_cores(grad_branch),
        mlp_weights,
        bias_up,
        chips,
    )
    grad_norm_two = grad_norm_two + swap_cores(grad_norm_other)
    branch = branch + swap_cores(branch_other) + bias_down
    block_output = (second + scale_two * branch).astype(jnp.bfloat16)
    grad_scale_two = jnp.sum(grad_rows * branch, axis=0)
    grad_bias_down = jnp.sum(grad_branch.astype(jnp.float32), axis=0)
    second_part, grad_gain_two, grad_shift_two = norm_two_back(grad_norm_two)
    grad_second = grad_rows + second_part
    grad_scale_one = jnp.sum(grad_second * projected, axis=0)
    grad_projected = (scale_one * grad_second).astype(jnp.bfloat16)
    grad_bias_out = jnp.sum(grad_projected.astype(jnp.float32), axis=0)
    grad_attended = inner_cols(grad_projected, whole_out).astype(jnp.bfloat16)
    grad_stream = lax.all_to_all(
        grad_attended.reshape(rows, group, lanes).transpose(1, 0, 2),
        seq,
        split_axis=0,
        concat_axis=0,
        tiled=True,
    ).reshape(length, lanes)
    grad_out = inner_rows(attended_rows, grad_projected).astype(jnp.bfloat16)
    grad_out = grad_out.reshape(chips, 2 * share, width)
    outer, inner = lax.axis_size("outer"), lax.axis_size("inner")
    grad_up, grad_out, grad_down = (
        value.reshape(outer, inner, line, -1, width) for value in (grad_up, grad_out, grad_down)
    )
    begun = (
        scatter_terms(grad_up, "inner", 1),
        scatter_terms(grad_out, "inner", 1),
        scatter_terms(grad_down, "outer", 0),
    )
    out_terms, whole_in, grad_stream = lax.optimization_barrier((begun[1], whole_in, grad_stream))
    begun = (begun[0], out_terms, begun[2])
    grad_mixed_stream = attend_back(starts, query, keys, values, wide, logs, grad_stream)
    grad_mixed = lax.all_to_all(
        grad_mixed_stream.reshape(group, rows, 3 * lanes), seq, split_axis=0, concat_axis=0, tiled=True
    )
    begun, grad_mixed_stream = lax.optimization_barrier((begun, grad_mixed_stream))
    grad_up, grad_out, grad_down = (rounded_sum(*terms) for terms in begun)
    grad_down = scatter_line(grad_down, "inner", 0)
    grad_up = scatter_line(jnp.concatenate([grad_up, grad_out], axis=2), "outer", 0)
    plane_sums = jnp.concatenate([grad_up, grad_down], axis=1)
    moving = scatter_send(scatter_payload(plane_sums, "line", None, 1), "line", 1)
    moving, grad_mixed = lax.optimization_barrier((moving, grad_mixed))
    grad_in = inner_rows(normed_one, grad_mixed_stream).astype(jnp.bfloat16)
    parts = grad_in.reshape(outer, inner, group * share, 3 * lanes)
    parts = scatter_line(scatter_line(parts, "inner", 1), "outer", 0)
    input_grad, grad_gain_one, grad_shift_one, mixed_sums = finish(
        grad_mixed, whole_in, tokens, grad_second, gain_one
    )
    for step in range(2, line):
        payload = scatter_payload(plane_sums, "line", moving, step)
        if step == 3:
            payload, parts, grad_gain_one = lax.optimization_barrier((payload, parts, grad_gain_one))
        moving = scatter_send(payload, "line", step)
    summed = rounded_sum(
        lax.dynamic_index_in_dim(plane_sums, lax.axis_index("line"), 0, keepdims=False), *moving
    )
    parts = parts.reshape(group, share, 3 * lanes)
    parts = lax.all_to_all(parts, seq, split_axis=0, concat_axis=0, tiled=True)
    parts = parts.astype(jnp.float32)
    summed_in = parts.reshape(group, share, 3, lanes).transpose(1, 2, 0, 3).reshape(share, 3 * width)
    up_sums = grad_bias_up.reshape(chips, unit_block)
    up_sums = jnp.where(
        (lax.broadcasted_iota(jnp.int32, (1, 2, 1), 1) == core), up_sums[:, None, :], 0.0
    )
    grad_small = jnp.concatenate(
        [
            jnp.stack(
                [
                    grad_gain_one[0],
                    grad_shift_one[0],
                    mixed_sums[0, 0],
                    mixed_sums[2, 0],
                    grad_bias_out,
                    grad_scale_one,
                    grad_gain_two,
                    grad_shift_two,
                    grad_bias_down,
                    grad_scale_two,
                ]
            ),
            up_sums.reshape(-1, width),
        ],
        axis=0,
    )
    small_rows = grad_small.shape[0]
    parts = grad_small.reshape(small_rows, count, share).transpose(1, 0, 2)
    parts = lax.all_to_all(
        parts.reshape(count, small_rows * share), everyone, split_axis=0, concat_axis=0, tiled=True
    )
    summed_gains = jnp.sum(parts, axis=0).reshape(small_rows, share)

    up_sum = summed[:up_end].reshape(folds, 2, share, width)
    out_sum = summed[up_end : up_end + 2 * share].reshape(1, 2, share, width)
    both_sums = jnp.concatenate([up_sum, out_sum], axis=0)
    own_sums = jnp.where(first_core, both_sums[:, 0], both_sums[:, 1])
    other_sums = swap_cores(jnp.where(first_core, both_sums[:, 1], both_sums[:, 0]))
    summed_down = summed[up_end + 2 * share :].astype(jnp.float32)
    summed_out = own_sums[folds].astype(jnp.float32) + other_sums[folds].astype(jnp.float32)
    own_up = own_sums[:folds].transpose(1, 0, 2).reshape(share, chips, 1, unit_block)
    other_up = other_sums[:folds].transpose(1, 0, 2).reshape(share, chips, 1, unit_block)
    summed_up = in_order(own_up, other_up, 2).reshape(share, FF).astype(jnp.float32)
    rate_out = max(1, 4 * D // IMG_LEN) ** (-0.5)
    new_in, new_moment_in, new_square_in = adamw(
        project_in, moment_in, square_in, summed_in, D ** (-0.5), 0.04
    )
    new_out, new_moment_out, new_square_out = adamw(
        project_out, moment_out, square_out, summed_out, rate_out, 0.04
    )
    new_up, new_moment_up, new_square_up = adamw(
        hidden_up, moment_up, square_up, summed_up, D ** (-0.5), 0.04
    )
    new_down, new_moment_down, new_square_down = adamw(
        hidden_down, moment_down, square_down, summed_down, FF ** (-0.5), 0.04
    )
    new_gains, new_moment_gains, new_square_gains = adamw(
        gains_biases, moment_gains, square_gains, summed_gains, 0.2, 0.0
    )
    return (
        block_output,
        input_grad,
        new_in,
        new_out,
        new_up,
        new_down,
        new_gains,
        new_moment_in,
        new_moment_out,
        new_moment_up,
        new_moment_down,
        new_moment_gains,
        new_square_in,
        new_square_out,
        new_square_up,
        new_square_down,
        new_square_gains,
        summed_gains[8],
    )


def solution(mesh):
    streams, group = mesh.shape["fsdp"], mesh.shape["seq"]
    outer = math.isqrt(streams)
    fine = jax.sharding.Mesh(
        mesh.devices.reshape(outer, streams // outer, group // 2, 2),
        ("outer", "inner", "line", "core"),
    )
    return jax.shard_map(
        on_device,
        mesh=fine,
        in_specs=(
            P(("outer", "inner", "line", "core"), None),
            P(("outer", "inner", "line", "core"), None),
            P(("outer", "inner", "line", "core")),
            P(("outer", "inner", "line", "core")),
            P(("outer", "inner", "line", "core"), None),
            P(("outer", "inner", "line", "core"), None),
            P(("outer", "inner", "line", "core"), None),
            P(("outer", "inner", "line", "core"), None),
            P(None, ("outer", "inner", "line", "core")),
            P(("outer", "inner", "line", "core"), None),
            P(("outer", "inner", "line", "core"), None),
            P(("outer", "inner", "line", "core"), None),
            P(("outer", "inner", "line", "core"), None),
            P(None, ("outer", "inner", "line", "core")),
            P(("outer", "inner", "line", "core"), None),
            P(("outer", "inner", "line", "core"), None),
            P(("outer", "inner", "line", "core"), None),
            P(("outer", "inner", "line", "core"), None),
            P(None, ("outer", "inner", "line", "core")),
        ),
        out_specs=(
            P(("outer", "inner", "line", "core"), None),
            P(("outer", "inner", "line", "core"), None),
            P(("outer", "inner", "line", "core"), None),
            P(("outer", "inner", "line", "core"), None),
            P(("outer", "inner", "line", "core"), None),
            P(("outer", "inner", "line", "core"), None),
            P(None, ("outer", "inner", "line", "core")),
            P(("outer", "inner", "line", "core"), None),
            P(("outer", "inner", "line", "core"), None),
            P(("outer", "inner", "line", "core"), None),
            P(("outer", "inner", "line", "core"), None),
            P(None, ("outer", "inner", "line", "core")),
            P(("outer", "inner", "line", "core"), None),
            P(("outer", "inner", "line", "core"), None),
            P(("outer", "inner", "line", "core"), None),
            P(("outer", "inner", "line", "core"), None),
            P(None, ("outer", "inner", "line", "core")),
            P(("outer", "inner", "line", "core")),
        ),
        check_vma=False,
    )
```
